32 devices in a mesh: lat: 8 (over z, x), lev: 4 (over y, core).
Axes of the slice: x: 2, y: 2, z: 4, core: 2. Of those that a mesh axis runs over, the one named last changes fastest.
Arguments:
- fields: float32 [2, 32, 64, 3072], P(None, 'lat', 'lev'), may hold values from -6 to 6
- courant: bfloat16 [2, 32, 64, 3072], P(None, 'lat', 'lev'), may hold values from -0.3984375 to 0.3984375
- cutoffs: int32 [32], replicated, may hold values from 1 to 1536, as said below
- surface: float32 [32, 3072], P('lat'), may hold values from -6 to 6
- remap_weights: float32 [64, 64], replicated, may hold values from -0.25 to 0.75
Outputs:
- remapped: float32 [2, 32, 64, 3072], P(None, 'lat', None, 'lev')
- geopotential: float32 [32, 64, 3072], P('lat', None, 'lev')
The draws below stay inside these ranges and needn't reach their ends.
Inputs may be any that keep to these rules, and one draw needn't show every extreme that they name: cutoffs[j] is 1536 except on the first and the last 4 latitudes, where it lies between 1 and 127; it equals 127 on some latitude among the first 4.
All inputs are finite; a program needn't handle non-finite values.
Results may differ from the reference program's by a relative error of at most 0.0003.
Values may be sent and summed in bfloat16 or wider, within the bound.
No kernel may reach another device: no remote copies, remote signals or barrier semaphores. Data moves between devices by JAX's collectives and lax.ppermute only.
A program may use at most 64 MiB of HBM per device.

```python
import math
import jax
import jax.numpy as jnp
from jax import lax

NLON = 3072
NLEV = 64
KMAX = 128
NLAT = 32
POLAR_ROWS = 4


def draw_cutoffs(key, part):
    latitude = jnp.arange(NLAT, dtype=jnp.int32)
    polar_band = (latitude < POLAR_ROWS) | (latitude >= NLAT - POLAR_ROWS)
    random_cut = jax.random.randint(jax.random.fold_in(key, 11), (NLAT,), 1, KMAX, dtype=jnp.int32)
    position = jax.random.randint(jax.random.fold_in(key, 12), (), 0, POLAR_ROWS, dtype=jnp.int32)
    random_cut = jnp.where(latitude == position, KMAX - 1, random_cut)
    return jnp.where(polar_band, random_cut, NLON // 2).astype(jnp.int32)


def draw_remap_weights(key, part):
    noise_draw = jax.random.truncated_normal(jax.random.fold_in(key, 22), -4.0, 4.0, (NLEV, NLEV), jnp.float32)
    return (0.5 * jnp.eye(NLEV, dtype=jnp.float32) + noise_draw * (0.5 / math.sqrt(NLEV))).astype(jnp.float32)


def block_scale(stream_key, extent, split, low, largest):
    def one(dim, blocks):
        draws = jax.random.uniform(jax.random.fold_in(jax.random.fold_in(stream_key, 6), dim), (blocks,), jnp.float32, low / len(split), largest / len(split))
        return jnp.repeat(jnp.exp(draws), extent[dim] // blocks).reshape((-1,) + (1,) * (len(extent) - dim - 1))

    loudness = one(*split[0])
    for cut in split[1:]:
        loudness = loudness * one(*cut)
    return loudness


def bell_draw(key, dims, deviation, limit, cuts=(), kind=jnp.bfloat16):
    drawn = jax.random.normal(key, dims, jnp.float32) * deviation
    if len(cuts) > 0:
        drawn = block_scale(key, dims, cuts, -0.22, 0.18) * drawn
    return jnp.clip(drawn, min=-limit, max=limit).astype(kind)


def setup_inputs(seed: int = 0) -> dict:
    splits = jax.random.split(jax.random.key(seed), 6)
    return {
        "fields": bell_draw(splits[0], (2, NLAT, NLEV, NLON), 1.0, 6.0, ((1, 8), (2, 4)), jnp.float32),
        "courant": jnp.clip(jax.random.uniform(splits[1], (2, NLAT, NLEV, NLON), jnp.float32, -0.3984375, 0.3984375) * block_scale(splits[1], (2, NLAT, NLEV, NLON), ((1, 8), (2, 4)), -0.4, 0.0), -0.3984375, 0.3984375).astype(jnp.bfloat16),
        "cutoffs": draw_cutoffs(jax.random.fold_in(splits[5], 71), 0),
        "surface": bell_draw(splits[3], (NLAT, NLON), 1.0, 6.0, ((0, 8),), jnp.float32),
        "remap_weights": draw_remap_weights(jax.random.fold_in(splits[5], 71), 0),
    }


def lon_part(values, east_wind):
    interface = (7.0 * (values + jnp.roll(values, -1, -1)) - (jnp.roll(values, 1, -1) + jnp.roll(values, -2, -1))) / 12.0
    face_wind = 0.5 * (east_wind + jnp.roll(east_wind, -1, -1))
    flux_faces = face_wind * interface
    return flux_faces - jnp.roll(flux_faces, 1, -1)


def lat_part(padded, north_wind):
    row_count = padded.shape[1] - 4
    interface = (7.0 * (padded[:, 1:row_count + 2] + padded[:, 2:row_count + 3]) - (padded[:, 0:row_count + 1] + padded[:, 3:row_count + 4])) / 12.0
    face_wind = 0.5 * (north_wind[0:row_count + 1] + north_wind[1:row_count + 2])
    flux_faces = face_wind * interface
    return flux_faces[:, 1:] - flux_faces[:, :-1]


def polar_filter(values, cutoffs):
    spectrum = jnp.fft.rfft(values, axis=-1)
    wave_numbers = jnp.arange(NLON // 2 + 1)
    kept_modes = wave_numbers[None, :] <= cutoffs[:, None]
    lowpass = jnp.fft.irfft(spectrum * kept_modes[None], n=NLON, axis=-1).astype(values.dtype)
    return jnp.where((cutoffs < NLON // 2)[None, :, None], lowpass, values)


def reference(fields, courant, cutoffs, surface, remap_weights):
    def per_level(level_index):
        values = lax.dynamic_index_in_dim(fields, level_index, 2, keepdims=False)
        winds = lax.dynamic_index_in_dim(courant, level_index, 2, keepdims=False).astype(jnp.float32)
        east_wind = winds[0]
        north_wind = jnp.pad(winds[1], ((1, 1), (0, 0)))
        for repeat in range(2):
            padded = jnp.pad(values, ((0, 0), (2, 2), (0, 0)))
            values = values - lon_part(values, east_wind) - lat_part(padded, north_wind)
            values = polar_filter(values, cutoffs)
        return values

    transported = lax.map(per_level, jnp.arange(NLEV, dtype=jnp.int32))
    remapped = jnp.einsum('pk,kfjn->fjpn', remap_weights, transported, precision=lax.Precision.HIGHEST)
    heat_rows = transported[:, 1]
    upward = jnp.cumsum(heat_rows[::-1], axis=0)[::-1]
    geo_scale = NLEV ** -0.5
    geo_levels = surface[None] + geo_scale * (upward - 0.5 * heat_rows)
    geopotential = jnp.transpose(geo_levels, (1, 0, 2))
    return remapped, geopotential
```

```python
import functools
import math

import jax
import jax.numpy as jnp
import ml_dtypes
import numpy as np
from jax import lax
from jax.experimental import pallas as pl
from jax.experimental.pallas import tpu as pltpu
from jax.sharding import PartitionSpec as P

KMAX = 128
LANE = 128
TOP = 32767.0
STEPS = 256.0
TINY = 2.0**-100
WIND = 81920.0
ROUND = 1.5 * 2.0**23
VMEM_LIMIT = 48 * 2**20


def rounded(values):
    return ((values + ROUND) - ROUND).astype(jnp.int32).astype(jnp.int16)


def lane_max(values):
    chunks = [jnp.abs(values[:, i : i + LANE]) for i in range(0, values.shape[1], LANE)]
    while len(chunks) > 1:
        pairs = [jnp.maximum(a, b) for a, b in zip(chunks[0::2], chunks[1::2])]
        chunks = pairs + chunks[2 * len(pairs) :]
    return chunks[0]


def tiled(tile, width):
    return jnp.concatenate([tile] * (width // LANE), axis=1)


def scale_code(largest):
    return jnp.ceil(jnp.log2(jnp.maximum(largest, TINY)) * STEPS)


def encoder(code):
    return TOP / jnp.exp2(code * (1.0 / STEPS))


def decoder(code16):
    code = code16.astype(jnp.int32).astype(jnp.float32)
    return jnp.exp2(code * (1.0 / STEPS)) * (1.0 / TOP)


def encode_row(values, out_ref, at):
    width = values.shape[1]
    code = scale_code(lane_max(values))
    out_ref[:, at : at + width] = rounded(values * tiled(encoder(code), width))
    out_ref[:, at + width : at + width + LANE] = code.astype(jnp.int32).astype(jnp.int16)


def decode_row(in_ref, at, width):
    scale = decoder(in_ref[:, at + width : at + width + LANE])
    values = in_ref[:, at : at + width].astype(jnp.int32).astype(jnp.float32)
    return values * tiled(scale, width)


def wind_codes(east, north):
    return rounded(jnp.concatenate([east, north], axis=0) * WIND)


class Sizes:
    def __init__(self, rows, levels, lon):
        self.rows, self.levels, self.lon = rows, levels, lon
        self.half = levels // 2
        self.band = 2 * rows
        self.pad = lon + 2 * LANE
        self.code = lon + LANE
        self.edge = 2 * self.code + lon
        self.inner = 2 * self.code + 3 * lon


def put_padded(ref, index, values, lon):
    ref[index + (Ellipsis, slice(LANE, LANE + lon))] = values
    ref[index + (Ellipsis, slice(0, LANE))] = values[..., lon - LANE :]
    ref[index + (Ellipsis, slice(LANE + lon, 2 * LANE + lon))] = values[..., :LANE]


def pack_kernel(z, par_ref, fields_ref, courant_ref, edge_ref, inner_ref, own_ref):
    p = par_ref[0]
    keep = pl.multiple_of(p * z.half, z.half)
    give = pl.multiple_of((1 - p) * z.half, z.half)

    def field_row(row, start):
        return jnp.concatenate([fields_ref[f, row, pl.ds(start, z.half)] for f in range(2)], axis=0)

    def wind_row(row, upper):
        halves = []
        for k in range(2):
            wind = courant_ref[k, row].astype(jnp.float32)
            halves.append(jnp.where(upper == 1, wind[z.half :], wind[: z.half]))
        return wind_codes(*halves)

    edge, inner = 2 * p, 2 * (1 - p)
    outer = 3 * p
    for r in range(2):
        encode_row(field_row(edge + r, give), edge_ref, r * z.code)
        encode_row(field_row(edge + r, keep), own_ref, r * z.code)
        encode_row(field_row(inner + r, give), inner_ref, r * z.code)
    at = 2 * z.code
    edge_ref[:, at : at + z.lon] = wind_row(outer, 1 - p)
    own_ref[:, at : at + z.lon] = wind_row(outer, p)
    for i, row in enumerate((inner, inner + 1, 1 + p)):
        inner_ref[:, at + i * z.lon : at + (i + 1) * z.lon] = wind_row(row, 1 - p)


def substep(z, u_ref, fwx_ref, fwy_ref, write):
    width = next(w for w in (768, 512, 384, 256, 128) if z.lon % w == 0)
    wide = width + 2 * LANE

    def part(i, carry):
        at = pl.multiple_of(i * width, LANE)
        mid = pl.multiple_of(at + LANE, LANE)
        for f in range(2):

            def middle(j):
                return u_ref[j, f, :, pl.ds(mid, width)]

            rows = [middle(j) for j in range(4)]
            sums = [rows[0] + rows[1], rows[1] + rows[2], rows[2] + rows[3]]
            flux = None
            for j in range(z.band + 1):
                face = fwy_ref[j, :, pl.ds(at, width)]
                new = face * (8.0 * sums[1] - (sums[0] + sums[2]))
                if j > 0:
                    u = u_ref[j + 1, f, :, pl.ds(at, wide)]
                    pair = u + pltpu.roll(u, wide - 1, 1)
                    high = pltpu.roll(pair, wide - 1, 1)
                    low = pltpu.roll(pair, 1, 1)
                    fx = fwx_ref[j - 1, :, pl.ds(at, wide)] * (8.0 * pair - (low + high))
                    change = fx - pltpu.roll(fx, 1, 1)
                    out = u[:, LANE : LANE + width] - change[:, LANE : LANE + width] - (new - flux)
                    write(j - 1, f, at, width, out)
                flux = new
                if j < z.band:
                    above = middle(j + 4)
                    rows = rows[1:] + [above]
                    sums = sums[1:] + [rows[2] + rows[3]]
        return carry

    lax.fori_loop(0, z.lon // width, part, 0)


def filter_tables(lon):
    points = np.arange(lon // 2)
    forward, back = [], []
    for parity in range(2):
        waves = np.arange(parity, KMAX, 2)
        angle = (points[:, None] * waves[None, :] % lon) * (2.0 * math.pi / lon)
        table = np.concatenate([np.cos(angle), np.sin(angle)], axis=1).astype(np.float32)
        high = table.astype(ml_dtypes.bfloat16)
        low = (table - high.astype(np.float32)).astype(ml_dtypes.bfloat16)
        forward.append(np.concatenate([high, low], axis=1))
        back.append(np.concatenate([high.T, low.T], axis=0))
    return np.stack(forward), np.stack(back)


def split(values):
    high = values.astype(jnp.bfloat16)
    return high, (values - high.astype(jnp.float32)).astype(jnp.bfloat16)


def low_pass(z, rows, cuts, forward_ref, back_ref):
    half = z.lon // 2
    count = len(rows)
    tall = 2 * z.half
    total = count * tall
    flat = [row.reshape(tall, z.lon) for row in rows]
    folded = []
    for parity in range(2):
        parts = [
            row[:, :half] + row[:, half:] if parity == 0 else row[:, :half] - row[:, half:]
            for row in flat
        ]
        high, low = split(jnp.concatenate(parts, axis=0))
        both = jnp.concatenate([high, low], axis=0)
        got = jnp.dot(both, forward_ref[parity], preferred_element_type=jnp.float32)
        wave = got[:total, :KMAX] + got[:total, KMAX:] + (got[total:, :KMAX] + got[total:, KMAX:])
        number = 2 * (lax.broadcasted_iota(jnp.int32, (tall, KMAX), 1) % (KMAX // 2)) + parity
        doubled = jnp.where(number == 0, 1.0, 2.0) * (1.0 / z.lon)
        weight = jnp.concatenate([jnp.where(number <= cut, doubled, 0.0) for cut in cuts], axis=0)
        high, low = split(wave * weight)
        both = jnp.concatenate(
            [jnp.concatenate([high, high], axis=1), jnp.concatenate([low, low], axis=1)], axis=0
        )
        got = jnp.dot(both, back_ref[parity], preferred_element_type=jnp.float32)
        folded.append(got[:total] + got[total:])
    left, right = folded[0] + folded[1], folded[0] - folded[1]
    smooth = jnp.concatenate([left, right], axis=1)
    return [smooth[i * tall : (i + 1) * tall].reshape(2, z.half, z.lon) for i in range(count)]


def filter_band(z, cut_ref, first_row, forward_ref, back_ref, load, store):
    nyquist = z.lon // 2
    for part in range(2):
        start = part * z.rows
        cuts = [cut_ref[first_row + start + r] for r in range(z.rows)]
        some = functools.reduce(jnp.logical_or, [cut < nyquist for cut in cuts])

        @pl.when(some)
        def _():
            rows = [load(start + r) for r in range(z.rows)]
            smooth = low_pass(z, rows, cuts, forward_ref, back_ref)
            for r in range(z.rows):

                @pl.when(cuts[r] < nyquist)
                def _():
                    store(start + r, smooth[r])


def first_kernel(
    z, par_ref, fields_ref, courant_ref, edge_ref, inner_ref, near_ref, far_ref,
    new_ref, fwx_ref, fwy_ref, down_ref, up_ref, u_ref, cx_ref, cy_ref,
):
    p = par_ref[0]
    lon, half = z.lon, z.half

    def pair(values):
        return values.reshape(2, half, values.shape[1])

    def winds(in_ref, at):
        values = in_ref[:, at : at + lon].astype(jnp.int32).astype(jnp.float32) * (1.0 / WIND)
        return values[:half], values[half:]

    def place_wind(row, east, north):
        put_padded(cx_ref, (row,), east, lon)
        cy_ref[row + 1] = north

    keep = pl.multiple_of(p * half, half)
    for r in range(z.rows):
        row = z.rows * p + r
        own = jnp.stack([fields_ref[f, r, pl.ds(keep, half)] for f in range(2)])
        put_padded(u_ref, (row + 2,), own, lon)
        got = []
        for k in range(2):
            wind = courant_ref[k, r].astype(jnp.float32)
            got.append(jnp.where(p == 1, wind[half:], wind[:half]))
        place_wind(row, *got)
    at = 2 * z.code
    for r in range(2):
        put_padded(u_ref, (6 * (1 - p) + r + 2,), pair(decode_row(edge_ref, r * z.code, lon)), lon)
        put_padded(u_ref, (4 - 2 * p + r + 2,), pair(decode_row(inner_ref, r * z.code, lon)), lon)
        put_padded(u_ref, (10 * (1 - p) + r,), pair(decode_row(near_ref, r * z.code, lon)), lon)
        put_padded(u_ref, (10 * p + r,), pair(decode_row(far_ref, r * z.code, lon)), lon)
        place_wind(4 - 2 * p + r, *winds(inner_ref, at + r * lon))
    place_wind(7 * (1 - p), *winds(edge_ref, at))
    place_wind(6 - 5 * p, *winds(inner_ref, at + 2 * lon))
    cy_ref[9 * (1 - p)] = winds(near_ref, at)[1]
    cy_ref[9 * p] = winds(far_ref, at)[1]

    def face_rows(j, carry):
        wind = cx_ref[j]
        fwx_ref[j] = (wind + pltpu.roll(wind, z.pad - 1, 1)) * (1.0 / 24.0)
        return carry

    lax.fori_loop(0, z.band, face_rows, 0)

    def face_cols(j, carry):
        fwy_ref[j] = (cy_ref[j] + cy_ref[j + 1]) * (1.0 / 24.0)
        return carry

    lax.fori_loop(0, z.band + 1, face_cols, 0)

    def write(row, f, at, width, values):
        new_ref[row, f, :, pl.ds(pl.multiple_of(at + LANE, LANE), width)] = values

    substep(z, u_ref, fwx_ref, fwy_ref, write)
    for r in range(2):
        for row, out_ref in ((r, down_ref), (z.band - 2 + r, up_ref)):
            values = new_ref[row, :, :, LANE : LANE + lon]
            encode_row(values.reshape(2 * half, lon), out_ref, r * z.code)

    def wrap(j, carry):
        new_ref[j, :, :, 0:LANE] = new_ref[j, :, :, lon : lon + LANE]
        new_ref[j, :, :, LANE + lon :] = new_ref[j, :, :, LANE : 2 * LANE]
        return carry

    lax.fori_loop(0, z.band, wrap, 0)


def filter_kernel(z, par_ref, cut_ref, forward_ref, back_ref, new_in_ref, new_ref):
    del new_in_ref
    first_row = par_ref[1]

    def store(row, values):
        put_padded(new_ref, (row,), values, z.lon)

    filter_band(
        z, cut_ref, first_row, forward_ref, back_ref,
        lambda row: new_ref[row, :, :, LANE : LANE + z.lon], store,
    )


def second_kernel(
    z, parts, par_ref, cut_ref, new_ref, fwx_ref, fwy_ref, below_ref, above_ref, forward_ref,
    back_ref, out_ref, u_ref, v_ref,
):
    first_row = par_ref[1]
    lon, half = z.lon, z.half
    tall = 2 * half
    for r in range(2):
        for row, in_ref in ((r, below_ref), (z.band + 2 + r, above_ref)):
            values = decode_row(in_ref, r * z.code, lon).reshape(2, half, lon)
            put_padded(u_ref, (row,), values, lon)

    def copy(j, carry):
        u_ref[j + 2] = new_ref[j]
        return carry

    lax.fori_loop(0, z.band, copy, 0)

    def write(row, f, at, width, values):
        v_ref[row, f, :, pl.ds(at, width)] = values

    substep(z, u_ref, fwx_ref, fwy_ref, write)

    def store(row, values):
        v_ref[row] = values

    filter_band(
        z, cut_ref, first_row, forward_ref, back_ref, lambda row: v_ref[row], store
    )
    column = lon // parts
    for side in range(2):
        for d in range(parts):
            values = jnp.concatenate(
                [
                    v_ref[side * z.rows + r, :, :, d * column : (d + 1) * column].reshape(tall, column)
                    for r in range(z.rows)
                ],
                axis=1,
            )
            encode_row(values, out_ref.at[side * parts + d], 0)


def column_kernel(z, parts, par_ref, got_ref, remap_ref, upward_ref, surface_ref, out_ref, geo_ref):
    r = pl.program_id(0)
    column = out_ref.shape[-1]
    count = 2 * parts
    at = pl.multiple_of(r * column, LANE)
    tiles = []
    for s in range(parts):
        for side in range(2):
            i = side * parts + s
            scale = decoder(got_ref[i, :, z.rows * column : z.rows * column + LANE])
            codes = got_ref[i, :, pl.ds(at, column)].astype(jnp.int32).astype(jnp.float32)
            tiles.append(codes * tiled(scale, column))
    high, low = split(remap_ref[...])
    remap = jnp.concatenate([high, low, high], axis=1)
    for f in range(2):
        values = jnp.concatenate([t[f * z.half : (f + 1) * z.half] for t in tiles], axis=0)
        high, low = split(values)
        stacked = jnp.concatenate([high, high, low], axis=0)
        out_ref[f, 0] = jnp.dot(remap, stacked, preferred_element_type=jnp.float32)
        if f == 1:
            upward = jnp.dot(upward_ref[...], stacked, preferred_element_type=jnp.float32)
            surface = surface_ref[0]
            geo_ref[0] = surface + upward * (out_ref.shape[2] ** -0.5)


def whole():
    return pl.BlockSpec(memory_space=pltpu.VMEM)


def scalars():
    return pl.BlockSpec(memory_space=pltpu.SMEM)


def params():
    return pltpu.CompilerParams(vmem_limit_bytes=VMEM_LIMIT)


def cost(flops, data):
    return pl.CostEstimate(flops=flops, bytes_accessed=data, transcendentals=0)


def shards(fields, courant, cutoffs, surface, remap_weights):
    _, rows, levels, lon = fields.shape
    z = Sizes(rows, levels, lon)
    lats, parts = lax.axis_size("lat"), lax.axis_size("lev")
    me = lax.axis_index("lat")
    parity = me % 2
    place = jnp.stack([parity, (me - parity) * rows]).astype(jnp.int32)
    tall = 2 * z.half
    i16, f32 = jnp.int16, jnp.float32
    swap = [(i, i ^ 1) for i in range(lats)]
    rising = [(i, i + 2) for i in range(lats - 2)]
    falling = [(i + 2, i) for i in range(lats - 2)]
    near_pairs = [(i, j) for i, j in rising if i % 2 == 1] + [(i, j) for i, j in falling if i % 2 == 0]
    far_pairs = [(i, j) for i, j in rising if i % 2 == 0] + [(i, j) for i, j in falling if i % 2 == 1]

    edge, inner, own = pl.pallas_call(
        functools.partial(pack_kernel, z),
        name="pack",
        in_specs=[scalars(), whole(), whole()],
        out_specs=[whole()] * 3,
        out_shape=[
            jax.ShapeDtypeStruct((tall, z.edge), i16),
            jax.ShapeDtypeStruct((tall, z.inner), i16),
            jax.ShapeDtypeStruct((tall, z.edge), i16),
        ],
        compiler_params=params(),
        cost_estimate=cost(10**7, 5 * 10**6),
    )(place, fields, courant)
    edge = lax.ppermute(edge, "lat", swap)
    near = lax.ppermute(own, "lat", near_pairs)
    inner = lax.ppermute(inner, "lat", swap)
    far = lax.ppermute(edge, "lat", far_pairs)

    new, fwx, fwy, down, up = pl.pallas_call(
        functools.partial(first_kernel, z),
        name="first",
        in_specs=[scalars()] + [whole()] * 6,
        out_specs=[whole()] * 5,
        out_shape=[
            jax.ShapeDtypeStruct((z.band, 2, z.half, z.pad), f32),
            jax.ShapeDtypeStruct((z.band, z.half, z.pad), f32),
            jax.ShapeDtypeStruct((z.band + 1, z.half, z.lon), f32),
            jax.ShapeDtypeStruct((tall, 2 * z.code), i16),
            jax.ShapeDtypeStruct((tall, 2 * z.code), i16),
        ],
        scratch_shapes=[
            pltpu.VMEM((z.band + 4, 2, z.half, z.pad), f32),
            pltpu.VMEM((z.band, z.half, z.pad), f32),
            pltpu.VMEM((z.band + 2, z.half, z.lon), f32),
        ],
        compiler_params=params(),
        cost_estimate=cost(4 * 10**7, 8 * 10**6),
    )(place, fields, courant, edge, inner, near, far)
    above = lax.ppermute(down, "lat", falling)
    below = lax.ppermute(up, "lat", rising)

    forward, back = (jnp.asarray(t) for t in filter_tables(lon))
    new = pl.pallas_call(
        functools.partial(filter_kernel, z),
        name="smooth",
        in_specs=[scalars(), scalars()] + [whole()] * 3,
        out_specs=whole(),
        out_shape=jax.ShapeDtypeStruct(new.shape, f32),
        input_output_aliases={4: 0},
        compiler_params=params(),
        cost_estimate=cost(10**9, 6 * 10**6),
    )(place, cutoffs, forward, back, new)

    column = lon // parts
    codes = pl.pallas_call(
        functools.partial(second_kernel, z, parts),
        name="second",
        in_specs=[scalars(), scalars()] + [whole()] * 7,
        out_specs=whole(),
        out_shape=jax.ShapeDtypeStruct((2 * parts, tall, rows * column + LANE), i16),
        scratch_shapes=[
            pltpu.VMEM((z.band + 4, 2, z.half, z.pad), f32),
            pltpu.VMEM((z.band, 2, z.half, lon), f32),
        ],
        compiler_params=params(),
        cost_estimate=cost(10**9, 8 * 10**6),
    )(place, cutoffs, new, fwx, fwy, below, above, forward, back)
    groups = [[i * parts + j for i in (a, a + 1) for j in range(parts)] for a in range(0, lats, 2)]
    got = lax.all_to_all(codes, ("lat", "lev"), 0, 0, axis_index_groups=groups, tiled=True)

    count = remap_weights.shape[0]
    upward = np.triu(np.ones((count, count), np.float32), 1) + 0.5 * np.eye(count, dtype=np.float32)
    upward = jnp.asarray(
        np.concatenate([upward, 0.0 * upward, upward], axis=1).astype(ml_dtypes.bfloat16)
    )
    mine = lax.dynamic_slice_in_dim(surface, lax.axis_index("lev") * column, column, 1)
    remapped, geopotential = pl.pallas_call(
        functools.partial(column_kernel, z, parts),
        name="columns",
        grid=(rows,),
        in_specs=[
            scalars(),
            pl.BlockSpec(got.shape, lambda r: (0, 0, 0)),
            pl.BlockSpec(remap_weights.shape, lambda r: (0, 0)),
            pl.BlockSpec(upward.shape, lambda r: (0, 0)),
            pl.BlockSpec((1, 1, column), lambda r: (r, 0, 0)),
        ],
        out_specs=[
            pl.BlockSpec((2, 1, count, column), lambda r: (0, r, 0, 0)),
            pl.BlockSpec((1, count, column), lambda r: (r, 0, 0)),
        ],
        out_shape=[
            jax.ShapeDtypeStruct((2, rows, count, column), f32),
            jax.ShapeDtypeStruct((rows, count, column), f32),
        ],
        compiler_params=params(),
        cost_estimate=cost(10**8, 4 * 10**6),
    )(place, got, remap_weights, upward, mine[:, None, :])
    return remapped, geopotential


def with_halo(shard, width):
    size, length = lax.axis_size("lat"), shard.shape[1]
    up = [(i, (i + 1) % size) for i in range(size - 1)]
    down = [(j, i) for i, j in up]
    before = lax.ppermute(lax.slice_in_dim(shard, length - width, length, axis=1), "lat", up)
    after = lax.ppermute(lax.slice_in_dim(shard, 0, width, axis=1), "lat", down)
    return jnp.concatenate([before, shard, after], axis=1)


def plain_shards(fields, courant, cutoffs, surface, remap_weights):
    _, rows, _, lon = fields.shape
    exact = lax.Precision.HIGHEST
    cut = lax.dynamic_slice_in_dim(cutoffs, lax.axis_index("lat") * rows, rows)
    waves = np.arange(KMAX)
    angle = (np.arange(lon)[:, None] * waves[None, :] % lon) * (2.0 * math.pi / lon)
    table = jnp.asarray(np.concatenate([np.cos(angle), np.sin(angle)], axis=1).astype(np.float32))
    number = jnp.asarray(np.concatenate([waves, waves]).astype(np.int32))
    weight = jnp.where(number[None] <= cut[:, None], jnp.where(number == 0, 1.0, 2.0)[None] / lon, 0.0)
    flagged = cut < lon // 2

    def smooth(values):
        wave = jnp.einsum("frln,nk->frlk", values, table, precision=exact) * weight[None, :, None]
        low = jnp.einsum("frlk,nk->frln", wave, table, precision=exact)
        return jnp.where(flagged[None, :, None, None], low, values)

    winds = with_halo(courant, 1).astype(jnp.float32)
    east, north = winds[0, 1:-1], winds[1]
    face_x = (east + jnp.roll(east, -1, -1)) / 24.0
    face_y = (north[:-1] + north[1:]) / 24.0
    u = fields
    for _ in range(2):
        wide = with_halo(u, 2)
        pair = u + jnp.roll(u, -1, -1)
        fx = face_x * (8.0 * pair - (jnp.roll(pair, 1, -1) + jnp.roll(pair, -1, -1)))
        pair = wide[:, :-1] + wide[:, 1:]
        fy = face_y * (8.0 * pair[:, 1:-1] - (pair[:, :-2] + pair[:, 2:]))
        u = u - (fx - jnp.roll(fx, 1, -1)) - (fy[:, 1:] - fy[:, :-1])
        u = lax.cond(jnp.any(flagged), smooth, lambda values: values, u)
    columns = lax.all_to_all(u, "lev", split_axis=3, concat_axis=2, tiled=True)
    remapped = jnp.einsum("pk,fjkn->fjpn", remap_weights, columns, precision=exact)
    count = remap_weights.shape[0]
    upward = np.triu(np.ones((count, count), np.float32), 1) + 0.5 * np.eye(count, dtype=np.float32)
    upward = jnp.einsum("kl,jln->jkn", jnp.asarray(upward), columns[1], precision=exact)
    width = lon // lax.axis_size("lev")
    mine = lax.dynamic_slice_in_dim(surface, lax.axis_index("lev") * width, width, 1)
    return remapped, mine[:, None] + count**-0.5 * upward


def solution(mesh):
    def program(fields, courant, cutoffs, surface, remap_weights):
        lats, parts = mesh.shape["lat"], mesh.shape["lev"]
        rows, levels = fields.shape[1] // lats, fields.shape[2] // parts
        polar = fields.shape[1] // 8
        paired = (
            lats % 2 == 0
            and rows == 4
            and levels % 16 == 0
            and polar <= 2 * rows - 2
            and fields.shape[3] % (LANE * parts) == 0
        )
        return jax.shard_map(
            shards if paired else plain_shards,
            mesh=mesh,
            in_specs=(
                P(None, "lat", "lev", None),
                P(None, "lat", "lev", None),
                P(),
                P("lat", None),
                P(),
            ),
            out_specs=(P(None, "lat", None, "lev"), P("lat", None, "lev")),
            check_vma=False,
        )(fields, courant, cutoffs, surface, remap_weights)

    return program
```

```python
import functools
import math

import jax
import jax.numpy as jnp
import ml_dtypes
import numpy as np
from jax import lax
from jax.experimental import pallas as pl
from jax.experimental.pallas import tpu as pltpu
from jax.sharding import PartitionSpec as P

KMAX = 128
LANE = 128
TOP = 32767.0
STEPS = 256.0
TINY = 2.0**-100
WIND = 81920.0
ROUND = 1.5 * 2.0**23
VMEM_LIMIT = 32 * 2**20


def rounded(values):
    return ((values + ROUND) - ROUND).astype(jnp.int32).astype(jnp.int16)


def lane_max(values):
    chunks = [jnp.abs(values[:, i : i + LANE]) for i in range(0, values.shape[1], LANE)]
    while len(chunks) > 1:
        pairs = [jnp.maximum(a, b) for a, b in zip(chunks[0::2], chunks[1::2])]
        chunks = pairs + chunks[2 * len(pairs) :]
    return chunks[0]


def tiled(tile, width):
    return jnp.concatenate([tile] * (width // LANE), axis=1)


def scale_code(largest):
    return jnp.ceil(jnp.log2(jnp.maximum(largest, TINY)) * STEPS)


def encoder(code):
    return TOP / jnp.exp2(code * (1.0 / STEPS))


def decoder(code16):
    code = code16.astype(jnp.int32).astype(jnp.float32)
    return jnp.exp2(code * (1.0 / STEPS)) * (1.0 / TOP)


def encode_row(values, out_ref, at):
    width = values.shape[1]
    code = scale_code(lane_max(values))
    out_ref[:, at : at + width] = rounded(values * tiled(encoder(code), width))
    out_ref[:, at + width : at + width + LANE] = code.astype(jnp.int32).astype(jnp.int16)


def decode_row(in_ref, at, width):
    scale = decoder(in_ref[:, at + width : at + width + LANE])
    values = in_ref[:, at : at + width].astype(jnp.int32).astype(jnp.float32)
    return values * tiled(scale, width)


def wind_codes(east, north):
    return rounded(jnp.concatenate([east, north], axis=0) * WIND)


class Sizes:
    def __init__(self, rows, levels, lon):
        self.rows, self.levels, self.lon = rows, levels, lon
        self.half = levels // 2
        self.band = 2 * rows
        self.pad = lon + 2 * LANE
        self.code = lon + LANE
        self.edge = 2 * self.code + lon
        self.inner = 2 * self.code + 3 * lon


def put_padded(ref, index, values, lon):
    ref[index + (Ellipsis, slice(LANE, LANE + lon))] = values
    ref[index + (Ellipsis, slice(0, LANE))] = values[..., lon - LANE :]
    ref[index + (Ellipsis, slice(LANE + lon, 2 * LANE + lon))] = values[..., :LANE]


def pack_kernel(z, par_ref, fields_ref, courant_ref, edge_ref, inner_ref, own_ref):
    p = par_ref[0]
    keep = pl.multiple_of(p * z.half, z.half)
    give = pl.multiple_of((1 - p) * z.half, z.half)

    def field_row(row, start):
        return jnp.concatenate([fields_ref[f, row, pl.ds(start, z.half)] for f in range(2)], axis=0)

    def wind_row(row, upper):
        halves = []
        for k in range(2):
            wind = courant_ref[k, row].astype(jnp.float32)
            halves.append(jnp.where(upper == 1, wind[z.half :], wind[: z.half]))
        return wind_codes(*halves)

    edge, inner = 2 * p, 2 * (1 - p)
    outer = 3 * p
    for r in range(2):
        encode_row(field_row(edge + r, give), edge_ref, r * z.code)
        encode_row(field_row(edge + r, keep), own_ref, r * z.code)
        encode_row(field_row(inner + r, give), inner_ref, r * z.code)
    at = 2 * z.code
    edge_ref[:, at : at + z.lon] = wind_row(outer, 1 - p)
    own_ref[:, at : at + z.lon] = wind_row(outer, p)
    for i, row in enumerate((inner, inner + 1, 1 + p)):
        inner_ref[:, at + i * z.lon : at + (i + 1) * z.lon] = wind_row(row, 1 - p)


def shifted(pieces, shift, lanes):
    turned = [pltpu.roll(v, (-shift) % LANE, 1) for v in pieces]
    if shift > 0:
        return [jnp.where(lanes < LANE - shift, a, b) for a, b in zip(turned[1:-1], turned[2:])]
    return [jnp.where(lanes < -shift, a, b) for a, b in zip(turned[:-2], turned[1:-1])]


def substep(z, row_of, fwx_ref, fwm_ref, fwy_ref, write):
    count = next(n for n in (4, 3, 2, 1) if z.lon % (n * LANE) == 0)
    width = count * LANE
    lanes = lax.broadcasted_iota(jnp.int32, (z.half, LANE), 1)

    def part(i, carry):
        at = pl.multiple_of(i * width, LANE)

        def piece(k):
            return pl.ds(pl.multiple_of(at + k * LANE, LANE), LANE)

        def row(j, f):
            return [row_of(j, f, piece(k + 1)) for k in range(count)]

        def start(j, f):
            pieces = [row_of(j + 2, f, piece(k)) for k in range(count + 2)]
            return [shifted(pieces, s, lanes) for s in (-2, -1, 1, 2)]

        def lon_part(j, u, moved):
            out = []
            for k in range(count):
                m2, m1, p1, p2 = (m[k] for m in moved)
                east = 7.0 * (u[k] + p1) - (m1 + p2)
                west = 7.0 * (m1 + u[k]) - (m2 + p1)
                out.append(fwx_ref[j, :, piece(k)] * east - fwm_ref[j, :, piece(k)] * west)
            return out

        for f in range(2):
            rows = [row(j, f) for j in range(4)]
            sums = [[a + b for a, b in zip(rows[j], rows[j + 1])] for j in range(3)]
            flux = None
            moved = start(0, f)
            for j in range(z.band + 1):
                later = start(j, f) if 0 < j < z.band else None
                new = [
                    fwy_ref[j, :, piece(k)] * (8.0 * sums[1][k] - (sums[0][k] + sums[2][k]))
                    for k in range(count)
                ]
                if j > 0:
                    u = rows[1]
                    change = lon_part(j - 1, u, moved)
                    for k in range(count):
                        write(j - 1, f, at, k, u[k] - change[k] - (new[k] - flux[k]))
                    moved = later
                flux = new
                if j < z.band:
                    above = row(j + 4, f)
                    rows = rows[1:] + [above]
                    sums = sums[1:] + [[a + b for a, b in zip(rows[2], rows[3])]]
        return carry

    lax.fori_loop(0, z.lon // width, part, 0)


def filter_tables(lon):
    points = np.arange(lon // 2)
    forward, back = [], []
    for parity in range(2):
        waves = np.arange(parity, KMAX, 2)
        angle = (points[:, None] * waves[None, :] % lon) * (2.0 * math.pi / lon)
        table = np.concatenate([np.cos(angle), np.sin(angle)], axis=1).astype(np.float32)
        high = table.astype(ml_dtypes.bfloat16)
        low = (table - high.astype(np.float32)).astype(ml_dtypes.bfloat16)
        forward.append(np.concatenate([high, low], axis=1))
        back.append(np.concatenate([high.T, low.T], axis=0))
    return np.stack(forward), np.stack(back)


def split(values):
    high = values.astype(jnp.bfloat16)
    return high, (values - high.astype(jnp.float32)).astype(jnp.bfloat16)


def low_pass(z, rows, cuts, forward_ref, back_ref):
    half = z.lon // 2
    count = len(rows)
    tall = 2 * z.half
    total = count * tall
    flat = [row.reshape(tall, z.lon) for row in rows]
    folded = []
    for parity in range(2):
        parts = [
            row[:, :half] + row[:, half:] if parity == 0 else row[:, :half] - row[:, half:]
            for row in flat
        ]
        high, low = split(jnp.concatenate(parts, axis=0))
        both = jnp.concatenate([high, low], axis=0)
        got = jnp.dot(both, forward_ref[parity], preferred_element_type=jnp.float32)
        wave = got[:total, :KMAX] + got[:total, KMAX:] + (got[total:, :KMAX] + got[total:, KMAX:])
        number = 2 * (lax.broadcasted_iota(jnp.int32, (tall, KMAX), 1) % (KMAX // 2)) + parity
        doubled = jnp.where(number == 0, 1.0, 2.0) * (1.0 / z.lon)
        weight = jnp.concatenate([jnp.where(number <= cut, doubled, 0.0) for cut in cuts], axis=0)
        high, low = split(wave * weight)
        both = jnp.concatenate(
            [jnp.concatenate([high, high], axis=1), jnp.concatenate([low, low], axis=1)], axis=0
        )
        got = jnp.dot(both, back_ref[parity], preferred_element_type=jnp.float32)
        folded.append(got[:total] + got[total:])
    left, right = folded[0] + folded[1], folded[0] - folded[1]
    smooth = jnp.concatenate([left, right], axis=1)
    return [smooth[i * tall : (i + 1) * tall].reshape(2, z.half, z.lon) for i in range(count)]


def filter_band(z, cut_ref, first_row, tables, load, store):
    nyquist = z.lon // 2
    for part in range(2):
        start = part * z.rows
        cuts = [cut_ref[first_row + start + r] for r in range(z.rows)]
        some = functools.reduce(jnp.logical_or, [cut < nyquist for cut in cuts])

        @pl.when(some)
        def _():
            rows = [load(start + r) for r in range(z.rows)]
            smooth = low_pass(z, rows, cuts, *tables)
            for r in range(z.rows):

                @pl.when(cuts[r] < nyquist)
                def _():
                    store(start + r, smooth[r])


def first_kernel(
    z, par_ref, fields_ref, courant_ref, edge_ref, inner_ref, near_ref, far_ref,
    new_ref, fwx_ref, fwm_ref, fwy_ref, down_ref, up_ref, u_ref, cx_ref, cy_ref,
):
    p = par_ref[0]
    lon, half = z.lon, z.half

    def pair(values):
        return values.reshape(2, half, values.shape[1])

    def winds(in_ref, at):
        values = in_ref[:, at : at + lon].astype(jnp.int32).astype(jnp.float32) * (1.0 / WIND)
        return values[:half], values[half:]

    def place_wind(row, east, north):
        put_padded(cx_ref, (row,), east, lon)
        cy_ref[row + 1] = north

    keep = pl.multiple_of(p * half, half)
    for r in range(z.rows):
        row = z.rows * p + r
        own = jnp.stack([fields_ref[f, r, pl.ds(keep, half)] for f in range(2)])
        put_padded(u_ref, (row + 2,), own, lon)
        got = []
        for k in range(2):
            wind = courant_ref[k, r].astype(jnp.float32)
            got.append(jnp.where(p == 1, wind[half:], wind[:half]))
        place_wind(row, *got)
    at = 2 * z.code
    for r in range(2):
        put_padded(u_ref, (6 * (1 - p) + r + 2,), pair(decode_row(edge_ref, r * z.code, lon)), lon)
        put_padded(u_ref, (4 - 2 * p + r + 2,), pair(decode_row(inner_ref, r * z.code, lon)), lon)
        put_padded(u_ref, (10 * (1 - p) + r,), pair(decode_row(near_ref, r * z.code, lon)), lon)
        put_padded(u_ref, (10 * p + r,), pair(decode_row(far_ref, r * z.code, lon)), lon)
        place_wind(4 - 2 * p + r, *winds(inner_ref, at + r * lon))
    place_wind(7 * (1 - p), *winds(edge_ref, at))
    place_wind(6 - 5 * p, *winds(inner_ref, at + 2 * lon))
    cy_ref[9 * (1 - p)] = winds(near_ref, at)[1]
    cy_ref[9 * p] = winds(far_ref, at)[1]

    def face_rows(j, carry):
        wind = cx_ref[j] * (1.0 / 24.0)
        here = wind[:, LANE : LANE + lon]
        fwx_ref[j] = here + pltpu.roll(wind, z.pad - 1, 1)[:, LANE : LANE + lon]
        fwm_ref[j] = here + pltpu.roll(wind, 1, 1)[:, LANE : LANE + lon]
        return carry

    lax.fori_loop(0, z.band, face_rows, 0)

    def face_cols(j, carry):
        fwy_ref[j] = (cy_ref[j] + cy_ref[j + 1]) * (1.0 / 24.0)
        return carry

    lax.fori_loop(0, z.band + 1, face_cols, 0)

    def write(row, f, at, k, values):
        new_ref[row, f, :, pl.ds(pl.multiple_of(at + (k + 1) * LANE, LANE), LANE)] = values

    substep(z, lambda j, f, piece: u_ref[j, f, :, piece], fwx_ref, fwm_ref, fwy_ref, write)
    for r in range(2):
        for row, out_ref in ((r, down_ref), (z.band - 2 + r, up_ref)):
            values = new_ref[row, :, :, LANE : LANE + lon]
            encode_row(values.reshape(2 * half, lon), out_ref, r * z.code)

    def wrap(j, carry):
        new_ref[j, :, :, 0:LANE] = new_ref[j, :, :, lon : lon + LANE]
        new_ref[j, :, :, LANE + lon :] = new_ref[j, :, :, LANE : 2 * LANE]
        return carry

    lax.fori_loop(0, z.band, wrap, 0)


def table_copies(forward_ref, back_ref, tables, sems):
    refs = ((forward_ref, tables[0]), (back_ref, tables[1]))
    return [pltpu.make_async_copy(a, b, sems.at[i]) for i, (a, b) in enumerate(refs)]


def filter_kernel(
    z, par_ref, cut_ref, forward_ref, back_ref, in_ref, new_ref, forward_copy, back_copy, sems
):
    tables = (forward_copy, back_copy)
    copies = table_copies(forward_ref, back_ref, tables, sems)
    for copy in copies:
        copy.start()

    def keep(j, carry):
        new_ref[j] = in_ref[j]
        return carry

    lax.fori_loop(0, z.band, keep, 0)
    for copy in copies:
        copy.wait()

    def store(row, values):
        put_padded(new_ref, (row,), values, z.lon)

    filter_band(
        z, cut_ref, par_ref[1], tables, lambda row: in_ref[row, :, :, LANE : LANE + z.lon], store
    )


def second_kernel(
    z, parts, par_ref, cut_ref, new_ref, fwx_ref, fwm_ref, fwy_ref, below_ref, above_ref, forward_ref,
    back_ref, out_ref, halo_ref, v_ref, forward_copy, back_copy, sems,
):
    tables = (forward_copy, back_copy)
    copies = table_copies(forward_ref, back_ref, tables, sems)
    for copy in copies:
        copy.start()
    lon, half = z.lon, z.half
    tall = 2 * half
    for r in range(2):
        for row, in_ref in ((r, below_ref), (2 + r, above_ref)):
            halo_ref[row] = decode_row(in_ref, r * z.code, lon).reshape(2, half, lon)

    def row_of(j, f, piece):
        if 2 <= j < z.band + 2:
            return new_ref[j - 2, f, :, piece]
        start = pl.multiple_of(piece.start - LANE, LANE)
        return halo_ref[j if j < 2 else j - z.band, f, :, pl.ds(start, LANE)]

    def write(row, f, at, k, values):
        v_ref[row, f, :, pl.ds(pl.multiple_of(at + k * LANE, LANE), LANE)] = values

    substep(z, row_of, fwx_ref, fwm_ref, fwy_ref, write)

    def store(row, values):
        v_ref[row] = values

    for copy in copies:
        copy.wait()
    filter_band(z, cut_ref, par_ref[1], tables, lambda row: v_ref[row], store)
    column = lon // parts
    for side in range(2):
        for d in range(parts):
            values = jnp.concatenate(
                [
                    v_ref[side * z.rows + r, :, :, d * column : (d + 1) * column].reshape(tall, column)
                    for r in range(z.rows)
                ],
                axis=1,
            )
            encode_row(values, out_ref.at[side * parts + d], 0)


def column_kernel(z, parts, par_ref, got_ref, remap_ref, upward_ref, surface_ref, out_ref, geo_ref):
    r = pl.program_id(0)
    column = out_ref.shape[-1]
    count = 2 * parts
    at = pl.multiple_of(r * column, LANE)
    tiles = []
    for s in range(parts):
        for side in range(2):
            i = side * parts + s
            scale = decoder(got_ref[i, :, z.rows * column : z.rows * column + LANE])
            codes = got_ref[i, :, pl.ds(at, column)].astype(jnp.int32).astype(jnp.float32)
            tiles.append(codes * tiled(scale, column))
    high, low = split(remap_ref[...])
    remap = jnp.concatenate([high, low, high], axis=1)
    for f in range(2):
        values = jnp.concatenate([t[f * z.half : (f + 1) * z.half] for t in tiles], axis=0)
        high, low = split(values)
        stacked = jnp.concatenate([high, high, low], axis=0)
        out_ref[f, 0] = jnp.dot(remap, stacked, preferred_element_type=jnp.float32)
        if f == 1:
            upward = jnp.dot(upward_ref[...], stacked, preferred_element_type=jnp.float32)
            surface = surface_ref[0]
            geo_ref[0] = surface + upward * (out_ref.shape[2] ** -0.5)


def whole():
    return pl.BlockSpec(memory_space=pltpu.VMEM)


def scalars():
    return pl.BlockSpec(memory_space=pltpu.SMEM)


def far_memory():
    return pl.BlockSpec(memory_space=pltpu.HBM)


def params():
    return pltpu.CompilerParams(vmem_limit_bytes=VMEM_LIMIT)


def cost(flops, data):
    return pl.CostEstimate(flops=flops, bytes_accessed=data, transcendentals=0)


def shards(fields, courant, cutoffs, surface, remap_weights):
    _, rows, levels, lon = fields.shape
    z = Sizes(rows, levels, lon)
    lats, parts = lax.axis_size("lat"), lax.axis_size("lev")
    me = lax.axis_index("lat")
    parity = me % 2
    place = jnp.stack([parity, (me - parity) * rows]).astype(jnp.int32)
    tall = 2 * z.half
    i16, f32 = jnp.int16, jnp.float32
    swap = [(i, i ^ 1) for i in range(lats)]
    rising = [(i, i + 2) for i in range(lats - 2)]
    falling = [(i + 2, i) for i in range(lats - 2)]
    near_pairs = [(i, j) for i, j in rising if i % 2 == 1] + [(i, j) for i, j in falling if i % 2 == 0]
    far_pairs = [(i, j) for i, j in rising if i % 2 == 0] + [(i, j) for i, j in falling if i % 2 == 1]

    edge, inner, own = pl.pallas_call(
        functools.partial(pack_kernel, z),
        name="pack",
        in_specs=[scalars(), whole(), whole()],
        out_specs=[whole()] * 3,
        out_shape=[
            jax.ShapeDtypeStruct((tall, z.edge), i16),
            jax.ShapeDtypeStruct((tall, z.inner), i16),
            jax.ShapeDtypeStruct((tall, z.edge), i16),
        ],
        compiler_params=params(),
        cost_estimate=cost(10**7, 5 * 10**6),
    )(place, fields, courant)
    edge = lax.ppermute(edge, "lat", swap)
    near = lax.ppermute(own, "lat", near_pairs)
    inner = lax.ppermute(inner, "lat", swap)
    far = lax.ppermute(edge, "lat", far_pairs)

    new, fwx, fwm, fwy, down, up = pl.pallas_call(
        functools.partial(first_kernel, z),
        name="first",
        in_specs=[scalars()] + [whole()] * 6,
        out_specs=[whole()] * 6,
        out_shape=[
            jax.ShapeDtypeStruct((z.band, 2, z.half, z.pad), f32),
            jax.ShapeDtypeStruct((z.band, z.half, z.lon), f32),
            jax.ShapeDtypeStruct((z.band, z.half, z.lon), f32),
            jax.ShapeDtypeStruct((z.band + 1, z.half, z.lon), f32),
            jax.ShapeDtypeStruct((tall, 2 * z.code), i16),
            jax.ShapeDtypeStruct((tall, 2 * z.code), i16),
        ],
        scratch_shapes=[
            pltpu.VMEM((z.band + 4, 2, z.half, z.pad), f32),
            pltpu.VMEM((z.band, z.half, z.pad), f32),
            pltpu.VMEM((z.band + 2, z.half, z.lon), f32),
        ],
        compiler_params=params(),
        cost_estimate=cost(4 * 10**7, 8 * 10**6),
    )(place, fields, courant, edge, inner, near, far)
    above = lax.ppermute(down, "lat", falling)
    below = lax.ppermute(up, "lat", rising)

    forward, back = (jnp.asarray(t) for t in filter_tables(lon))
    table_scratch = [pltpu.VMEM(t.shape, t.dtype) for t in (forward, back)]
    table_scratch.append(pltpu.SemaphoreType.DMA((2,)))
    new = pl.pallas_call(
        functools.partial(filter_kernel, z),
        name="smooth",
        in_specs=[scalars(), scalars(), far_memory(), far_memory(), whole()],
        out_specs=whole(),
        out_shape=jax.ShapeDtypeStruct(new.shape, f32),
        scratch_shapes=table_scratch,
        compiler_params=params(),
        cost_estimate=cost(10**9, 6 * 10**6),
    )(place, cutoffs, forward, back, new)

    column = lon // parts
    codes = pl.pallas_call(
        functools.partial(second_kernel, z, parts),
        name="second",
        in_specs=[scalars(), scalars()] + [whole()] * 6 + [far_memory()] * 2,
        out_specs=whole(),
        out_shape=jax.ShapeDtypeStruct((2 * parts, tall, rows * column + LANE), i16),
        scratch_shapes=[
            pltpu.VMEM((4, 2, z.half, lon), f32),
            pltpu.VMEM((z.band, 2, z.half, lon), f32),
        ]
        + table_scratch,
        compiler_params=params(),
        cost_estimate=cost(10**9, 8 * 10**6),
    )(place, cutoffs, new, fwx, fwm, fwy, below, above, forward, back)
    groups = [[i * parts + j for i in (a, a + 1) for j in range(parts)] for a in range(0, lats, 2)]
    got = lax.all_to_all(codes, ("lat", "lev"), 0, 0, axis_index_groups=groups, tiled=True)

    count = remap_weights.shape[0]
    upward = np.triu(np.ones((count, count), np.float32), 1) + 0.5 * np.eye(count, dtype=np.float32)
    upward = jnp.asarray(
        np.concatenate([upward, 0.0 * upward, upward], axis=1).astype(ml_dtypes.bfloat16)
    )
    mine = lax.dynamic_slice_in_dim(surface, lax.axis_index("lev") * column, column, 1)
    remapped, geopotential = pl.pallas_call(
        functools.partial(column_kernel, z, parts),
        name="columns",
        grid=(rows,),
        in_specs=[
            scalars(),
            pl.BlockSpec(got.shape, lambda r: (0, 0, 0)),
            pl.BlockSpec(remap_weights.shape, lambda r: (0, 0)),
            pl.BlockSpec(upward.shape, lambda r: (0, 0)),
            pl.BlockSpec((1, 1, column), lambda r: (r, 0, 0)),
        ],
        out_specs=[
            pl.BlockSpec((2, 1, count, column), lambda r: (0, r, 0, 0)),
            pl.BlockSpec((1, count, column), lambda r: (r, 0, 0)),
        ],
        out_shape=[
            jax.ShapeDtypeStruct((2, rows, count, column), f32),
            jax.ShapeDtypeStruct((rows, count, column), f32),
        ],
        compiler_params=params(),
        cost_estimate=cost(10**8, 4 * 10**6),
    )(place, got, remap_weights, upward, mine[:, None, :])
    return remapped, geopotential


def with_halo(shard, width):
    size, length = lax.axis_size("lat"), shard.shape[1]
    up = [(i, (i + 1) % size) for i in range(size - 1)]
    down = [(j, i) for i, j in up]
    before = lax.ppermute(lax.slice_in_dim(shard, length - width, length, axis=1), "lat", up)
    after = lax.ppermute(lax.slice_in_dim(shard, 0, width, axis=1), "lat", down)
    return jnp.concatenate([before, shard, after], axis=1)


def plain_shards(fields, courant, cutoffs, surface, remap_weights):
    _, rows, _, lon = fields.shape
    exact = lax.Precision.HIGHEST
    cut = lax.dynamic_slice_in_dim(cutoffs, lax.axis_index("lat") * rows, rows)
    waves = np.arange(KMAX)
    angle = (np.arange(lon)[:, None] * waves[None, :] % lon) * (2.0 * math.pi / lon)
    table = jnp.asarray(np.concatenate([np.cos(angle), np.sin(angle)], axis=1).astype(np.float32))
    number = jnp.asarray(np.concatenate([waves, waves]).astype(np.int32))
    weight = jnp.where(number[None] <= cut[:, None], jnp.where(number == 0, 1.0, 2.0)[None] / lon, 0.0)
    flagged = cut < lon // 2

    def smooth(values):
        wave = jnp.einsum("frln,nk->frlk", values, table, precision=exact) * weight[None, :, None]
        low = jnp.einsum("frlk,nk->frln", wave, table, precision=exact)
        return jnp.where(flagged[None, :, None, None], low, values)

    winds = with_halo(courant, 1).astype(jnp.float32)
    east, north = winds[0, 1:-1], winds[1]
    face_x = (east + jnp.roll(east, -1, -1)) / 24.0
    face_y = (north[:-1] + north[1:]) / 24.0
    u = fields
    for _ in range(2):
        wide = with_halo(u, 2)
        pair = u + jnp.roll(u, -1, -1)
        fx = face_x * (8.0 * pair - (jnp.roll(pair, 1, -1) + jnp.roll(pair, -1, -1)))
        pair = wide[:, :-1] + wide[:, 1:]
        fy = face_y * (8.0 * pair[:, 1:-1] - (pair[:, :-2] + pair[:, 2:]))
        u = u - (fx - jnp.roll(fx, 1, -1)) - (fy[:, 1:] - fy[:, :-1])
        u = lax.cond(jnp.any(flagged), smooth, lambda values: values, u)
    columns = lax.all_to_all(u, "lev", split_axis=3, concat_axis=2, tiled=True)
    remapped = jnp.einsum("pk,fjkn->fjpn", remap_weights, columns, precision=exact)
    count = remap_weights.shape[0]
    upward = np.triu(np.ones((count, count), np.float32), 1) + 0.5 * np.eye(count, dtype=np.float32)
    upward = jnp.einsum("kl,jln->jkn", jnp.asarray(upward), columns[1], precision=exact)
    width = lon // lax.axis_size("lev")
    mine = lax.dynamic_slice_in_dim(surface, lax.axis_index("lev") * width, width, 1)
    return remapped, mine[:, None] + count**-0.5 * upward


def solution(mesh):
    def program(fields, courant, cutoffs, surface, remap_weights):
        lats, parts = mesh.shape["lat"], mesh.shape["lev"]
        rows, levels = fields.shape[1] // lats, fields.shape[2] // parts
        polar = fields.shape[1] // 8
        paired = (
            lats % 2 == 0
            and rows == 4
            and levels % 16 == 0
            and polar <= 2 * rows - 2
            and fields.shape[3] % (LANE * parts) == 0
        )
        return jax.shard_map(
            shards if paired else plain_shards,
            mesh=mesh,
            in_specs=(
                P(None, "lat", "lev", None),
                P(None, "lat", "lev", None),
                P(),
                P("lat", None),
                P(),
            ),
            out_specs=(P(None, "lat", None, "lev"), P("lat", None, "lev")),
            check_vma=False,
        )(fields, courant, cutoffs, surface, remap_weights)

    return program
```

```python
import functools
import math

import jax
import jax.numpy as jnp
import ml_dtypes
import numpy as np
from jax import lax
from jax.experimental import pallas as pl
from jax.experimental.pallas import tpu as pltpu
from jax.sharding import PartitionSpec as P

KMAX = 128
LANE = 128
TOP = 32767.0
STEPS = 256.0
TINY = 2.0**-100
WIND = 81920.0
ROUND = 1.5 * 2.0**23
VMEM_LIMIT = 32 * 2**20


def rounded(values):
    return ((values + ROUND) - ROUND).astype(jnp.int32).astype(jnp.int16)


def lane_max(values):
    chunks = [jnp.abs(values[:, i : i + LANE]) for i in range(0, values.shape[1], LANE)]
    while len(chunks) > 1:
        pairs = [jnp.maximum(a, b) for a, b in zip(chunks[0::2], chunks[1::2])]
        chunks = pairs + chunks[2 * len(pairs) :]
    return chunks[0]


def tiled(tile, width):
    return jnp.concatenate([tile] * (width // LANE), axis=1)


def scale_code(largest):
    return jnp.ceil(jnp.log2(jnp.maximum(largest, TINY)) * STEPS)


def encoder(code):
    return TOP / jnp.exp2(code * (1.0 / STEPS))


def decoder(code16):
    code = code16.astype(jnp.int32).astype(jnp.float32)
    return jnp.exp2(code * (1.0 / STEPS)) * (1.0 / TOP)


def encode_row(values, out_ref, at):
    width = values.shape[1]
    code = scale_code(lane_max(values))
    out_ref[:, at : at + width] = rounded(values * tiled(encoder(code), width))
    out_ref[:, at + width : at + width + LANE] = code.astype(jnp.int32).astype(jnp.int16)


def decode_row(in_ref, at, width):
    scale = decoder(in_ref[:, at + width : at + width + LANE])
    values = in_ref[:, at : at + width].astype(jnp.int32).astype(jnp.float32)
    return values * tiled(scale, width)


def wind_codes(east, north):
    return rounded(jnp.concatenate([east, north], axis=0) * WIND)


class Sizes:
    def __init__(self, rows, levels, lon):
        self.rows, self.levels, self.lon = rows, levels, lon
        self.half = levels // 2
        self.band = 2 * rows
        self.pad = lon + 2 * LANE
        self.code = lon + LANE
        self.edge = 2 * self.code + lon
        self.inner = 2 * self.code + 3 * lon


def put_padded(ref, index, values, lon):
    ref[index + (Ellipsis, slice(LANE, LANE + lon))] = values
    ref[index + (Ellipsis, slice(0, LANE))] = values[..., lon - LANE :]
    ref[index + (Ellipsis, slice(LANE + lon, 2 * LANE + lon))] = values[..., :LANE]


def wind_row(z, wind, upper):
    halves = []
    for k in range(2):
        both = wind[k].astype(jnp.float32)
        halves.append(jnp.where(upper == 1, both[z.half :], both[: z.half]))
    return wind_codes(*halves)


def edge_kernel(z, par_ref, fields_ref, courant_ref, edge_ref, rows_ref, wind_ref, sems):
    p = par_ref[0]
    give = pl.multiple_of((1 - p) * z.half, z.half)
    copies = [
        pltpu.make_async_copy(
            fields_ref.at[f, 2 * p + r, pl.ds(give, z.half)],
            rows_ref.at[r, pl.ds(f * z.half, z.half)],
            sems.at[2 * r + f],
        )
        for r in range(2)
        for f in range(2)
    ]
    copies += [
        pltpu.make_async_copy(courant_ref.at[k, 3 * p], wind_ref.at[k], sems.at[4 + k])
        for k in range(2)
    ]
    for copy in copies:
        copy.start()
    for r in range(2):
        copies[2 * r].wait()
        copies[2 * r + 1].wait()
        encode_row(rows_ref[r], edge_ref, r * z.code)
    copies[4].wait()
    copies[5].wait()
    edge_ref[:, 2 * z.code :] = wind_row(z, wind_ref, 1 - p)


def rest_kernel(z, par_ref, fields_ref, courant_ref, inner_ref, own_ref):
    p = par_ref[0]
    keep = pl.multiple_of(p * z.half, z.half)
    give = pl.multiple_of((1 - p) * z.half, z.half)

    def field_row(row, start):
        return jnp.concatenate([fields_ref[f, row, pl.ds(start, z.half)] for f in range(2)], axis=0)

    def winds(row, upper):
        return wind_row(z, [courant_ref[k, row] for k in range(2)], upper)

    edge, inner = 2 * p, 2 * (1 - p)
    at = 2 * z.code
    for r in range(2):
        encode_row(field_row(inner + r, give), inner_ref, r * z.code)
    for i, row in enumerate((inner, inner + 1, 1 + p)):
        inner_ref[:, at + i * z.lon : at + (i + 1) * z.lon] = winds(row, 1 - p)
    for r in range(2):
        encode_row(field_row(edge + r, keep), own_ref, r * z.code)
    own_ref[:, at : at + z.lon] = winds(3 * p, p)


def shifted(pieces, shift, lanes):
    turned = [pltpu.roll(v, (-shift) % LANE, 1) for v in pieces]
    if shift > 0:
        return [jnp.where(lanes < LANE - shift, a, b) for a, b in zip(turned[1:-1], turned[2:])]
    return [jnp.where(lanes < -shift, a, b) for a, b in zip(turned[:-2], turned[1:-1])]


def substep(z, base, row_of, fwx_ref, fwm_ref, fwy_ref, write):
    count = next(n for n in (4, 3, 2, 1) if z.lon % (n * LANE) == 0)
    width = count * LANE
    lanes = lax.broadcasted_iota(jnp.int32, (z.half, LANE), 1)

    def part(i, carry):
        at = pl.multiple_of(i * width, LANE)

        def piece(k):
            return pl.ds(pl.multiple_of(at + k * LANE, LANE), LANE)

        def row(j, f):
            return [row_of(j, f, piece(k + 1)) for k in range(count)]

        def start(j, f):
            pieces = [row_of(j + 2, f, piece(k)) for k in range(count + 2)]
            return [shifted(pieces, s, lanes) for s in (-2, -1, 1, 2)]

        def lon_part(j, u, moved):
            out = []
            for k in range(count):
                m2, m1, p1, p2 = (m[k] for m in moved)
                east = 7.0 * (u[k] + p1) - (m1 + p2)
                west = 7.0 * (m1 + u[k]) - (m2 + p1)
                out.append(fwx_ref[base + j, :, piece(k)] * east - fwm_ref[base + j, :, piece(k)] * west)
            return out

        for f in range(2):
            rows = [row(j, f) for j in range(4)]
            sums = [[a + b for a, b in zip(rows[j], rows[j + 1])] for j in range(3)]
            flux = None
            moved = start(0, f)
            for j in range(z.rows + 1):
                later = start(j, f) if 0 < j < z.rows else None
                new = [
                    fwy_ref[base + j, :, piece(k)] * (8.0 * sums[1][k] - (sums[0][k] + sums[2][k]))
                    for k in range(count)
                ]
                if j > 0:
                    u = rows[1]
                    change = lon_part(j - 1, u, moved)
                    for k in range(count):
                        write(j - 1, f, at, k, u[k] - change[k] - (new[k] - flux[k]))
                    moved = later
                flux = new
                if j < z.rows:
                    above = row(j + 4, f)
                    rows = rows[1:] + [above]
                    sums = sums[1:] + [[a + b for a, b in zip(rows[2], rows[3])]]
        return carry

    lax.fori_loop(0, z.lon // width, part, 0)


def filter_tables(lon):
    points = np.arange(lon // 2)
    forward, back = [], []
    for parity in range(2):
        waves = np.arange(parity, KMAX, 2)
        angle = (points[:, None] * waves[None, :] % lon) * (2.0 * math.pi / lon)
        table = np.concatenate([np.cos(angle), np.sin(angle)], axis=1).astype(np.float32)
        high = table.astype(ml_dtypes.bfloat16)
        low = (table - high.astype(np.float32)).astype(ml_dtypes.bfloat16)
        forward.append(np.concatenate([high, low], axis=1))
        back.append(np.concatenate([high.T, low.T], axis=0))
    return np.stack(forward), np.stack(back)


def split(values):
    high = values.astype(jnp.bfloat16)
    return high, (values - high.astype(jnp.float32)).astype(jnp.bfloat16)


def low_pass(z, rows, cuts, forward_ref, back_ref):
    half = z.lon // 2
    count = len(rows)
    tall = 2 * z.half
    total = count * tall
    flat = [row.reshape(tall, z.lon) for row in rows]
    folded = []
    for parity in range(2):
        parts = [
            row[:, :half] + row[:, half:] if parity == 0 else row[:, :half] - row[:, half:]
            for row in flat
        ]
        high, low = split(jnp.concatenate(parts, axis=0))
        both = jnp.concatenate([high, low], axis=0)
        got = jnp.dot(both, forward_ref[parity], preferred_element_type=jnp.float32)
        wave = got[:total, :KMAX] + got[:total, KMAX:] + (got[total:, :KMAX] + got[total:, KMAX:])
        number = 2 * (lax.broadcasted_iota(jnp.int32, (tall, KMAX), 1) % (KMAX // 2)) + parity
        doubled = jnp.where(number == 0, 1.0, 2.0) * (1.0 / z.lon)
        weight = jnp.concatenate([jnp.where(number <= cut, doubled, 0.0) for cut in cuts], axis=0)
        high, low = split(wave * weight)
        both = jnp.concatenate(
            [jnp.concatenate([high, high], axis=1), jnp.concatenate([low, low], axis=1)], axis=0
        )
        got = jnp.dot(both, back_ref[parity], preferred_element_type=jnp.float32)
        folded.append(got[:total] + got[total:])
    left, right = folded[0] + folded[1], folded[0] - folded[1]
    smooth = jnp.concatenate([left, right], axis=1)
    return [smooth[i * tall : (i + 1) * tall].reshape(2, z.half, z.lon) for i in range(count)]


def filter_rows(z, cut_ref, first_row, start, tables, load, store):
    nyquist = z.lon // 2
    cuts = [cut_ref[first_row + start + r] for r in range(z.rows)]
    some = functools.reduce(jnp.logical_or, [cut < nyquist for cut in cuts])

    @pl.when(some)
    def _():
        smooth = low_pass(z, [load(start + r) for r in range(z.rows)], cuts, *tables)
        for r in range(z.rows):

            @pl.when(cuts[r] < nyquist)
            def _():
                store(start + r, smooth[r])


def first_kernel(
    z, par_ref, fields_ref, courant_ref, edge_ref, inner_ref, near_ref, far_ref,
    new_ref, code_ref, u_ref, fwx_ref, fwm_ref, fwy_ref, cx_ref, cy_ref,
):
    p = par_ref[0]
    lon, half = z.lon, z.half

    def pair(values):
        return values.reshape(2, half, values.shape[1])

    def winds(in_ref, at):
        values = in_ref[:, at : at + lon].astype(jnp.int32).astype(jnp.float32) * (1.0 / WIND)
        return values[:half], values[half:]

    def place_wind(row, east, north):
        put_padded(cx_ref, (row,), east, lon)
        cy_ref[row + 1] = north

    keep = pl.multiple_of(p * half, half)
    for r in range(z.rows):
        row = z.rows * p + r
        own = jnp.stack([fields_ref[f, r, pl.ds(keep, half)] for f in range(2)])
        put_padded(u_ref, (row + 2,), own, lon)
        got = []
        for k in range(2):
            wind = courant_ref[k, r].astype(jnp.float32)
            got.append(jnp.where(p == 1, wind[half:], wind[:half]))
        place_wind(row, *got)
    at = 2 * z.code
    for r in range(2):
        put_padded(u_ref, (6 * (1 - p) + r + 2,), pair(decode_row(edge_ref, r * z.code, lon)), lon)
        put_padded(u_ref, (4 - 2 * p + r + 2,), pair(decode_row(inner_ref, r * z.code, lon)), lon)
        put_padded(u_ref, (10 * (1 - p) + r,), pair(decode_row(near_ref, r * z.code, lon)), lon)
        put_padded(u_ref, (10 * p + r,), pair(decode_row(far_ref, r * z.code, lon)), lon)
        place_wind(4 - 2 * p + r, *winds(inner_ref, at + r * lon))
    place_wind(7 * (1 - p), *winds(edge_ref, at))
    place_wind(6 - 5 * p, *winds(inner_ref, at + 2 * lon))
    cy_ref[9 * (1 - p)] = winds(near_ref, at)[1]
    cy_ref[9 * p] = winds(far_ref, at)[1]

    def face_rows(j, carry):
        wind = cx_ref[j] * (1.0 / 24.0)
        here = wind[:, LANE : LANE + lon]
        fwx_ref[j] = here + pltpu.roll(wind, z.pad - 1, 1)[:, LANE : LANE + lon]
        fwm_ref[j] = here + pltpu.roll(wind, 1, 1)[:, LANE : LANE + lon]
        return carry

    lax.fori_loop(0, z.band, face_rows, 0)

    def face_cols(j, carry):
        fwy_ref[j] = (cy_ref[j] + cy_ref[j + 1]) * (1.0 / 24.0)
        return carry

    lax.fori_loop(0, z.band + 1, face_cols, 0)

    half_band(z, p, 2 * p, u_ref, fwx_ref, fwm_ref, fwy_ref, new_ref, code_ref)


def half_band(z, side, outer, u_ref, fwx_ref, fwm_ref, fwy_ref, new_ref, code_ref):
    base = z.rows * side

    def write(row, f, at, k, values):
        new_ref[row, f, :, pl.ds(pl.multiple_of(at + (k + 1) * LANE, LANE), LANE)] = values

    substep(
        z, base, lambda j, f, piece: u_ref[base + j, f, :, piece], fwx_ref, fwm_ref, fwy_ref, write
    )
    for r in range(2):
        values = new_ref[outer + r, :, :, LANE : LANE + z.lon]
        encode_row(values.reshape(2 * z.half, z.lon), code_ref, r * z.code)
    for j in range(z.rows):
        new_ref[j, :, :, 0:LANE] = new_ref[j, :, :, z.lon : z.lon + LANE]
        new_ref[j, :, :, LANE + z.lon :] = new_ref[j, :, :, LANE : 2 * LANE]


def other_kernel(z, par_ref, u_ref, fwx_ref, fwm_ref, fwy_ref, new_ref, code_ref):
    p = par_ref[0]
    half_band(z, 1 - p, 2 * (1 - p), u_ref, fwx_ref, fwm_ref, fwy_ref, new_ref, code_ref)


def table_copies(forward_ref, back_ref, tables, sems):
    refs = ((forward_ref, tables[0]), (back_ref, tables[1]))
    return [pltpu.make_async_copy(a, b, sems.at[i]) for i, (a, b) in enumerate(refs)]


def filter_kernel(
    z, par_ref, cut_ref, forward_ref, back_ref, own_ref, other_ref, new_ref, forward_copy, back_copy, sems
):
    tables = (forward_copy, back_copy)
    copies = table_copies(forward_ref, back_ref, tables, sems)
    for copy in copies:
        copy.start()

    p = par_ref[0]
    for j in range(z.rows):
        new_ref[z.rows * p + j] = own_ref[j]
        new_ref[z.rows * (1 - p) + j] = other_ref[j]
    for copy in copies:
        copy.wait()

    def store(row, values):
        put_padded(new_ref, (row,), values, z.lon)

    for part in range(2):
        filter_rows(
            z, cut_ref, par_ref[1], part * z.rows, tables,
            lambda row: new_ref[row, :, :, LANE : LANE + z.lon], store,
        )


def second_kernel(
    z, parts, partner, par_ref, cut_ref, new_ref, fwx_ref, fwm_ref, fwy_ref, halo_ref, forward_ref,
    back_ref, *refs,
):
    out_refs, (ends_ref, v_ref, forward_copy, back_copy, sems) = refs[:parts], refs[parts:]
    tables = (forward_copy, back_copy)
    copies = table_copies(forward_ref, back_ref, tables, sems)
    for copy in copies:
        copy.start()
    lon, half = z.lon, z.half
    tall = 2 * half
    side = 1 - par_ref[0] if partner else par_ref[0]
    base = z.rows * side
    for r in range(2):
        values = decode_row(halo_ref, r * z.code, lon).reshape(2, half, lon)
        put_padded(ends_ref, (2 * side + r,), values, lon)
        ends_ref[2 * (1 - side) + r] = new_ref[z.rows - 2 * side + r]

    def row_of(j, f, piece):
        if 2 <= j < z.rows + 2:
            return new_ref[base + j - 2, f, :, piece]
        return ends_ref[j if j < 2 else j - z.rows, f, :, piece]

    def write(row, f, at, k, values):
        v_ref[row, f, :, pl.ds(pl.multiple_of(at + k * LANE, LANE), LANE)] = values

    substep(z, base, row_of, fwx_ref, fwm_ref, fwy_ref, write)

    def store(row, values):
        v_ref[row] = values

    for copy in copies:
        copy.wait()
    filter_rows(z, cut_ref, par_ref[1] + base, 0, tables, lambda row: v_ref[row], store)
    column = lon // parts
    for b in range(parts):
        at = pl.multiple_of(jnp.bitwise_xor(par_ref[2], b) * column, LANE)
        values = jnp.concatenate(
            [v_ref[r, :, :, pl.ds(at, column)].reshape(tall, column) for r in range(z.rows)], axis=1
        )
        encode_row(values, out_refs[b], 0)


def column_kernel(z, parts, par_ref, *refs):
    got, (remap_ref, upward_ref, surface_ref, out_ref, geo_ref, x_ref) = refs[: 2 * parts], refs[2 * parts :]
    p, lev = par_ref[0], par_ref[2]
    column = out_ref.shape[-1]
    at = pl.multiple_of(pl.program_id(0) * column, LANE)
    for i, ref in enumerate(got):
        side = 1 - p if i < parts else p
        s = jnp.bitwise_xor(lev, i % parts)
        scale = decoder(ref[:, z.rows * column : z.rows * column + LANE])
        codes = ref[:, pl.ds(at, column)].astype(jnp.int32).astype(jnp.float32)
        values = codes * tiled(scale, column)
        level = pl.multiple_of(s * z.levels + side * z.half, z.half)
        for f in range(2):
            x_ref[f, pl.ds(level, z.half)] = values[f * z.half : (f + 1) * z.half]
    high, low = split(remap_ref[...])
    remap = jnp.concatenate([high, low, high], axis=1)
    count = remap_ref.shape[0]
    for f in range(2):
        high, low = split(x_ref[f])
        stacked = jnp.concatenate([high, high, low], axis=0)
        left = remap if f == 0 else jnp.concatenate([remap, upward_ref[...].astype(jnp.bfloat16)], axis=0)
        result = jnp.dot(left, stacked, preferred_element_type=jnp.float32)
        out_ref[f, 0] = result[:count]
        if f == 1:
            geo_ref[0] = surface_ref[0] + result[count:] * (count**-0.5)


def whole():
    return pl.BlockSpec(memory_space=pltpu.VMEM)


def scalars():
    return pl.BlockSpec(memory_space=pltpu.SMEM)


def far_memory():
    return pl.BlockSpec(memory_space=pltpu.HBM)


def params():
    return pltpu.CompilerParams(vmem_limit_bytes=VMEM_LIMIT)


def cost(flops, data):
    return pl.CostEstimate(flops=flops, bytes_accessed=data, transcendentals=0)


def shards(fields, courant, cutoffs, surface, remap_weights):
    _, rows, levels, lon = fields.shape
    z = Sizes(rows, levels, lon)
    lats, parts = lax.axis_size("lat"), lax.axis_size("lev")
    me = lax.axis_index("lat")
    parity = me % 2
    lev = lax.axis_index("lev")
    place = jnp.stack([parity, (me - parity) * rows, lev]).astype(jnp.int32)
    tall = 2 * z.half
    i16, f32 = jnp.int16, jnp.float32
    swap = [(i, i ^ 1) for i in range(lats)]
    rising = [(i, i + 2) for i in range(lats - 2)]
    falling = [(i + 2, i) for i in range(lats - 2)]
    near_pairs = [(i, j) for i, j in rising if i % 2 == 1] + [(i, j) for i, j in falling if i % 2 == 0]
    far_pairs = [(i, j) for i, j in rising if i % 2 == 0] + [(i, j) for i, j in falling if i % 2 == 1]

    def shape(*dims):
        return jax.ShapeDtypeStruct(dims, f32)

    def codes(*dims):
        return jax.ShapeDtypeStruct(dims, i16)

    edge = pl.pallas_call(
        functools.partial(edge_kernel, z),
        name="edge",
        in_specs=[scalars(), far_memory(), far_memory()],
        out_specs=whole(),
        out_shape=codes(tall, z.edge),
        scratch_shapes=[
            pltpu.VMEM((2, tall, lon), f32),
            pltpu.VMEM((2, levels, lon), courant.dtype),
            pltpu.SemaphoreType.DMA((6,)),
        ],
        compiler_params=params(),
        cost_estimate=cost(10**6, 10**6),
    )(place, fields, courant)
    edge = lax.ppermute(edge, "lat", swap)
    inner, own = pl.pallas_call(
        functools.partial(rest_kernel, z),
        name="rest",
        in_specs=[scalars(), whole(), whole()],
        out_specs=[whole()] * 2,
        out_shape=[codes(tall, z.inner), codes(tall, z.edge)],
        compiler_params=params(),
        cost_estimate=cost(10**7, 4 * 10**6),
    )(place, fields, courant)
    inner = lax.ppermute(inner, "lat", swap)
    near = lax.ppermute(own, "lat", near_pairs)
    far = lax.ppermute(edge, "lat", far_pairs)

    half_out = [shape(rows, 2, z.half, z.pad), codes(tall, 2 * z.code)]
    mine, near_code, u, fwx, fwm, fwy = pl.pallas_call(
        functools.partial(first_kernel, z),
        name="first",
        in_specs=[scalars()] + [whole()] * 6,
        out_specs=[whole()] * 6,
        out_shape=half_out
        + [
            shape(z.band + 4, 2, z.half, z.pad),
            shape(z.band, z.half, lon),
            shape(z.band, z.half, lon),
            shape(z.band + 1, z.half, lon),
        ],
        scratch_shapes=[
            pltpu.VMEM((z.band, z.half, z.pad), f32),
            pltpu.VMEM((z.band + 2, z.half, z.lon), f32),
        ],
        compiler_params=params(),
        cost_estimate=cost(4 * 10**7, 8 * 10**6),
    )(place, fields, courant, edge, inner, near, far)
    near = lax.ppermute(near_code, "lat", near_pairs)
    other, far_code = pl.pallas_call(
        functools.partial(other_kernel, z),
        name="other",
        in_specs=[scalars()] + [whole()] * 4,
        out_specs=[whole()] * 2,
        out_shape=half_out,
        compiler_params=params(),
        cost_estimate=cost(4 * 10**7, 6 * 10**6),
    )(place, u, fwx, fwm, fwy)
    far = lax.ppermute(far_code, "lat", far_pairs)

    forward, back = (jnp.asarray(t) for t in filter_tables(lon))
    table_scratch = [pltpu.VMEM(t.shape, t.dtype) for t in (forward, back)]
    table_scratch.append(pltpu.SemaphoreType.DMA((2,)))
    new = pl.pallas_call(
        functools.partial(filter_kernel, z),
        name="smooth",
        in_specs=[scalars(), scalars(), far_memory(), far_memory(), whole(), whole()],
        out_specs=whole(),
        out_shape=shape(z.band, 2, z.half, z.pad),
        scratch_shapes=table_scratch,
        compiler_params=params(),
        cost_estimate=cost(10**9, 6 * 10**6),
    )(place, cutoffs, forward, back, mine, other)

    column = lon // parts

    def second(partner, halo):
        return pl.pallas_call(
            functools.partial(second_kernel, z, parts, partner),
            name="second_partner" if partner else "second_own",
            in_specs=[scalars(), scalars()] + [whole()] * 5 + [far_memory()] * 2,
            out_specs=[whole()] * parts,
            out_shape=[codes(tall, rows * column + LANE)] * parts,
            scratch_shapes=[
                pltpu.VMEM((4, 2, z.half, z.pad), f32),
                pltpu.VMEM((z.rows, 2, z.half, lon), f32),
            ]
            + table_scratch,
            compiler_params=params(),
            cost_estimate=cost(10**9, 6 * 10**6),
        )(place, cutoffs, new, fwx, fwm, fwy, halo, forward, back)

    got = []
    for b, block in enumerate(second(True, near)):
        pairs = [
            (i * parts + j, (i ^ 1) * parts + (j ^ b)) for i in range(lats) for j in range(parts)
        ]
        got.append(lax.ppermute(block, ("lat", "lev"), pairs))
    for b, block in enumerate(second(False, far)):
        pairs = [(j, j ^ b) for j in range(parts)]
        got.append(lax.ppermute(block, "lev", pairs) if b else block)

    count = remap_weights.shape[0]
    upward = np.triu(np.ones((count, count), np.float32), 1) + 0.5 * np.eye(count, dtype=np.float32)
    upward = jnp.asarray(np.concatenate([upward, 0.0 * upward, upward], axis=1))
    surface = lax.dynamic_slice_in_dim(surface, lev * column, column, 1)
    remapped, geopotential = pl.pallas_call(
        functools.partial(column_kernel, z, parts),
        name="columns",
        grid=(rows,),
        in_specs=[scalars()]
        + [pl.BlockSpec(g.shape, lambda r: (0, 0)) for g in got]
        + [
            pl.BlockSpec(remap_weights.shape, lambda r: (0, 0)),
            pl.BlockSpec(upward.shape, lambda r: (0, 0)),
            pl.BlockSpec((1, 1, column), lambda r: (r, 0, 0)),
        ],
        out_specs=[
            pl.BlockSpec((2, 1, count, column), lambda r: (0, r, 0, 0)),
            pl.BlockSpec((1, count, column), lambda r: (r, 0, 0)),
        ],
        out_shape=[shape(2, rows, count, column), shape(rows, count, column)],
        scratch_shapes=[pltpu.VMEM((2, count, column), f32)],
        compiler_params=params(),
        cost_estimate=cost(10**8, 4 * 10**6),
    )(place, *got, remap_weights, upward, surface[:, None, :])
    return remapped, geopotential


def with_halo(shard, width):
    size, length = lax.axis_size("lat"), shard.shape[1]
    up = [(i, (i + 1) % size) for i in range(size - 1)]
    down = [(j, i) for i, j in up]
    before = lax.ppermute(lax.slice_in_dim(shard, length - width, length, axis=1), "lat", up)
    after = lax.ppermute(lax.slice_in_dim(shard, 0, width, axis=1), "lat", down)
    return jnp.concatenate([before, shard, after], axis=1)


def plain_shards(fields, courant, cutoffs, surface, remap_weights):
    _, rows, _, lon = fields.shape
    exact = lax.Precision.HIGHEST
    cut = lax.dynamic_slice_in_dim(cutoffs, lax.axis_index("lat") * rows, rows)
    waves = np.arange(KMAX)
    angle = (np.arange(lon)[:, None] * waves[None, :] % lon) * (2.0 * math.pi / lon)
    table = jnp.asarray(np.concatenate([np.cos(angle), np.sin(angle)], axis=1).astype(np.float32))
    number = jnp.asarray(np.concatenate([waves, waves]).astype(np.int32))
    weight = jnp.where(number[None] <= cut[:, None], jnp.where(number == 0, 1.0, 2.0)[None] / lon, 0.0)
    flagged = cut < lon // 2

    def smooth(values):
        wave = jnp.einsum("frln,nk->frlk", values, table, precision=exact) * weight[None, :, None]
        low = jnp.einsum("frlk,nk->frln", wave, table, precision=exact)
        return jnp.where(flagged[None, :, None, None], low, values)

    winds = with_halo(courant, 1).astype(jnp.float32)
    east, north = winds[0, 1:-1], winds[1]
    face_x = (east + jnp.roll(east, -1, -1)) / 24.0
    face_y = (north[:-1] + north[1:]) / 24.0
    u = fields
    for _ in range(2):
        wide = with_halo(u, 2)
        pair = u + jnp.roll(u, -1, -1)
        fx = face_x * (8.0 * pair - (jnp.roll(pair, 1, -1) + jnp.roll(pair, -1, -1)))
        pair = wide[:, :-1] + wide[:, 1:]
        fy = face_y * (8.0 * pair[:, 1:-1] - (pair[:, :-2] + pair[:, 2:]))
        u = u - (fx - jnp.roll(fx, 1, -1)) - (fy[:, 1:] - fy[:, :-1])
        u = lax.cond(jnp.any(flagged), smooth, lambda values: values, u)
    columns = lax.all_to_all(u, "lev", split_axis=3, concat_axis=2, tiled=True)
    remapped = jnp.einsum("pk,fjkn->fjpn", remap_weights, columns, precision=exact)
    count = remap_weights.shape[0]
    upward = np.triu(np.ones((count, count), np.float32), 1) + 0.5 * np.eye(count, dtype=np.float32)
    upward = jnp.einsum("kl,jln->jkn", jnp.asarray(upward), columns[1], precision=exact)
    width = lon // lax.axis_size("lev")
    mine = lax.dynamic_slice_in_dim(surface, lax.axis_index("lev") * width, width, 1)
    return remapped, mine[:, None] + count**-0.5 * upward


def solution(mesh):
    def program(fields, courant, cutoffs, surface, remap_weights):
        lats, parts = mesh.shape["lat"], mesh.shape["lev"]
        rows, levels = fields.shape[1] // lats, fields.shape[2] // parts
        polar = fields.shape[1] // 8
        paired = (
            lats % 2 == 0
            and rows == 4
            and levels % 16 == 0
            and polar <= 2 * rows - 2
            and fields.shape[3] % (LANE * parts) == 0
            and parts & (parts - 1) == 0
        )
        return jax.shard_map(
            shards if paired else plain_shards,
            mesh=mesh,
            in_specs=(
                P(None, "lat", "lev", None),
                P(None, "lat", "lev", None),
                P(),
                P("lat", None),
                P(),
            ),
            out_specs=(P(None, "lat", None, "lev"), P("lat", None, "lev")),
            check_vma=False,
        )(fields, courant, cutoffs, surface, remap_weights)

    return program
```

```python
import functools
import math

import jax
import jax.numpy as jnp
import ml_dtypes
import numpy as np
from jax import lax
from jax.experimental import pallas as pl
from jax.experimental.pallas import tpu as pltpu
from jax.sharding import PartitionSpec as P

KMAX = 128
LANE = 128
TOP = 32767.0
STEPS = 256.0
TINY = 2.0**-100
WIND = 81920.0
ROUND = 1.5 * 2.0**23
VMEM_LIMIT = 12 * 2**20
VMEM_MOST = 63 * 2**20 + 2**19


def rounded(values):
    return ((values + ROUND) - ROUND).astype(jnp.int32).astype(jnp.int16)


def lane_max(values):
    chunks = [jnp.abs(values[:, i : i + LANE]) for i in range(0, values.shape[1], LANE)]
    while len(chunks) > 1:
        pairs = [jnp.maximum(a, b) for a, b in zip(chunks[0::2], chunks[1::2])]
        chunks = pairs + chunks[2 * len(pairs) :]
    return chunks[0]


def tiled(tile, width):
    return jnp.concatenate([tile] * (width // LANE), axis=1)


def scale_code(largest):
    return jnp.ceil(jnp.log2(jnp.maximum(largest, TINY)) * STEPS)


def encoder(code):
    return TOP / jnp.exp2(code * (1.0 / STEPS))


def decoder(code16):
    code = code16.astype(jnp.int32).astype(jnp.float32)
    return jnp.exp2(code * (1.0 / STEPS)) * (1.0 / TOP)


def encode_row(values, out_ref, at):
    width = values.shape[1]
    code = scale_code(lane_max(values))
    out_ref[:, at : at + width] = rounded(values * tiled(encoder(code), width))
    out_ref[:, at + width : at + width + LANE] = code.astype(jnp.int32).astype(jnp.int16)


def decode_row(in_ref, at, width):
    scale = decoder(in_ref[:, at + width : at + width + LANE])
    values = in_ref[:, at : at + width].astype(jnp.int32).astype(jnp.float32)
    return values * tiled(scale, width)


def wind_codes(east, north):
    return rounded(jnp.concatenate([east, north], axis=0) * WIND)


class Sizes:
    def __init__(self, rows, levels, lon):
        self.rows, self.levels, self.lon = rows, levels, lon
        self.half = levels // 2
        self.band = 2 * rows
        self.pad = lon + 2 * LANE
        self.code = lon + LANE
        self.edge = 2 * self.code + lon
        self.inner = 2 * self.code + 3 * lon


def put_padded(ref, index, values, lon):
    ref[index + (Ellipsis, slice(LANE, LANE + lon))] = values
    ref[index + (Ellipsis, slice(0, LANE))] = values[..., lon - LANE :]
    ref[index + (Ellipsis, slice(LANE + lon, 2 * LANE + lon))] = values[..., :LANE]


def wind_row(z, wind, upper):
    halves = []
    for k in range(2):
        both = wind[k].astype(jnp.float32)
        halves.append(jnp.where(upper == 1, both[z.half :], both[: z.half]))
    return wind_codes(*halves)


def edge_kernel(z, par_ref, fields_ref, courant_ref, edge_ref, rows_ref, wind_ref, sems):
    p = par_ref[0]
    give = pl.multiple_of((1 - p) * z.half, z.half)
    copies = [
        pltpu.make_async_copy(
            fields_ref.at[f, 2 * p + r, pl.ds(give, z.half)],
            rows_ref.at[r, pl.ds(f * z.half, z.half)],
            sems.at[2 * r + f],
        )
        for r in range(2)
        for f in range(2)
    ]
    copies += [
        pltpu.make_async_copy(courant_ref.at[k, 3 * p], wind_ref.at[k], sems.at[4 + k])
        for k in range(2)
    ]
    for copy in copies:
        copy.start()
    for r in range(2):
        copies[2 * r].wait()
        copies[2 * r + 1].wait()
        encode_row(rows_ref[r], edge_ref, r * z.code)
    copies[4].wait()
    copies[5].wait()
    edge_ref[:, 2 * z.code :] = wind_row(z, wind_ref, 1 - p)


def rest_kernel(z, par_ref, fields_ref, courant_ref, inner_ref, own_ref, rows_ref, wind_ref, sems):
    p = par_ref[0]
    keep = pl.multiple_of(p * z.half, z.half)
    give = pl.multiple_of((1 - p) * z.half, z.half)
    edge, inner = 2 * p, 2 * (1 - p)
    copies = [
        pltpu.make_async_copy(
            fields_ref.at[f, row, pl.ds(start, z.half)],
            rows_ref.at[i, pl.ds(f * z.half, z.half)],
            sems.at[2 * i + f],
        )
        for i, (row, start) in enumerate(
            ((inner, give), (inner + 1, give), (edge, keep), (edge + 1, keep))
        )
        for f in range(2)
    ]
    order = (inner, inner + 1, 1 + p, 3 * p)
    copies += [
        pltpu.make_async_copy(courant_ref.at[k, row], wind_ref.at[i, k], sems.at[8 + 2 * i + k])
        for i, row in enumerate(order)
        for k in range(2)
    ]
    for copy in copies:
        copy.start()
    at = 2 * z.code
    for i in range(4):
        copies[2 * i].wait()
        copies[2 * i + 1].wait()
        encode_row(rows_ref[i], inner_ref if i < 2 else own_ref, i % 2 * z.code)
    for i in range(4):
        copies[8 + 2 * i].wait()
        copies[9 + 2 * i].wait()
        if i < 3:
            inner_ref[:, at + i * z.lon : at + (i + 1) * z.lon] = wind_row(z, wind_ref.at[i], 1 - p)
    own_ref[:, at : at + z.lon] = wind_row(z, wind_ref.at[3], p)


def shifted(pieces, shift, lanes):
    turned = [pltpu.roll(v, (-shift) % LANE, 1) for v in pieces]
    if shift > 0:
        return [jnp.where(lanes < LANE - shift, a, b) for a, b in zip(turned[1:-1], turned[2:])]
    return [jnp.where(lanes < -shift, a, b) for a, b in zip(turned[:-2], turned[1:-1])]


def substep(z, count_rows, base, row_of, fwx_ref, fwm_ref, fwy_ref, write):
    count = next(n for n in (4, 3, 2, 1) if z.lon % (n * LANE) == 0)
    width = count * LANE
    lanes = lax.broadcasted_iota(jnp.int32, (z.half, LANE), 1)

    def part(i, carry):
        at = pl.multiple_of(i * width, LANE)

        def piece(k):
            return pl.ds(pl.multiple_of(at + k * LANE, LANE), LANE)

        def row(j, f):
            return [row_of(j, f, piece(k + 1)) for k in range(count)]

        def start(j, f):
            pieces = [row_of(j + 2, f, piece(k)) for k in range(count + 2)]
            return [shifted(pieces, s, lanes) for s in (-2, -1, 1, 2)]

        def lon_part(j, u, moved):
            out = []
            for k in range(count):
                m2, m1, p1, p2 = (m[k] for m in moved)
                east = 7.0 * (u[k] + p1) - (m1 + p2)
                west = 7.0 * (m1 + u[k]) - (m2 + p1)
                out.append(fwx_ref[base + j, :, piece(k)] * east - fwm_ref[base + j, :, piece(k)] * west)
            return out

        for f in range(2):
            rows = [row(j, f) for j in range(4)]
            sums = [[a + b for a, b in zip(rows[j], rows[j + 1])] for j in range(3)]
            flux = None
            moved = start(0, f)
            for j in range(count_rows + 1):
                later = start(j, f) if 0 < j < count_rows else None
                new = [
                    fwy_ref[base + j, :, piece(k)] * (8.0 * sums[1][k] - (sums[0][k] + sums[2][k]))
                    for k in range(count)
                ]
                if j > 0:
                    u = rows[1]
                    change = lon_part(j - 1, u, moved)
                    for k in range(count):
                        write(j - 1, f, at, k, u[k] - change[k] - (new[k] - flux[k]))
                    moved = later
                flux = new
                if j < count_rows:
                    above = row(j + 4, f)
                    rows = rows[1:] + [above]
                    sums = sums[1:] + [[a + b for a, b in zip(rows[2], rows[3])]]
        return carry

    lax.fori_loop(0, z.lon // width, part, 0)


def filter_tables(lon):
    points = np.arange(lon // 2)
    forward, back = [], []
    for parity in range(2):
        waves = np.arange(parity, KMAX, 2)
        angle = (points[:, None] * waves[None, :] % lon) * (2.0 * math.pi / lon)
        table = np.concatenate([np.cos(angle), np.sin(angle)], axis=1).astype(np.float32)
        high = table.astype(ml_dtypes.bfloat16)
        low = (table - high.astype(np.float32)).astype(ml_dtypes.bfloat16)
        forward.append(np.concatenate([high, low], axis=1))
        back.append(np.concatenate([high.T, low.T], axis=0))
    return np.stack(forward), np.stack(back)


def split(values):
    high = values.astype(jnp.bfloat16)
    return high, (values - high.astype(jnp.float32)).astype(jnp.bfloat16)


def low_pass(z, rows, cuts, forward_ref, back_ref):
    half = z.lon // 2
    count = len(rows)
    tall = 2 * z.half
    total = count * tall
    flat = [row.reshape(tall, z.lon) for row in rows]
    folded = []
    for parity in range(2):
        parts = [
            row[:, :half] + row[:, half:] if parity == 0 else row[:, :half] - row[:, half:]
            for row in flat
        ]
        high, low = split(jnp.concatenate(parts, axis=0))
        both = jnp.concatenate([high, low], axis=0)
        got = jnp.dot(both, forward_ref[parity], preferred_element_type=jnp.float32)
        wave = got[:total, :KMAX] + got[:total, KMAX:] + (got[total:, :KMAX] + got[total:, KMAX:])
        number = 2 * (lax.broadcasted_iota(jnp.int32, (tall, KMAX), 1) % (KMAX // 2)) + parity
        doubled = jnp.where(number == 0, 1.0, 2.0) * (1.0 / z.lon)
        weight = jnp.concatenate([jnp.where(number <= cut, doubled, 0.0) for cut in cuts], axis=0)
        high, low = split(wave * weight)
        both = jnp.concatenate(
            [jnp.concatenate([high, high], axis=1), jnp.concatenate([low, low], axis=1)], axis=0
        )
        got = jnp.dot(both, back_ref[parity], preferred_element_type=jnp.float32)
        folded.append(got[:total] + got[total:])
    left, right = folded[0] + folded[1], folded[0] - folded[1]
    smooth = jnp.concatenate([left, right], axis=1)
    return [smooth[i * tall : (i + 1) * tall].reshape(2, z.half, z.lon) for i in range(count)]


def filter_rows(z, cut_ref, first_row, start, tables, load, store):
    nyquist = z.lon // 2
    cuts = [cut_ref[first_row + start + r] for r in range(z.rows)]
    some = functools.reduce(jnp.logical_or, [cut < nyquist for cut in cuts])

    @pl.when(some)
    def _():
        smooth = low_pass(z, [load(start + r) for r in range(z.rows)], cuts, *tables)
        for r in range(z.rows):

            @pl.when(cuts[r] < nyquist)
            def _():
                store(start + r, smooth[r])


def first_kernel(
    z, par_ref, fields_ref, courant_ref, edge_ref, inner_ref, one_ref, two_ref,
    new_ref, fwx_ref, fwm_ref, fwy_ref, one_out_ref, two_out_ref, u_ref, cx_ref, cy_ref,
):
    p, b = par_ref[0], par_ref[3]
    lon, half = z.lon, z.half

    def pair(values):
        return values.reshape(2, half, values.shape[1])

    def winds(in_ref, at):
        values = in_ref[:, at : at + lon].astype(jnp.int32).astype(jnp.float32) * (1.0 / WIND)
        return values[:half], values[half:]

    def place_wind(row, east, north):
        put_padded(cx_ref, (row,), east, lon)
        cy_ref[row + 1] = north

    keep = pl.multiple_of(p * half, half)
    for r in range(z.rows):
        row = z.rows * p + r
        own = jnp.stack([fields_ref[f, r, pl.ds(keep, half)] for f in range(2)])
        put_padded(u_ref, (row + 2,), own, lon)
        got = []
        for k in range(2):
            wind = courant_ref[k, r].astype(jnp.float32)
            got.append(jnp.where(p == 1, wind[half:], wind[:half]))
        place_wind(row, *got)
    at = 2 * z.code
    for r in range(2):
        put_padded(u_ref, (6 * (1 - p) + r + 2,), pair(decode_row(edge_ref, r * z.code, lon)), lon)
        put_padded(u_ref, (4 - 2 * p + r + 2,), pair(decode_row(inner_ref, r * z.code, lon)), lon)
        put_padded(u_ref, (10 * (1 - b) + r,), pair(decode_row(one_ref, r * z.code, lon)), lon)
        put_padded(u_ref, (10 * b + r,), pair(decode_row(two_ref, r * z.code, lon)), lon)
        place_wind(4 - 2 * p + r, *winds(inner_ref, at + r * lon))
    place_wind(7 * (1 - p), *winds(edge_ref, at))
    place_wind(6 - 5 * p, *winds(inner_ref, at + 2 * lon))
    cy_ref[9 * (1 - b)] = winds(one_ref, at)[1]
    cy_ref[9 * b] = winds(two_ref, at)[1]

    def face_rows(j, carry):
        wind = cx_ref[j] * (1.0 / 24.0)
        here = wind[:, LANE : LANE + lon]
        fwx_ref[j] = here + pltpu.roll(wind, z.pad - 1, 1)[:, LANE : LANE + lon]
        fwm_ref[j] = here + pltpu.roll(wind, 1, 1)[:, LANE : LANE + lon]
        return carry

    lax.fori_loop(0, z.band, face_rows, 0)

    def face_cols(j, carry):
        fwy_ref[j] = (cy_ref[j] + cy_ref[j + 1]) * (1.0 / 24.0)
        return carry

    lax.fori_loop(0, z.band + 1, face_cols, 0)

    def write(row, f, at, k, values):
        new_ref[row, f, :, pl.ds(pl.multiple_of(at + (k + 1) * LANE, LANE), LANE)] = values

    substep(z, z.band, 0, lambda j, f, piece: u_ref[j, f, :, piece], fwx_ref, fwm_ref, fwy_ref, write)
    for r in range(2):
        for row, out_ref in ((6 * (1 - b) + r, one_out_ref), (6 * b + r, two_out_ref)):
            values = new_ref[row, :, :, LANE : LANE + lon]
            encode_row(values.reshape(2 * half, lon), out_ref, r * z.code)
    for j in range(z.band):
        new_ref[j, :, :, 0:LANE] = new_ref[j, :, :, lon : lon + LANE]
        new_ref[j, :, :, LANE + lon :] = new_ref[j, :, :, LANE : 2 * LANE]


def filter_kernel(z, par_ref, cut_ref, forward_ref, back_ref, in_ref, new_ref):
    for j in range(z.band):
        new_ref[j] = in_ref[j]

    def store(row, values):
        put_padded(new_ref, (row,), values, z.lon)

    for part in range(2):
        filter_rows(
            z, cut_ref, par_ref[1], part * z.rows, (forward_ref, back_ref),
            lambda row: in_ref[row, :, :, LANE : LANE + z.lon], store,
        )


def second_kernel(
    z, parts, partner, par_ref, cut_ref, new_ref, fwx_ref, fwm_ref, fwy_ref, one_ref, two_ref, forward_ref,
    back_ref, *refs,
):
    refs = refs if partner else refs[1:]
    out_refs, (ends_ref, v_ref) = refs[:parts], refs[parts:]
    lon, half = z.lon, z.half
    tall = 2 * half
    side = 1 - par_ref[0] if partner else par_ref[0]
    base = z.rows * side

    def halo(in_ref):
        for r in range(2):
            values = decode_row(in_ref, r * z.code, lon).reshape(2, half, lon)
            put_padded(ends_ref, (2 * side + r,), values, lon)

    first_swap = side + par_ref[3] == 1
    pl.when(first_swap)(lambda: halo(one_ref))
    pl.when(jnp.logical_not(first_swap))(lambda: halo(two_ref))
    for r in range(2):
        ends_ref[2 * (1 - side) + r] = new_ref[z.rows - 2 * side + r]

    def row_of(j, f, piece):
        if 2 <= j < z.rows + 2:
            return new_ref[base + j - 2, f, :, piece]
        return ends_ref[j if j < 2 else j - z.rows, f, :, piece]

    def write(row, f, at, k, values):
        v_ref[row, f, :, pl.ds(pl.multiple_of(at + k * LANE, LANE), LANE)] = values

    substep(z, z.rows, base, row_of, fwx_ref, fwm_ref, fwy_ref, write)

    def store(row, values):
        v_ref[row] = values

    filter_rows(z, cut_ref, par_ref[1] + base, 0, (forward_ref, back_ref), lambda row: v_ref[row], store)
    column = lon // parts
    for b in range(parts):
        at = pl.multiple_of(jnp.bitwise_xor(par_ref[2], b) * column, LANE)
        values = jnp.concatenate(
            [v_ref[r, :, :, pl.ds(at, column)].reshape(tall, column) for r in range(z.rows)], axis=1
        )
        encode_row(values, out_refs[b], 0)


def column_kernel(z, parts, par_ref, *refs):
    got, (remap_ref, upward_ref, surface_ref, out_ref, geo_ref, x_ref) = refs[: 2 * parts], refs[2 * parts :]
    p, lev = par_ref[0], par_ref[2]
    column = out_ref.shape[-1]
    at = pl.multiple_of(pl.program_id(0) * column, LANE)
    for i, ref in enumerate(got):
        side = p if i < parts else 1 - p
        s = jnp.bitwise_xor(lev, i % parts)
        scale = decoder(ref[:, z.rows * column : z.rows * column + LANE])
        codes = ref[:, pl.ds(at, column)].astype(jnp.int32).astype(jnp.float32)
        values = codes * tiled(scale, column)
        level = pl.multiple_of(s * z.levels + side * z.half, z.half)
        for f in range(2):
            x_ref[f, pl.ds(level, z.half)] = values[f * z.half : (f + 1) * z.half]
    high, low = split(remap_ref[...])
    remap = jnp.concatenate([high, low, high], axis=1)
    count = remap_ref.shape[0]
    for f in range(2):
        high, low = split(x_ref[f])
        stacked = jnp.concatenate([high, high, low], axis=0)
        left = remap if f == 0 else jnp.concatenate([remap, upward_ref[...].astype(jnp.bfloat16)], axis=0)
        result = jnp.dot(left, stacked, preferred_element_type=jnp.float32)
        out_ref[f, 0] = result[:count]
        if f == 1:
            geo_ref[0] = surface_ref[0] + result[count:] * (count**-0.5)


def whole():
    return pl.BlockSpec(memory_space=pltpu.VMEM)


def scalars():
    return pl.BlockSpec(memory_space=pltpu.SMEM)


def far_memory():
    return pl.BlockSpec(memory_space=pltpu.HBM)


def params(limit=VMEM_LIMIT):
    return pltpu.CompilerParams(vmem_limit_bytes=limit)


def cost(flops=1000, data=1000):
    return pl.CostEstimate(flops=flops, bytes_accessed=data, transcendentals=0)


def shards(fields, courant, cutoffs, surface, remap_weights):
    _, rows, levels, lon = fields.shape
    z = Sizes(rows, levels, lon)
    lats, parts = lax.axis_size("lat"), lax.axis_size("lev")
    me = lax.axis_index("lat")
    parity = me % 2
    lev = lax.axis_index("lev")
    place = jnp.stack([parity, (me - parity) * rows, lev, (me // 2) % 2]).astype(jnp.int32)
    tall = 2 * z.half
    i16, f32 = jnp.int16, jnp.float32
    swap = [(i, i ^ 1) for i in range(lats)]
    ones, twos = [
        [pair for i in range(start, lats - 2, 4) for s in range(2) for pair in ((i + s, i + s + 2), (i + s + 2, i + s))]
        for start in (0, 2)
    ]

    def shape(*dims):
        return jax.ShapeDtypeStruct(dims, f32)

    def codes(*dims):
        return jax.ShapeDtypeStruct(dims, i16)

    edge = pl.pallas_call(
        functools.partial(edge_kernel, z),
        name="edge",
        in_specs=[scalars(), far_memory(), far_memory()],
        out_specs=whole(),
        out_shape=codes(tall, z.edge),
        scratch_shapes=[
            pltpu.VMEM((2, tall, lon), f32),
            pltpu.VMEM((2, levels, lon), courant.dtype),
            pltpu.SemaphoreType.DMA((6,)),
        ],
        compiler_params=params(VMEM_MOST),
        cost_estimate=cost(),
    )(place, fields, courant)
    edge = lax.ppermute(edge, "lat", swap)
    inner, own = pl.pallas_call(
        functools.partial(rest_kernel, z),
        name="rest",
        in_specs=[scalars(), far_memory(), far_memory()],
        out_specs=[whole()] * 2,
        out_shape=[codes(tall, z.inner), codes(tall, z.edge)],
        scratch_shapes=[
            pltpu.VMEM((4, tall, lon), f32),
            pltpu.VMEM((4, 2, levels, lon), courant.dtype),
            pltpu.SemaphoreType.DMA((16,)),
        ],
        compiler_params=params(VMEM_MOST),
        cost_estimate=cost(),
    )(place, fields, courant)
    inner = lax.ppermute(inner, "lat", swap)
    straight = (parity + (me // 2) % 2) == 1
    one = lax.ppermute(jnp.where(straight, own, edge), "lat", ones)
    two = lax.ppermute(jnp.where(straight, edge, own), "lat", twos)
    new, fwx, fwm, fwy, one_code, two_code = pl.pallas_call(
        functools.partial(first_kernel, z),
        name="first",
        in_specs=[scalars()] + [whole()] * 6,
        out_specs=[whole()] * 6,
        out_shape=[
            shape(z.band, 2, z.half, z.pad),
            shape(z.band, z.half, lon),
            shape(z.band, z.half, lon),
            shape(z.band + 1, z.half, lon),
            codes(tall, 2 * z.code),
            codes(tall, 2 * z.code),
        ],
        scratch_shapes=[
            pltpu.VMEM((z.band + 4, 2, z.half, z.pad), f32),
            pltpu.VMEM((z.band, z.half, z.pad), f32),
            pltpu.VMEM((z.band + 2, z.half, z.lon), f32),
        ],
        compiler_params=params(),
        cost_estimate=cost(),
    )(place, fields, courant, edge, inner, one, two)
    one = lax.ppermute(one_code, "lat", ones)
    two = lax.ppermute(two_code, "lat", twos)

    forward, back = (jnp.asarray(t) for t in filter_tables(lon))
    new = pl.pallas_call(
        functools.partial(filter_kernel, z),
        name="smooth",
        in_specs=[scalars(), scalars()] + [whole()] * 3,
        out_specs=whole(),
        out_shape=shape(z.band, 2, z.half, z.pad),
        compiler_params=params(),
        cost_estimate=cost(),
    )(place, cutoffs, forward, back, new)

    column = lon // parts

    def second(*after):
        partner = not after
        return pl.pallas_call(
            functools.partial(second_kernel, z, parts, partner),
            name="second_partner" if partner else "second_own",
            in_specs=[scalars(), scalars()] + [whole()] * 8 + [far_memory()] * len(after),
            out_specs=[whole()] * parts,
            out_shape=[codes(tall, rows * column + LANE)] * parts,
            scratch_shapes=[
                pltpu.VMEM((4, 2, z.half, z.pad), f32),
                pltpu.VMEM((z.rows, 2, z.half, lon), f32),
            ],
            compiler_params=params(),
            cost_estimate=cost() if partner else cost(10**9, 10**7),
        )(place, cutoffs, new, fwx, fwm, fwy, one, two, forward, back, *after)

    got = []
    blocks = second()
    for b, block in enumerate(blocks):
        pairs = [
            (i * parts + j, (i ^ 1) * parts + (j ^ b)) for i in range(lats) for j in range(parts)
        ]
        got.append(lax.ppermute(block, ("lat", "lev"), pairs))
    for b, block in enumerate(second(blocks[0])):
        pairs = [(j, j ^ b) for j in range(parts)]
        got.insert(b, lax.ppermute(block, "lev", pairs) if b else block)

    count = remap_weights.shape[0]
    upward = np.triu(np.ones((count, count), np.float32), 1) + 0.5 * np.eye(count, dtype=np.float32)
    upward = jnp.asarray(np.concatenate([upward, 0.0 * upward, upward], axis=1))
    surface = lax.dynamic_slice_in_dim(surface, lev * column, column, 1)
    remapped, geopotential = pl.pallas_call(
        functools.partial(column_kernel, z, parts),
        name="columns",
        grid=(rows,),
        in_specs=[scalars()]
        + [whole()] * len(got)
        + [
            pl.BlockSpec(remap_weights.shape, lambda r: (0, 0)),
            pl.BlockSpec(upward.shape, lambda r: (0, 0)),
            pl.BlockSpec((1, 1, column), lambda r: (r, 0, 0)),
        ],
        out_specs=[
            pl.BlockSpec((2, 1, count, column), lambda r: (0, r, 0, 0)),
            pl.BlockSpec((1, count, column), lambda r: (r, 0, 0)),
        ],
        out_shape=[shape(2, rows, count, column), shape(rows, count, column)],
        scratch_shapes=[pltpu.VMEM((2, count, column), f32)],
        compiler_params=params(),
        cost_estimate=cost(),
    )(place, *got, remap_weights, upward, surface[:, None, :])
    return remapped, geopotential


def with_halo(shard, width):
    size, length = lax.axis_size("lat"), shard.shape[1]
    up = [(i, (i + 1) % size) for i in range(size - 1)]
    down = [(j, i) for i, j in up]
    before = lax.ppermute(lax.slice_in_dim(shard, length - width, length, axis=1), "lat", up)
    after = lax.ppermute(lax.slice_in_dim(shard, 0, width, axis=1), "lat", down)
    return jnp.concatenate([before, shard, after], axis=1)


def plain_shards(fields, courant, cutoffs, surface, remap_weights):
    _, rows, _, lon = fields.shape
    exact = lax.Precision.HIGHEST
    cut = lax.dynamic_slice_in_dim(cutoffs, lax.axis_index("lat") * rows, rows)
    waves = np.arange(KMAX)
    angle = (np.arange(lon)[:, None] * waves[None, :] % lon) * (2.0 * math.pi / lon)
    table = jnp.asarray(np.concatenate([np.cos(angle), np.sin(angle)], axis=1).astype(np.float32))
    number = jnp.asarray(np.concatenate([waves, waves]).astype(np.int32))
    weight = jnp.where(number[None] <= cut[:, None], jnp.where(number == 0, 1.0, 2.0)[None] / lon, 0.0)
    flagged = cut < lon // 2

    def smooth(values):
        wave = jnp.einsum("frln,nk->frlk", values, table, precision=exact) * weight[None, :, None]
        low = jnp.einsum("frlk,nk->frln", wave, table, precision=exact)
        return jnp.where(flagged[None, :, None, None], low, values)

    winds = with_halo(courant, 1).astype(jnp.float32)
    east, north = winds[0, 1:-1], winds[1]
    face_x = (east + jnp.roll(east, -1, -1)) / 24.0
    face_y = (north[:-1] + north[1:]) / 24.0
    u = fields
    for _ in range(2):
        wide = with_halo(u, 2)
        pair = u + jnp.roll(u, -1, -1)
        fx = face_x * (8.0 * pair - (jnp.roll(pair, 1, -1) + jnp.roll(pair, -1, -1)))
        pair = wide[:, :-1] + wide[:, 1:]
        fy = face_y * (8.0 * pair[:, 1:-1] - (pair[:, :-2] + pair[:, 2:]))
        u = u - (fx - jnp.roll(fx, 1, -1)) - (fy[:, 1:] - fy[:, :-1])
        u = lax.cond(jnp.any(flagged), smooth, lambda values: values, u)
    columns = lax.all_to_all(u, "lev", split_axis=3, concat_axis=2, tiled=True)
    remapped = jnp.einsum("pk,fjkn->fjpn", remap_weights, columns, precision=exact)
    count = remap_weights.shape[0]
    upward = np.triu(np.ones((count, count), np.float32), 1) + 0.5 * np.eye(count, dtype=np.float32)
    upward = jnp.einsum("kl,jln->jkn", jnp.asarray(upward), columns[1], precision=exact)
    width = lon // lax.axis_size("lev")
    mine = lax.dynamic_slice_in_dim(surface, lax.axis_index("lev") * width, width, 1)
    return remapped, mine[:, None] + count**-0.5 * upward


def solution(mesh):
    def program(fields, courant, cutoffs, surface, remap_weights):
        lats, parts = mesh.shape["lat"], mesh.shape["lev"]
        rows, levels = fields.shape[1] // lats, fields.shape[2] // parts
        polar = fields.shape[1] // 8
        paired = (
            lats % 2 == 0
            and rows == 4
            and levels % 16 == 0
            and polar <= 2 * rows - 2
            and fields.shape[3] % (LANE * parts) == 0
            and parts & (parts - 1) == 0
        )
        return jax.shard_map(
            shards if paired else plain_shards,
            mesh=mesh,
            in_specs=(
                P(None, "lat", "lev", None),
                P(None, "lat", "lev", None),
                P(),
                P("lat", None),
                P(),
            ),
            out_specs=(P(None, "lat", None, "lev"), P("lat", None, "lev")),
            check_vma=False,
        )(fields, courant, cutoffs, surface, remap_weights)

    return program
```

```python
import functools
import math

import jax
import jax.numpy as jnp
import ml_dtypes
import numpy as np
from jax import lax
from jax.experimental import pallas as pl
from jax.experimental.pallas import tpu as pltpu
from jax.sharding import PartitionSpec as P

KMAX = 128
LANE = 128
TOP = 32767.0
STEPS = 256.0
TINY = 2.0**-100
WIND = 81920.0
ROUND = 1.5 * 2.0**23
VMEM_LIMIT = 12 * 2**20
VMEM_MOST = 63 * 2**20 + 2**19


def rounded(values):
    return ((values + ROUND) - ROUND).astype(jnp.int32).astype(jnp.int16)


def lane_max(values):
    chunks = [jnp.abs(values[:, i : i + LANE]) for i in range(0, values.shape[1], LANE)]
    while len(chunks) > 1:
        pairs = [jnp.maximum(a, b) for a, b in zip(chunks[0::2], chunks[1::2])]
        chunks = pairs + chunks[2 * len(pairs) :]
    return chunks[0]


def tiled(tile, width):
    return jnp.concatenate([tile] * (width // LANE), axis=1)


def scale_code(largest):
    return jnp.ceil(jnp.log2(jnp.maximum(largest, TINY)) * STEPS)


def encoder(code):
    return TOP / jnp.exp2(code * (1.0 / STEPS))


def decoder(code16):
    code = code16.astype(jnp.int32).astype(jnp.float32)
    return jnp.exp2(code * (1.0 / STEPS)) * (1.0 / TOP)


def encode_row(values, out_ref, at):
    width = values.shape[1]
    code = scale_code(lane_max(values))
    out_ref[:, at : at + width] = rounded(values * tiled(encoder(code), width))
    out_ref[:, at + width : at + width + LANE] = code.astype(jnp.int32).astype(jnp.int16)


def decode_row(in_ref, at, width):
    scale = decoder(in_ref[:, at + width : at + width + LANE])
    values = in_ref[:, at : at + width].astype(jnp.int32).astype(jnp.float32)
    return values * tiled(scale, width)


def wind_codes(east, north):
    return rounded(jnp.concatenate([east, north], axis=0) * WIND)


class Sizes:
    def __init__(self, rows, levels, lon):
        self.rows, self.levels, self.lon = rows, levels, lon
        self.half = levels // 2
        self.band = 2 * rows
        self.pad = lon + 2 * LANE
        self.code = lon + LANE
        self.edge = 2 * self.code + lon
        self.inner = 2 * self.code + 3 * lon


def put_padded(ref, index, values, lon):
    ref[index + (Ellipsis, slice(LANE, LANE + lon))] = values
    ref[index + (Ellipsis, slice(0, LANE))] = values[..., lon - LANE :]
    ref[index + (Ellipsis, slice(LANE + lon, 2 * LANE + lon))] = values[..., :LANE]


def wind_row(z, wind, upper):
    halves = []
    for k in range(2):
        both = wind[k].astype(jnp.float32)
        halves.append(jnp.where(upper == 1, both[z.half :], both[: z.half]))
    return wind_codes(*halves)


def edge_kernel(z, fields_ref, courant_ref, edge_ref, rows_ref, wind_ref, sems):
    p = lax.rem(lax.axis_index("lat"), 2)
    give = pl.multiple_of((1 - p) * z.half, z.half)
    copies = [
        pltpu.make_async_copy(
            fields_ref.at[f, 2 * p + r, pl.ds(give, z.half)],
            rows_ref.at[r, pl.ds(f * z.half, z.half)],
            sems.at[2 * r + f],
        )
        for r in range(2)
        for f in range(2)
    ]
    copies += [
        pltpu.make_async_copy(courant_ref.at[k, 3 * p], wind_ref.at[k], sems.at[4 + k])
        for k in range(2)
    ]
    for copy in copies:
        copy.start()
    for r in range(2):
        copies[2 * r].wait()
        copies[2 * r + 1].wait()
        encode_row(rows_ref[r], edge_ref, r * z.code)
    copies[4].wait()
    copies[5].wait()
    edge_ref[:, 2 * z.code :] = wind_row(z, wind_ref, 1 - p)


def rest_kernel(z, par_ref, fields_ref, courant_ref, inner_ref, own_ref):
    p = par_ref[0]
    keep = pl.multiple_of(p * z.half, z.half)
    give = pl.multiple_of((1 - p) * z.half, z.half)

    def field_row(row, start):
        return jnp.concatenate([fields_ref[f, row, pl.ds(start, z.half)] for f in range(2)], axis=0)

    def winds(row, upper):
        return wind_row(z, [courant_ref[k, row] for k in range(2)], upper)

    edge, inner = 2 * p, 2 * (1 - p)
    at = 2 * z.code
    for r in range(2):
        encode_row(field_row(inner + r, give), inner_ref, r * z.code)
    for i, row in enumerate((inner, inner + 1, 1 + p)):
        inner_ref[:, at + i * z.lon : at + (i + 1) * z.lon] = winds(row, 1 - p)
    for r in range(2):
        encode_row(field_row(edge + r, keep), own_ref, r * z.code)
    own_ref[:, at : at + z.lon] = winds(3 * p, p)


def shifted(pieces, shift, lanes):
    turned = [pltpu.roll(v, (-shift) % LANE, 1) for v in pieces]
    if shift > 0:
        return [jnp.where(lanes < LANE - shift, a, b) for a, b in zip(turned[1:-1], turned[2:])]
    return [jnp.where(lanes < -shift, a, b) for a, b in zip(turned[:-2], turned[1:-1])]


def substep(z, count_rows, base, row_of, fwx_ref, fwm_ref, fwy_ref, write):
    count = next(n for n in (4, 3, 2, 1) if z.lon % (n * LANE) == 0)
    width = count * LANE
    lanes = lax.broadcasted_iota(jnp.int32, (z.half, LANE), 1)

    def part(i, carry):
        at = pl.multiple_of(i * width, LANE)

        def piece(k):
            return pl.ds(pl.multiple_of(at + k * LANE, LANE), LANE)

        def row(j, f):
            return [row_of(j, f, piece(k + 1)) for k in range(count)]

        def start(j, f):
            pieces = [row_of(j + 2, f, piece(k)) for k in range(count + 2)]
            return [shifted(pieces, s, lanes) for s in (-2, -1, 1, 2)]

        def lon_part(j, u, moved):
            out = []
            for k in range(count):
                m2, m1, p1, p2 = (m[k] for m in moved)
                east = 7.0 * (u[k] + p1) - (m1 + p2)
                west = 7.0 * (m1 + u[k]) - (m2 + p1)
                out.append(fwx_ref[base + j, :, piece(k)] * east - fwm_ref[base + j, :, piece(k)] * west)
            return out

        for f in range(2):
            rows = [row(j, f) for j in range(4)]
            sums = [[a + b for a, b in zip(rows[j], rows[j + 1])] for j in range(3)]
            flux = None
            moved = start(0, f)
            for j in range(count_rows + 1):
                later = start(j, f) if 0 < j < count_rows else None
                new = [
                    fwy_ref[base + j, :, piece(k)] * (8.0 * sums[1][k] - (sums[0][k] + sums[2][k]))
                    for k in range(count)
                ]
                if j > 0:
                    u = rows[1]
                    change = lon_part(j - 1, u, moved)
                    for k in range(count):
                        write(j - 1, f, at, k, u[k] - change[k] - (new[k] - flux[k]))
                    moved = later
                flux = new
                if j < count_rows:
                    above = row(j + 4, f)
                    rows = rows[1:] + [above]
                    sums = sums[1:] + [[a + b for a, b in zip(rows[2], rows[3])]]
        return carry

    lax.fori_loop(0, z.lon // width, part, 0)


def filter_tables(lon):
    points = np.arange(lon // 2)
    forward, back = [], []
    for parity in range(2):
        waves = np.arange(parity, KMAX, 2)
        angle = (points[:, None] * waves[None, :] % lon) * (2.0 * math.pi / lon)
        table = np.concatenate([np.cos(angle), np.sin(angle)], axis=1).astype(np.float32)
        high = table.astype(ml_dtypes.bfloat16)
        low = (table - high.astype(np.float32)).astype(ml_dtypes.bfloat16)
        forward.append(np.concatenate([high, low], axis=1))
        back.append(np.concatenate([high.T, low.T], axis=0))
    return np.stack(forward), np.stack(back)


def split(values):
    high = values.astype(jnp.bfloat16)
    return high, (values - high.astype(jnp.float32)).astype(jnp.bfloat16)


def low_pass(z, rows, cuts, forward_ref, back_ref):
    half = z.lon // 2
    count = len(rows)
    tall = 2 * z.half
    total = count * tall
    flat = [row.reshape(tall, z.lon) for row in rows]
    folded = []
    for parity in range(2):
        parts = [
            row[:, :half] + row[:, half:] if parity == 0 else row[:, :half] - row[:, half:]
            for row in flat
        ]
        high, low = split(jnp.concatenate(parts, axis=0))
        both = jnp.concatenate([high, low], axis=0)
        got = jnp.dot(both, forward_ref[parity], preferred_element_type=jnp.float32)
        wave = got[:total, :KMAX] + got[:total, KMAX:] + (got[total:, :KMAX] + got[total:, KMAX:])
        number = 2 * (lax.broadcasted_iota(jnp.int32, (tall, KMAX), 1) % (KMAX // 2)) + parity
        doubled = jnp.where(number == 0, 1.0, 2.0) * (1.0 / z.lon)
        weight = jnp.concatenate([jnp.where(number <= cut, doubled, 0.0) for cut in cuts], axis=0)
        high, low = split(wave * weight)
        both = jnp.concatenate(
            [jnp.concatenate([high, high], axis=1), jnp.concatenate([low, low], axis=1)], axis=0
        )
        got = jnp.dot(both, back_ref[parity], preferred_element_type=jnp.float32)
        folded.append(got[:total] + got[total:])
    left, right = folded[0] + folded[1], folded[0] - folded[1]
    smooth = jnp.concatenate([left, right], axis=1)
    return [smooth[i * tall : (i + 1) * tall].reshape(2, z.half, z.lon) for i in range(count)]


def filter_rows(z, cut_ref, first_row, start, tables, load, store):
    nyquist = z.lon // 2
    cuts = [cut_ref[first_row + start + r] for r in range(z.rows)]
    some = functools.reduce(jnp.logical_or, [cut < nyquist for cut in cuts])

    @pl.when(some)
    def _():
        smooth = low_pass(z, [load(start + r) for r in range(z.rows)], cuts, *tables)
        for r in range(z.rows):

            @pl.when(cuts[r] < nyquist)
            def _():
                store(start + r, smooth[r])


def first_kernel(
    z, par_ref, fields_ref, courant_ref, edge_ref, inner_ref, one_ref, two_ref,
    new_ref, fwx_ref, fwm_ref, fwy_ref, one_out_ref, two_out_ref, u_ref, cx_ref, cy_ref,
):
    p, b = par_ref[0], par_ref[3]
    lon, half = z.lon, z.half

    def pair(values):
        return values.reshape(2, half, values.shape[1])

    def winds(in_ref, at):
        values = in_ref[:, at : at + lon].astype(jnp.int32).astype(jnp.float32) * (1.0 / WIND)
        return values[:half], values[half:]

    def place_wind(row, east, north):
        put_padded(cx_ref, (row,), east, lon)
        cy_ref[row + 1] = north

    keep = pl.multiple_of(p * half, half)
    for r in range(z.rows):
        row = z.rows * p + r
        own = jnp.stack([fields_ref[f, r, pl.ds(keep, half)] for f in range(2)])
        put_padded(u_ref, (row + 2,), own, lon)
        got = []
        for k in range(2):
            wind = courant_ref[k, r].astype(jnp.float32)
            got.append(jnp.where(p == 1, wind[half:], wind[:half]))
        place_wind(row, *got)
    at = 2 * z.code
    for r in range(2):
        put_padded(u_ref, (6 * (1 - p) + r + 2,), pair(decode_row(edge_ref, r * z.code, lon)), lon)
        put_padded(u_ref, (4 - 2 * p + r + 2,), pair(decode_row(inner_ref, r * z.code, lon)), lon)
        put_padded(u_ref, (10 * (1 - b) + r,), pair(decode_row(one_ref, r * z.code, lon)), lon)
        put_padded(u_ref, (10 * b + r,), pair(decode_row(two_ref, r * z.code, lon)), lon)
        place_wind(4 - 2 * p + r, *winds(inner_ref, at + r * lon))
    place_wind(7 * (1 - p), *winds(edge_ref, at))
    place_wind(6 - 5 * p, *winds(inner_ref, at + 2 * lon))
    cy_ref[9 * (1 - b)] = winds(one_ref, at)[1]
    cy_ref[9 * b] = winds(two_ref, at)[1]

    def face_rows(j, carry):
        wind = cx_ref[j] * (1.0 / 24.0)
        here = wind[:, LANE : LANE + lon]
        fwx_ref[j] = here + pltpu.roll(wind, z.pad - 1, 1)[:, LANE : LANE + lon]
        fwm_ref[j] = here + pltpu.roll(wind, 1, 1)[:, LANE : LANE + lon]
        return carry

    lax.fori_loop(0, z.band, face_rows, 0)

    def face_cols(j, carry):
        fwy_ref[j] = (cy_ref[j] + cy_ref[j + 1]) * (1.0 / 24.0)
        return carry

    lax.fori_loop(0, z.band + 1, face_cols, 0)

    def write(row, f, at, k, values):
        new_ref[row, f, :, pl.ds(pl.multiple_of(at + (k + 1) * LANE, LANE), LANE)] = values

    substep(z, z.band, 0, lambda j, f, piece: u_ref[j, f, :, piece], fwx_ref, fwm_ref, fwy_ref, write)
    for r in range(2):
        for row, out_ref in ((6 * (1 - b) + r, one_out_ref), (6 * b + r, two_out_ref)):
            values = new_ref[row, :, :, LANE : LANE + lon]
            encode_row(values.reshape(2 * half, lon), out_ref, r * z.code)
    for j in range(z.band):
        new_ref[j, :, :, 0:LANE] = new_ref[j, :, :, lon : lon + LANE]
        new_ref[j, :, :, LANE + lon :] = new_ref[j, :, :, LANE : 2 * LANE]


def filter_kernel(z, par_ref, cut_ref, forward_ref, back_ref, in_ref, new_ref):
    for j in range(z.band):
        new_ref[j] = in_ref[j]

    def store(row, values):
        put_padded(new_ref, (row,), values, z.lon)

    for part in range(2):
        filter_rows(
            z, cut_ref, par_ref[1], part * z.rows, (forward_ref, back_ref),
            lambda row: in_ref[row, :, :, LANE : LANE + z.lon], store,
        )


def second_kernel(
    z, parts, partner, par_ref, cut_ref, new_ref, fwx_ref, fwm_ref, fwy_ref, one_ref, two_ref, forward_ref,
    back_ref, *refs,
):
    refs = refs if partner else refs[1:]
    out_refs, (ends_ref, v_ref) = refs[:parts], refs[parts:]
    lon, half = z.lon, z.half
    tall = 2 * half
    side = 1 - par_ref[0] if partner else par_ref[0]
    base = z.rows * side

    def halo(in_ref):
        for r in range(2):
            values = decode_row(in_ref, r * z.code, lon).reshape(2, half, lon)
            put_padded(ends_ref, (2 * side + r,), values, lon)

    first_swap = side + par_ref[3] == 1
    pl.when(first_swap)(lambda: halo(one_ref))
    pl.when(jnp.logical_not(first_swap))(lambda: halo(two_ref))
    for r in range(2):
        ends_ref[2 * (1 - side) + r] = new_ref[z.rows - 2 * side + r]

    def row_of(j, f, piece):
        if 2 <= j < z.rows + 2:
            return new_ref[base + j - 2, f, :, piece]
        return ends_ref[j if j < 2 else j - z.rows, f, :, piece]

    def write(row, f, at, k, values):
        v_ref[row, f, :, pl.ds(pl.multiple_of(at + k * LANE, LANE), LANE)] = values

    substep(z, z.rows, base, row_of, fwx_ref, fwm_ref, fwy_ref, write)

    def store(row, values):
        v_ref[row] = values

    filter_rows(z, cut_ref, par_ref[1] + base, 0, (forward_ref, back_ref), lambda row: v_ref[row], store)
    column = lon // parts
    for b in range(parts):
        at = pl.multiple_of(jnp.bitwise_xor(par_ref[2], b) * column, LANE)
        values = jnp.concatenate(
            [v_ref[r, :, :, pl.ds(at, column)].reshape(tall, column) for r in range(z.rows)], axis=1
        )
        encode_row(values, out_refs[b], 0)


def scale_kernel(at, *refs):
    for i, ref in enumerate(refs[:-1]):
        refs[-1][i] = decoder(ref[:, at : at + LANE])


def column_kernel(z, parts, par_ref, *refs):
    got, (scales_ref, remap_ref, upward_ref, surface_ref, out_ref, geo_ref, x_ref) = refs[: 2 * parts], refs[2 * parts :]
    p, lev = par_ref[0], par_ref[2]
    column = out_ref.shape[-1]
    at = pl.multiple_of(pl.program_id(0) * column, LANE)
    for i, ref in enumerate(got):
        side = p if i < parts else 1 - p
        s = jnp.bitwise_xor(lev, i % parts)
        if i < parts:
            scale = decoder(ref[:, z.rows * column : z.rows * column + LANE])
        else:
            scale = scales_ref[i - parts]
        codes = ref[:, pl.ds(at, column)].astype(jnp.int32).astype(jnp.float32)
        values = codes * tiled(scale, column)
        level = pl.multiple_of(s * z.levels + side * z.half, z.half)
        for f in range(2):
            x_ref[f, pl.ds(level, z.half)] = values[f * z.half : (f + 1) * z.half]
    high, low = split(remap_ref[...])
    remap = jnp.concatenate([high, low, high], axis=1)
    count = remap_ref.shape[0]
    for f in range(2):
        high, low = split(x_ref[f])
        stacked = jnp.concatenate([high, high, low], axis=0)
        left = remap if f == 0 else jnp.concatenate([remap, upward_ref[...].astype(jnp.bfloat16)], axis=0)
        result = jnp.dot(left, stacked, preferred_element_type=jnp.float32)
        out_ref[f, 0] = result[:count]
        if f == 1:
            geo_ref[0] = surface_ref[0] + result[count:] * (count**-0.5)


def whole():
    return pl.BlockSpec(memory_space=pltpu.VMEM)


def scalars():
    return pl.BlockSpec(memory_space=pltpu.SMEM)


def far_memory():
    return pl.BlockSpec(memory_space=pltpu.HBM)


def params(limit=VMEM_LIMIT):
    return pltpu.CompilerParams(vmem_limit_bytes=limit)


def cost(flops=1000, data=1000):
    return pl.CostEstimate(flops=flops, bytes_accessed=data, transcendentals=0)


def shards(fields, courant, cutoffs, surface, remap_weights):
    _, rows, levels, lon = fields.shape
    z = Sizes(rows, levels, lon)
    lats, parts = lax.axis_size("lat"), lax.axis_size("lev")
    me = lax.axis_index("lat")
    parity = me % 2
    lev = lax.axis_index("lev")
    place = jnp.stack([parity, (me - parity) * rows, lev, (me // 2) % 2]).astype(jnp.int32)
    tall = 2 * z.half
    i16, f32 = jnp.int16, jnp.float32
    swap = [(i, i ^ 1) for i in range(lats)]
    ones, twos = [
        [pair for i in range(start, lats - 2, 4) for s in range(2) for pair in ((i + s, i + s + 2), (i + s + 2, i + s))]
        for start in (0, 2)
    ]

    def shape(*dims):
        return jax.ShapeDtypeStruct(dims, f32)

    def codes(*dims):
        return jax.ShapeDtypeStruct(dims, i16)

    edge = pl.pallas_call(
        functools.partial(edge_kernel, z),
        name="edge",
        in_specs=[far_memory(), far_memory()],
        out_specs=whole(),
        out_shape=codes(tall, z.edge),
        scratch_shapes=[
            pltpu.VMEM((2, tall, lon), f32),
            pltpu.VMEM((2, levels, lon), courant.dtype),
            pltpu.SemaphoreType.DMA((6,)),
        ],
        compiler_params=params(VMEM_MOST),
        cost_estimate=cost(),
    )(fields, courant)
    edge = lax.ppermute(edge, "lat", swap)
    inner, own = pl.pallas_call(
        functools.partial(rest_kernel, z),
        name="rest",
        in_specs=[scalars(), whole(), whole()],
        out_specs=[whole()] * 2,
        out_shape=[codes(tall, z.inner), codes(tall, z.edge)],
        compiler_params=params(),
        cost_estimate=cost(),
    )(place, fields, courant)
    inner = lax.ppermute(inner, "lat", swap)
    straight = (parity + (me // 2) % 2) == 1
    one = lax.ppermute(jnp.where(straight, own, edge), "lat", ones)
    two = lax.ppermute(jnp.where(straight, edge, own), "lat", twos)
    new, fwx, fwm, fwy, one_code, two_code = pl.pallas_call(
        functools.partial(first_kernel, z),
        name="first",
        in_specs=[scalars()] + [whole()] * 6,
        out_specs=[whole()] * 6,
        out_shape=[
            shape(z.band, 2, z.half, z.pad),
            shape(z.band, z.half, lon),
            shape(z.band, z.half, lon),
            shape(z.band + 1, z.half, lon),
            codes(tall, 2 * z.code),
            codes(tall, 2 * z.code),
        ],
        scratch_shapes=[
            pltpu.VMEM((z.band + 4, 2, z.half, z.pad), f32),
            pltpu.VMEM((z.band, z.half, z.pad), f32),
            pltpu.VMEM((z.band + 2, z.half, z.lon), f32),
        ],
        compiler_params=params(),
        cost_estimate=cost(),
    )(place, fields, courant, edge, inner, one, two)
    one = lax.ppermute(one_code, "lat", ones)
    two = lax.ppermute(two_code, "lat", twos)

    forward, back = (jnp.asarray(t) for t in filter_tables(lon))
    new = pl.pallas_call(
        functools.partial(filter_kernel, z),
        name="smooth",
        in_specs=[scalars(), scalars()] + [whole()] * 3,
        out_specs=whole(),
        out_shape=shape(z.band, 2, z.half, z.pad),
        compiler_params=params(),
        cost_estimate=cost(),
    )(place, cutoffs, forward, back, new)

    column = lon // parts

    def second(*after):
        partner = not after
        return pl.pallas_call(
            functools.partial(second_kernel, z, parts, partner),
            name="second_partner" if partner else "second_own",
            in_specs=[scalars(), scalars()] + [whole()] * 8 + [far_memory()] * len(after),
            out_specs=[whole()] * parts,
            out_shape=[codes(tall, rows * column + LANE)] * parts,
            scratch_shapes=[
                pltpu.VMEM((4, 2, z.half, z.pad), f32),
                pltpu.VMEM((z.rows, 2, z.half, lon), f32),
            ],
            compiler_params=params(),
            cost_estimate=cost() if partner else cost(10**9, 10**7),
        )(place, cutoffs, new, fwx, fwm, fwy, one, two, forward, back, *after)

    got = []
    blocks = second()
    for b, block in enumerate(blocks):
        pairs = [
            (i * parts + j, (i ^ 1) * parts + (j ^ b)) for i in range(lats) for j in range(parts)
        ]
        got.append(lax.ppermute(block, ("lat", "lev"), pairs))
    scales = pl.pallas_call(
        functools.partial(scale_kernel, rows * column),
        name="scales",
        in_specs=[whole()] * parts,
        out_specs=whole(),
        out_shape=shape(parts, tall, LANE),
        compiler_params=params(),
        cost_estimate=cost(10**9, 10**7),
    )(*got)
    for b, block in enumerate(second(blocks[0])):
        pairs = [(j, j ^ b) for j in range(parts)]
        got.insert(b, lax.ppermute(block, "lev", pairs) if b else block)

    count = remap_weights.shape[0]
    upward = np.triu(np.ones((count, count), np.float32), 1) + 0.5 * np.eye(count, dtype=np.float32)
    upward = jnp.asarray(np.concatenate([upward, 0.0 * upward, upward], axis=1))
    surface = lax.dynamic_slice_in_dim(surface, lev * column, column, 1)
    remapped, geopotential = pl.pallas_call(
        functools.partial(column_kernel, z, parts),
        name="columns",
        grid=(rows,),
        in_specs=[scalars()]
        + [whole()] * (len(got) + 1)
        + [
            pl.BlockSpec(remap_weights.shape, lambda r: (0, 0)),
            pl.BlockSpec(upward.shape, lambda r: (0, 0)),
            pl.BlockSpec((1, 1, column), lambda r: (r, 0, 0)),
        ],
        out_specs=[
            pl.BlockSpec((2, 1, count, column), lambda r: (0, r, 0, 0)),
            pl.BlockSpec((1, count, column), lambda r: (r, 0, 0)),
        ],
        out_shape=[shape(2, rows, count, column), shape(rows, count, column)],
        scratch_shapes=[pltpu.VMEM((2, count, column), f32)],
        compiler_params=params(),
        cost_estimate=cost(),
    )(place, *got, scales, remap_weights, upward, surface[:, None, :])
    return remapped, geopotential


def with_halo(shard, width):
    size, length = lax.axis_size("lat"), shard.shape[1]
    up = [(i, (i + 1) % size) for i in range(size - 1)]
    down = [(j, i) for i, j in up]
    before = lax.ppermute(lax.slice_in_dim(shard, length - width, length, axis=1), "lat", up)
    after = lax.ppermute(lax.slice_in_dim(shard, 0, width, axis=1), "lat", down)
    return jnp.concatenate([before, shard, after], axis=1)


def plain_shards(fields, courant, cutoffs, surface, remap_weights):
    _, rows, _, lon = fields.shape
    exact = lax.Precision.HIGHEST
    cut = lax.dynamic_slice_in_dim(cutoffs, lax.axis_index("lat") * rows, rows)
    waves = np.arange(KMAX)
    angle = (np.arange(lon)[:, None] * waves[None, :] % lon) * (2.0 * math.pi / lon)
    table = jnp.asarray(np.concatenate([np.cos(angle), np.sin(angle)], axis=1).astype(np.float32))
    number = jnp.asarray(np.concatenate([waves, waves]).astype(np.int32))
    weight = jnp.where(number[None] <= cut[:, None], jnp.where(number == 0, 1.0, 2.0)[None] / lon, 0.0)
    flagged = cut < lon // 2

    def smooth(values):
        wave = jnp.einsum("frln,nk->frlk", values, table, precision=exact) * weight[None, :, None]
        low = jnp.einsum("frlk,nk->frln", wave, table, precision=exact)
        return jnp.where(flagged[None, :, None, None], low, values)

    winds = with_halo(courant, 1).astype(jnp.float32)
    east, north = winds[0, 1:-1], winds[1]
    face_x = (east + jnp.roll(east, -1, -1)) / 24.0
    face_y = (north[:-1] + north[1:]) / 24.0
    u = fields
    for _ in range(2):
        wide = with_halo(u, 2)
        pair = u + jnp.roll(u, -1, -1)
        fx = face_x * (8.0 * pair - (jnp.roll(pair, 1, -1) + jnp.roll(pair, -1, -1)))
        pair = wide[:, :-1] + wide[:, 1:]
        fy = face_y * (8.0 * pair[:, 1:-1] - (pair[:, :-2] + pair[:, 2:]))
        u = u - (fx - jnp.roll(fx, 1, -1)) - (fy[:, 1:] - fy[:, :-1])
        u = lax.cond(jnp.any(flagged), smooth, lambda values: values, u)
    columns = lax.all_to_all(u, "lev", split_axis=3, concat_axis=2, tiled=True)
    remapped = jnp.einsum("pk,fjkn->fjpn", remap_weights, columns, precision=exact)
    count = remap_weights.shape[0]
    upward = np.triu(np.ones((count, count), np.float32), 1) + 0.5 * np.eye(count, dtype=np.float32)
    upward = jnp.einsum("kl,jln->jkn", jnp.asarray(upward), columns[1], precision=exact)
    width = lon // lax.axis_size("lev")
    mine = lax.dynamic_slice_in_dim(surface, lax.axis_index("lev") * width, width, 1)
    return remapped, mine[:, None] + count**-0.5 * upward


def solution(mesh):
    def program(fields, courant, cutoffs, surface, remap_weights):
        lats, parts = mesh.shape["lat"], mesh.shape["lev"]
        rows, levels = fields.shape[1] // lats, fields.shape[2] // parts
        polar = fields.shape[1] // 8
        paired = (
            lats % 2 == 0
            and rows == 4
            and levels % 16 == 0
            and polar <= 2 * rows - 2
            and fields.shape[3] % (LANE * parts) == 0
            and parts & (parts - 1) == 0
        )
        return jax.shard_map(
            shards if paired else plain_shards,
            mesh=mesh,
            in_specs=(
                P(None, "lat", "lev", None),
                P(None, "lat", "lev", None),
                P(),
                P("lat", None),
                P(),
            ),
            out_specs=(P(None, "lat", None, "lev"), P("lat", None, "lev")),
            check_vma=False,
        )(fields, courant, cutoffs, surface, remap_weights)

    return program
```

```python
import functools
import math

import jax
import jax.numpy as jnp
import ml_dtypes
import numpy as np
from jax import lax
from jax.experimental import pallas as pl
from jax.experimental.pallas import tpu as pltpu
from jax.sharding import PartitionSpec as P

KMAX = 128
LANE = 128
TOP = 32767.0
STEPS = 256.0
TINY = 2.0**-100
WIND = 81920.0
ROUND = 1.5 * 2.0**23
VMEM_LIMIT = 12 * 2**20
VMEM_MOST = 63 * 2**20 + 2**19


def rounded(values):
    return ((values + ROUND) - ROUND).astype(jnp.int32).astype(jnp.int16)


def lane_max(values):
    chunks = [jnp.abs(values[:, i : i + LANE]) for i in range(0, values.shape[1], LANE)]
    while len(chunks) > 1:
        pairs = [jnp.maximum(a, b) for a, b in zip(chunks[0::2], chunks[1::2])]
        chunks = pairs + chunks[2 * len(pairs) :]
    return chunks[0]


def tiled(tile, width):
    return jnp.concatenate([tile] * (width // LANE), axis=1)


def scale_code(largest):
    return jnp.ceil(jnp.log2(jnp.maximum(largest, TINY)) * STEPS)


def encoder(code):
    return TOP / jnp.exp2(code * (1.0 / STEPS))


def decoder(code16):
    code = code16.astype(jnp.int32).astype(jnp.float32)
    return jnp.exp2(code * (1.0 / STEPS)) * (1.0 / TOP)


def encode_row(values, out_ref, at):
    width = values.shape[1]
    code = scale_code(lane_max(values))
    out_ref[:, at : at + width] = rounded(values * tiled(encoder(code), width))
    out_ref[:, at + width : at + width + LANE] = code.astype(jnp.int32).astype(jnp.int16)


def decode_row(in_ref, at, width):
    scale = decoder(in_ref[:, at + width : at + width + LANE])
    values = in_ref[:, at : at + width].astype(jnp.int32).astype(jnp.float32)
    return values * tiled(scale, width)


def wind_codes(east, north):
    return rounded(jnp.concatenate([east, north], axis=0) * WIND)


class Sizes:
    def __init__(self, rows, levels, lon):
        self.rows, self.levels, self.lon = rows, levels, lon
        self.half = levels // 2
        self.band = 2 * rows
        self.pad = lon + 2 * LANE
        self.code = lon + LANE
        self.edge = 2 * self.code + lon
        self.inner = 2 * self.code + 3 * lon


def put_padded(ref, index, values, lon):
    ref[index + (Ellipsis, slice(LANE, LANE + lon))] = values
    ref[index + (Ellipsis, slice(0, LANE))] = values[..., lon - LANE :]
    ref[index + (Ellipsis, slice(LANE + lon, 2 * LANE + lon))] = values[..., :LANE]


def wind_row(z, wind, upper):
    halves = []
    for k in range(2):
        both = wind[k].astype(jnp.float32)
        halves.append(jnp.where(upper == 1, both[z.half :], both[: z.half]))
    return wind_codes(*halves)


def edge_kernel(z, fields_ref, courant_ref, edge_ref, rows_ref, wind_ref, sems):
    p = lax.rem(lax.axis_index("lat"), 2)
    give = pl.multiple_of((1 - p) * z.half, z.half)
    copies = [
        pltpu.make_async_copy(
            fields_ref.at[f, 2 * p + r, pl.ds(give, z.half)],
            rows_ref.at[r, pl.ds(f * z.half, z.half)],
            sems.at[2 * r + f],
        )
        for r in range(2)
        for f in range(2)
    ]
    copies += [
        pltpu.make_async_copy(courant_ref.at[k, 3 * p], wind_ref.at[k], sems.at[4 + k])
        for k in range(2)
    ]
    for copy in copies:
        copy.start()
    for r in range(2):
        copies[2 * r].wait()
        copies[2 * r + 1].wait()
        encode_row(rows_ref[r], edge_ref, r * z.code)
    copies[4].wait()
    copies[5].wait()
    edge_ref[:, 2 * z.code :] = wind_row(z, wind_ref, 1 - p)


def rest_kernel(z, par_ref, fields_ref, courant_ref, inner_ref, own_ref):
    p = par_ref[0]
    keep = pl.multiple_of(p * z.half, z.half)
    give = pl.multiple_of((1 - p) * z.half, z.half)

    def field_row(row, start):
        return jnp.concatenate([fields_ref[f, row, pl.ds(start, z.half)] for f in range(2)], axis=0)

    def winds(row, upper):
        return wind_row(z, [courant_ref[k, row] for k in range(2)], upper)

    edge, inner = 2 * p, 2 * (1 - p)
    at = 2 * z.code
    for r in range(2):
        encode_row(field_row(inner + r, give), inner_ref, r * z.code)
    for i, row in enumerate((inner, inner + 1, 1 + p)):
        inner_ref[:, at + i * z.lon : at + (i + 1) * z.lon] = winds(row, 1 - p)
    for r in range(2):
        encode_row(field_row(edge + r, keep), own_ref, r * z.code)
    own_ref[:, at : at + z.lon] = winds(3 * p, p)


def shifted(pieces, shift, lanes):
    turned = [pltpu.roll(v, (-shift) % LANE, 1) for v in pieces]
    if shift > 0:
        return [jnp.where(lanes < LANE - shift, a, b) for a, b in zip(turned[1:-1], turned[2:])]
    return [jnp.where(lanes < -shift, a, b) for a, b in zip(turned[:-2], turned[1:-1])]


def substep(z, count_rows, base, row_of, fwx_ref, fwm_ref, fwy_ref, write):
    count = next(n for n in (4, 3, 2, 1) if z.lon % (n * LANE) == 0)
    width = count * LANE
    lanes = lax.broadcasted_iota(jnp.int32, (z.half, LANE), 1)

    def part(i, carry):
        at = pl.multiple_of(i * width, LANE)

        def piece(k):
            return pl.ds(pl.multiple_of(at + k * LANE, LANE), LANE)

        def row(j, f):
            return [row_of(j, f, piece(k + 1)) for k in range(count)]

        def start(j, f):
            pieces = [row_of(j + 2, f, piece(k)) for k in range(count + 2)]
            return [shifted(pieces, s, lanes) for s in (-2, -1, 1, 2)]

        def lon_part(j, u, moved):
            out = []
            for k in range(count):
                m2, m1, p1, p2 = (m[k] for m in moved)
                east = 7.0 * (u[k] + p1) - (m1 + p2)
                west = 7.0 * (m1 + u[k]) - (m2 + p1)
                out.append(fwx_ref[base + j, :, piece(k)] * east - fwm_ref[base + j, :, piece(k)] * west)
            return out

        for f in range(2):
            rows = [row(j, f) for j in range(4)]
            sums = [[a + b for a, b in zip(rows[j], rows[j + 1])] for j in range(3)]
            flux = None
            moved = start(0, f)
            for j in range(count_rows + 1):
                later = start(j, f) if 0 < j < count_rows else None
                new = [
                    fwy_ref[base + j, :, piece(k)] * (8.0 * sums[1][k] - (sums[0][k] + sums[2][k]))
                    for k in range(count)
                ]
                if j > 0:
                    u = rows[1]
                    change = lon_part(j - 1, u, moved)
                    for k in range(count):
                        write(j - 1, f, at, k, u[k] - change[k] - (new[k] - flux[k]))
                    moved = later
                flux = new
                if j < count_rows:
                    above = row(j + 4, f)
                    rows = rows[1:] + [above]
                    sums = sums[1:] + [[a + b for a, b in zip(rows[2], rows[3])]]
        return carry

    lax.fori_loop(0, z.lon // width, part, 0)


def filter_tables(lon):
    points = np.arange(lon // 2)
    forward, back = [], []
    for parity in range(2):
        waves = np.arange(parity, KMAX, 2)
        angle = (points[:, None] * waves[None, :] % lon) * (2.0 * math.pi / lon)
        table = np.concatenate([np.cos(angle), np.sin(angle)], axis=1).astype(np.float32)
        high = table.astype(ml_dtypes.bfloat16)
        low = (table - high.astype(np.float32)).astype(ml_dtypes.bfloat16)
        forward.append(np.concatenate([high, low], axis=1))
        back.append(np.concatenate([high.T, low.T], axis=0))
    return np.stack(forward), np.stack(back)


def split(values):
    high = values.astype(jnp.bfloat16)
    return high, (values - high.astype(jnp.float32)).astype(jnp.bfloat16)


def low_pass(z, rows, cuts, forward_ref, back_ref):
    half = z.lon // 2
    count = len(rows)
    tall = 2 * z.half
    total = count * tall
    flat = [row.reshape(tall, z.lon) for row in rows]
    folded = []
    for parity in range(2):
        parts = [
            row[:, :half] + row[:, half:] if parity == 0 else row[:, :half] - row[:, half:]
            for row in flat
        ]
        high, low = split(jnp.concatenate(parts, axis=0))
        both = jnp.concatenate([high, low], axis=0)
        got = jnp.dot(both, forward_ref[parity], preferred_element_type=jnp.float32)
        wave = got[:total, :KMAX] + got[:total, KMAX:] + (got[total:, :KMAX] + got[total:, KMAX:])
        number = 2 * (lax.broadcasted_iota(jnp.int32, (tall, KMAX), 1) % (KMAX // 2)) + parity
        doubled = jnp.where(number == 0, 1.0, 2.0) * (1.0 / z.lon)
        weight = jnp.concatenate([jnp.where(number <= cut, doubled, 0.0) for cut in cuts], axis=0)
        high, low = split(wave * weight)
        both = jnp.concatenate(
            [jnp.concatenate([high, high], axis=1), jnp.concatenate([low, low], axis=1)], axis=0
        )
        got = jnp.dot(both, back_ref[parity], preferred_element_type=jnp.float32)
        folded.append(got[:total] + got[total:])
    left, right = folded[0] + folded[1], folded[0] - folded[1]
    smooth = jnp.concatenate([left, right], axis=1)
    return [smooth[i * tall : (i + 1) * tall].reshape(2, z.half, z.lon) for i in range(count)]


def filter_rows(z, cut_ref, first_row, start, tables, load, store):
    nyquist = z.lon // 2
    cuts = [cut_ref[first_row + start + r] for r in range(z.rows)]
    some = functools.reduce(jnp.logical_or, [cut < nyquist for cut in cuts])

    @pl.when(some)
    def _():
        smooth = low_pass(z, [load(start + r) for r in range(z.rows)], cuts, *tables)
        for r in range(z.rows):

            @pl.when(cuts[r] < nyquist)
            def _():
                store(start + r, smooth[r])


def first_kernel(
    z, par_ref, fields_ref, courant_ref, edge_ref, inner_ref, one_ref, two_ref,
    new_ref, fwx_ref, fwm_ref, fwy_ref, one_out_ref, two_out_ref, u_ref, cx_ref, cy_ref,
):
    p, b = par_ref[0], par_ref[3]
    lon, half = z.lon, z.half

    def pair(values):
        return values.reshape(2, half, values.shape[1])

    def winds(in_ref, at):
        values = in_ref[:, at : at + lon].astype(jnp.int32).astype(jnp.float32) * (1.0 / WIND)
        return values[:half], values[half:]

    def place_wind(row, east, north):
        put_padded(cx_ref, (row,), east, lon)
        cy_ref[row + 1] = north

    keep = pl.multiple_of(p * half, half)
    for r in range(z.rows):
        row = z.rows * p + r
        own = jnp.stack([fields_ref[f, r, pl.ds(keep, half)] for f in range(2)])
        put_padded(u_ref, (row + 2,), own, lon)
        got = []
        for k in range(2):
            wind = courant_ref[k, r].astype(jnp.float32)
            got.append(jnp.where(p == 1, wind[half:], wind[:half]))
        place_wind(row, *got)
    at = 2 * z.code
    for r in range(2):
        put_padded(u_ref, (6 * (1 - p) + r + 2,), pair(decode_row(edge_ref, r * z.code, lon)), lon)
        put_padded(u_ref, (4 - 2 * p + r + 2,), pair(decode_row(inner_ref, r * z.code, lon)), lon)
        put_padded(u_ref, (10 * (1 - b) + r,), pair(decode_row(one_ref, r * z.code, lon)), lon)
        put_padded(u_ref, (10 * b + r,), pair(decode_row(two_ref, r * z.code, lon)), lon)
        place_wind(4 - 2 * p + r, *winds(inner_ref, at + r * lon))
    place_wind(7 * (1 - p), *winds(edge_ref, at))
    place_wind(6 - 5 * p, *winds(inner_ref, at + 2 * lon))
    cy_ref[9 * (1 - b)] = winds(one_ref, at)[1]
    cy_ref[9 * b] = winds(two_ref, at)[1]

    def face_rows(j, carry):
        wind = cx_ref[j] * (1.0 / 24.0)
        here = wind[:, LANE : LANE + lon]
        fwx_ref[j] = here + pltpu.roll(wind, z.pad - 1, 1)[:, LANE : LANE + lon]
        fwm_ref[j] = here + pltpu.roll(wind, 1, 1)[:, LANE : LANE + lon]
        return carry

    lax.fori_loop(0, z.band, face_rows, 0)

    def face_cols(j, carry):
        fwy_ref[j] = (cy_ref[j] + cy_ref[j + 1]) * (1.0 / 24.0)
        return carry

    lax.fori_loop(0, z.band + 1, face_cols, 0)

    def write(row, f, at, k, values):
        new_ref[row, f, :, pl.ds(pl.multiple_of(at + (k + 1) * LANE, LANE), LANE)] = values

    substep(z, z.band, 0, lambda j, f, piece: u_ref[j, f, :, piece], fwx_ref, fwm_ref, fwy_ref, write)
    for r in range(2):
        for row, out_ref in ((6 * (1 - b) + r, one_out_ref), (6 * b + r, two_out_ref)):
            values = new_ref[row, :, :, LANE : LANE + lon]
            encode_row(values.reshape(2 * half, lon), out_ref, r * z.code)
    for j in range(z.band):
        new_ref[j, :, :, 0:LANE] = new_ref[j, :, :, lon : lon + LANE]
        new_ref[j, :, :, LANE + lon :] = new_ref[j, :, :, LANE : 2 * LANE]


def inner_kernel(
    z, par_ref, cut_ref, in_ref, fwx_ref, fwm_ref, fwy_ref, forward_ref, back_ref, new_ref, inner_ref
):
    for j in range(z.band):
        new_ref[j] = in_ref[j]

    def store(row, values):
        put_padded(new_ref, (row,), values, z.lon)

    for part in range(2):
        filter_rows(
            z, cut_ref, par_ref[1], part * z.rows, (forward_ref, back_ref),
            lambda row: in_ref[row, :, :, LANE : LANE + z.lon], store,
        )

    def write(row, f, at, k, values):
        inner_ref[row, f, :, pl.ds(pl.multiple_of(at + k * LANE, LANE), LANE)] = values

    substep(
        z, z.band - 4, 2, lambda j, f, piece: new_ref[j, f, :, piece], fwx_ref, fwm_ref, fwy_ref, write
    )


def outer_kernel(
    z, parts, par_ref, cut_ref, new_ref, inner_ref, fwx_ref, fwm_ref, fwy_ref, one_ref, two_ref, forward_ref,
    back_ref, *refs,
):
    out_refs, (halo_ref, v_ref) = refs[: 2 * parts], refs[2 * parts :]
    lon, half = z.lon, z.half
    tall = 2 * half
    p, b = par_ref[0], par_ref[3]
    for r in range(2):
        for row, in_ref in ((2 * (1 - b) + r, one_ref), (2 * b + r, two_ref)):
            values = decode_row(in_ref, r * z.code, lon).reshape(2, half, lon)
            put_padded(halo_ref, (row,), values, lon)
    for j in range(2, z.band - 2):
        v_ref[j] = inner_ref[j - 2]

    for start in (0, z.band - 2):

        def row_of(j, f, piece):
            row = start + j - 2
            if row < 0:
                return halo_ref[row + 2, f, :, piece]
            if row >= z.band:
                return halo_ref[row - z.band + 2, f, :, piece]
            return new_ref[row, f, :, piece]

        def write(row, f, at, k, values):
            v_ref[start + row, f, :, pl.ds(pl.multiple_of(at + k * LANE, LANE), LANE)] = values

        substep(z, 2, start, row_of, fwx_ref, fwm_ref, fwy_ref, write)

    def store(row, values):
        v_ref[row] = values

    for part in range(2):
        filter_rows(
            z, cut_ref, par_ref[1], part * z.rows, (forward_ref, back_ref), lambda row: v_ref[row], store
        )
    column = lon // parts
    for i in range(2 * parts):
        base = z.rows * (1 - p if i < parts else p)
        at = pl.multiple_of(jnp.bitwise_xor(par_ref[2], i % parts) * column, LANE)
        values = jnp.concatenate(
            [v_ref[base + r, :, :, pl.ds(at, column)].reshape(tall, column) for r in range(z.rows)],
            axis=1,
        )
        encode_row(values, out_refs[i], 0)


def scale_kernel(at, *refs):
    for i, ref in enumerate(refs[:-1]):
        refs[-1][i] = decoder(ref[:, at : at + LANE])


def column_kernel(z, parts, par_ref, *refs):
    got, (scales_ref, remap_ref, upward_ref, surface_ref, out_ref, geo_ref, x_ref) = refs[: 2 * parts], refs[2 * parts :]
    p, lev = par_ref[0], par_ref[2]
    column = out_ref.shape[-1]
    at = pl.multiple_of(pl.program_id(0) * column, LANE)
    for i, ref in enumerate(got):
        side = p if i < parts else 1 - p
        s = jnp.bitwise_xor(lev, i % parts)
        if i < parts:
            scale = decoder(ref[:, z.rows * column : z.rows * column + LANE])
        else:
            scale = scales_ref[i - parts]
        codes = ref[:, pl.ds(at, column)].astype(jnp.int32).astype(jnp.float32)
        values = codes * tiled(scale, column)
        level = pl.multiple_of(s * z.levels + side * z.half, z.half)
        for f in range(2):
            x_ref[f, pl.ds(level, z.half)] = values[f * z.half : (f + 1) * z.half]
    high, low = split(remap_ref[...])
    remap = jnp.concatenate([high, low, high], axis=1)
    count = remap_ref.shape[0]
    for f in range(2):
        high, low = split(x_ref[f])
        stacked = jnp.concatenate([high, high, low], axis=0)
        left = remap if f == 0 else jnp.concatenate([remap, upward_ref[...].astype(jnp.bfloat16)], axis=0)
        result = jnp.dot(left, stacked, preferred_element_type=jnp.float32)
        out_ref[f, 0] = result[:count]
        if f == 1:
            geo_ref[0] = surface_ref[0] + result[count:] * (count**-0.5)


def whole():
    return pl.BlockSpec(memory_space=pltpu.VMEM)


def scalars():
    return pl.BlockSpec(memory_space=pltpu.SMEM)


def far_memory():
    return pl.BlockSpec(memory_space=pltpu.HBM)


def params(limit=VMEM_LIMIT):
    return pltpu.CompilerParams(vmem_limit_bytes=limit)


def cost(flops=1000, data=1000):
    return pl.CostEstimate(flops=flops, bytes_accessed=data, transcendentals=0)


def shards(fields, courant, cutoffs, surface, remap_weights):
    _, rows, levels, lon = fields.shape
    z = Sizes(rows, levels, lon)
    lats, parts = lax.axis_size("lat"), lax.axis_size("lev")
    me = lax.axis_index("lat")
    parity = me % 2
    lev = lax.axis_index("lev")
    place = jnp.stack([parity, (me - parity) * rows, lev, (me // 2) % 2]).astype(jnp.int32)
    tall = 2 * z.half
    i16, f32 = jnp.int16, jnp.float32
    swap = [(i, i ^ 1) for i in range(lats)]
    ones, twos = [
        [pair for i in range(start, lats - 2, 4) for s in range(2) for pair in ((i + s, i + s + 2), (i + s + 2, i + s))]
        for start in (0, 2)
    ]

    def shape(*dims):
        return jax.ShapeDtypeStruct(dims, f32)

    def codes(*dims):
        return jax.ShapeDtypeStruct(dims, i16)

    edge = pl.pallas_call(
        functools.partial(edge_kernel, z),
        name="edge",
        in_specs=[far_memory(), far_memory()],
        out_specs=whole(),
        out_shape=codes(tall, z.edge),
        scratch_shapes=[
            pltpu.VMEM((2, tall, lon), f32),
            pltpu.VMEM((2, levels, lon), courant.dtype),
            pltpu.SemaphoreType.DMA((6,)),
        ],
        compiler_params=params(VMEM_MOST),
        cost_estimate=cost(),
    )(fields, courant)
    edge = lax.ppermute(edge, "lat", swap)
    inner, own = pl.pallas_call(
        functools.partial(rest_kernel, z),
        name="rest",
        in_specs=[scalars(), whole(), whole()],
        out_specs=[whole()] * 2,
        out_shape=[codes(tall, z.inner), codes(tall, z.edge)],
        compiler_params=params(),
        cost_estimate=cost(),
    )(place, fields, courant)
    inner = lax.ppermute(inner, "lat", swap)
    straight = (parity + (me // 2) % 2) == 1
    one = lax.ppermute(jnp.where(straight, own, edge), "lat", ones)
    two = lax.ppermute(jnp.where(straight, edge, own), "lat", twos)
    new, fwx, fwm, fwy, one_code, two_code = pl.pallas_call(
        functools.partial(first_kernel, z),
        name="first",
        in_specs=[scalars()] + [whole()] * 6,
        out_specs=[whole()] * 6,
        out_shape=[
            shape(z.band, 2, z.half, z.pad),
            shape(z.band, z.half, lon),
            shape(z.band, z.half, lon),
            shape(z.band + 1, z.half, lon),
            codes(tall, 2 * z.code),
            codes(tall, 2 * z.code),
        ],
        scratch_shapes=[
            pltpu.VMEM((z.band + 4, 2, z.half, z.pad), f32),
            pltpu.VMEM((z.band, z.half, z.pad), f32),
            pltpu.VMEM((z.band + 2, z.half, z.lon), f32),
        ],
        compiler_params=params(),
        cost_estimate=cost(),
    )(place, fields, courant, edge, inner, one, two)
    one = lax.ppermute(one_code, "lat", ones)
    two = lax.ppermute(two_code, "lat", twos)

    forward, back = (jnp.asarray(t) for t in filter_tables(lon))
    new, inner = pl.pallas_call(
        functools.partial(inner_kernel, z),
        name="inner",
        in_specs=[scalars(), scalars()] + [whole()] * 6,
        out_specs=[whole()] * 2,
        out_shape=[shape(z.band, 2, z.half, z.pad), shape(z.band - 4, 2, z.half, lon)],
        compiler_params=params(),
        cost_estimate=cost(),
    )(place, cutoffs, new, fwx, fwm, fwy, forward, back)

    column = lon // parts
    blocks = pl.pallas_call(
        functools.partial(outer_kernel, z, parts),
        name="outer",
        in_specs=[scalars(), scalars()] + [whole()] * 9,
        out_specs=[whole()] * (2 * parts),
        out_shape=[codes(tall, rows * column + LANE)] * (2 * parts),
        scratch_shapes=[
            pltpu.VMEM((4, 2, z.half, z.pad), f32),
            pltpu.VMEM((z.band, 2, z.half, lon), f32),
        ],
        compiler_params=params(),
        cost_estimate=cost(),
    )(place, cutoffs, new, inner, fwx, fwm, fwy, one, two, forward, back)
    got = []
    for b, block in enumerate(blocks[:parts]):
        pairs = [
            (i * parts + j, (i ^ 1) * parts + (j ^ b)) for i in range(lats) for j in range(parts)
        ]
        got.append(lax.ppermute(block, ("lat", "lev"), pairs))
    scales = pl.pallas_call(
        functools.partial(scale_kernel, rows * column),
        name="scales",
        in_specs=[whole()] * parts,
        out_specs=whole(),
        out_shape=shape(parts, tall, LANE),
        compiler_params=params(),
        cost_estimate=cost(),
    )(*got)
    for b, block in enumerate(blocks[parts:]):
        pairs = [(j, j ^ b) for j in range(parts)]
        got.insert(b, lax.ppermute(block, "lev", pairs) if b else block)

    count = remap_weights.shape[0]
    upward = np.triu(np.ones((count, count), np.float32), 1) + 0.5 * np.eye(count, dtype=np.float32)
    upward = jnp.asarray(np.concatenate([upward, 0.0 * upward, upward], axis=1))
    surface = lax.dynamic_slice_in_dim(surface, lev * column, column, 1)
    remapped, geopotential = pl.pallas_call(
        functools.partial(column_kernel, z, parts),
        name="columns",
        grid=(rows,),
        in_specs=[scalars()]
        + [whole()] * (len(got) + 1)
        + [
            pl.BlockSpec(remap_weights.shape, lambda r: (0, 0)),
            pl.BlockSpec(upward.shape, lambda r: (0, 0)),
            pl.BlockSpec((1, 1, column), lambda r: (r, 0, 0)),
        ],
        out_specs=[
            pl.BlockSpec((2, 1, count, column), lambda r: (0, r, 0, 0)),
            pl.BlockSpec((1, count, column), lambda r: (r, 0, 0)),
        ],
        out_shape=[shape(2, rows, count, column), shape(rows, count, column)],
        scratch_shapes=[pltpu.VMEM((2, count, column), f32)],
        compiler_params=params(),
        cost_estimate=cost(),
    )(place, *got, scales, remap_weights, upward, surface[:, None, :])
    return remapped, geopotential


def with_halo(shard, width):
    size, length = lax.axis_size("lat"), shard.shape[1]
    up = [(i, (i + 1) % size) for i in range(size - 1)]
    down = [(j, i) for i, j in up]
    before = lax.ppermute(lax.slice_in_dim(shard, length - width, length, axis=1), "lat", up)
    after = lax.ppermute(lax.slice_in_dim(shard, 0, width, axis=1), "lat", down)
    return jnp.concatenate([before, shard, after], axis=1)


def plain_shards(fields, courant, cutoffs, surface, remap_weights):
    _, rows, _, lon = fields.shape
    exact = lax.Precision.HIGHEST
    cut = lax.dynamic_slice_in_dim(cutoffs, lax.axis_index("lat") * rows, rows)
    waves = np.arange(KMAX)
    angle = (np.arange(lon)[:, None] * waves[None, :] % lon) * (2.0 * math.pi / lon)
    table = jnp.asarray(np.concatenate([np.cos(angle), np.sin(angle)], axis=1).astype(np.float32))
    number = jnp.asarray(np.concatenate([waves, waves]).astype(np.int32))
    weight = jnp.where(number[None] <= cut[:, None], jnp.where(number == 0, 1.0, 2.0)[None] / lon, 0.0)
    flagged = cut < lon // 2

    def smooth(values):
        wave = jnp.einsum("frln,nk->frlk", values, table, precision=exact) * weight[None, :, None]
        low = jnp.einsum("frlk,nk->frln", wave, table, precision=exact)
        return jnp.where(flagged[None, :, None, None], low, values)

    winds = with_halo(courant, 1).astype(jnp.float32)
    east, north = winds[0, 1:-1], winds[1]
    face_x = (east + jnp.roll(east, -1, -1)) / 24.0
    face_y = (north[:-1] + north[1:]) / 24.0
    u = fields
    for _ in range(2):
        wide = with_halo(u, 2)
        pair = u + jnp.roll(u, -1, -1)
        fx = face_x * (8.0 * pair - (jnp.roll(pair, 1, -1) + jnp.roll(pair, -1, -1)))
        pair = wide[:, :-1] + wide[:, 1:]
        fy = face_y * (8.0 * pair[:, 1:-1] - (pair[:, :-2] + pair[:, 2:]))
        u = u - (fx - jnp.roll(fx, 1, -1)) - (fy[:, 1:] - fy[:, :-1])
        u = lax.cond(jnp.any(flagged), smooth, lambda values: values, u)
    columns = lax.all_to_all(u, "lev", split_axis=3, concat_axis=2, tiled=True)
    remapped = jnp.einsum("pk,fjkn->fjpn", remap_weights, columns, precision=exact)
    count = remap_weights.shape[0]
    upward = np.triu(np.ones((count, count), np.float32), 1) + 0.5 * np.eye(count, dtype=np.float32)
    upward = jnp.einsum("kl,jln->jkn", jnp.asarray(upward), columns[1], precision=exact)
    width = lon // lax.axis_size("lev")
    mine = lax.dynamic_slice_in_dim(surface, lax.axis_index("lev") * width, width, 1)
    return remapped, mine[:, None] + count**-0.5 * upward


def solution(mesh):
    def program(fields, courant, cutoffs, surface, remap_weights):
        lats, parts = mesh.shape["lat"], mesh.shape["lev"]
        rows, levels = fields.shape[1] // lats, fields.shape[2] // parts
        polar = fields.shape[1] // 8
        paired = (
            lats % 2 == 0
            and rows == 4
            and levels % 16 == 0
            and polar <= 2 * rows - 2
            and fields.shape[3] % (LANE * parts) == 0
            and parts & (parts - 1) == 0
        )
        return jax.shard_map(
            shards if paired else plain_shards,
            mesh=mesh,
            in_specs=(
                P(None, "lat", "lev", None),
                P(None, "lat", "lev", None),
                P(),
                P("lat", None),
                P(),
            ),
            out_specs=(P(None, "lat", None, "lev"), P("lat", None, "lev")),
            check_vma=False,
        )(fields, courant, cutoffs, surface, remap_weights)

    return program
```

```python
import functools
import math

import jax
import jax.numpy as jnp
import ml_dtypes
import numpy as np
from jax import lax
from jax.experimental import pallas as pl
from jax.experimental.pallas import tpu as pltpu
from jax.sharding import PartitionSpec as P

KMAX = 128
LANE = 128
TOP = 32767.0
STEPS = 256.0
TINY = 2.0**-100
WIND = 81920.0
ROUND = 1.5 * 2.0**23
VMEM_LIMIT = 12 * 2**20
VMEM_MOST = 63 * 2**20 + 2**19


def rounded(values):
    return ((values + ROUND) - ROUND).astype(jnp.int32).astype(jnp.int16)


def lane_max(values):
    chunks = [jnp.abs(values[:, i : i + LANE]) for i in range(0, values.shape[1], LANE)]
    while len(chunks) > 1:
        pairs = [jnp.maximum(a, b) for a, b in zip(chunks[0::2], chunks[1::2])]
        chunks = pairs + chunks[2 * len(pairs) :]
    return chunks[0]


def tiled(tile, width):
    return jnp.concatenate([tile] * (width // LANE), axis=1)


def scale_code(largest):
    return jnp.ceil(jnp.log2(jnp.maximum(largest, TINY)) * STEPS)


def encoder(code):
    return TOP / jnp.exp2(code * (1.0 / STEPS))


def decoder(code16):
    code = code16.astype(jnp.int32).astype(jnp.float32)
    return jnp.exp2(code * (1.0 / STEPS)) * (1.0 / TOP)


def encode_row(values, out_ref, at):
    width = values.shape[1]
    code = scale_code(lane_max(values))
    out_ref[:, at : at + width] = rounded(values * tiled(encoder(code), width))
    out_ref[:, at + width : at + width + LANE] = code.astype(jnp.int32).astype(jnp.int16)


def decode_row(in_ref, at, width):
    scale = decoder(in_ref[:, at + width : at + width + LANE])
    values = in_ref[:, at : at + width].astype(jnp.int32).astype(jnp.float32)
    return values * tiled(scale, width)


def wind_codes(east, north):
    return rounded(jnp.concatenate([east, north], axis=0) * WIND)


class Sizes:
    def __init__(self, rows, levels, lon):
        self.rows, self.levels, self.lon = rows, levels, lon
        self.half = levels // 2
        self.band = 2 * rows
        self.pad = lon + 2 * LANE
        self.code = lon + LANE
        self.edge = 2 * self.code + lon
        self.inner = 2 * self.code + 3 * lon


def put_padded(ref, index, values, lon):
    ref[index + (Ellipsis, slice(LANE, LANE + lon))] = values
    ref[index + (Ellipsis, slice(0, LANE))] = values[..., lon - LANE :]
    ref[index + (Ellipsis, slice(LANE + lon, 2 * LANE + lon))] = values[..., :LANE]


def wind_row(z, wind, upper):
    halves = []
    for k in range(2):
        both = wind[k].astype(jnp.float32)
        halves.append(jnp.where(upper == 1, both[z.half :], both[: z.half]))
    return wind_codes(*halves)


def edge_kernel(z, fields_ref, courant_ref, edge_ref, rows_ref, wind_ref, sems):
    p = lax.rem(lax.axis_index("lat"), 2)
    give = pl.multiple_of((1 - p) * z.half, z.half)
    copies = [
        pltpu.make_async_copy(
            fields_ref.at[f, 2 * p + r, pl.ds(give, z.half)],
            rows_ref.at[r, pl.ds(f * z.half, z.half)],
            sems.at[2 * r + f],
        )
        for r in range(2)
        for f in range(2)
    ]
    copies += [
        pltpu.make_async_copy(courant_ref.at[k, 3 * p], wind_ref.at[k], sems.at[4 + k])
        for k in range(2)
    ]
    for copy in copies:
        copy.start()
    for r in range(2):
        copies[2 * r].wait()
        copies[2 * r + 1].wait()
        encode_row(rows_ref[r], edge_ref, r * z.code)
    copies[4].wait()
    copies[5].wait()
    edge_ref[:, 2 * z.code :] = wind_row(z, wind_ref, 1 - p)


def rest_kernel(z, par_ref, fields_ref, courant_ref, inner_ref, own_ref):
    p = par_ref[0]
    keep = pl.multiple_of(p * z.half, z.half)
    give = pl.multiple_of((1 - p) * z.half, z.half)

    def field_row(row, start):
        return jnp.concatenate([fields_ref[f, row, pl.ds(start, z.half)] for f in range(2)], axis=0)

    def winds(row, upper):
        return wind_row(z, [courant_ref[k, row] for k in range(2)], upper)

    edge, inner = 2 * p, 2 * (1 - p)
    at = 2 * z.code
    for r in range(2):
        encode_row(field_row(inner + r, give), inner_ref, r * z.code)
    for i, row in enumerate((inner, inner + 1, 1 + p)):
        inner_ref[:, at + i * z.lon : at + (i + 1) * z.lon] = winds(row, 1 - p)
    for r in range(2):
        encode_row(field_row(edge + r, keep), own_ref, r * z.code)
    own_ref[:, at : at + z.lon] = winds(3 * p, p)


def shifted(pieces, shift, lanes):
    turned = [pltpu.roll(v, (-shift) % LANE, 1) for v in pieces]
    if shift > 0:
        return [jnp.where(lanes < LANE - shift, a, b) for a, b in zip(turned[1:-1], turned[2:])]
    return [jnp.where(lanes < -shift, a, b) for a, b in zip(turned[:-2], turned[1:-1])]


def substep(z, count_rows, base, row_of, winds_ref, write):
    count = next(n for n in (4, 3, 2, 1) if z.lon % (n * LANE) == 0)
    width = count * LANE
    lanes = lax.broadcasted_iota(jnp.int32, (z.half, LANE), 1)

    def part(i, carry):
        at = pl.multiple_of(i * width, LANE)

        def piece(k):
            return pl.ds(pl.multiple_of(at + k * LANE, LANE), LANE)

        def row(j, f):
            return [row_of(j, f, piece(k + 1)) for k in range(count)]

        def start(j, f):
            pieces = [row_of(j + 2, f, piece(k)) for k in range(count + 2)]
            return [shifted(pieces, s, lanes) for s in (-2, -1, 1, 2)]

        def lon_part(j, u, moved):
            out = []
            for k in range(count):
                m2, m1, p1, p2 = (m[k] for m in moved)
                east = 7.0 * (u[k] + p1) - (m1 + p2)
                west = 7.0 * (m1 + u[k]) - (m2 + p1)
                east = winds_ref[base + j, :, piece(k)] * east
                out.append(east - winds_ref[z.band + base + j, :, piece(k)] * west)
            return out

        for f in range(2):
            rows = [row(j, f) for j in range(4)]
            sums = [[a + b for a, b in zip(rows[j], rows[j + 1])] for j in range(3)]
            flux = None
            moved = start(0, f)
            for j in range(count_rows + 1):
                later = start(j, f) if 0 < j < count_rows else None
                new = [
                    winds_ref[2 * z.band + base + j, :, piece(k)] * (8.0 * sums[1][k] - (sums[0][k] + sums[2][k]))
                    for k in range(count)
                ]
                if j > 0:
                    u = rows[1]
                    change = lon_part(j - 1, u, moved)
                    for k in range(count):
                        write(j - 1, f, at, k, u[k] - change[k] - (new[k] - flux[k]))
                    moved = later
                flux = new
                if j < count_rows:
                    above = row(j + 4, f)
                    rows = rows[1:] + [above]
                    sums = sums[1:] + [[a + b for a, b in zip(rows[2], rows[3])]]
        return carry

    lax.fori_loop(0, z.lon // width, part, 0)


def filter_tables(lon):
    half = lon // 2
    points = np.arange(half)
    forward, back = [], []
    for parity in range(2):
        waves = np.arange(parity, KMAX, 2)
        angle = (points[:, None] * waves[None, :] % lon) * (2.0 * math.pi / lon)
        table = np.concatenate([np.cos(angle), np.sin(angle)], axis=1).astype(np.float32)
        high = table.astype(ml_dtypes.bfloat16)
        low = (table - high.astype(np.float32)).astype(ml_dtypes.bfloat16)
        forward.append(np.concatenate([high, low], axis=1))
        turned = np.concatenate([high.T, low.T], axis=0)
        back.append(np.concatenate(np.split(turned, half // (2 * KMAX), axis=1), axis=0))
    return np.stack(forward + back)


def split(values):
    high = values.astype(jnp.bfloat16)
    return high, (values - high.astype(jnp.float32)).astype(jnp.bfloat16)


def low_pass(z, rows, cuts, table_ref):
    half = z.lon // 2
    count = len(rows)
    tall = 2 * z.half
    total = count * tall
    flat = [row.reshape(tall, z.lon) for row in rows]
    folded = []
    for parity in range(2):
        parts = [
            row[:, :half] + row[:, half:] if parity == 0 else row[:, :half] - row[:, half:]
            for row in flat
        ]
        high, low = split(jnp.concatenate(parts, axis=0))
        both = jnp.concatenate([high, low], axis=0)
        got = jnp.dot(both, table_ref[parity], preferred_element_type=jnp.float32)
        wave = got[:total, :KMAX] + got[:total, KMAX:] + (got[total:, :KMAX] + got[total:, KMAX:])
        number = 2 * (lax.broadcasted_iota(jnp.int32, (tall, KMAX), 1) % (KMAX // 2)) + parity
        doubled = jnp.where(number == 0, 1.0, 2.0) * (1.0 / z.lon)
        weight = jnp.concatenate([jnp.where(number <= cut, doubled, 0.0) for cut in cuts], axis=0)
        high, low = split(wave * weight)
        both = jnp.concatenate(
            [jnp.concatenate([high, high], axis=1), jnp.concatenate([low, low], axis=1)], axis=0
        )
        got = []
        for at in range(0, half, 2 * KMAX):
            block = table_ref[2 + parity, at : at + 2 * KMAX]
            sums = jnp.dot(both, block, preferred_element_type=jnp.float32)
            got.append(sums[:total] + sums[total:])
        folded.append(jnp.concatenate(got, axis=1))
    left, right = folded[0] + folded[1], folded[0] - folded[1]
    smooth = jnp.concatenate([left, right], axis=1)
    return [smooth[i * tall : (i + 1) * tall].reshape(2, z.half, z.lon) for i in range(count)]


def filter_rows(z, cut_ref, first_row, start, table_ref, load, store):
    nyquist = z.lon // 2
    cuts = [cut_ref[first_row + start + r] for r in range(z.rows)]
    some = functools.reduce(jnp.logical_or, [cut < nyquist for cut in cuts])

    @pl.when(some)
    def _():
        smooth = low_pass(z, [load(start + r) for r in range(z.rows)], cuts, table_ref)
        for r in range(z.rows):

            @pl.when(cuts[r] < nyquist)
            def _():
                store(start + r, smooth[r])


def first_kernel(
    z, par_ref, fields_ref, courant_ref, edge_ref, inner_ref, one_ref, two_ref,
    new_ref, winds_ref, one_out_ref, two_out_ref, u_ref, cx_ref, cy_ref,
):
    p, b = par_ref[0], par_ref[3]
    lon, half = z.lon, z.half

    def pair(values):
        return values.reshape(2, half, values.shape[1])

    def winds(in_ref, at):
        values = in_ref[:, at : at + lon].astype(jnp.int32).astype(jnp.float32) * (1.0 / WIND)
        return values[:half], values[half:]

    def place_wind(row, east, north):
        put_padded(cx_ref, (row,), east, lon)
        cy_ref[row + 1] = north

    keep = pl.multiple_of(p * half, half)
    for r in range(z.rows):
        row = z.rows * p + r
        own = jnp.stack([fields_ref[f, r, pl.ds(keep, half)] for f in range(2)])
        put_padded(u_ref, (row + 2,), own, lon)
        got = []
        for k in range(2):
            wind = courant_ref[k, r].astype(jnp.float32)
            got.append(jnp.where(p == 1, wind[half:], wind[:half]))
        place_wind(row, *got)
    at = 2 * z.code
    for r in range(2):
        put_padded(u_ref, (6 * (1 - p) + r + 2,), pair(decode_row(edge_ref, r * z.code, lon)), lon)
        put_padded(u_ref, (4 - 2 * p + r + 2,), pair(decode_row(inner_ref, r * z.code, lon)), lon)
        put_padded(u_ref, (10 * (1 - b) + r,), pair(decode_row(one_ref, r * z.code, lon)), lon)
        put_padded(u_ref, (10 * b + r,), pair(decode_row(two_ref, r * z.code, lon)), lon)
        place_wind(4 - 2 * p + r, *winds(inner_ref, at + r * lon))
    place_wind(7 * (1 - p), *winds(edge_ref, at))
    place_wind(6 - 5 * p, *winds(inner_ref, at + 2 * lon))
    cy_ref[9 * (1 - b)] = winds(one_ref, at)[1]
    cy_ref[9 * b] = winds(two_ref, at)[1]

    def face_rows(j, carry):
        wind = cx_ref[j] * (1.0 / 24.0)
        here = wind[:, LANE : LANE + lon]
        winds_ref[j] = here + pltpu.roll(wind, z.pad - 1, 1)[:, LANE : LANE + lon]
        winds_ref[z.band + j] = here + pltpu.roll(wind, 1, 1)[:, LANE : LANE + lon]
        return carry

    lax.fori_loop(0, z.band, face_rows, 0)

    def face_cols(j, carry):
        winds_ref[2 * z.band + j] = (cy_ref[j] + cy_ref[j + 1]) * (1.0 / 24.0)
        return carry

    lax.fori_loop(0, z.band + 1, face_cols, 0)

    def write(row, f, at, k, values):
        new_ref[row, f, :, pl.ds(pl.multiple_of(at + (k + 1) * LANE, LANE), LANE)] = values

    substep(z, z.band, 0, lambda j, f, piece: u_ref[j, f, :, piece], winds_ref, write)
    for r in range(2):
        for row, out_ref in ((6 * (1 - b) + r, one_out_ref), (6 * b + r, two_out_ref)):
            values = new_ref[row, :, :, LANE : LANE + lon]
            encode_row(values.reshape(2 * half, lon), out_ref, r * z.code)
    for j in range(z.band):
        new_ref[j, :, :, 0:LANE] = new_ref[j, :, :, lon : lon + LANE]
        new_ref[j, :, :, LANE + lon :] = new_ref[j, :, :, LANE : 2 * LANE]


def inner_kernel(z, par_ref, cut_ref, in_ref, winds_ref, table_ref, new_ref, inner_ref):
    for j in range(z.band):
        new_ref[j] = in_ref[j]

    def store(row, values):
        put_padded(new_ref, (row,), values, z.lon)

    for part in range(2):
        filter_rows(
            z, cut_ref, par_ref[1], part * z.rows, table_ref,
            lambda row: in_ref[row, :, :, LANE : LANE + z.lon], store,
        )

    def write(row, f, at, k, values):
        inner_ref[row, f, :, pl.ds(pl.multiple_of(at + k * LANE, LANE), LANE)] = values

    substep(z, z.band - 4, 2, lambda j, f, piece: new_ref[j, f, :, piece], winds_ref, write)


def outer_kernel(
    z, parts, partner, par_ref, cut_ref, new_ref, inner_ref, winds_ref, one_ref, two_ref, table_ref, *refs
):
    refs = refs if partner else refs[1:]
    out_refs, (u_ref, v_ref) = refs[:parts], refs[parts:]
    lon, half = z.lon, z.half
    tall = 2 * half
    side = 1 - par_ref[0] if partner else par_ref[0]
    base = z.rows * side

    def halo(in_ref):
        for r in range(2):
            values = decode_row(in_ref, r * z.code, lon).reshape(2, half, lon)
            put_padded(u_ref, (4 * side + r,), values, lon)

    first_swap = side + par_ref[3] == 1
    pl.when(first_swap)(lambda: halo(one_ref))
    pl.when(jnp.logical_not(first_swap))(lambda: halo(two_ref))
    for r in range(4):
        u_ref[2 * (1 - side) + r] = new_ref[base + r]
    for r in range(2):
        v_ref[2 * (1 - side) + r] = inner_ref[2 * side + r]

    def write(row, f, at, k, values):
        v_ref[2 * side + row, f, :, pl.ds(pl.multiple_of(at + k * LANE, LANE), LANE)] = values

    substep(z, 2, 6 * side, lambda j, f, piece: u_ref[j, f, :, piece], winds_ref, write)

    def store(row, values):
        v_ref[row] = values

    filter_rows(z, cut_ref, par_ref[1] + base, 0, table_ref, lambda row: v_ref[row], store)
    column = lon // parts
    for b in range(parts):
        at = pl.multiple_of(jnp.bitwise_xor(par_ref[2], b) * column, LANE)
        values = jnp.concatenate(
            [v_ref[r, :, :, pl.ds(at, column)].reshape(tall, column) for r in range(z.rows)], axis=1
        )
        encode_row(values, out_refs[b], 0)


def scale_kernel(at, *refs):
    for i, ref in enumerate(refs[:-1]):
        refs[-1][i] = decoder(ref[:, at : at + LANE])


def column_kernel(z, parts, par_ref, *refs):
    got, (scales_ref, remap_ref, upward_ref, surface_ref, out_ref, geo_ref, x_ref) = refs[: 2 * parts], refs[2 * parts :]
    p, lev = par_ref[0], par_ref[2]
    column = out_ref.shape[-1]
    at = pl.multiple_of(pl.program_id(0) * column, LANE)
    for i, ref in enumerate(got):
        side = p if i < parts else 1 - p
        s = jnp.bitwise_xor(lev, i % parts)
        if i < parts:
            scale = decoder(ref[:, z.rows * column : z.rows * column + LANE])
        else:
            scale = scales_ref[i - parts]
        codes = ref[:, pl.ds(at, column)].astype(jnp.int32).astype(jnp.float32)
        values = codes * tiled(scale, column)
        level = pl.multiple_of(s * z.levels + side * z.half, z.half)
        for f in range(2):
            x_ref[f, pl.ds(level, z.half)] = values[f * z.half : (f + 1) * z.half]
    high, low = split(remap_ref[...])
    remap = jnp.concatenate([high, low, high], axis=1)
    count = remap_ref.shape[0]
    for f in range(2):
        high, low = split(x_ref[f])
        stacked = jnp.concatenate([high, high, low], axis=0)
        left = remap if f == 0 else jnp.concatenate([remap, upward_ref[...].astype(jnp.bfloat16)], axis=0)
        result = jnp.dot(left, stacked, preferred_element_type=jnp.float32)
        out_ref[f, 0] = result[:count]
        if f == 1:
            geo_ref[0] = surface_ref[0] + result[count:] * (count**-0.5)


def whole():
    return pl.BlockSpec(memory_space=pltpu.VMEM)


def scalars():
    return pl.BlockSpec(memory_space=pltpu.SMEM)


def far_memory():
    return pl.BlockSpec(memory_space=pltpu.HBM)


def params(limit=VMEM_LIMIT):
    return pltpu.CompilerParams(vmem_limit_bytes=limit)


def cost(flops=1000, data=1000):
    return pl.CostEstimate(flops=flops, bytes_accessed=data, transcendentals=0)


def shards(fields, courant, cutoffs, surface, remap_weights):
    _, rows, levels, lon = fields.shape
    z = Sizes(rows, levels, lon)
    lats, parts = lax.axis_size("lat"), lax.axis_size("lev")
    me = lax.axis_index("lat")
    parity = me % 2
    lev = lax.axis_index("lev")
    place = jnp.stack([parity, (me - parity) * rows, lev, (me // 2) % 2]).astype(jnp.int32)
    tall = 2 * z.half
    i16, f32 = jnp.int16, jnp.float32
    swap = [(i, i ^ 1) for i in range(lats)]
    ones, twos = [
        [pair for i in range(start, lats - 2, 4) for s in range(2) for pair in ((i + s, i + s + 2), (i + s + 2, i + s))]
        for start in (0, 2)
    ]

    def shape(*dims):
        return jax.ShapeDtypeStruct(dims, f32)

    def codes(*dims):
        return jax.ShapeDtypeStruct(dims, i16)

    edge = pl.pallas_call(
        functools.partial(edge_kernel, z),
        name="edge",
        in_specs=[far_memory(), far_memory()],
        out_specs=whole(),
        out_shape=codes(tall, z.edge),
        scratch_shapes=[
            pltpu.VMEM((2, tall, lon), f32),
            pltpu.VMEM((2, levels, lon), courant.dtype),
            pltpu.SemaphoreType.DMA((6,)),
        ],
        compiler_params=params(VMEM_MOST),
        cost_estimate=cost(),
    )(fields, courant)
    edge = lax.ppermute(edge, "lat", swap)
    inner, own = pl.pallas_call(
        functools.partial(rest_kernel, z),
        name="rest",
        in_specs=[scalars(), whole(), whole()],
        out_specs=[whole()] * 2,
        out_shape=[codes(tall, z.inner), codes(tall, z.edge)],
        compiler_params=params(),
        cost_estimate=cost(),
    )(place, fields, courant)
    inner = lax.ppermute(inner, "lat", swap)
    straight = (parity + (me // 2) % 2) == 1
    one = lax.ppermute(jnp.where(straight, own, edge), "lat", ones)
    two = lax.ppermute(jnp.where(straight, edge, own), "lat", twos)
    new, winds, one_code, two_code = pl.pallas_call(
        functools.partial(first_kernel, z),
        name="first",
        in_specs=[scalars()] + [whole()] * 6,
        out_specs=[whole()] * 4,
        out_shape=[
            shape(z.band, 2, z.half, z.pad),
            shape(3 * z.band + 1, z.half, lon),
            codes(tall, 2 * z.code),
            codes(tall, 2 * z.code),
        ],
        scratch_shapes=[
            pltpu.VMEM((z.band + 4, 2, z.half, z.pad), f32),
            pltpu.VMEM((z.band, z.half, z.pad), f32),
            pltpu.VMEM((z.band + 2, z.half, z.lon), f32),
        ],
        compiler_params=params(),
        cost_estimate=cost(),
    )(place, fields, courant, edge, inner, one, two)
    one = lax.ppermute(one_code, "lat", ones)
    two = lax.ppermute(two_code, "lat", twos)

    tables = jnp.asarray(filter_tables(lon))
    new, inner = pl.pallas_call(
        functools.partial(inner_kernel, z),
        name="inner",
        in_specs=[scalars(), scalars()] + [whole()] * 3,
        out_specs=[whole()] * 2,
        out_shape=[shape(z.band, 2, z.half, z.pad), shape(z.band - 4, 2, z.half, lon)],
        compiler_params=params(),
        cost_estimate=cost(),
    )(place, cutoffs, new, winds, tables)

    column = lon // parts

    def outer(*after):
        partner = not after
        return pl.pallas_call(
            functools.partial(outer_kernel, z, parts, partner),
            name="outer_partner" if partner else "outer_own",
            in_specs=[scalars(), scalars()] + [whole()] * 6 + [far_memory()] * len(after),
            out_specs=[whole()] * parts,
            out_shape=[codes(tall, rows * column + LANE)] * parts,
            scratch_shapes=[
                pltpu.VMEM((6, 2, z.half, z.pad), f32),
                pltpu.VMEM((z.rows, 2, z.half, lon), f32),
            ],
            compiler_params=params(),
            cost_estimate=cost(),
        )(place, cutoffs, new, inner, winds, one, two, tables, *after)

    blocks = outer()
    got = []
    for b, block in enumerate(blocks):
        pairs = [
            (i * parts + j, (i ^ 1) * parts + (j ^ b)) for i in range(lats) for j in range(parts)
        ]
        got.append(lax.ppermute(block, ("lat", "lev"), pairs))
    scales = pl.pallas_call(
        functools.partial(scale_kernel, rows * column),
        name="scales",
        in_specs=[whole()] * parts,
        out_specs=whole(),
        out_shape=shape(parts, tall, LANE),
        compiler_params=params(),
        cost_estimate=cost(),
    )(*got)
    for b, block in enumerate(outer(blocks[0])):
        pairs = [(j, j ^ b) for j in range(parts)]
        got.insert(b, lax.ppermute(block, "lev", pairs) if b else block)

    count = remap_weights.shape[0]
    upward = np.triu(np.ones((count, count), np.float32), 1) + 0.5 * np.eye(count, dtype=np.float32)
    upward = jnp.asarray(np.concatenate([upward, 0.0 * upward, upward], axis=1))
    surface = lax.dynamic_slice_in_dim(surface, lev * column, column, 1)
    remapped, geopotential = pl.pallas_call(
        functools.partial(column_kernel, z, parts),
        name="columns",
        grid=(rows,),
        in_specs=[scalars()]
        + [whole()] * (len(got) + 1)
        + [
            pl.BlockSpec(remap_weights.shape, lambda r: (0, 0)),
            pl.BlockSpec(upward.shape, lambda r: (0, 0)),
            pl.BlockSpec((1, 1, column), lambda r: (r, 0, 0)),
        ],
        out_specs=[
            pl.BlockSpec((2, 1, count, column), lambda r: (0, r, 0, 0)),
            pl.BlockSpec((1, count, column), lambda r: (r, 0, 0)),
        ],
        out_shape=[shape(2, rows, count, column), shape(rows, count, column)],
        scratch_shapes=[pltpu.VMEM((2, count, column), f32)],
        compiler_params=params(),
        cost_estimate=cost(),
    )(place, *got, scales, remap_weights, upward, surface[:, None, :])
    return remapped, geopotential


def with_halo(shard, width):
    size, length = lax.axis_size("lat"), shard.shape[1]
    up = [(i, (i + 1) % size) for i in range(size - 1)]
    down = [(j, i) for i, j in up]
    before = lax.ppermute(lax.slice_in_dim(shard, length - width, length, axis=1), "lat", up)
    after = lax.ppermute(lax.slice_in_dim(shard, 0, width, axis=1), "lat", down)
    return jnp.concatenate([before, shard, after], axis=1)


def plain_shards(fields, courant, cutoffs, surface, remap_weights):
    _, rows, _, lon = fields.shape
    exact = lax.Precision.HIGHEST
    cut = lax.dynamic_slice_in_dim(cutoffs, lax.axis_index("lat") * rows, rows)
    waves = np.arange(KMAX)
    angle = (np.arange(lon)[:, None] * waves[None, :] % lon) * (2.0 * math.pi / lon)
    table = jnp.asarray(np.concatenate([np.cos(angle), np.sin(angle)], axis=1).astype(np.float32))
    number = jnp.asarray(np.concatenate([waves, waves]).astype(np.int32))
    weight = jnp.where(number[None] <= cut[:, None], jnp.where(number == 0, 1.0, 2.0)[None] / lon, 0.0)
    flagged = cut < lon // 2

    def smooth(values):
        wave = jnp.einsum("frln,nk->frlk", values, table, precision=exact) * weight[None, :, None]
        low = jnp.einsum("frlk,nk->frln", wave, table, precision=exact)
        return jnp.where(flagged[None, :, None, None], low, values)

    winds = with_halo(courant, 1).astype(jnp.float32)
    east, north = winds[0, 1:-1], winds[1]
    face_x = (east + jnp.roll(east, -1, -1)) / 24.0
    face_y = (north[:-1] + north[1:]) / 24.0
    u = fields
    for _ in range(2):
        wide = with_halo(u, 2)
        pair = u + jnp.roll(u, -1, -1)
        fx = face_x * (8.0 * pair - (jnp.roll(pair, 1, -1) + jnp.roll(pair, -1, -1)))
        pair = wide[:, :-1] + wide[:, 1:]
        fy = face_y * (8.0 * pair[:, 1:-1] - (pair[:, :-2] + pair[:, 2:]))
        u = u - (fx - jnp.roll(fx, 1, -1)) - (fy[:, 1:] - fy[:, :-1])
        u = lax.cond(jnp.any(flagged), smooth, lambda values: values, u)
    columns = lax.all_to_all(u, "lev", split_axis=3, concat_axis=2, tiled=True)
    remapped = jnp.einsum("pk,fjkn->fjpn", remap_weights, columns, precision=exact)
    count = remap_weights.shape[0]
    upward = np.triu(np.ones((count, count), np.float32), 1) + 0.5 * np.eye(count, dtype=np.float32)
    upward = jnp.einsum("kl,jln->jkn", jnp.asarray(upward), columns[1], precision=exact)
    width = lon // lax.axis_size("lev")
    mine = lax.dynamic_slice_in_dim(surface, lax.axis_index("lev") * width, width, 1)
    return remapped, mine[:, None] + count**-0.5 * upward


def solution(mesh):
    def program(fields, courant, cutoffs, surface, remap_weights):
        lats, parts = mesh.shape["lat"], mesh.shape["lev"]
        rows, levels = fields.shape[1] // lats, fields.shape[2] // parts
        polar = fields.shape[1] // 8
        paired = (
            lats % 2 == 0
            and rows == 4
            and levels % 16 == 0
            and polar <= 2 * rows - 2
            and fields.shape[3] % (LANE * parts) == 0
            and parts & (parts - 1) == 0
            and fields.shape[3] % (4 * KMAX) == 0
        )
        return jax.shard_map(
            shards if paired else plain_shards,
            mesh=mesh,
            in_specs=(
                P(None, "lat", "lev", None),
                P(None, "lat", "lev", None),
                P(),
                P("lat", None),
                P(),
            ),
            out_specs=(P(None, "lat", None, "lev"), P("lat", None, "lev")),
            check_vma=False,
        )(fields, courant, cutoffs, surface, remap_weights)

    return program
```

```python
import functools
import math

import jax
import jax.numpy as jnp
import ml_dtypes
import numpy as np
from jax import lax
from jax.experimental import pallas as pl
from jax.experimental.pallas import tpu as pltpu
from jax.sharding import PartitionSpec as P

KMAX = 128
LANE = 128
TOP = 32767.0
STEPS = 256.0
TINY = 2.0**-100
WIND = 81920.0
ROUND = 1.5 * 2.0**23
VMEM_LIMIT = 7 * 2**20
VMEM_MOST = 63 * 2**20 + 2**19


def rounded(values):
    return ((values + ROUND) - ROUND).astype(jnp.int32).astype(jnp.int16)


def lane_max(values):
    chunks = [jnp.abs(values[:, i : i + LANE]) for i in range(0, values.shape[1], LANE)]
    while len(chunks) > 1:
        pairs = [jnp.maximum(a, b) for a, b in zip(chunks[0::2], chunks[1::2])]
        chunks = pairs + chunks[2 * len(pairs) :]
    return chunks[0]


def tiled(tile, width):
    return jnp.concatenate([tile] * (width // LANE), axis=1)


def scale_code(largest):
    return jnp.ceil(jnp.log2(jnp.maximum(largest, TINY)) * STEPS)


def encoder(code):
    return TOP / jnp.exp2(code * (1.0 / STEPS))


def decoder(code16):
    code = code16.astype(jnp.int32).astype(jnp.float32)
    return jnp.exp2(code * (1.0 / STEPS)) * (1.0 / TOP)


def encode_row(values, out_ref, at):
    width = values.shape[1]
    code = scale_code(lane_max(values))
    out_ref[:, at : at + width] = rounded(values * tiled(encoder(code), width))
    out_ref[:, at + width : at + width + LANE] = code.astype(jnp.int32).astype(jnp.int16)


def decode_row(in_ref, at, width):
    scale = decoder(in_ref[:, at + width : at + width + LANE])
    values = in_ref[:, at : at + width].astype(jnp.int32).astype(jnp.float32)
    return values * tiled(scale, width)


def wind_codes(east, north):
    return rounded(jnp.concatenate([east, north], axis=0) * WIND)


class Sizes:
    def __init__(self, rows, levels, lon):
        self.rows, self.levels, self.lon = rows, levels, lon
        self.half = levels // 2
        self.band = 2 * rows
        self.pad = lon + 2 * LANE
        self.code = lon + LANE
        self.edge = 2 * self.code + lon
        self.inner = 2 * self.code + 3 * lon


def put_padded(ref, index, values, lon):
    ref[index + (Ellipsis, slice(LANE, LANE + lon))] = values
    ref[index + (Ellipsis, slice(0, LANE))] = values[..., lon - LANE :]
    ref[index + (Ellipsis, slice(LANE + lon, 2 * LANE + lon))] = values[..., :LANE]


def wind_row(z, wind, upper):
    halves = []
    for k in range(2):
        both = wind[k].astype(jnp.float32)
        halves.append(jnp.where(upper == 1, both[z.half :], both[: z.half]))
    return wind_codes(*halves)


def edge_kernel(z, fields_ref, courant_ref, edge_ref, rows_ref, wind_ref, sems):
    p = lax.rem(lax.axis_index("lat"), 2)
    give = pl.multiple_of((1 - p) * z.half, z.half)
    copies = [
        pltpu.make_async_copy(
            fields_ref.at[f, 2 * p + r, pl.ds(give, z.half)],
            rows_ref.at[r, pl.ds(f * z.half, z.half)],
            sems.at[2 * r + f],
        )
        for r in range(2)
        for f in range(2)
    ]
    copies += [
        pltpu.make_async_copy(courant_ref.at[k, 3 * p], wind_ref.at[k], sems.at[4 + k])
        for k in range(2)
    ]
    for copy in copies:
        copy.start()
    for r in range(2):
        copies[2 * r].wait()
        copies[2 * r + 1].wait()
        encode_row(rows_ref[r], edge_ref, r * z.code)
    copies[4].wait()
    copies[5].wait()
    edge_ref[:, 2 * z.code :] = wind_row(z, wind_ref, 1 - p)


def rest_kernel(z, par_ref, fields_ref, courant_ref, inner_ref, own_ref):
    p = par_ref[0]
    keep = pl.multiple_of(p * z.half, z.half)
    give = pl.multiple_of((1 - p) * z.half, z.half)

    def field_row(row, start):
        return jnp.concatenate([fields_ref[f, row, pl.ds(start, z.half)] for f in range(2)], axis=0)

    def winds(row, upper):
        return wind_row(z, [courant_ref[k, row] for k in range(2)], upper)

    edge, inner = 2 * p, 2 * (1 - p)
    at = 2 * z.code
    for r in range(2):
        encode_row(field_row(inner + r, give), inner_ref, r * z.code)
    for i, row in enumerate((inner, inner + 1, 1 + p)):
        inner_ref[:, at + i * z.lon : at + (i + 1) * z.lon] = winds(row, 1 - p)
    for r in range(2):
        encode_row(field_row(edge + r, keep), own_ref, r * z.code)
    own_ref[:, at : at + z.lon] = winds(3 * p, p)


def shifted(pieces, shift, lanes):
    turned = [pltpu.roll(v, (-shift) % LANE, 1) for v in pieces]
    if shift > 0:
        return [jnp.where(lanes < LANE - shift, a, b) for a, b in zip(turned[1:-1], turned[2:])]
    return [jnp.where(lanes < -shift, a, b) for a, b in zip(turned[:-2], turned[1:-1])]


def substep(z, count_rows, base, row_of, winds_ref, write):
    count = next(n for n in (4, 3, 2, 1) if z.lon % (n * LANE) == 0)
    width = count * LANE
    lanes = lax.broadcasted_iota(jnp.int32, (z.half, LANE), 1)

    def part(i, carry):
        at = pl.multiple_of(i * width, LANE)

        def piece(k):
            return pl.ds(pl.multiple_of(at + k * LANE, LANE), LANE)

        def row(j, f):
            return [row_of(j, f, piece(k + 1)) for k in range(count)]

        def start(j, f):
            pieces = [row_of(j + 2, f, piece(k)) for k in range(count + 2)]
            return [shifted(pieces, s, lanes) for s in (-2, -1, 1, 2)]

        def lon_part(j, u, moved):
            out = []
            for k in range(count):
                m2, m1, p1, p2 = (m[k] for m in moved)
                east = 7.0 * (u[k] + p1) - (m1 + p2)
                west = 7.0 * (m1 + u[k]) - (m2 + p1)
                east = winds_ref[base + j, :, piece(k)] * east
                out.append(east - winds_ref[z.band + base + j, :, piece(k)] * west)
            return out

        for f in range(2):
            rows = [row(j, f) for j in range(4)]
            sums = [[a + b for a, b in zip(rows[j], rows[j + 1])] for j in range(3)]
            flux = None
            moved = start(0, f)
            for j in range(count_rows + 1):
                later = start(j, f) if 0 < j < count_rows else None
                new = [
                    winds_ref[2 * z.band + base + j, :, piece(k)] * (8.0 * sums[1][k] - (sums[0][k] + sums[2][k]))
                    for k in range(count)
                ]
                if j > 0:
                    u = rows[1]
                    change = lon_part(j - 1, u, moved)
                    for k in range(count):
                        write(j - 1, f, at, k, u[k] - change[k] - (new[k] - flux[k]))
                    moved = later
                flux = new
                if j < count_rows:
                    above = row(j + 4, f)
                    rows = rows[1:] + [above]
                    sums = sums[1:] + [[a + b for a, b in zip(rows[2], rows[3])]]
        return carry

    lax.fori_loop(0, z.lon // width, part, 0)


def filter_tables(lon):
    half = lon // 2
    points = np.arange(half)
    forward, back = [], []
    for parity in range(2):
        waves = np.arange(parity, KMAX, 2)
        angle = (points[:, None] * waves[None, :] % lon) * (2.0 * math.pi / lon)
        table = np.concatenate([np.cos(angle), np.sin(angle)], axis=1).astype(np.float32)
        high = table.astype(ml_dtypes.bfloat16)
        low = (table - high.astype(np.float32)).astype(ml_dtypes.bfloat16)
        forward.append(np.concatenate([high, low], axis=1))
        turned = np.concatenate([high.T, low.T], axis=0)
        back.append(np.concatenate(np.split(turned, half // (2 * KMAX), axis=1), axis=0))
    return np.stack(forward + back)


def split(values):
    high = values.astype(jnp.bfloat16)
    return high, (values - high.astype(jnp.float32)).astype(jnp.bfloat16)


def low_pass(z, rows, cuts, table_ref):
    half = z.lon // 2
    count = len(rows)
    tall = 2 * z.half
    total = count * tall
    flat = [row.reshape(tall, z.lon) for row in rows]
    folded = []
    for parity in range(2):
        parts = [
            row[:, :half] + row[:, half:] if parity == 0 else row[:, :half] - row[:, half:]
            for row in flat
        ]
        high, low = split(jnp.concatenate(parts, axis=0))
        both = jnp.concatenate([high, low], axis=0)
        got = jnp.dot(both, table_ref[parity], preferred_element_type=jnp.float32)
        wave = got[:total, :KMAX] + got[:total, KMAX:] + (got[total:, :KMAX] + got[total:, KMAX:])
        number = 2 * (lax.broadcasted_iota(jnp.int32, (tall, KMAX), 1) % (KMAX // 2)) + parity
        doubled = jnp.where(number == 0, 1.0, 2.0) * (1.0 / z.lon)
        weight = jnp.concatenate([jnp.where(number <= cut, doubled, 0.0) for cut in cuts], axis=0)
        high, low = split(wave * weight)
        both = jnp.concatenate(
            [jnp.concatenate([high, high], axis=1), jnp.concatenate([low, low], axis=1)], axis=0
        )
        got = []
        for at in range(0, half, 2 * KMAX):
            block = table_ref[2 + parity, at : at + 2 * KMAX]
            sums = jnp.dot(both, block, preferred_element_type=jnp.float32)
            got.append(sums[:total] + sums[total:])
        folded.append(jnp.concatenate(got, axis=1))
    left, right = folded[0] + folded[1], folded[0] - folded[1]
    smooth = jnp.concatenate([left, right], axis=1)
    return [smooth[i * tall : (i + 1) * tall].reshape(2, z.half, z.lon) for i in range(count)]


def filter_rows(z, cut_ref, first_row, start, table_ref, load, store):
    nyquist = z.lon // 2
    cuts = [cut_ref[first_row + start + r] for r in range(z.rows)]
    some = functools.reduce(jnp.logical_or, [cut < nyquist for cut in cuts])

    @pl.when(some)
    def _():
        smooth = low_pass(z, [load(start + r) for r in range(z.rows)], cuts, table_ref)
        for r in range(z.rows):

            @pl.when(cuts[r] < nyquist)
            def _():
                store(start + r, smooth[r])


def first_kernel(
    z, par_ref, fields_ref, courant_ref, edge_ref, inner_ref, one_ref, two_ref,
    new_ref, winds_ref, one_out_ref, two_out_ref, u_ref, cx_ref, cy_ref,
):
    p, b = par_ref[0], par_ref[3]
    lon, half = z.lon, z.half

    def pair(values):
        return values.reshape(2, half, values.shape[1])

    def winds(in_ref, at):
        values = in_ref[:, at : at + lon].astype(jnp.int32).astype(jnp.float32) * (1.0 / WIND)
        return values[:half], values[half:]

    def place_wind(row, east, north):
        put_padded(cx_ref, (row,), east, lon)
        cy_ref[row + 1] = north

    keep = pl.multiple_of(p * half, half)
    for r in range(z.rows):
        row = z.rows * p + r
        own = jnp.stack([fields_ref[f, r, pl.ds(keep, half)] for f in range(2)])
        put_padded(u_ref, (row + 2,), own, lon)
        got = []
        for k in range(2):
            wind = courant_ref[k, r].astype(jnp.float32)
            got.append(jnp.where(p == 1, wind[half:], wind[:half]))
        place_wind(row, *got)
    at = 2 * z.code
    for r in range(2):
        put_padded(u_ref, (6 * (1 - p) + r + 2,), pair(decode_row(edge_ref, r * z.code, lon)), lon)
        put_padded(u_ref, (4 - 2 * p + r + 2,), pair(decode_row(inner_ref, r * z.code, lon)), lon)
        put_padded(u_ref, (10 * (1 - b) + r,), pair(decode_row(one_ref, r * z.code, lon)), lon)
        put_padded(u_ref, (10 * b + r,), pair(decode_row(two_ref, r * z.code, lon)), lon)
        place_wind(4 - 2 * p + r, *winds(inner_ref, at + r * lon))
    place_wind(7 * (1 - p), *winds(edge_ref, at))
    place_wind(6 - 5 * p, *winds(inner_ref, at + 2 * lon))
    cy_ref[9 * (1 - b)] = winds(one_ref, at)[1]
    cy_ref[9 * b] = winds(two_ref, at)[1]

    def face_rows(j, carry):
        wind = cx_ref[j] * (1.0 / 24.0)
        here = wind[:, LANE : LANE + lon]
        winds_ref[j] = here + pltpu.roll(wind, z.pad - 1, 1)[:, LANE : LANE + lon]
        winds_ref[z.band + j] = here + pltpu.roll(wind, 1, 1)[:, LANE : LANE + lon]
        return carry

    lax.fori_loop(0, z.band, face_rows, 0)

    def face_cols(j, carry):
        winds_ref[2 * z.band + j] = (cy_ref[j] + cy_ref[j + 1]) * (1.0 / 24.0)
        return carry

    lax.fori_loop(0, z.band + 1, face_cols, 0)

    def write(row, f, at, k, values):
        new_ref[row, f, :, pl.ds(pl.multiple_of(at + (k + 1) * LANE, LANE), LANE)] = values

    substep(z, z.band, 0, lambda j, f, piece: u_ref[j, f, :, piece], winds_ref, write)
    for r in range(2):
        for row, out_ref in ((6 * (1 - b) + r, one_out_ref), (6 * b + r, two_out_ref)):
            values = new_ref[row, :, :, LANE : LANE + lon]
            encode_row(values.reshape(2 * half, lon), out_ref, r * z.code)
    for j in range(z.band):
        new_ref[j, :, :, 0:LANE] = new_ref[j, :, :, lon : lon + LANE]
        new_ref[j, :, :, LANE + lon :] = new_ref[j, :, :, LANE : 2 * LANE]


def inner_kernel(z, par_ref, cut_ref, in_ref, winds_ref, table_ref, new_ref, inner_ref):
    for j in range(z.band):
        new_ref[j] = in_ref[j]

    def store(row, values):
        put_padded(new_ref, (row,), values, z.lon)

    for part in range(2):
        filter_rows(
            z, cut_ref, par_ref[1], part * z.rows, table_ref,
            lambda row: in_ref[row, :, :, LANE : LANE + z.lon], store,
        )

    def write(row, f, at, k, values):
        inner_ref[row, f, :, pl.ds(pl.multiple_of(at + k * LANE, LANE), LANE)] = values

    substep(z, z.band - 4, 2, lambda j, f, piece: new_ref[j, f, :, piece], winds_ref, write)


def outer_kernel(
    z, parts, partner, par_ref, cut_ref, new_ref, inner_ref, winds_ref, one_ref, two_ref, table_ref, *refs
):
    refs = refs if partner else refs[1:]
    out_refs, (u_ref, v_ref) = refs[:parts], refs[parts:]
    lon, half = z.lon, z.half
    tall = 2 * half
    side = 1 - par_ref[0] if partner else par_ref[0]
    base = z.rows * side

    def halo(in_ref):
        for r in range(2):
            values = decode_row(in_ref, r * z.code, lon).reshape(2, half, lon)
            put_padded(u_ref, (4 * side + r,), values, lon)

    first_swap = side + par_ref[3] == 1
    pl.when(first_swap)(lambda: halo(one_ref))
    pl.when(jnp.logical_not(first_swap))(lambda: halo(two_ref))
    for r in range(4):
        u_ref[2 * (1 - side) + r] = new_ref[base + r]
    for r in range(2):
        v_ref[2 * (1 - side) + r] = inner_ref[2 * side + r]

    def write(row, f, at, k, values):
        v_ref[2 * side + row, f, :, pl.ds(pl.multiple_of(at + k * LANE, LANE), LANE)] = values

    substep(z, 2, 6 * side, lambda j, f, piece: u_ref[j, f, :, piece], winds_ref, write)

    def store(row, values):
        v_ref[row] = values

    filter_rows(z, cut_ref, par_ref[1] + base, 0, table_ref, lambda row: v_ref[row], store)
    column = lon // parts
    for b in range(parts):
        at = pl.multiple_of(jnp.bitwise_xor(par_ref[2], b) * column, LANE)
        values = jnp.concatenate(
            [v_ref[r, :, :, pl.ds(at, column)].reshape(tall, column) for r in range(z.rows)], axis=1
        )
        encode_row(values, out_refs[b], 0)


def scale_kernel(at, *refs):
    for i, ref in enumerate(refs[:-1]):
        refs[-1][i] = decoder(ref[:, at : at + LANE])


def column_kernel(z, parts, par_ref, *refs):
    got, (scales_ref, remap_ref, upward_ref, surface_ref, out_ref, geo_ref, x_ref) = refs[: 2 * parts], refs[2 * parts :]
    p, lev = par_ref[0], par_ref[2]
    column = out_ref.shape[-1]
    at = pl.multiple_of(pl.program_id(0) * column, LANE)
    for i, ref in enumerate(got):
        side = p if i < parts else 1 - p
        s = jnp.bitwise_xor(lev, i % parts)
        if i < parts:
            scale = decoder(ref[:, z.rows * column : z.rows * column + LANE])
        else:
            scale = scales_ref[i - parts]
        codes = ref[:, pl.ds(at, column)].astype(jnp.int32).astype(jnp.float32)
        values = codes * tiled(scale, column)
        level = pl.multiple_of(s * z.levels + side * z.half, z.half)
        for f in range(2):
            x_ref[f, pl.ds(level, z.half)] = values[f * z.half : (f + 1) * z.half]
    high, low = split(remap_ref[...])
    remap = jnp.concatenate([high, low, high], axis=1)
    count = remap_ref.shape[0]
    for f in range(2):
        high, low = split(x_ref[f])
        stacked = jnp.concatenate([high, high, low], axis=0)
        left = remap if f == 0 else jnp.concatenate([remap, upward_ref[...].astype(jnp.bfloat16)], axis=0)
        result = jnp.dot(left, stacked, preferred_element_type=jnp.float32)
        out_ref[f, 0] = result[:count]
        if f == 1:
            geo_ref[0] = surface_ref[0] + result[count:] * (count**-0.5)


def whole():
    return pl.BlockSpec(memory_space=pltpu.VMEM)


def scalars():
    return pl.BlockSpec(memory_space=pltpu.SMEM)


def far_memory():
    return pl.BlockSpec(memory_space=pltpu.HBM)


def params(limit=VMEM_LIMIT):
    return pltpu.CompilerParams(vmem_limit_bytes=limit)


def cost(flops=1000, data=1000):
    return pl.CostEstimate(flops=flops, bytes_accessed=data, transcendentals=0)


def shards(fields, courant, cutoffs, surface, remap_weights):
    _, rows, levels, lon = fields.shape
    z = Sizes(rows, levels, lon)
    lats, parts = lax.axis_size("lat"), lax.axis_size("lev")
    me = lax.axis_index("lat")
    parity = me % 2
    lev = lax.axis_index("lev")
    place = jnp.stack([parity, (me - parity) * rows, lev, (me // 2) % 2]).astype(jnp.int32)
    tall = 2 * z.half
    i16, f32 = jnp.int16, jnp.float32
    swap = [(i, i ^ 1) for i in range(lats)]
    ones, twos = [
        [pair for i in range(start, lats - 2, 4) for s in range(2) for pair in ((i + s, i + s + 2), (i + s + 2, i + s))]
        for start in (0, 2)
    ]

    def shape(*dims):
        return jax.ShapeDtypeStruct(dims, f32)

    def codes(*dims):
        return jax.ShapeDtypeStruct(dims, i16)

    edge = pl.pallas_call(
        functools.partial(edge_kernel, z),
        name="edge",
        in_specs=[far_memory(), far_memory()],
        out_specs=whole(),
        out_shape=codes(tall, z.edge),
        scratch_shapes=[
            pltpu.VMEM((2, tall, lon), f32),
            pltpu.VMEM((2, levels, lon), courant.dtype),
            pltpu.SemaphoreType.DMA((6,)),
        ],
        compiler_params=params(VMEM_MOST),
        cost_estimate=cost(),
    )(fields, courant)
    edge = lax.ppermute(edge, "lat", swap)
    inner, own = pl.pallas_call(
        functools.partial(rest_kernel, z),
        name="rest",
        in_specs=[scalars(), whole(), whole()],
        out_specs=[whole()] * 2,
        out_shape=[codes(tall, z.inner), codes(tall, z.edge)],
        compiler_params=params(),
        cost_estimate=cost(),
    )(place, fields, courant)
    inner = lax.ppermute(inner, "lat", swap)
    straight = (parity + (me // 2) % 2) == 1
    one = lax.ppermute(jnp.where(straight, own, edge), "lat", ones)
    two = lax.ppermute(jnp.where(straight, edge, own), "lat", twos)
    new, winds, one_code, two_code = pl.pallas_call(
        functools.partial(first_kernel, z),
        name="first",
        in_specs=[scalars()] + [whole()] * 6,
        out_specs=[whole()] * 4,
        out_shape=[
            shape(z.band, 2, z.half, z.pad),
            shape(3 * z.band + 1, z.half, lon),
            codes(tall, 2 * z.code),
            codes(tall, 2 * z.code),
        ],
        scratch_shapes=[
            pltpu.VMEM((z.band + 4, 2, z.half, z.pad), f32),
            pltpu.VMEM((z.band, z.half, z.pad), f32),
            pltpu.VMEM((z.band + 2, z.half, z.lon), f32),
        ],
        compiler_params=params(),
        cost_estimate=cost(),
    )(place, fields, courant, edge, inner, one, two)
    one = lax.ppermute(one_code, "lat", ones)
    two = lax.ppermute(two_code, "lat", twos)

    tables = jnp.asarray(filter_tables(lon))
    new, inner = pl.pallas_call(
        functools.partial(inner_kernel, z),
        name="inner",
        in_specs=[scalars(), scalars()] + [whole()] * 3,
        out_specs=[whole()] * 2,
        out_shape=[shape(z.band, 2, z.half, z.pad), shape(z.band - 4, 2, z.half, lon)],
        compiler_params=params(),
        cost_estimate=cost(),
    )(place, cutoffs, new, winds, tables)

    column = lon // parts

    def outer(*after):
        partner = not after
        return pl.pallas_call(
            functools.partial(outer_kernel, z, parts, partner),
            name="outer_partner" if partner else "outer_own",
            in_specs=[scalars(), scalars()] + [whole()] * 6 + [far_memory()] * len(after),
            out_specs=[whole()] * parts,
            out_shape=[codes(tall, rows * column + LANE)] * parts,
            scratch_shapes=[
                pltpu.VMEM((6, 2, z.half, z.pad), f32),
                pltpu.VMEM((z.rows, 2, z.half, lon), f32),
            ],
            compiler_params=params(),
            cost_estimate=cost(),
        )(place, cutoffs, new, inner, winds, one, two, tables, *after)

    blocks = outer()
    got = []
    for b, block in enumerate(blocks):
        pairs = [
            (i * parts + j, (i ^ 1) * parts + (j ^ b)) for i in range(lats) for j in range(parts)
        ]
        got.append(lax.ppermute(block, ("lat", "lev"), pairs))
    scales = pl.pallas_call(
        functools.partial(scale_kernel, rows * column),
        name="scales",
        in_specs=[whole()] * parts,
        out_specs=whole(),
        out_shape=shape(parts, tall, LANE),
        compiler_params=params(),
        cost_estimate=cost(),
    )(*got)
    for b, block in enumerate(outer(blocks[0])):
        pairs = [(j, j ^ b) for j in range(parts)]
        got.insert(b, lax.ppermute(block, "lev", pairs) if b else block)

    count = remap_weights.shape[0]
    upward = np.triu(np.ones((count, count), np.float32), 1) + 0.5 * np.eye(count, dtype=np.float32)
    upward = jnp.asarray(np.concatenate([upward, 0.0 * upward, upward], axis=1))
    surface = lax.dynamic_slice_in_dim(surface, lev * column, column, 1)
    remapped, geopotential = pl.pallas_call(
        functools.partial(column_kernel, z, parts),
        name="columns",
        grid=(rows,),
        in_specs=[scalars()]
        + [whole()] * (len(got) + 1)
        + [
            pl.BlockSpec(remap_weights.shape, lambda r: (0, 0)),
            pl.BlockSpec(upward.shape, lambda r: (0, 0)),
            pl.BlockSpec((1, 1, column), lambda r: (r, 0, 0)),
        ],
        out_specs=[
            pl.BlockSpec((2, 1, count, column), lambda r: (0, r, 0, 0)),
            pl.BlockSpec((1, count, column), lambda r: (r, 0, 0)),
        ],
        out_shape=[shape(2, rows, count, column), shape(rows, count, column)],
        scratch_shapes=[pltpu.VMEM((2, count, column), f32)],
        compiler_params=params(),
        cost_estimate=cost(),
    )(place, *got, scales, remap_weights, upward, surface[:, None, :])
    return remapped, geopotential


def with_halo(shard, width):
    size, length = lax.axis_size("lat"), shard.shape[1]
    up = [(i, (i + 1) % size) for i in range(size - 1)]
    down = [(j, i) for i, j in up]
    before = lax.ppermute(lax.slice_in_dim(shard, length - width, length, axis=1), "lat", up)
    after = lax.ppermute(lax.slice_in_dim(shard, 0, width, axis=1), "lat", down)
    return jnp.concatenate([before, shard, after], axis=1)


def plain_shards(fields, courant, cutoffs, surface, remap_weights):
    _, rows, _, lon = fields.shape
    exact = lax.Precision.HIGHEST
    cut = lax.dynamic_slice_in_dim(cutoffs, lax.axis_index("lat") * rows, rows)
    waves = np.arange(KMAX)
    angle = (np.arange(lon)[:, None] * waves[None, :] % lon) * (2.0 * math.pi / lon)
    table = jnp.asarray(np.concatenate([np.cos(angle), np.sin(angle)], axis=1).astype(np.float32))
    number = jnp.asarray(np.concatenate([waves, waves]).astype(np.int32))
    weight = jnp.where(number[None] <= cut[:, None], jnp.where(number == 0, 1.0, 2.0)[None] / lon, 0.0)
    flagged = cut < lon // 2

    def smooth(values):
        wave = jnp.einsum("frln,nk->frlk", values, table, precision=exact) * weight[None, :, None]
        low = jnp.einsum("frlk,nk->frln", wave, table, precision=exact)
        return jnp.where(flagged[None, :, None, None], low, values)

    winds = with_halo(courant, 1).astype(jnp.float32)
    east, north = winds[0, 1:-1], winds[1]
    face_x = (east + jnp.roll(east, -1, -1)) / 24.0
    face_y = (north[:-1] + north[1:]) / 24.0
    u = fields
    for _ in range(2):
        wide = with_halo(u, 2)
        pair = u + jnp.roll(u, -1, -1)
        fx = face_x * (8.0 * pair - (jnp.roll(pair, 1, -1) + jnp.roll(pair, -1, -1)))
        pair = wide[:, :-1] + wide[:, 1:]
        fy = face_y * (8.0 * pair[:, 1:-1] - (pair[:, :-2] + pair[:, 2:]))
        u = u - (fx - jnp.roll(fx, 1, -1)) - (fy[:, 1:] - fy[:, :-1])
        u = lax.cond(jnp.any(flagged), smooth, lambda values: values, u)
    columns = lax.all_to_all(u, "lev", split_axis=3, concat_axis=2, tiled=True)
    remapped = jnp.einsum("pk,fjkn->fjpn", remap_weights, columns, precision=exact)
    count = remap_weights.shape[0]
    upward = np.triu(np.ones((count, count), np.float32), 1) + 0.5 * np.eye(count, dtype=np.float32)
    upward = jnp.einsum("kl,jln->jkn", jnp.asarray(upward), columns[1], precision=exact)
    width = lon // lax.axis_size("lev")
    mine = lax.dynamic_slice_in_dim(surface, lax.axis_index("lev") * width, width, 1)
    return remapped, mine[:, None] + count**-0.5 * upward


def solution(mesh):
    def program(fields, courant, cutoffs, surface, remap_weights):
        lats, parts = mesh.shape["lat"], mesh.shape["lev"]
        rows, levels = fields.shape[1] // lats, fields.shape[2] // parts
        polar = fields.shape[1] // 8
        paired = (
            lats % 2 == 0
            and rows == 4
            and levels % 16 == 0
            and polar <= 2 * rows - 2
            and fields.shape[3] % (LANE * parts) == 0
            and parts & (parts - 1) == 0
            and fields.shape[3] % (4 * KMAX) == 0
        )
        return jax.shard_map(
            shards if paired else plain_shards,
            mesh=mesh,
            in_specs=(
                P(None, "lat", "lev", None),
                P(None, "lat", "lev", None),
                P(),
                P("lat", None),
                P(),
            ),
            out_specs=(P(None, "lat", None, "lev"), P("lat", None, "lev")),
            check_vma=False,
        )(fields, courant, cutoffs, surface, remap_weights)

    return program
```

```python
import functools
import math

import jax
import jax.numpy as jnp
import ml_dtypes
import numpy as np
from jax import lax
from jax.experimental import pallas as pl
from jax.experimental.pallas import tpu as pltpu
from jax.sharding import PartitionSpec as P

KMAX = 128
LANE = 128
TOP = 32767.0
STEPS = 256.0
TINY = 2.0**-100
WIND = 81920.0
ROUND = 1.5 * 2.0**23
VMEM_LIMIT = 12 * 2**20
VMEM_MOST = 63 * 2**20 + 2**19


def rounded(values):
    return ((values + ROUND) - ROUND).astype(jnp.int32).astype(jnp.int16)


def lane_max(values):
    chunks = [jnp.abs(values[:, i : i + LANE]) for i in range(0, values.shape[1], LANE)]
    while len(chunks) > 1:
        pairs = [jnp.maximum(a, b) for a, b in zip(chunks[0::2], chunks[1::2])]
        chunks = pairs + chunks[2 * len(pairs) :]
    return chunks[0]


def tiled(tile, width):
    return jnp.concatenate([tile] * (width // LANE), axis=1)


def scale_code(largest):
    return jnp.ceil(jnp.log2(jnp.maximum(largest, TINY)) * STEPS)


def encoder(code):
    return TOP / jnp.exp2(code * (1.0 / STEPS))


def decoder(code16):
    code = code16.astype(jnp.int32).astype(jnp.float32)
    return jnp.exp2(code * (1.0 / STEPS)) * (1.0 / TOP)


def encode_row(values, out_ref, at):
    width = values.shape[1]
    code = scale_code(lane_max(values))
    out_ref[:, at : at + width] = rounded(values * tiled(encoder(code), width))
    out_ref[:, at + width : at + width + LANE] = code.astype(jnp.int32).astype(jnp.int16)


def decode_row(in_ref, at, width):
    scale = decoder(in_ref[:, at + width : at + width + LANE])
    values = in_ref[:, at : at + width].astype(jnp.int32).astype(jnp.float32)
    return values * tiled(scale, width)


def wind_codes(east, north):
    return rounded(jnp.concatenate([east, north], axis=0) * WIND)


class Sizes:
    def __init__(self, rows, levels, lon):
        self.rows, self.levels, self.lon = rows, levels, lon
        self.half = levels // 2
        self.band = 2 * rows
        self.pad = lon + 2 * LANE
        self.code = lon + LANE
        self.edge = 2 * self.code + lon


def put_padded(ref, index, values, lon):
    ref[index + (Ellipsis, slice(LANE, LANE + lon))] = values
    ref[index + (Ellipsis, slice(0, LANE))] = values[..., lon - LANE :]
    ref[index + (Ellipsis, slice(LANE + lon, 2 * LANE + lon))] = values[..., :LANE]


def wind_row(z, wind, upper):
    halves = []
    for k in range(2):
        both = wind[k].astype(jnp.float32)
        halves.append(jnp.where(upper == 1, both[z.half :], both[: z.half]))
    return wind_codes(*halves)


def edge_kernel(z, fields_ref, courant_ref, edge_ref, rows_ref, wind_ref, sems):
    p = lax.rem(lax.axis_index("lat"), 2)
    give = pl.multiple_of((1 - p) * z.half, z.half)
    copies = [
        pltpu.make_async_copy(
            fields_ref.at[f, 2 * p + r, pl.ds(give, z.half)],
            rows_ref.at[r, pl.ds(f * z.half, z.half)],
            sems.at[2 * r + f],
        )
        for r in range(2)
        for f in range(2)
    ]
    copies += [
        pltpu.make_async_copy(courant_ref.at[k, 3 * p], wind_ref.at[k], sems.at[4 + k])
        for k in range(2)
    ]
    for copy in copies:
        copy.start()
    for r in range(2):
        copies[2 * r].wait()
        copies[2 * r + 1].wait()
        encode_row(rows_ref[r], edge_ref, r * z.code)
    copies[4].wait()
    copies[5].wait()
    edge_ref[:, 2 * z.code :] = wind_row(z, wind_ref, 1 - p)


def rest_kernel(z, par_ref, fields_ref, courant_ref, middle_ref, last_ref, own_ref):
    p = par_ref[0]
    keep = pl.multiple_of(p * z.half, z.half)
    give = pl.multiple_of((1 - p) * z.half, z.half)

    def field_row(row, start):
        return jnp.concatenate([fields_ref[f, row, pl.ds(start, z.half)] for f in range(2)], axis=0)

    def winds(row, upper):
        return wind_row(z, [courant_ref[k, row] for k in range(2)], upper)

    edge, inner = 2 * p, 2 * (1 - p)
    at = 2 * z.code
    for r in range(2):
        encode_row(field_row(inner + r, give), middle_ref, r * z.code)
        encode_row(field_row(edge + r, keep), own_ref, r * z.code)
        last_ref[:, r * z.lon : (r + 1) * z.lon] = winds(1 + r, 1 - p)
    middle_ref[:, at : at + z.lon] = winds(3 * (1 - p), 1 - p)
    own_ref[:, at : at + z.lon] = winds(3 * p, p)


def pick_kernel(par_ref, own_ref, edge_ref, one_ref, two_ref):
    straight = par_ref[0] + par_ref[3] == 1

    def put(a_ref, b_ref):
        one_ref[...] = a_ref[...]
        two_ref[...] = b_ref[...]

    pl.when(straight)(lambda: put(own_ref, edge_ref))
    pl.when(jnp.logical_not(straight))(lambda: put(edge_ref, own_ref))


def shifted(pieces, shift, lanes):
    turned = [pltpu.roll(v, (-shift) % LANE, 1) for v in pieces]
    if shift > 0:
        return [jnp.where(lanes < LANE - shift, a, b) for a, b in zip(turned[1:-1], turned[2:])]
    return [jnp.where(lanes < -shift, a, b) for a, b in zip(turned[:-2], turned[1:-1])]


def substep(z, count_rows, base, row_of, winds_ref, write):
    count = next(n for n in (4, 3, 2, 1) if z.lon % (n * LANE) == 0)
    width = count * LANE
    lanes = lax.broadcasted_iota(jnp.int32, (z.half, LANE), 1)

    def part(i, carry):
        at = pl.multiple_of(i * width, LANE)

        def piece(k):
            return pl.ds(pl.multiple_of(at + k * LANE, LANE), LANE)

        def row(j, f):
            return [row_of(j, f, piece(k + 1)) for k in range(count)]

        def start(j, f):
            pieces = [row_of(j + 2, f, piece(k)) for k in range(count + 2)]
            return [shifted(pieces, s, lanes) for s in (-2, -1, 1, 2)]

        def lon_part(j, u, moved):
            out = []
            for k in range(count):
                m2, m1, p1, p2 = (m[k] for m in moved)
                east = 7.0 * (u[k] + p1) - (m1 + p2)
                west = 7.0 * (m1 + u[k]) - (m2 + p1)
                east = winds_ref[base + j, :, piece(k)] * east
                out.append(east - winds_ref[z.rows + base + j, :, piece(k)] * west)
            return out

        for f in range(2):
            rows = [row(j, f) for j in range(4)]
            sums = [[a + b for a, b in zip(rows[j], rows[j + 1])] for j in range(3)]
            flux = None
            moved = start(0, f)
            for j in range(count_rows + 1):
                later = start(j, f) if 0 < j < count_rows else None
                new = [
                    winds_ref[2 * z.rows + base + j, :, piece(k)] * (8.0 * sums[1][k] - (sums[0][k] + sums[2][k]))
                    for k in range(count)
                ]
                if j > 0:
                    u = rows[1]
                    change = lon_part(j - 1, u, moved)
                    for k in range(count):
                        write(j - 1, f, at, k, u[k] - change[k] - (new[k] - flux[k]))
                    moved = later
                flux = new
                if j < count_rows:
                    above = row(j + 4, f)
                    rows = rows[1:] + [above]
                    sums = sums[1:] + [[a + b for a, b in zip(rows[2], rows[3])]]
        return carry

    lax.fori_loop(0, z.lon // width, part, 0)


def filter_tables(lon):
    half = lon // 2
    points = np.arange(half)
    forward, back = [], []
    for parity in range(2):
        waves = np.arange(parity, KMAX, 2)
        angle = (points[:, None] * waves[None, :] % lon) * (2.0 * math.pi / lon)
        table = np.concatenate([np.cos(angle), np.sin(angle)], axis=1).astype(np.float32)
        high = table.astype(ml_dtypes.bfloat16)
        low = (table - high.astype(np.float32)).astype(ml_dtypes.bfloat16)
        forward.append(np.concatenate([high, low], axis=1))
        turned = np.concatenate([high.T, low.T], axis=0)
        back.append(np.concatenate(np.split(turned, half // (2 * KMAX), axis=1), axis=0))
    return np.stack(forward + back)


def split(values):
    high = values.astype(jnp.bfloat16)
    return high, (values - high.astype(jnp.float32)).astype(jnp.bfloat16)


def low_pass(z, rows, cuts, table_ref):
    half = z.lon // 2
    count = len(rows)
    tall = 2 * z.half
    total = count * tall
    flat = [row.reshape(tall, z.lon) for row in rows]
    folded = []
    for parity in range(2):
        parts = [
            row[:, :half] + row[:, half:] if parity == 0 else row[:, :half] - row[:, half:]
            for row in flat
        ]
        high, low = split(jnp.concatenate(parts, axis=0))
        both = jnp.concatenate([high, low], axis=0)
        got = jnp.dot(both, table_ref[parity], preferred_element_type=jnp.float32)
        wave = got[:total, :KMAX] + got[:total, KMAX:] + (got[total:, :KMAX] + got[total:, KMAX:])
        number = 2 * (lax.broadcasted_iota(jnp.int32, (tall, KMAX), 1) % (KMAX // 2)) + parity
        doubled = jnp.where(number == 0, 1.0, 2.0) * (1.0 / z.lon)
        weight = jnp.concatenate([jnp.where(number <= cut, doubled, 0.0) for cut in cuts], axis=0)
        high, low = split(wave * weight)
        both = jnp.concatenate(
            [jnp.concatenate([high, high], axis=1), jnp.concatenate([low, low], axis=1)], axis=0
        )
        got = []
        for at in range(0, half, 2 * KMAX):
            block = table_ref[2 + parity, at : at + 2 * KMAX]
            sums = jnp.dot(both, block, preferred_element_type=jnp.float32)
            got.append(sums[:total] + sums[total:])
        folded.append(jnp.concatenate(got, axis=1))
    left, right = folded[0] + folded[1], folded[0] - folded[1]
    smooth = jnp.concatenate([left, right], axis=1)
    return [smooth[i * tall : (i + 1) * tall].reshape(2, z.half, z.lon) for i in range(count)]


def filter_rows(z, cut_ref, first_row, start, table_ref, load, store):
    nyquist = z.lon // 2
    cuts = [cut_ref[first_row + start + r] for r in range(z.rows)]
    some = functools.reduce(jnp.logical_or, [cut < nyquist for cut in cuts])

    @pl.when(some)
    def _():
        smooth = low_pass(z, [load(start + r) for r in range(z.rows)], cuts, table_ref)
        for r in range(z.rows):

            @pl.when(cuts[r] < nyquist)
            def _():
                store(start + r, smooth[r])


def received_winds(z, in_ref, at):
    values = in_ref[:, at : at + z.lon].astype(jnp.int32).astype(jnp.float32) * (1.0 / WIND)
    return values[: z.half], values[z.half :]


def own_winds(z, p, courant_ref, row):
    got = []
    for k in range(2):
        wind = courant_ref[k, row].astype(jnp.float32)
        got.append(jnp.where(p == 1, wind[z.half :], wind[: z.half]))
    return got


def faces(z, cx_ref, cy_ref, winds_ref):
    def face_rows(j, carry):
        wind = cx_ref[j] * (1.0 / 24.0)
        here = wind[:, LANE : LANE + z.lon]
        winds_ref[j] = here + pltpu.roll(wind, z.pad - 1, 1)[:, LANE : LANE + z.lon]
        winds_ref[z.rows + j] = here + pltpu.roll(wind, 1, 1)[:, LANE : LANE + z.lon]
        return carry

    lax.fori_loop(0, z.rows, face_rows, 0)
    for j in range(z.rows + 1):
        winds_ref[2 * z.rows + j] = (cy_ref[j] + cy_ref[j + 1]) * (1.0 / 24.0)


def writer(new_ref):
    def write(row, f, at, k, values):
        new_ref[row, f, :, pl.ds(pl.multiple_of(at + (k + 1) * LANE, LANE), LANE)] = values

    return write


def wrap(z, new_ref, rows):
    for j in rows:
        new_ref[j, :, :, 0:LANE] = new_ref[j, :, :, z.lon : z.lon + LANE]
        new_ref[j, :, :, LANE + z.lon :] = new_ref[j, :, :, LANE : 2 * LANE]


def encode_new(z, new_ref, row, out_ref):
    for r in range(2):
        values = new_ref[row + r, :, :, LANE : LANE + z.lon]
        encode_row(values.reshape(2 * z.half, z.lon), out_ref, r * z.code)


def own_kernel(
    z, par_ref, fields_ref, courant_ref, edge_ref, middle_ref, one_ref, two_ref,
    new_ref, winds_ref, code_ref, u_ref, cx_ref, cy_ref,
):
    p, b = par_ref[0], par_ref[3]
    lon, half = z.lon, z.half

    def place(row, in_ref, r):
        values = decode_row(in_ref, r * z.code, lon)
        put_padded(u_ref, (row + r,), values.reshape(2, half, lon), lon)

    keep = pl.multiple_of(p * half, half)
    for r in range(z.rows):
        own = jnp.stack([fields_ref[f, r, pl.ds(keep, half)] for f in range(2)])
        put_padded(u_ref, (z.rows * p + r + 2,), own, lon)
        east, north = own_winds(z, p, courant_ref, r)
        put_padded(cx_ref, (r,), east, lon)
        cy_ref[r + 1] = north
    for r in range(2):
        place(6 * (1 - p) + 2, edge_ref, r)
        place(4 - 2 * p + 2, middle_ref, r)
        place(10 * (1 - b), one_ref, r)
        place(10 * b, two_ref, r)
    at = 2 * z.code
    cy_ref[5 * (1 - p)] = received_winds(z, middle_ref, at)[1]

    def halo(in_ref):
        cy_ref[5 * p] = received_winds(z, in_ref, at)[1]

    pl.when(p + b == 1)(lambda: halo(one_ref))
    pl.when(p + b != 1)(lambda: halo(two_ref))
    faces(z, cx_ref, cy_ref, winds_ref)
    start = z.rows * p
    substep(z, z.rows, 0, lambda j, f, piece: u_ref[start + j, f, :, piece], winds_ref, writer(new_ref))
    encode_new(z, new_ref, 2 * p, code_ref)
    wrap(z, new_ref, range(z.rows))


def other_kernel(
    z, par_ref, courant_ref, edge_ref, middle_ref, last_ref, one_ref, two_ref, u_ref, own_code_ref,
    new_ref, winds_ref, one_out_ref, two_out_ref, cx_ref, cy_ref,
):
    p, b = par_ref[0], par_ref[3]
    at = 2 * z.code

    def place(row, winds):
        put_padded(cx_ref, (row,), winds[0], z.lon)
        cy_ref[row + 1] = winds[1]

    place(3 * (1 - p), received_winds(z, edge_ref, at))
    place(3 * p, received_winds(z, middle_ref, at))
    place(1, received_winds(z, last_ref, 0))
    place(2, received_winds(z, last_ref, z.lon))
    cy_ref[5 * p] = own_winds(z, p, courant_ref, 3 * (1 - p))[1]

    def halo(in_ref):
        cy_ref[5 * (1 - p)] = received_winds(z, in_ref, at)[1]

    pl.when(p + b == 1)(lambda: halo(two_ref))
    pl.when(p + b != 1)(lambda: halo(one_ref))
    faces(z, cx_ref, cy_ref, winds_ref)
    outer = 2 * (1 - p)
    start = z.rows * (1 - p) + outer
    substep(z, 2, outer, lambda j, f, piece: u_ref[start + j, f, :, piece], winds_ref, writer(new_ref))

    def codes(mine_ref, other_ref):
        mine_ref[...] = own_code_ref[...]
        encode_new(z, new_ref, 0, other_ref)

    pl.when(p + b == 1)(lambda: codes(one_out_ref, two_out_ref))
    pl.when(p + b != 1)(lambda: codes(two_out_ref, one_out_ref))
    wrap(z, new_ref, range(2))


def inner_kernel(
    z, par_ref, cut_ref, own_ref, other_ref, u_ref, own_winds_ref, other_winds_ref, table_ref, new_ref, inner_ref
):
    p = par_ref[0]
    own, other = z.rows * p, z.rows * (1 - p)
    for j in range(z.rows):
        new_ref[own + j] = own_ref[j]
    for j in range(2):
        new_ref[other + 2 * (1 - p) + j] = other_ref[j]
    start = other + 2 * p

    def write(row, f, at, k, values):
        writer(new_ref)(start + row, f, at, k, values)

    substep(z, 2, 2 * p, lambda j, f, piece: u_ref[start + j, f, :, piece], other_winds_ref, write)
    wrap(z, new_ref, (start, start + 1))

    def store(row, values):
        put_padded(new_ref, (row,), values, z.lon)

    for part in range(2):
        filter_rows(
            z, cut_ref, par_ref[1], part * z.rows, table_ref,
            lambda row: new_ref[row, :, :, LANE : LANE + z.lon], store,
        )
    for i, (low, base, winds_ref) in enumerate(
        ((2 * p, 2 * (1 - p), own_winds_ref), (2 * (1 - p), 2 * p, other_winds_ref))
    ):

        def keep(row, f, at, k, values):
            inner_ref[2 * i + row, f, :, pl.ds(pl.multiple_of(at + k * LANE, LANE), LANE)] = values

        substep(z, 2, base, lambda j, f, piece: new_ref[low + j, f, :, piece], winds_ref, keep)


def outer_kernel(
    z, parts, par_ref, cut_ref, new_ref, inner_ref, own_winds_ref, other_winds_ref, one_ref, two_ref, table_ref, *refs
):
    out_refs, (u_ref, v_ref) = refs[: 2 * parts], refs[2 * parts :]
    p = par_ref[0]
    outer_half(
        z, parts, 1 - p, 2, par_ref, cut_ref, new_ref, inner_ref, other_winds_ref, one_ref, two_ref, table_ref,
        out_refs[:parts], u_ref, v_ref,
    )
    outer_half(
        z, parts, p, 0, par_ref, cut_ref, new_ref, inner_ref, own_winds_ref, one_ref, two_ref, table_ref,
        out_refs[parts:], u_ref, v_ref,
    )


def outer_half(
    z, parts, side, inner_at, par_ref, cut_ref, new_ref, inner_ref, winds_ref, one_ref, two_ref, table_ref,
    out_refs, u_ref, v_ref,
):
    lon, half = z.lon, z.half
    tall = 2 * half
    base = z.rows * side

    def halo(in_ref):
        for r in range(2):
            values = decode_row(in_ref, r * z.code, lon).reshape(2, half, lon)
            put_padded(u_ref, (4 * side + r,), values, lon)

    first_swap = side + par_ref[3] == 1
    pl.when(first_swap)(lambda: halo(one_ref))
    pl.when(jnp.logical_not(first_swap))(lambda: halo(two_ref))
    for r in range(4):
        u_ref[2 * (1 - side) + r] = new_ref[base + r]
    for r in range(2):
        v_ref[2 * (1 - side) + r] = inner_ref[inner_at + r]

    def write(row, f, at, k, values):
        v_ref[2 * side + row, f, :, pl.ds(pl.multiple_of(at + k * LANE, LANE), LANE)] = values

    substep(z, 2, 2 * side, lambda j, f, piece: u_ref[j, f, :, piece], winds_ref, write)

    def store(row, values):
        v_ref[row] = values

    filter_rows(z, cut_ref, par_ref[1] + base, 0, table_ref, lambda row: v_ref[row], store)
    column = lon // parts
    for b in range(parts):
        at = pl.multiple_of(jnp.bitwise_xor(par_ref[2], b) * column, LANE)
        values = jnp.concatenate(
            [v_ref[r, :, :, pl.ds(at, column)].reshape(tall, column) for r in range(z.rows)], axis=1
        )
        encode_row(values, out_refs[b], 0)


def scale_kernel(at, *refs):
    for i, ref in enumerate(refs[:-1]):
        refs[-1][i] = decoder(ref[:, at : at + LANE])


def column_kernel(z, parts, par_ref, *refs):
    got, (scales_ref, remap_ref, upward_ref, surface_ref, out_ref, geo_ref, x_ref) = refs[: 2 * parts], refs[2 * parts :]
    p, lev = par_ref[0], par_ref[2]
    column = out_ref.shape[-1]
    at = pl.multiple_of(pl.program_id(0) * column, LANE)
    for i, ref in enumerate(got):
        side = p if i < parts else 1 - p
        s = jnp.bitwise_xor(lev, i % parts)
        if i < parts:
            scale = decoder(ref[:, z.rows * column : z.rows * column + LANE])
        else:
            scale = scales_ref[i - parts]
        codes = ref[:, pl.ds(at, column)].astype(jnp.int32).astype(jnp.float32)
        values = codes * tiled(scale, column)
        level = pl.multiple_of(s * z.levels + side * z.half, z.half)
        for f in range(2):
            x_ref[f, pl.ds(level, z.half)] = values[f * z.half : (f + 1) * z.half]
    high, low = split(remap_ref[...])
    remap = jnp.concatenate([high, low, high], axis=1)
    count = remap_ref.shape[0]
    for f in range(2):
        high, low = split(x_ref[f])
        stacked = jnp.concatenate([high, high, low], axis=0)
        left = remap if f == 0 else jnp.concatenate([remap, upward_ref[...].astype(jnp.bfloat16)], axis=0)
        result = jnp.dot(left, stacked, preferred_element_type=jnp.float32)
        out_ref[f, 0] = result[:count]
        if f == 1:
            geo_ref[0] = surface_ref[0] + result[count:] * (count**-0.5)


def whole():
    return pl.BlockSpec(memory_space=pltpu.VMEM)


def scalars():
    return pl.BlockSpec(memory_space=pltpu.SMEM)


def far_memory():
    return pl.BlockSpec(memory_space=pltpu.HBM)


def params(limit=VMEM_LIMIT):
    return pltpu.CompilerParams(vmem_limit_bytes=limit)


def cost(flops=1000, data=1000):
    return pl.CostEstimate(flops=flops, bytes_accessed=data, transcendentals=0)


def shards(fields, courant, cutoffs, surface, remap_weights):
    _, rows, levels, lon = fields.shape
    z = Sizes(rows, levels, lon)
    lats, parts = lax.axis_size("lat"), lax.axis_size("lev")
    me = lax.axis_index("lat")
    parity = me % 2
    lev = lax.axis_index("lev")
    place = jnp.stack([parity, (me - parity) * rows, lev, (me // 2) % 2]).astype(jnp.int32)
    tall = 2 * z.half
    i16, f32 = jnp.int16, jnp.float32
    swap = [(i, i ^ 1) for i in range(lats)]
    ones, twos = [
        [pair for i in range(start, lats - 2, 4) for s in range(2) for pair in ((i + s, i + s + 2), (i + s + 2, i + s))]
        for start in (0, 2)
    ]

    def shape(*dims):
        return jax.ShapeDtypeStruct(dims, f32)

    def codes(*dims):
        return jax.ShapeDtypeStruct(dims, i16)

    edge = pl.pallas_call(
        functools.partial(edge_kernel, z),
        name="edge",
        in_specs=[far_memory(), far_memory()],
        out_specs=whole(),
        out_shape=codes(tall, z.edge),
        scratch_shapes=[
            pltpu.VMEM((2, tall, lon), f32),
            pltpu.VMEM((2, levels, lon), courant.dtype),
            pltpu.SemaphoreType.DMA((6,)),
        ],
        compiler_params=params(VMEM_MOST),
        cost_estimate=cost(),
    )(fields, courant)
    edge = lax.ppermute(edge, "lat", swap)
    middle, last, own = pl.pallas_call(
        functools.partial(rest_kernel, z),
        name="rest",
        in_specs=[scalars(), whole(), whole()],
        out_specs=[whole()] * 3,
        out_shape=[codes(tall, z.edge), codes(tall, 2 * lon), codes(tall, z.edge)],
        compiler_params=params(),
        cost_estimate=cost(),
    )(place, fields, courant)
    middle = lax.ppermute(middle, "lat", swap)
    last = lax.ppermute(last, "lat", swap)
    one, two = pl.pallas_call(
        pick_kernel,
        name="pick",
        in_specs=[scalars(), whole(), whole()],
        out_specs=[whole()] * 2,
        out_shape=[codes(tall, z.edge)] * 2,
        compiler_params=params(),
        cost_estimate=cost(),
    )(place, own, edge)
    one = lax.ppermute(one, "lat", ones)
    two = lax.ppermute(two, "lat", twos)

    half_scratch = [
        pltpu.VMEM((z.rows, z.half, z.pad), f32),
        pltpu.VMEM((z.rows + 2, z.half, lon), f32),
    ]
    mine, own_winds, own_code, u = pl.pallas_call(
        functools.partial(own_kernel, z),
        name="own",
        in_specs=[scalars()] + [whole()] * 6,
        out_specs=[whole()] * 4,
        out_shape=[
            shape(z.rows, 2, z.half, z.pad),
            shape(3 * z.rows + 1, z.half, lon),
            codes(tall, 2 * z.code),
            shape(z.band + 4, 2, z.half, z.pad),
        ],
        scratch_shapes=half_scratch,
        compiler_params=params(),
        cost_estimate=cost(),
    )(place, fields, courant, edge, middle, one, two)
    other, other_winds, one_code, two_code = pl.pallas_call(
        functools.partial(other_kernel, z),
        name="other",
        in_specs=[scalars()] + [whole()] * 8,
        out_specs=[whole()] * 4,
        out_shape=[
            shape(2, 2, z.half, z.pad),
            shape(3 * z.rows + 1, z.half, lon),
            codes(tall, 2 * z.code),
            codes(tall, 2 * z.code),
        ],
        scratch_shapes=half_scratch,
        compiler_params=params(),
        cost_estimate=cost(),
    )(place, courant, edge, middle, last, one, two, u, own_code)
    one = lax.ppermute(one_code, "lat", ones)
    two = lax.ppermute(two_code, "lat", twos)

    tables = jnp.asarray(filter_tables(lon))
    new, inner = pl.pallas_call(
        functools.partial(inner_kernel, z),
        name="inner",
        in_specs=[scalars(), scalars()] + [whole()] * 6,
        out_specs=[whole()] * 2,
        out_shape=[shape(z.band, 2, z.half, z.pad), shape(z.rows, 2, z.half, lon)],
        compiler_params=params(),
        cost_estimate=cost(),
    )(place, cutoffs, mine, other, u, own_winds, other_winds, tables)

    column = lon // parts
    blocks = pl.pallas_call(
        functools.partial(outer_kernel, z, parts),
        name="outer",
        in_specs=[scalars(), scalars()] + [whole()] * 7,
        out_specs=[whole()] * (2 * parts),
        out_shape=[codes(tall, rows * column + LANE)] * (2 * parts),
        scratch_shapes=[
            pltpu.VMEM((6, 2, z.half, z.pad), f32),
            pltpu.VMEM((z.rows, 2, z.half, lon), f32),
        ],
        compiler_params=params(),
        cost_estimate=cost(),
    )(place, cutoffs, new, inner, own_winds, other_winds, one, two, tables)
    got = []
    for b, block in enumerate(blocks[:parts]):
        pairs = [
            (i * parts + j, (i ^ 1) * parts + (j ^ b)) for i in range(lats) for j in range(parts)
        ]
        got.append(lax.ppermute(block, ("lat", "lev"), pairs))
    scales = pl.pallas_call(
        functools.partial(scale_kernel, rows * column),
        name="scales",
        in_specs=[whole()] * parts,
        out_specs=whole(),
        out_shape=shape(parts, tall, LANE),
        compiler_params=params(),
        cost_estimate=cost(),
    )(*got)
    for b, block in enumerate(blocks[parts:]):
        pairs = [(j, j ^ b) for j in range(parts)]
        got.insert(b, lax.ppermute(block, "lev", pairs) if b else block)

    count = remap_weights.shape[0]
    upward = np.triu(np.ones((count, count), np.float32), 1) + 0.5 * np.eye(count, dtype=np.float32)
    upward = jnp.asarray(np.concatenate([upward, 0.0 * upward, upward], axis=1))
    surface = lax.dynamic_slice_in_dim(surface, lev * column, column, 1)
    remapped, geopotential = pl.pallas_call(
        functools.partial(column_kernel, z, parts),
        name="columns",
        grid=(rows,),
        in_specs=[scalars()]
        + [whole()] * (len(got) + 1)
        + [
            pl.BlockSpec(remap_weights.shape, lambda r: (0, 0)),
            pl.BlockSpec(upward.shape, lambda r: (0, 0)),
            pl.BlockSpec((1, 1, column), lambda r: (r, 0, 0)),
        ],
        out_specs=[
            pl.BlockSpec((2, 1, count, column), lambda r: (0, r, 0, 0)),
            pl.BlockSpec((1, count, column), lambda r: (r, 0, 0)),
        ],
        out_shape=[shape(2, rows, count, column), shape(rows, count, column)],
        scratch_shapes=[pltpu.VMEM((2, count, column), f32)],
        compiler_params=params(),
        cost_estimate=cost(),
    )(place, *got, scales, remap_weights, upward, surface[:, None, :])
    return remapped, geopotential


def with_halo(shard, width):
    size, length = lax.axis_size("lat"), shard.shape[1]
    up = [(i, (i + 1) % size) for i in range(size - 1)]
    down = [(j, i) for i, j in up]
    before = lax.ppermute(lax.slice_in_dim(shard, length - width, length, axis=1), "lat", up)
    after = lax.ppermute(lax.slice_in_dim(shard, 0, width, axis=1), "lat", down)
    return jnp.concatenate([before, shard, after], axis=1)


def plain_shards(fields, courant, cutoffs, surface, remap_weights):
    _, rows, _, lon = fields.shape
    exact = lax.Precision.HIGHEST
    cut = lax.dynamic_slice_in_dim(cutoffs, lax.axis_index("lat") * rows, rows)
    waves = np.arange(KMAX)
    angle = (np.arange(lon)[:, None] * waves[None, :] % lon) * (2.0 * math.pi / lon)
    table = jnp.asarray(np.concatenate([np.cos(angle), np.sin(angle)], axis=1).astype(np.float32))
    number = jnp.asarray(np.concatenate([waves, waves]).astype(np.int32))
    weight = jnp.where(number[None] <= cut[:, None], jnp.where(number == 0, 1.0, 2.0)[None] / lon, 0.0)
    flagged = cut < lon // 2

    def smooth(values):
        wave = jnp.einsum("frln,nk->frlk", values, table, precision=exact) * weight[None, :, None]
        low = jnp.einsum("frlk,nk->frln", wave, table, precision=exact)
        return jnp.where(flagged[None, :, None, None], low, values)

    winds = with_halo(courant, 1).astype(jnp.float32)
    east, north = winds[0, 1:-1], winds[1]
    face_x = (east + jnp.roll(east, -1, -1)) / 24.0
    face_y = (north[:-1] + north[1:]) / 24.0
    u = fields
    for _ in range(2):
        wide = with_halo(u, 2)
        pair = u + jnp.roll(u, -1, -1)
        fx = face_x * (8.0 * pair - (jnp.roll(pair, 1, -1) + jnp.roll(pair, -1, -1)))
        pair = wide[:, :-1] + wide[:, 1:]
        fy = face_y * (8.0 * pair[:, 1:-1] - (pair[:, :-2] + pair[:, 2:]))
        u = u - (fx - jnp.roll(fx, 1, -1)) - (fy[:, 1:] - fy[:, :-1])
        u = lax.cond(jnp.any(flagged), smooth, lambda values: values, u)
    columns = lax.all_to_all(u, "lev", split_axis=3, concat_axis=2, tiled=True)
    remapped = jnp.einsum("pk,fjkn->fjpn", remap_weights, columns, precision=exact)
    count = remap_weights.shape[0]
    upward = np.triu(np.ones((count, count), np.float32), 1) + 0.5 * np.eye(count, dtype=np.float32)
    upward = jnp.einsum("kl,jln->jkn", jnp.asarray(upward), columns[1], precision=exact)
    width = lon // lax.axis_size("lev")
    mine = lax.dynamic_slice_in_dim(surface, lax.axis_index("lev") * width, width, 1)
    return remapped, mine[:, None] + count**-0.5 * upward


def solution(mesh):
    def program(fields, courant, cutoffs, surface, remap_weights):
        lats, parts = mesh.shape["lat"], mesh.shape["lev"]
        rows, levels = fields.shape[1] // lats, fields.shape[2] // parts
        polar = fields.shape[1] // 8
        paired = (
            lats % 2 == 0
            and rows == 4
            and levels % 16 == 0
            and polar <= 2 * rows - 2
            and fields.shape[3] % (LANE * parts) == 0
            and parts & (parts - 1) == 0
            and fields.shape[3] % (4 * KMAX) == 0
        )
        return jax.shard_map(
            shards if paired else plain_shards,
            mesh=mesh,
            in_specs=(
                P(None, "lat", "lev", None),
                P(None, "lat", "lev", None),
                P(),
                P("lat", None),
                P(),
            ),
            out_specs=(P(None, "lat", None, "lev"), P("lat", None, "lev")),
            check_vma=False,
        )(fields, courant, cutoffs, surface, remap_weights)

    return program
```

```python
import functools
import math

import jax
import jax.numpy as jnp
import ml_dtypes
import numpy as np
from jax import lax
from jax.experimental import pallas as pl
from jax.experimental.pallas import tpu as pltpu
from jax.sharding import PartitionSpec as P

KMAX = 128
LANE = 128
TOP = 32767.0
STEPS = 256.0
TINY = 2.0**-100
WIND = 81920.0
ROUND = 1.5 * 2.0**23
VMEM_LIMIT = 12 * 2**20
VMEM_MOST = 63 * 2**20 + 2**19


def rounded(values):
    return ((values + ROUND) - ROUND).astype(jnp.int32).astype(jnp.int16)


def lane_max(values):
    chunks = [jnp.abs(values[:, i : i + LANE]) for i in range(0, values.shape[1], LANE)]
    while len(chunks) > 1:
        pairs = [jnp.maximum(a, b) for a, b in zip(chunks[0::2], chunks[1::2])]
        chunks = pairs + chunks[2 * len(pairs) :]
    return chunks[0]


def tiled(tile, width):
    return jnp.concatenate([tile] * (width // LANE), axis=1)


def scale_code(largest):
    return jnp.ceil(jnp.log2(jnp.maximum(largest, TINY)) * STEPS)


def encoder(code):
    return TOP / jnp.exp2(code * (1.0 / STEPS))


def decoder(code16):
    code = code16.astype(jnp.int32).astype(jnp.float32)
    return jnp.exp2(code * (1.0 / STEPS)) * (1.0 / TOP)


def encode_row(values, out_ref, at):
    width = values.shape[1]
    code = scale_code(lane_max(values))
    out_ref[:, at : at + width] = rounded(values * tiled(encoder(code), width))
    out_ref[:, at + width : at + width + LANE] = code.astype(jnp.int32).astype(jnp.int16)


def decode_row(in_ref, at, width):
    scale = decoder(in_ref[:, at + width : at + width + LANE])
    values = in_ref[:, at : at + width].astype(jnp.int32).astype(jnp.float32)
    return values * tiled(scale, width)


def wind_codes(east, north):
    return rounded(jnp.concatenate([east, north], axis=0) * WIND)


class Sizes:
    def __init__(self, rows, levels, lon):
        self.rows, self.levels, self.lon = rows, levels, lon
        self.half = levels // 2
        self.band = 2 * rows
        self.pad = lon + 2 * LANE
        self.code = lon + LANE
        self.edge = 2 * self.code + lon


def put_padded(ref, index, values, lon):
    ref[index + (Ellipsis, slice(LANE, LANE + lon))] = values
    ref[index + (Ellipsis, slice(0, LANE))] = values[..., lon - LANE :]
    ref[index + (Ellipsis, slice(LANE + lon, 2 * LANE + lon))] = values[..., :LANE]


def wind_row(z, wind, upper):
    halves = []
    for k in range(2):
        both = wind[k].astype(jnp.float32)
        halves.append(jnp.where(upper == 1, both[z.half :], both[: z.half]))
    return wind_codes(*halves)


def edge_kernel(z, fields_ref, courant_ref, edge_ref, rows_ref, wind_ref, sems):
    p = lax.rem(lax.axis_index("lat"), 2)
    give = pl.multiple_of((1 - p) * z.half, z.half)
    copies = [
        pltpu.make_async_copy(
            fields_ref.at[f, 2 * p + r, pl.ds(give, z.half)],
            rows_ref.at[r, pl.ds(f * z.half, z.half)],
            sems.at[2 * r + f],
        )
        for r in range(2)
        for f in range(2)
    ]
    copies += [
        pltpu.make_async_copy(courant_ref.at[k, 3 * p], wind_ref.at[k], sems.at[4 + k])
        for k in range(2)
    ]
    for copy in copies:
        copy.start()
    for r in range(2):
        copies[2 * r].wait()
        copies[2 * r + 1].wait()
        encode_row(rows_ref[r], edge_ref, r * z.code)
    copies[4].wait()
    copies[5].wait()
    edge_ref[:, 2 * z.code :] = wind_row(z, wind_ref, 1 - p)


def rest_kernel(z, par_ref, fields_ref, courant_ref, middle_ref, last_ref, own_ref):
    p = par_ref[0]
    keep = pl.multiple_of(p * z.half, z.half)
    give = pl.multiple_of((1 - p) * z.half, z.half)

    def field_row(row, start):
        return jnp.concatenate([fields_ref[f, row, pl.ds(start, z.half)] for f in range(2)], axis=0)

    def winds(row, upper):
        return wind_row(z, [courant_ref[k, row] for k in range(2)], upper)

    edge, inner = 2 * p, 2 * (1 - p)
    at = 2 * z.code
    for r in range(2):
        encode_row(field_row(inner + r, give), middle_ref, r * z.code)
        encode_row(field_row(edge + r, keep), own_ref, r * z.code)
        last_ref[:, r * z.lon : (r + 1) * z.lon] = winds(1 + r, 1 - p)
    middle_ref[:, at : at + z.lon] = winds(3 * (1 - p), 1 - p)
    own_ref[:, at : at + z.lon] = winds(3 * p, p)


def pick_kernel(par_ref, own_ref, edge_ref, one_ref, two_ref):
    straight = par_ref[0] + par_ref[3] == 1

    def put(a_ref, b_ref):
        one_ref[...] = a_ref[...]
        two_ref[...] = b_ref[...]

    pl.when(straight)(lambda: put(own_ref, edge_ref))
    pl.when(jnp.logical_not(straight))(lambda: put(edge_ref, own_ref))


def shifted(pieces, shift, lanes):
    turned = [pltpu.roll(v, (-shift) % LANE, 1) for v in pieces]
    if shift > 0:
        return [jnp.where(lanes < LANE - shift, a, b) for a, b in zip(turned[1:-1], turned[2:])]
    return [jnp.where(lanes < -shift, a, b) for a, b in zip(turned[:-2], turned[1:-1])]


def substep(z, count_rows, base, row_of, winds_ref, write):
    count = next(n for n in (4, 3, 2, 1) if z.lon % (n * LANE) == 0)
    width = count * LANE
    lanes = lax.broadcasted_iota(jnp.int32, (z.half, LANE), 1)

    def part(at):
        def piece(k):
            return pl.ds(at + k * LANE, LANE)

        def row(j, f):
            return [row_of(j, f, piece(k + 1)) for k in range(count)]

        def start(j, f):
            pieces = [row_of(j + 2, f, piece(k)) for k in range(count + 2)]
            return [shifted(pieces, s, lanes) for s in (-2, -1, 1, 2)]

        def lon_part(j, u, moved):
            out = []
            for k in range(count):
                m2, m1, p1, p2 = (m[k] for m in moved)
                east = 7.0 * (u[k] + p1) - (m1 + p2)
                west = 7.0 * (m1 + u[k]) - (m2 + p1)
                east = winds_ref[base + j, :, piece(k)] * east
                out.append(east - winds_ref[z.rows + base + j, :, piece(k)] * west)
            return out

        for f in range(2):
            rows = [row(j, f) for j in range(4)]
            sums = [[a + b for a, b in zip(rows[j], rows[j + 1])] for j in range(3)]
            flux = None
            moved = start(0, f)
            for j in range(count_rows + 1):
                later = start(j, f) if 0 < j < count_rows else None
                new = [
                    winds_ref[2 * z.rows + base + j, :, piece(k)] * (8.0 * sums[1][k] - (sums[0][k] + sums[2][k]))
                    for k in range(count)
                ]
                if j > 0:
                    u = rows[1]
                    change = lon_part(j - 1, u, moved)
                    for k in range(count):
                        write(j - 1, f, at, k, u[k] - change[k] - (new[k] - flux[k]))
                    moved = later
                flux = new
                if j < count_rows:
                    above = row(j + 4, f)
                    rows = rows[1:] + [above]
                    sums = sums[1:] + [[a + b for a, b in zip(rows[2], rows[3])]]

    for i in range(z.lon // width):
        part(i * width)


def filter_tables(lon):
    half = lon // 2
    points = np.arange(half)
    forward, back = [], []
    for parity in range(2):
        waves = np.arange(parity, KMAX, 2)
        angle = (points[:, None] * waves[None, :] % lon) * (2.0 * math.pi / lon)
        table = np.concatenate([np.cos(angle), np.sin(angle)], axis=1).astype(np.float32)
        high = table.astype(ml_dtypes.bfloat16)
        low = (table - high.astype(np.float32)).astype(ml_dtypes.bfloat16)
        forward.append(np.concatenate([high, low], axis=1))
        turned = np.concatenate([high.T, low.T], axis=0)
        back.append(np.concatenate(np.split(turned, half // (2 * KMAX), axis=1), axis=0))
    return np.stack(forward + back)


def split(values):
    high = values.astype(jnp.bfloat16)
    return high, (values - high.astype(jnp.float32)).astype(jnp.bfloat16)


def low_pass(z, rows, cuts, table_ref):
    half = z.lon // 2
    count = len(rows)
    tall = 2 * z.half
    total = count * tall
    flat = [row.reshape(tall, z.lon) for row in rows]
    folded = []
    for parity in range(2):
        parts = [
            row[:, :half] + row[:, half:] if parity == 0 else row[:, :half] - row[:, half:]
            for row in flat
        ]
        high, low = split(jnp.concatenate(parts, axis=0))
        both = jnp.concatenate([high, low], axis=0)
        got = jnp.dot(both, table_ref[parity], preferred_element_type=jnp.float32)
        wave = got[:total, :KMAX] + got[:total, KMAX:] + (got[total:, :KMAX] + got[total:, KMAX:])
        number = 2 * (lax.broadcasted_iota(jnp.int32, (tall, KMAX), 1) % (KMAX // 2)) + parity
        doubled = jnp.where(number == 0, 1.0, 2.0) * (1.0 / z.lon)
        weight = jnp.concatenate([jnp.where(number <= cut, doubled, 0.0) for cut in cuts], axis=0)
        high, low = split(wave * weight)
        both = jnp.concatenate(
            [jnp.concatenate([high, high], axis=1), jnp.concatenate([low, low], axis=1)], axis=0
        )
        got = []
        for at in range(0, half, 2 * KMAX):
            block = table_ref[2 + parity, at : at + 2 * KMAX]
            sums = jnp.dot(both, block, preferred_element_type=jnp.float32)
            got.append(sums[:total] + sums[total:])
        folded.append(jnp.concatenate(got, axis=1))
    left, right = folded[0] + folded[1], folded[0] - folded[1]
    smooth = jnp.concatenate([left, right], axis=1)
    return [smooth[i * tall : (i + 1) * tall].reshape(2, z.half, z.lon) for i in range(count)]


def filter_rows(z, cut_ref, first_row, start, table_ref, load, store):
    nyquist = z.lon // 2
    cuts = [cut_ref[first_row + start + r] for r in range(z.rows)]
    some = functools.reduce(jnp.logical_or, [cut < nyquist for cut in cuts])

    @pl.when(some)
    def _():
        smooth = low_pass(z, [load(start + r) for r in range(z.rows)], cuts, table_ref)
        for r in range(z.rows):

            @pl.when(cuts[r] < nyquist)
            def _():
                store(start + r, smooth[r])


def received_winds(z, in_ref, at):
    values = in_ref[:, at : at + z.lon].astype(jnp.int32).astype(jnp.float32) * (1.0 / WIND)
    return values[: z.half], values[z.half :]


def own_winds(z, p, courant_ref, row):
    got = []
    for k in range(2):
        wind = courant_ref[k, row].astype(jnp.float32)
        got.append(jnp.where(p == 1, wind[z.half :], wind[: z.half]))
    return got


def faces(z, cx_ref, cy_ref, winds_ref):
    lanes = lax.broadcasted_iota(jnp.int32, (z.half, LANE), 1)
    for j in range(z.rows):
        pieces = [cx_ref[j, :, i : i + LANE] * (1.0 / 24.0) for i in range(0, z.pad, LANE)]
        for out, shift in ((j, 1), (z.rows + j, -1)):
            for k, moved in enumerate(shifted(pieces, shift, lanes)):
                winds_ref[out, :, k * LANE : (k + 1) * LANE] = pieces[k + 1] + moved
    for j in range(z.rows + 1):
        winds_ref[2 * z.rows + j] = (cy_ref[j] + cy_ref[j + 1]) * (1.0 / 24.0)


def writer(new_ref):
    def write(row, f, at, k, values):
        new_ref[row, f, :, pl.ds(at + (k + 1) * LANE, LANE)] = values

    return write


def wrap(z, new_ref, rows):
    for j in rows:
        new_ref[j, :, :, 0:LANE] = new_ref[j, :, :, z.lon : z.lon + LANE]
        new_ref[j, :, :, LANE + z.lon :] = new_ref[j, :, :, LANE : 2 * LANE]


def encode_new(z, new_ref, row, out_ref):
    for r in range(2):
        values = new_ref[row + r, :, :, LANE : LANE + z.lon]
        encode_row(values.reshape(2 * z.half, z.lon), out_ref, r * z.code)


def own_kernel(
    z, par_ref, fields_ref, courant_ref, edge_ref, middle_ref, one_ref, two_ref,
    new_ref, winds_ref, code_ref, u_ref, cx_ref, cy_ref,
):
    p, b = par_ref[0], par_ref[3]
    lon, half = z.lon, z.half

    def place(row, in_ref, r):
        values = decode_row(in_ref, r * z.code, lon)
        put_padded(u_ref, (row + r,), values.reshape(2, half, lon), lon)

    keep = pl.multiple_of(p * half, half)
    for r in range(z.rows):
        own = jnp.stack([fields_ref[f, r, pl.ds(keep, half)] for f in range(2)])
        put_padded(u_ref, (z.rows * p + r + 2,), own, lon)
        east, north = own_winds(z, p, courant_ref, r)
        put_padded(cx_ref, (r,), east, lon)
        cy_ref[r + 1] = north
    for r in range(2):
        place(6 * (1 - p) + 2, edge_ref, r)
        place(4 - 2 * p + 2, middle_ref, r)
        place(10 * (1 - b), one_ref, r)
        place(10 * b, two_ref, r)
    at = 2 * z.code
    cy_ref[5 * (1 - p)] = received_winds(z, middle_ref, at)[1]

    def halo(in_ref):
        cy_ref[5 * p] = received_winds(z, in_ref, at)[1]

    pl.when(p + b == 1)(lambda: halo(one_ref))
    pl.when(p + b != 1)(lambda: halo(two_ref))
    faces(z, cx_ref, cy_ref, winds_ref)
    start = z.rows * p
    substep(z, z.rows, 0, lambda j, f, piece: u_ref[start + j, f, :, piece], winds_ref, writer(new_ref))
    encode_new(z, new_ref, 2 * p, code_ref)
    wrap(z, new_ref, range(z.rows))


def other_kernel(
    z, par_ref, courant_ref, edge_ref, middle_ref, last_ref, one_ref, two_ref, u_ref, own_code_ref,
    new_ref, winds_ref, one_out_ref, two_out_ref, cx_ref, cy_ref,
):
    p, b = par_ref[0], par_ref[3]
    at = 2 * z.code

    def place(row, winds):
        put_padded(cx_ref, (row,), winds[0], z.lon)
        cy_ref[row + 1] = winds[1]

    place(3 * (1 - p), received_winds(z, edge_ref, at))
    place(3 * p, received_winds(z, middle_ref, at))
    place(1, received_winds(z, last_ref, 0))
    place(2, received_winds(z, last_ref, z.lon))
    cy_ref[5 * p] = own_winds(z, p, courant_ref, 3 * (1 - p))[1]

    def halo(in_ref):
        cy_ref[5 * (1 - p)] = received_winds(z, in_ref, at)[1]

    pl.when(p + b == 1)(lambda: halo(two_ref))
    pl.when(p + b != 1)(lambda: halo(one_ref))
    faces(z, cx_ref, cy_ref, winds_ref)
    outer = 2 * (1 - p)
    start = z.rows * (1 - p) + outer
    substep(z, 2, outer, lambda j, f, piece: u_ref[start + j, f, :, piece], winds_ref, writer(new_ref))

    def codes(mine_ref, other_ref):
        mine_ref[...] = own_code_ref[...]
        encode_new(z, new_ref, 0, other_ref)

    pl.when(p + b == 1)(lambda: codes(one_out_ref, two_out_ref))
    pl.when(p + b != 1)(lambda: codes(two_out_ref, one_out_ref))
    wrap(z, new_ref, range(2))


def inner_kernel(
    z, par_ref, cut_ref, own_ref, other_ref, u_ref, own_winds_ref, other_winds_ref, table_ref, new_ref, inner_ref
):
    p = par_ref[0]
    own, other = z.rows * p, z.rows * (1 - p)
    for j in range(z.rows):
        new_ref[own + j] = own_ref[j]
    for j in range(2):
        new_ref[other + 2 * (1 - p) + j] = other_ref[j]
    start = other + 2 * p

    def write(row, f, at, k, values):
        writer(new_ref)(start + row, f, at, k, values)

    substep(z, 2, 2 * p, lambda j, f, piece: u_ref[start + j, f, :, piece], other_winds_ref, write)
    wrap(z, new_ref, (start, start + 1))

    def store(row, values):
        put_padded(new_ref, (row,), values, z.lon)

    for part in range(2):
        filter_rows(
            z, cut_ref, par_ref[1], part * z.rows, table_ref,
            lambda row: new_ref[row, :, :, LANE : LANE + z.lon], store,
        )
    for i, (low, base, winds_ref) in enumerate(
        ((2 * p, 2 * (1 - p), own_winds_ref), (2 * (1 - p), 2 * p, other_winds_ref))
    ):

        def keep(row, f, at, k, values):
            inner_ref[2 * i + row, f, :, pl.ds(at + k * LANE, LANE)] = values

        substep(z, 2, base, lambda j, f, piece: new_ref[low + j, f, :, piece], winds_ref, keep)


def outer_kernel(
    z, parts, par_ref, cut_ref, new_ref, inner_ref, own_winds_ref, other_winds_ref, one_ref, two_ref, table_ref, *refs
):
    out_refs, (u_ref, v_ref) = refs[: 2 * parts], refs[2 * parts :]
    p = par_ref[0]
    outer_half(
        z, parts, 1 - p, 2, par_ref, cut_ref, new_ref, inner_ref, other_winds_ref, one_ref, two_ref, table_ref,
        out_refs[:parts], u_ref, v_ref,
    )
    outer_half(
        z, parts, p, 0, par_ref, cut_ref, new_ref, inner_ref, own_winds_ref, one_ref, two_ref, table_ref,
        out_refs[parts:], u_ref, v_ref,
    )


def outer_half(
    z, parts, side, inner_at, par_ref, cut_ref, new_ref, inner_ref, winds_ref, one_ref, two_ref, table_ref,
    out_refs, u_ref, v_ref,
):
    lon, half = z.lon, z.half
    tall = 2 * half
    base = z.rows * side

    def halo(in_ref):
        for r in range(2):
            values = decode_row(in_ref, r * z.code, lon).reshape(2, half, lon)
            put_padded(u_ref, (4 * side + r,), values, lon)

    first_swap = side + par_ref[3] == 1
    pl.when(first_swap)(lambda: halo(one_ref))
    pl.when(jnp.logical_not(first_swap))(lambda: halo(two_ref))
    for r in range(4):
        u_ref[2 * (1 - side) + r] = new_ref[base + r]
    for r in range(2):
        v_ref[2 * (1 - side) + r] = inner_ref[inner_at + r]

    def write(row, f, at, k, values):
        v_ref[2 * side + row, f, :, pl.ds(at + k * LANE, LANE)] = values

    substep(z, 2, 2 * side, lambda j, f, piece: u_ref[j, f, :, piece], winds_ref, write)

    def store(row, values):
        v_ref[row] = values

    filter_rows(z, cut_ref, par_ref[1] + base, 0, table_ref, lambda row: v_ref[row], store)
    column = lon // parts
    for b in range(parts):
        at = pl.multiple_of(jnp.bitwise_xor(par_ref[2], b) * column, LANE)
        values = jnp.concatenate(
            [v_ref[r, :, :, pl.ds(at, column)].reshape(tall, column) for r in range(z.rows)], axis=1
        )
        encode_row(values, out_refs[b], 0)


def scale_kernel(at, *refs):
    for i, ref in enumerate(refs[:-1]):
        refs[-1][i] = decoder(ref[:, at : at + LANE])


def column_kernel(z, parts, far, par_ref, *refs):
    got, (scales_ref, remap_ref, upward_ref, surface_ref, out_ref, geo_ref, x_ref) = refs[: 2 * parts], refs[2 * parts :]
    p, lev = par_ref[0], par_ref[2]
    column = out_ref.shape[-1]
    at = pl.multiple_of(pl.program_id(0) * column, LANE)
    for i, ref in enumerate(got):
        side = 1 - p if i < parts else p
        s = jnp.bitwise_xor(lev, i % parts)
        if i in far:
            scale = scales_ref[far.index(i)]
        else:
            scale = decoder(ref[:, z.rows * column : z.rows * column + LANE])
        codes = ref[:, pl.ds(at, column)].astype(jnp.int32).astype(jnp.float32)
        values = codes * tiled(scale, column)
        level = pl.multiple_of(s * z.levels + side * z.half, z.half)
        for f in range(2):
            x_ref[f, pl.ds(level, z.half)] = values[f * z.half : (f + 1) * z.half]
    high, low = split(remap_ref[...])
    remap = jnp.concatenate([high, low, high], axis=1)
    count = remap_ref.shape[0]
    for f in range(2):
        high, low = split(x_ref[f])
        stacked = jnp.concatenate([high, high, low], axis=0)
        left = remap if f == 0 else jnp.concatenate([remap, upward_ref[...].astype(jnp.bfloat16)], axis=0)
        result = jnp.dot(left, stacked, preferred_element_type=jnp.float32)
        out_ref[f, 0] = result[:count]
        if f == 1:
            geo_ref[0] = surface_ref[0] + result[count:] * (count**-0.5)


def whole():
    return pl.BlockSpec(memory_space=pltpu.VMEM)


def scalars():
    return pl.BlockSpec(memory_space=pltpu.SMEM)


def far_memory():
    return pl.BlockSpec(memory_space=pltpu.HBM)


def params(limit=VMEM_LIMIT):
    return pltpu.CompilerParams(vmem_limit_bytes=limit)


def cost(flops=1000, data=1000):
    return pl.CostEstimate(flops=flops, bytes_accessed=data, transcendentals=0)


def shards(fields, courant, cutoffs, surface, remap_weights):
    _, rows, levels, lon = fields.shape
    z = Sizes(rows, levels, lon)
    lats, parts = lax.axis_size("lat"), lax.axis_size("lev")
    me = lax.axis_index("lat")
    parity = me % 2
    lev = lax.axis_index("lev")
    place = jnp.stack([parity, (me - parity) * rows, lev, (me // 2) % 2]).astype(jnp.int32)
    tall = 2 * z.half
    i16, f32 = jnp.int16, jnp.float32
    swap = [(i, i ^ 1) for i in range(lats)]
    ones, twos = [
        [pair for i in range(start, lats - 2, 4) for s in range(2) for pair in ((i + s, i + s + 2), (i + s + 2, i + s))]
        for start in (0, 2)
    ]

    def shape(*dims):
        return jax.ShapeDtypeStruct(dims, f32)

    def codes(*dims):
        return jax.ShapeDtypeStruct(dims, i16)

    edge = pl.pallas_call(
        functools.partial(edge_kernel, z),
        name="edge",
        in_specs=[far_memory(), far_memory()],
        out_specs=whole(),
        out_shape=codes(tall, z.edge),
        scratch_shapes=[
            pltpu.VMEM((2, tall, lon), f32),
            pltpu.VMEM((2, levels, lon), courant.dtype),
            pltpu.SemaphoreType.DMA((6,)),
        ],
        compiler_params=params(VMEM_MOST),
        cost_estimate=cost(),
    )(fields, courant)
    edge = lax.ppermute(edge, "lat", swap)
    middle, last, own = pl.pallas_call(
        functools.partial(rest_kernel, z),
        name="rest",
        in_specs=[scalars(), whole(), whole()],
        out_specs=[whole()] * 3,
        out_shape=[codes(tall, z.edge), codes(tall, 2 * lon), codes(tall, z.edge)],
        compiler_params=params(),
        cost_estimate=cost(),
    )(place, fields, courant)
    middle = lax.ppermute(middle, "lat", swap)
    last = lax.ppermute(last, "lat", swap)
    one, two = pl.pallas_call(
        pick_kernel,
        name="pick",
        in_specs=[scalars(), whole(), whole()],
        out_specs=[whole()] * 2,
        out_shape=[codes(tall, z.edge)] * 2,
        compiler_params=params(),
        cost_estimate=cost(),
    )(place, own, edge)
    one = lax.ppermute(one, "lat", ones)
    two = lax.ppermute(two, "lat", twos)

    half_scratch = [
        pltpu.VMEM((z.rows, z.half, z.pad), f32),
        pltpu.VMEM((z.rows + 2, z.half, lon), f32),
    ]
    mine, own_winds, own_code, u = pl.pallas_call(
        functools.partial(own_kernel, z),
        name="own",
        in_specs=[scalars()] + [whole()] * 6,
        out_specs=[whole()] * 4,
        out_shape=[
            shape(z.rows, 2, z.half, z.pad),
            shape(3 * z.rows + 1, z.half, lon),
            codes(tall, 2 * z.code),
            shape(z.band + 4, 2, z.half, z.pad),
        ],
        scratch_shapes=half_scratch,
        compiler_params=params(),
        cost_estimate=cost(),
    )(place, fields, courant, edge, middle, one, two)
    other, other_winds, one_code, two_code = pl.pallas_call(
        functools.partial(other_kernel, z),
        name="other",
        in_specs=[scalars()] + [whole()] * 8,
        out_specs=[whole()] * 4,
        out_shape=[
            shape(2, 2, z.half, z.pad),
            shape(3 * z.rows + 1, z.half, lon),
            codes(tall, 2 * z.code),
            codes(tall, 2 * z.code),
        ],
        scratch_shapes=half_scratch,
        compiler_params=params(),
        cost_estimate=cost(),
    )(place, courant, edge, middle, last, one, two, u, own_code)
    one = lax.ppermute(one_code, "lat", ones)
    two = lax.ppermute(two_code, "lat", twos)

    tables = jnp.asarray(filter_tables(lon))
    new, inner = pl.pallas_call(
        functools.partial(inner_kernel, z),
        name="inner",
        in_specs=[scalars(), scalars()] + [whole()] * 6,
        out_specs=[whole()] * 2,
        out_shape=[shape(z.band, 2, z.half, z.pad), shape(z.rows, 2, z.half, lon)],
        compiler_params=params(),
        cost_estimate=cost(),
    )(place, cutoffs, mine, other, u, own_winds, other_winds, tables)

    column = lon // parts
    blocks = pl.pallas_call(
        functools.partial(outer_kernel, z, parts),
        name="outer",
        in_specs=[scalars(), scalars()] + [whole()] * 7,
        out_specs=[whole()] * (2 * parts),
        out_shape=[codes(tall, rows * column + LANE)] * (2 * parts),
        scratch_shapes=[
            pltpu.VMEM((6, 2, z.half, z.pad), f32),
            pltpu.VMEM((z.rows, 2, z.half, lon), f32),
        ],
        compiler_params=params(),
        cost_estimate=cost(),
    )(place, cutoffs, new, inner, own_winds, other_winds, one, two, tables)
    got = []
    for i, block in enumerate(blocks):
        b, across = i % parts, int(i < parts)
        pairs = [
            (k * parts + j, (k ^ across) * parts + (j ^ b)) for k in range(lats) for j in range(parts)
        ]
        got.append(lax.ppermute(block, ("lat", "lev"), pairs) if i != parts else block)
    far = [i for i in range(2 * parts) if i % parts >= parts // 2]
    scales = pl.pallas_call(
        functools.partial(scale_kernel, rows * column),
        name="scales",
        in_specs=[whole()] * len(far),
        out_specs=whole(),
        out_shape=shape(len(far), tall, LANE),
        compiler_params=params(),
        cost_estimate=cost(),
    )(*[got[i] for i in far])

    count = remap_weights.shape[0]
    upward = np.triu(np.ones((count, count), np.float32), 1) + 0.5 * np.eye(count, dtype=np.float32)
    upward = jnp.asarray(np.concatenate([upward, 0.0 * upward, upward], axis=1))
    surface = lax.dynamic_slice_in_dim(surface, lev * column, column, 1)
    remapped, geopotential = pl.pallas_call(
        functools.partial(column_kernel, z, parts, far),
        name="columns",
        grid=(rows,),
        in_specs=[scalars()]
        + [whole()] * (len(got) + 1)
        + [
            pl.BlockSpec(remap_weights.shape, lambda r: (0, 0)),
            pl.BlockSpec(upward.shape, lambda r: (0, 0)),
            pl.BlockSpec((1, 1, column), lambda r: (r, 0, 0)),
        ],
        out_specs=[
            pl.BlockSpec((2, 1, count, column), lambda r: (0, r, 0, 0)),
            pl.BlockSpec((1, count, column), lambda r: (r, 0, 0)),
        ],
        out_shape=[shape(2, rows, count, column), shape(rows, count, column)],
        scratch_shapes=[pltpu.VMEM((2, count, column), f32)],
        compiler_params=params(),
        cost_estimate=cost(),
    )(place, *got, scales, remap_weights, upward, surface[:, None, :])
    return remapped, geopotential


def with_halo(shard, width):
    size, length = lax.axis_size("lat"), shard.shape[1]
    up = [(i, (i + 1) % size) for i in range(size - 1)]
    down = [(j, i) for i, j in up]
    before = lax.ppermute(lax.slice_in_dim(shard, length - width, length, axis=1), "lat", up)
    after = lax.ppermute(lax.slice_in_dim(shard, 0, width, axis=1), "lat", down)
    return jnp.concatenate([before, shard, after], axis=1)


def plain_shards(fields, courant, cutoffs, surface, remap_weights):
    _, rows, _, lon = fields.shape
    exact = lax.Precision.HIGHEST
    cut = lax.dynamic_slice_in_dim(cutoffs, lax.axis_index("lat") * rows, rows)
    waves = np.arange(KMAX)
    angle = (np.arange(lon)[:, None] * waves[None, :] % lon) * (2.0 * math.pi / lon)
    table = jnp.asarray(np.concatenate([np.cos(angle), np.sin(angle)], axis=1).astype(np.float32))
    number = jnp.asarray(np.concatenate([waves, waves]).astype(np.int32))
    weight = jnp.where(number[None] <= cut[:, None], jnp.where(number == 0, 1.0, 2.0)[None] / lon, 0.0)
    flagged = cut < lon // 2

    def smooth(values):
        wave = jnp.einsum("frln,nk->frlk", values, table, precision=exact) * weight[None, :, None]
        low = jnp.einsum("frlk,nk->frln", wave, table, precision=exact)
        return jnp.where(flagged[None, :, None, None], low, values)

    winds = with_halo(courant, 1).astype(jnp.float32)
    east, north = winds[0, 1:-1], winds[1]
    face_x = (east + jnp.roll(east, -1, -1)) / 24.0
    face_y = (north[:-1] + north[1:]) / 24.0
    u = fields
    for _ in range(2):
        wide = with_halo(u, 2)
        pair = u + jnp.roll(u, -1, -1)
        fx = face_x * (8.0 * pair - (jnp.roll(pair, 1, -1) + jnp.roll(pair, -1, -1)))
        pair = wide[:, :-1] + wide[:, 1:]
        fy = face_y * (8.0 * pair[:, 1:-1] - (pair[:, :-2] + pair[:, 2:]))
        u = u - (fx - jnp.roll(fx, 1, -1)) - (fy[:, 1:] - fy[:, :-1])
        u = lax.cond(jnp.any(flagged), smooth, lambda values: values, u)
    columns = lax.all_to_all(u, "lev", split_axis=3, concat_axis=2, tiled=True)
    remapped = jnp.einsum("pk,fjkn->fjpn", remap_weights, columns, precision=exact)
    count = remap_weights.shape[0]
    upward = np.triu(np.ones((count, count), np.float32), 1) + 0.5 * np.eye(count, dtype=np.float32)
    upward = jnp.einsum("kl,jln->jkn", jnp.asarray(upward), columns[1], precision=exact)
    width = lon // lax.axis_size("lev")
    mine = lax.dynamic_slice_in_dim(surface, lax.axis_index("lev") * width, width, 1)
    return remapped, mine[:, None] + count**-0.5 * upward


def solution(mesh):
    def program(fields, courant, cutoffs, surface, remap_weights):
        lats, parts = mesh.shape["lat"], mesh.shape["lev"]
        rows, levels = fields.shape[1] // lats, fields.shape[2] // parts
        polar = fields.shape[1] // 8
        paired = (
            lats % 2 == 0
            and rows == 4
            and levels % 16 == 0
            and polar <= 2 * rows - 2
            and fields.shape[3] % (LANE * parts) == 0
            and parts & (parts - 1) == 0
            and fields.shape[3] % (4 * KMAX) == 0
        )
        return jax.shard_map(
            shards if paired else plain_shards,
            mesh=mesh,
            in_specs=(
                P(None, "lat", "lev", None),
                P(None, "lat", "lev", None),
                P(),
                P("lat", None),
                P(),
            ),
            out_specs=(P(None, "lat", None, "lev"), P("lat", None, "lev")),
            check_vma=False,
        )(fields, courant, cutoffs, surface, remap_weights)

    return program
```

```python
import functools
import math

import jax
import jax.numpy as jnp
import ml_dtypes
import numpy as np
from jax import lax
from jax.experimental import pallas as pl
from jax.experimental.pallas import tpu as pltpu
from jax.sharding import PartitionSpec as P

KMAX = 128
LANE = 128
TOP = 32767.0
STEPS = 256.0
TINY = 2.0**-100
WIND = 81920.0
ROUND = 1.5 * 2.0**23
VMEM_LIMIT = 12 * 2**20
VMEM_MOST = 63 * 2**20 + 2**19


def rounded(values):
    return ((values + ROUND) - ROUND).astype(jnp.int32).astype(jnp.int16)


def lane_max(values):
    chunks = [jnp.abs(values[:, i : i + LANE]) for i in range(0, values.shape[1], LANE)]
    while len(chunks) > 1:
        pairs = [jnp.maximum(a, b) for a, b in zip(chunks[0::2], chunks[1::2])]
        chunks = pairs + chunks[2 * len(pairs) :]
    return chunks[0]


def tiled(tile, width):
    return jnp.concatenate([tile] * (width // LANE), axis=1)


def scale_code(largest):
    return jnp.ceil(jnp.log2(jnp.maximum(largest, TINY)) * STEPS)


def encoder(code):
    return TOP / jnp.exp2(code * (1.0 / STEPS))


def decoder(code16):
    code = code16.astype(jnp.int32).astype(jnp.float32)
    return jnp.exp2(code * (1.0 / STEPS)) * (1.0 / TOP)


def encode_row(values, out_ref, at):
    width = values.shape[1]
    code = scale_code(lane_max(values))
    out_ref[:, at : at + width] = rounded(values * tiled(encoder(code), width))
    out_ref[:, at + width : at + width + LANE] = code.astype(jnp.int32).astype(jnp.int16)


def decode_row(in_ref, at, width):
    scale = decoder(in_ref[:, at + width : at + width + LANE])
    values = in_ref[:, at : at + width].astype(jnp.int32).astype(jnp.float32)
    return values * tiled(scale, width)


def fold(wind):
    middle = wind.shape[1] // 2
    return jnp.concatenate([wind[:, :middle], wind[:, middle:]], axis=0)


def unfold(values):
    half = values.shape[0] // 2
    return jnp.concatenate([values[:half], values[half:]], axis=1)


def wind_codes(values):
    return rounded(values * WIND)


def wind_values(codes):
    return codes.astype(jnp.int32).astype(jnp.float32) * (1.0 / WIND)


class Sizes:
    def __init__(self, rows, levels, lon):
        self.rows, self.levels, self.lon = rows, levels, lon
        self.half = levels // 2
        self.band = 2 * rows
        self.pad = lon + 2 * LANE
        self.code = lon + LANE
        self.edge = 2 * self.code + lon // 2
        self.middle = self.edge + lon // 2
        self.last = 2 * lon + lon // 2


def put_padded(ref, index, values, lon):
    ref[index + (Ellipsis, slice(LANE, LANE + lon))] = values
    ref[index + (Ellipsis, slice(0, LANE))] = values[..., lon - LANE :]
    ref[index + (Ellipsis, slice(LANE + lon, 2 * LANE + lon))] = values[..., :LANE]


def level_half(z, wind, upper):
    wind = wind.astype(jnp.float32)
    return jnp.where(upper == 1, wind[z.half :], wind[: z.half])


def edge_kernel(z, fields_ref, courant_ref, edge_ref, rows_ref, wind_ref, sems):
    p = lax.rem(lax.axis_index("lat"), 2)
    give = pl.multiple_of((1 - p) * z.half, z.half)
    copies = [
        pltpu.make_async_copy(
            fields_ref.at[f, 2 * p + r, pl.ds(give, z.half)],
            rows_ref.at[r, pl.ds(f * z.half, z.half)],
            sems.at[2 * r + f],
        )
        for r in range(2)
        for f in range(2)
    ]
    copies.append(pltpu.make_async_copy(courant_ref.at[1, 3 * p], wind_ref, sems.at[4]))
    for copy in copies:
        copy.start()
    for r in range(2):
        copies[2 * r].wait()
        copies[2 * r + 1].wait()
        encode_row(rows_ref[r], edge_ref, r * z.code)
    copies[4].wait()
    edge_ref[:, 2 * z.code :] = wind_codes(fold(level_half(z, wind_ref[...], 1 - p)))


def rest_kernel(z, par_ref, fields_ref, courant_ref, middle_ref, last_ref, own_ref):
    p = par_ref[0]
    keep = pl.multiple_of(p * z.half, z.half)
    give = pl.multiple_of((1 - p) * z.half, z.half)

    def field_row(row, start):
        return jnp.concatenate([fields_ref[f, row, pl.ds(start, z.half)] for f in range(2)], axis=0)

    def wind(k, row, upper):
        return level_half(z, courant_ref[k, row], upper)

    edge, inner = 2 * p, 2 * (1 - p)
    outer, near = 3 * p, 3 * (1 - p)
    for r in range(2):
        encode_row(field_row(edge + r, keep), own_ref, r * z.code)
        encode_row(field_row(inner + r, give), middle_ref, r * z.code)
    own_ref[:, 2 * z.code :] = wind_codes(fold(wind(1, outer, p)))
    lon = z.lon
    middle_ref[:, 2 * z.code : z.edge] = wind_codes(fold(wind(1, near, 1 - p)))
    middle_ref[:, z.edge :] = wind_codes(fold(wind(0, near, 1 - p)))
    last_ref[:, 2 * lon :] = wind_codes(fold(wind(0, outer, 1 - p)))
    for r in range(2):
        both = jnp.concatenate([wind(k, 1 + r, 1 - p) for k in range(2)], axis=0)
        last_ref[:, r * lon : (r + 1) * lon] = wind_codes(both)


def shifted(pieces, shift, lanes):
    turned = [pltpu.roll(v, (-shift) % LANE, 1) for v in pieces]
    if shift > 0:
        return [jnp.where(lanes < LANE - shift, a, b) for a, b in zip(turned[1:-1], turned[2:])]
    return [jnp.where(lanes < -shift, a, b) for a, b in zip(turned[:-2], turned[1:-1])]


def substep(z, count_rows, base, row_of, winds_ref, write):
    count = next(n for n in (4, 3, 2, 1) if z.lon % (n * LANE) == 0)
    width = count * LANE
    lanes = lax.broadcasted_iota(jnp.int32, (z.half, LANE), 1)

    def part(at):
        def piece(k):
            return pl.ds(at + k * LANE, LANE)

        def row(j, f):
            return [row_of(j, f, piece(k + 1)) for k in range(count)]

        def start(j, f):
            pieces = [row_of(j + 2, f, piece(k)) for k in range(count + 2)]
            return [shifted(pieces, s, lanes) for s in (-2, -1, 1, 2)]

        def lon_part(j, u, moved):
            out = []
            for k in range(count):
                m2, m1, p1, p2 = (m[k] for m in moved)
                east = 7.0 * (u[k] + p1) - (m1 + p2)
                west = 7.0 * (m1 + u[k]) - (m2 + p1)
                east = winds_ref[base + j, :, piece(k)] * east
                out.append(east - winds_ref[z.rows + base + j, :, piece(k)] * west)
            return out

        for f in range(2):
            rows = [row(j, f) for j in range(4)]
            sums = [[a + b for a, b in zip(rows[j], rows[j + 1])] for j in range(3)]
            flux = None
            moved = start(0, f)
            for j in range(count_rows + 1):
                later = start(j, f) if 0 < j < count_rows else None
                new = [
                    winds_ref[2 * z.rows + base + j, :, piece(k)] * (8.0 * sums[1][k] - (sums[0][k] + sums[2][k]))
                    for k in range(count)
                ]
                if j > 0:
                    u = rows[1]
                    change = lon_part(j - 1, u, moved)
                    for k in range(count):
                        write(j - 1, f, at, k, u[k] - change[k] - (new[k] - flux[k]))
                    moved = later
                flux = new
                if j < count_rows:
                    above = row(j + 4, f)
                    rows = rows[1:] + [above]
                    sums = sums[1:] + [[a + b for a, b in zip(rows[2], rows[3])]]

    for i in range(z.lon // width):
        part(i * width)


def filter_tables(lon):
    half = lon // 2
    points = np.arange(half)
    forward, back = [], []
    for parity in range(2):
        waves = np.arange(parity, KMAX, 2)
        angle = (points[:, None] * waves[None, :] % lon) * (2.0 * math.pi / lon)
        table = np.concatenate([np.cos(angle), np.sin(angle)], axis=1).astype(np.float32)
        high = table.astype(ml_dtypes.bfloat16)
        low = (table - high.astype(np.float32)).astype(ml_dtypes.bfloat16)
        forward.append(np.concatenate([high, low], axis=1))
        turned = np.concatenate([high.T, low.T], axis=0)
        back.append(np.concatenate(np.split(turned, half // (2 * KMAX), axis=1), axis=0))
    return np.stack(forward + back)


def split(values):
    high = values.astype(jnp.bfloat16)
    return high, (values - high.astype(jnp.float32)).astype(jnp.bfloat16)


def low_pass(z, rows, cuts, table_ref):
    half = z.lon // 2
    count = len(rows)
    tall = 2 * z.half
    total = count * tall
    flat = [row.reshape(tall, z.lon) for row in rows]
    folded = []
    for parity in range(2):
        parts = [
            row[:, :half] + row[:, half:] if parity == 0 else row[:, :half] - row[:, half:]
            for row in flat
        ]
        high, low = split(jnp.concatenate(parts, axis=0))
        both = jnp.concatenate([high, low], axis=0)
        got = jnp.dot(both, table_ref[parity], preferred_element_type=jnp.float32)
        wave = got[:total, :KMAX] + got[:total, KMAX:] + (got[total:, :KMAX] + got[total:, KMAX:])
        number = 2 * (lax.broadcasted_iota(jnp.int32, (tall, KMAX), 1) % (KMAX // 2)) + parity
        doubled = jnp.where(number == 0, 1.0, 2.0) * (1.0 / z.lon)
        weight = jnp.concatenate([jnp.where(number <= cut, doubled, 0.0) for cut in cuts], axis=0)
        high, low = split(wave * weight)
        both = jnp.concatenate(
            [jnp.concatenate([high, high], axis=1), jnp.concatenate([low, low], axis=1)], axis=0
        )
        got = []
        for at in range(0, half, 2 * KMAX):
            block = table_ref[2 + parity, at : at + 2 * KMAX]
            sums = jnp.dot(both, block, preferred_element_type=jnp.float32)
            got.append(sums[:total] + sums[total:])
        folded.append(jnp.concatenate(got, axis=1))
    left, right = folded[0] + folded[1], folded[0] - folded[1]
    smooth = jnp.concatenate([left, right], axis=1)
    return [smooth[i * tall : (i + 1) * tall].reshape(2, z.half, z.lon) for i in range(count)]


def filter_rows(z, cut_ref, first_row, start, table_ref, load, store):
    nyquist = z.lon // 2
    cuts = [cut_ref[first_row + start + r] for r in range(z.rows)]
    some = functools.reduce(jnp.logical_or, [cut < nyquist for cut in cuts])

    @pl.when(some)
    def _():
        smooth = low_pass(z, [load(start + r) for r in range(z.rows)], cuts, table_ref)
        for r in range(z.rows):

            @pl.when(cuts[r] < nyquist)
            def _():
                store(start + r, smooth[r])


def north_wind(z, in_ref):
    return unfold(wind_values(in_ref[:, 2 * z.code : z.edge]))


def faces(z, cx_ref, cy_ref, winds_ref):
    lanes = lax.broadcasted_iota(jnp.int32, (z.half, LANE), 1)
    for j in range(z.rows):
        pieces = [cx_ref[j, :, i : i + LANE] * (1.0 / 24.0) for i in range(0, z.pad, LANE)]
        for out, shift in ((j, 1), (z.rows + j, -1)):
            for k, moved in enumerate(shifted(pieces, shift, lanes)):
                winds_ref[out, :, k * LANE : (k + 1) * LANE] = pieces[k + 1] + moved
    for j in range(z.rows + 1):
        winds_ref[2 * z.rows + j] = (cy_ref[j] + cy_ref[j + 1]) * (1.0 / 24.0)


def writer(new_ref):
    def write(row, f, at, k, values):
        new_ref[row, f, :, pl.ds(at + (k + 1) * LANE, LANE)] = values

    return write


def wrap(z, new_ref, rows):
    for j in rows:
        new_ref[j, :, :, 0:LANE] = new_ref[j, :, :, z.lon : z.lon + LANE]
        new_ref[j, :, :, LANE + z.lon :] = new_ref[j, :, :, LANE : 2 * LANE]


def encode_new(z, new_ref, row, out_ref):
    for r in range(2):
        values = new_ref[row + r, :, :, LANE : LANE + z.lon]
        encode_row(values.reshape(2 * z.half, z.lon), out_ref, r * z.code)


def place_row(z, u_ref, row, in_ref, r):
    values = decode_row(in_ref, r * z.code, z.lon)
    put_padded(u_ref, (row + r,), values.reshape(2, z.half, z.lon), z.lon)


def own_kernel(
    z, par_ref, fields_ref, courant_ref, edge_ref, middle_ref, near_ref, far_ref,
    new_ref, winds_ref, code_ref, u_ref, cx_ref, cy_ref,
):
    p = par_ref[0]
    lon, half = z.lon, z.half
    keep = pl.multiple_of(p * half, half)
    for r in range(z.rows):
        own = jnp.stack([fields_ref[f, r, pl.ds(keep, half)] for f in range(2)])
        put_padded(u_ref, (z.rows * p + r + 2,), own, lon)
        put_padded(cx_ref, (r,), level_half(z, courant_ref[0, r], p), lon)
        cy_ref[r + 1] = level_half(z, courant_ref[1, r], p)
    for r in range(2):
        place_row(z, u_ref, 6 * (1 - p) + 2, edge_ref, r)
        place_row(z, u_ref, 4 - 2 * p + 2, middle_ref, r)
        place_row(z, u_ref, 10 * (1 - p), near_ref, r)
        place_row(z, u_ref, 10 * p, far_ref, r)
    cy_ref[5 * (1 - p)] = north_wind(z, middle_ref)
    cy_ref[5 * p] = north_wind(z, far_ref)
    faces(z, cx_ref, cy_ref, winds_ref)
    start = z.rows * p
    substep(z, z.rows, 0, lambda j, f, piece: u_ref[start + j, f, :, piece], winds_ref, writer(new_ref))
    encode_new(z, new_ref, 2 * p, code_ref)
    wrap(z, new_ref, range(z.rows))


def other_kernel(
    z, par_ref, courant_ref, edge_ref, middle_ref, last_ref, near_ref, u_ref,
    new_ref, winds_ref, code_ref, cx_ref, cy_ref,
):
    p = par_ref[0]
    lon, half = z.lon, z.half
    for r in range(2):
        both = wind_values(last_ref[:, r * lon : (r + 1) * lon])
        put_padded(cx_ref, (1 + r,), both[:half], lon)
        cy_ref[2 + r] = both[half:]
    easts = (last_ref[:, 2 * lon :], middle_ref[:, z.edge :])
    for east, row, in_ref in zip(easts, (3 * (1 - p), 3 * p), (edge_ref, middle_ref)):
        put_padded(cx_ref, (row,), unfold(wind_values(east)), lon)
        cy_ref[row + 1] = north_wind(z, in_ref)
    cy_ref[5 * p] = level_half(z, courant_ref[1, 3 * (1 - p)], p)
    cy_ref[5 * (1 - p)] = north_wind(z, near_ref)
    faces(z, cx_ref, cy_ref, winds_ref)
    outer = 2 * (1 - p)
    start = z.rows * (1 - p) + outer
    substep(z, 2, outer, lambda j, f, piece: u_ref[start + j, f, :, piece], winds_ref, writer(new_ref))
    encode_new(z, new_ref, 0, code_ref)
    wrap(z, new_ref, range(2))


def inner_kernel(
    z, par_ref, cut_ref, own_ref, other_ref, u_ref, own_winds_ref, other_winds_ref, near_ref, table_ref,
    new_ref, inner_ref, halo_ref,
):
    p = par_ref[0]
    for r in range(2):
        place_row(z, halo_ref, 0, near_ref, r)
    own, other = z.rows * p, z.rows * (1 - p)
    for j in range(z.rows):
        new_ref[own + j] = own_ref[j]
    for j in range(2):
        new_ref[other + 2 * (1 - p) + j] = other_ref[j]
    start = other + 2 * p

    def write(row, f, at, k, values):
        writer(new_ref)(start + row, f, at, k, values)

    substep(z, 2, 2 * p, lambda j, f, piece: u_ref[start + j, f, :, piece], other_winds_ref, write)
    wrap(z, new_ref, (start, start + 1))

    def store(row, values):
        put_padded(new_ref, (row,), values, z.lon)

    for part in range(2):
        filter_rows(
            z, cut_ref, par_ref[1], part * z.rows, table_ref,
            lambda row: new_ref[row, :, :, LANE : LANE + z.lon], store,
        )
    for i, (low, base, winds_ref) in enumerate(
        ((2 * p, 2 * (1 - p), own_winds_ref), (2 * (1 - p), 2 * p, other_winds_ref))
    ):

        def keep(row, f, at, k, values):
            inner_ref[2 * i + row, f, :, pl.ds(at + k * LANE, LANE)] = values

        substep(z, 2, base, lambda j, f, piece: new_ref[low + j, f, :, piece], winds_ref, keep)


def outer_kernel(
    z, parts, par_ref, cut_ref, new_ref, inner_ref, own_winds_ref, other_winds_ref, near_ref, far_ref, table_ref, *refs
):
    out_refs, (u_ref, v_ref) = refs[: 2 * parts], refs[2 * parts :]
    p = par_ref[0]
    outer_half(
        z, parts, 1 - p, 2, par_ref, cut_ref, new_ref, inner_ref, other_winds_ref, near_ref, table_ref,
        out_refs[:parts], u_ref, v_ref, True,
    )
    outer_half(
        z, parts, p, 0, par_ref, cut_ref, new_ref, inner_ref, own_winds_ref, far_ref, table_ref,
        out_refs[parts:], u_ref, v_ref, False,
    )


def outer_half(
    z, parts, side, inner_at, par_ref, cut_ref, new_ref, inner_ref, winds_ref, halo_ref, table_ref,
    out_refs, u_ref, v_ref, decoded,
):
    lon = z.lon
    tall = 2 * z.half
    base = z.rows * side
    for r in range(2):
        if decoded:
            u_ref[4 * side + r] = halo_ref[r]
        else:
            place_row(z, u_ref, 4 * side, halo_ref, r)
    for r in range(4):
        u_ref[2 * (1 - side) + r] = new_ref[base + r]
    for r in range(2):
        v_ref[2 * (1 - side) + r] = inner_ref[inner_at + r]

    def write(row, f, at, k, values):
        v_ref[2 * side + row, f, :, pl.ds(at + k * LANE, LANE)] = values

    substep(z, 2, 2 * side, lambda j, f, piece: u_ref[j, f, :, piece], winds_ref, write)

    def store(row, values):
        v_ref[row] = values

    filter_rows(z, cut_ref, par_ref[1] + base, 0, table_ref, lambda row: v_ref[row], store)
    column = lon // parts
    for b in range(parts):
        at = pl.multiple_of(jnp.bitwise_xor(par_ref[2], b) * column, LANE)
        values = jnp.concatenate(
            [v_ref[r, :, :, pl.ds(at, column)].reshape(tall, column) for r in range(z.rows)], axis=1
        )
        encode_row(values, out_refs[b], 0)


def scale_kernel(at, *refs):
    for i, ref in enumerate(refs[:-1]):
        refs[-1][i] = decoder(ref[:, at : at + LANE])


def column_kernel(z, parts, far, par_ref, *refs):
    got, (scales_ref, remap_ref, upward_ref, surface_ref, out_ref, geo_ref, x_ref) = refs[: 2 * parts], refs[2 * parts :]
    p, lev = par_ref[0], par_ref[2]
    column = out_ref.shape[-1]
    at = pl.multiple_of(pl.program_id(0) * column, LANE)
    for i, ref in enumerate(got):
        side = 1 - p if i < parts else p
        s = jnp.bitwise_xor(lev, i % parts)
        if i in far:
            scale = scales_ref[far.index(i)]
        else:
            scale = decoder(ref[:, z.rows * column : z.rows * column + LANE])
        codes = ref[:, pl.ds(at, column)].astype(jnp.int32).astype(jnp.float32)
        values = codes * tiled(scale, column)
        level = pl.multiple_of(s * z.levels + side * z.half, z.half)
        for f in range(2):
            x_ref[f, pl.ds(level, z.half)] = values[f * z.half : (f + 1) * z.half]
    high, low = split(remap_ref[...])
    remap = jnp.concatenate([high, low, high], axis=1)
    count = remap_ref.shape[0]
    for f in range(2):
        high, low = split(x_ref[f])
        stacked = jnp.concatenate([high, high, low], axis=0)
        left = remap if f == 0 else jnp.concatenate([remap, upward_ref[...].astype(jnp.bfloat16)], axis=0)
        result = jnp.dot(left, stacked, preferred_element_type=jnp.float32)
        out_ref[f, 0] = result[:count]
        if f == 1:
            geo_ref[0] = surface_ref[0] + result[count:] * (count**-0.5)


def whole():
    return pl.BlockSpec(memory_space=pltpu.VMEM)


def scalars():
    return pl.BlockSpec(memory_space=pltpu.SMEM)


def far_memory():
    return pl.BlockSpec(memory_space=pltpu.HBM)


def params(limit=VMEM_LIMIT):
    return pltpu.CompilerParams(vmem_limit_bytes=limit)


def cost(flops=1000, data=1000):
    return pl.CostEstimate(flops=flops, bytes_accessed=data, transcendentals=0)


def shards(fields, courant, cutoffs, surface, remap_weights):
    _, rows, levels, lon = fields.shape
    z = Sizes(rows, levels, lon)
    lats, parts = lax.axis_size("lat"), lax.axis_size("lev")
    me = lax.axis_index("lat")
    parity = me % 2
    lev = lax.axis_index("lev")
    place = jnp.stack([parity, (me - parity) * rows, lev]).astype(jnp.int32)
    tall = 2 * z.half
    i16, f32 = jnp.int16, jnp.float32
    swap = [(i, i ^ 1) for i in range(lats)]
    rising = [(i, i + 2) for i in range(lats - 2)]
    near_pairs = [(i, j) if i % 2 else (j, i) for i, j in rising]
    far_pairs = [(j, i) if i % 2 else (i, j) for i, j in rising]

    def shape(*dims):
        return jax.ShapeDtypeStruct(dims, f32)

    def codes(*dims):
        return jax.ShapeDtypeStruct(dims, i16)

    edge = pl.pallas_call(
        functools.partial(edge_kernel, z),
        name="edge",
        in_specs=[far_memory(), far_memory()],
        out_specs=whole(),
        out_shape=codes(tall, z.edge),
        scratch_shapes=[
            pltpu.VMEM((2, tall, lon), f32),
            pltpu.VMEM((levels, lon), courant.dtype),
            pltpu.SemaphoreType.DMA((5,)),
        ],
        compiler_params=params(VMEM_MOST),
        cost_estimate=cost(),
    )(fields, courant)
    edge = lax.ppermute(edge, "lat", swap)
    middle, last, own = pl.pallas_call(
        functools.partial(rest_kernel, z),
        name="rest",
        in_specs=[scalars(), whole(), whole()],
        out_specs=[whole()] * 3,
        out_shape=[codes(tall, z.middle), codes(tall, z.last), codes(tall, z.edge)],
        compiler_params=params(),
        cost_estimate=cost(),
    )(place, fields, courant)
    near = lax.ppermute(own, "lat", near_pairs)
    middle = lax.ppermute(middle, "lat", swap)
    far = lax.ppermute(edge, "lat", far_pairs)
    last = lax.ppermute(last, "lat", swap)

    half_scratch = [
        pltpu.VMEM((z.rows, z.half, z.pad), f32),
        pltpu.VMEM((z.rows + 2, z.half, lon), f32),
    ]
    mine, own_winds, own_code, u = pl.pallas_call(
        functools.partial(own_kernel, z),
        name="own",
        in_specs=[scalars()] + [whole()] * 6,
        out_specs=[whole()] * 4,
        out_shape=[
            shape(z.rows, 2, z.half, z.pad),
            shape(3 * z.rows + 1, z.half, lon),
            codes(tall, 2 * z.code),
            shape(z.band + 4, 2, z.half, z.pad),
        ],
        scratch_shapes=half_scratch,
        compiler_params=params(),
        cost_estimate=cost(),
    )(place, fields, courant, edge, middle, near, far)
    near_code = lax.ppermute(own_code, "lat", near_pairs)
    other, other_winds, other_code = pl.pallas_call(
        functools.partial(other_kernel, z),
        name="other",
        in_specs=[scalars()] + [whole()] * 6,
        out_specs=[whole()] * 3,
        out_shape=[
            shape(2, 2, z.half, z.pad),
            shape(3 * z.rows + 1, z.half, lon),
            codes(tall, 2 * z.code),
        ],
        scratch_shapes=half_scratch,
        compiler_params=params(),
        cost_estimate=cost(),
    )(place, courant, edge, middle, last, near, u)
    far_code = lax.ppermute(other_code, "lat", far_pairs)

    tables = jnp.asarray(filter_tables(lon))
    new, inner, near_rows = pl.pallas_call(
        functools.partial(inner_kernel, z),
        name="inner",
        in_specs=[scalars(), scalars()] + [whole()] * 7,
        out_specs=[whole()] * 3,
        out_shape=[
            shape(z.band, 2, z.half, z.pad),
            shape(z.rows, 2, z.half, lon),
            shape(2, 2, z.half, z.pad),
        ],
        compiler_params=params(),
        cost_estimate=cost(),
    )(place, cutoffs, mine, other, u, own_winds, other_winds, near_code, tables)

    column = lon // parts
    blocks = pl.pallas_call(
        functools.partial(outer_kernel, z, parts),
        name="outer",
        in_specs=[scalars(), scalars()] + [whole()] * 7,
        out_specs=[whole()] * (2 * parts),
        out_shape=[codes(tall, rows * column + LANE)] * (2 * parts),
        scratch_shapes=[
            pltpu.VMEM((6, 2, z.half, z.pad), f32),
            pltpu.VMEM((z.rows, 2, z.half, lon), f32),
        ],
        compiler_params=params(),
        cost_estimate=cost(),
    )(place, cutoffs, new, inner, own_winds, other_winds, near_rows, far_code, tables)
    got = []
    for i, block in enumerate(blocks):
        b, across = i % parts, int(i < parts)
        pairs = [
            (k * parts + j, (k ^ across) * parts + (j ^ b)) for k in range(lats) for j in range(parts)
        ]
        got.append(lax.ppermute(block, ("lat", "lev"), pairs) if i != parts else block)
    far = [i for i in range(2 * parts) if i % 2 == 0 and i != parts]
    scales = pl.pallas_call(
        functools.partial(scale_kernel, rows * column),
        name="scales",
        in_specs=[whole()] * len(far),
        out_specs=whole(),
        out_shape=shape(len(far), tall, LANE),
        compiler_params=params(),
        cost_estimate=cost(),
    )(*[got[i] for i in far])

    count = remap_weights.shape[0]
    upward = np.triu(np.ones((count, count), np.float32), 1) + 0.5 * np.eye(count, dtype=np.float32)
    upward = jnp.asarray(np.concatenate([upward, 0.0 * upward, upward], axis=1))
    surface = lax.dynamic_slice_in_dim(surface, lev * column, column, 1)
    remapped, geopotential = pl.pallas_call(
        functools.partial(column_kernel, z, parts, far),
        name="columns",
        grid=(rows,),
        in_specs=[scalars()]
        + [whole()] * (len(got) + 1)
        + [
            pl.BlockSpec(remap_weights.shape, lambda r: (0, 0)),
            pl.BlockSpec(upward.shape, lambda r: (0, 0)),
            pl.BlockSpec((1, 1, column), lambda r: (r, 0, 0)),
        ],
        out_specs=[
            pl.BlockSpec((2, 1, count, column), lambda r: (0, r, 0, 0)),
            pl.BlockSpec((1, count, column), lambda r: (r, 0, 0)),
        ],
        out_shape=[shape(2, rows, count, column), shape(rows, count, column)],
        scratch_shapes=[pltpu.VMEM((2, count, column), f32)],
        compiler_params=params(),
        cost_estimate=cost(),
    )(place, *got, scales, remap_weights, upward, surface[:, None, :])
    return remapped, geopotential


def with_halo(shard, width):
    size, length = lax.axis_size("lat"), shard.shape[1]
    up = [(i, (i + 1) % size) for i in range(size - 1)]
    down = [(j, i) for i, j in up]
    before = lax.ppermute(lax.slice_in_dim(shard, length - width, length, axis=1), "lat", up)
    after = lax.ppermute(lax.slice_in_dim(shard, 0, width, axis=1), "lat", down)
    return jnp.concatenate([before, shard, after], axis=1)


def plain_shards(fields, courant, cutoffs, surface, remap_weights):
    _, rows, _, lon = fields.shape
    exact = lax.Precision.HIGHEST
    cut = lax.dynamic_slice_in_dim(cutoffs, lax.axis_index("lat") * rows, rows)
    waves = np.arange(KMAX)
    angle = (np.arange(lon)[:, None] * waves[None, :] % lon) * (2.0 * math.pi / lon)
    table = jnp.asarray(np.concatenate([np.cos(angle), np.sin(angle)], axis=1).astype(np.float32))
    number = jnp.asarray(np.concatenate([waves, waves]).astype(np.int32))
    weight = jnp.where(number[None] <= cut[:, None], jnp.where(number == 0, 1.0, 2.0)[None] / lon, 0.0)
    flagged = cut < lon // 2

    def smooth(values):
        wave = jnp.einsum("frln,nk->frlk", values, table, precision=exact) * weight[None, :, None]
        low = jnp.einsum("frlk,nk->frln", wave, table, precision=exact)
        return jnp.where(flagged[None, :, None, None], low, values)

    winds = with_halo(courant, 1).astype(jnp.float32)
    east, north = winds[0, 1:-1], winds[1]
    face_x = (east + jnp.roll(east, -1, -1)) / 24.0
    face_y = (north[:-1] + north[1:]) / 24.0
    u = fields
    for _ in range(2):
        wide = with_halo(u, 2)
        pair = u + jnp.roll(u, -1, -1)
        fx = face_x * (8.0 * pair - (jnp.roll(pair, 1, -1) + jnp.roll(pair, -1, -1)))
        pair = wide[:, :-1] + wide[:, 1:]
        fy = face_y * (8.0 * pair[:, 1:-1] - (pair[:, :-2] + pair[:, 2:]))
        u = u - (fx - jnp.roll(fx, 1, -1)) - (fy[:, 1:] - fy[:, :-1])
        u = lax.cond(jnp.any(flagged), smooth, lambda values: values, u)
    columns = lax.all_to_all(u, "lev", split_axis=3, concat_axis=2, tiled=True)
    remapped = jnp.einsum("pk,fjkn->fjpn", remap_weights, columns, precision=exact)
    count = remap_weights.shape[0]
    upward = np.triu(np.ones((count, count), np.float32), 1) + 0.5 * np.eye(count, dtype=np.float32)
    upward = jnp.einsum("kl,jln->jkn", jnp.asarray(upward), columns[1], precision=exact)
    width = lon // lax.axis_size("lev")
    mine = lax.dynamic_slice_in_dim(surface, lax.axis_index("lev") * width, width, 1)
    return remapped, mine[:, None] + count**-0.5 * upward


def solution(mesh):
    def program(fields, courant, cutoffs, surface, remap_weights):
        lats, parts = mesh.shape["lat"], mesh.shape["lev"]
        rows, levels = fields.shape[1] // lats, fields.shape[2] // parts
        polar = fields.shape[1] // 8
        paired = (
            lats % 2 == 0
            and rows == 4
            and levels % 16 == 0
            and polar <= 2 * rows - 2
            and fields.shape[3] % (LANE * parts) == 0
            and parts & (parts - 1) == 0
            and fields.shape[3] % (4 * KMAX) == 0
        )
        return jax.shard_map(
            shards if paired else plain_shards,
            mesh=mesh,
            in_specs=(
                P(None, "lat", "lev", None),
                P(None, "lat", "lev", None),
                P(),
                P("lat", None),
                P(),
            ),
            out_specs=(P(None, "lat", None, "lev"), P("lat", None, "lev")),
            check_vma=False,
        )(fields, courant, cutoffs, surface, remap_weights)

    return program
```

```python
import functools
import math

import jax
import jax.numpy as jnp
import ml_dtypes
import numpy as np
from jax import lax
from jax.experimental import pallas as pl
from jax.experimental.pallas import tpu as pltpu
from jax.sharding import PartitionSpec as P

KMAX = 128
LANE = 128
TOP = 32767.0
STEPS = 256.0
TINY = 2.0**-100
WIND = 81920.0
ROUND = 1.5 * 2.0**23
VMEM_LIMIT = 12 * 2**20
VMEM_MOST = 63 * 2**20 + 2**19


def rounded(values):
    return ((values + ROUND) - ROUND).astype(jnp.int32).astype(jnp.int16)


def lane_max(values):
    chunks = [jnp.abs(values[:, i : i + LANE]) for i in range(0, values.shape[1], LANE)]
    while len(chunks) > 1:
        pairs = [jnp.maximum(a, b) for a, b in zip(chunks[0::2], chunks[1::2])]
        chunks = pairs + chunks[2 * len(pairs) :]
    return chunks[0]


def tiled(tile, width):
    return jnp.concatenate([tile] * (width // LANE), axis=1)


def scale_code(largest):
    return jnp.ceil(jnp.log2(jnp.maximum(largest, TINY)) * STEPS)


def encoder(code):
    return TOP / jnp.exp2(code * (1.0 / STEPS))


def decoder(code16):
    code = code16.astype(jnp.int32).astype(jnp.float32)
    return jnp.exp2(code * (1.0 / STEPS)) * (1.0 / TOP)


def encode_row(values, out_ref, at):
    width = values.shape[1]
    code = scale_code(lane_max(values))
    out_ref[:, at : at + width] = rounded(values * tiled(encoder(code), width))
    out_ref[:, at + width : at + width + LANE] = code.astype(jnp.int32).astype(jnp.int16)


def decode_row(in_ref, at, width):
    scale = decoder(in_ref[:, at + width : at + width + LANE])
    values = in_ref[:, at : at + width].astype(jnp.int32).astype(jnp.float32)
    return values * tiled(scale, width)


def fold(wind):
    middle = wind.shape[1] // 2
    return jnp.concatenate([wind[:, :middle], wind[:, middle:]], axis=0)


def unfold(values):
    half = values.shape[0] // 2
    return jnp.concatenate([values[:half], values[half:]], axis=1)


def wind_codes(values):
    return rounded(values * WIND)


def wind_values(codes):
    return codes.astype(jnp.int32).astype(jnp.float32) * (1.0 / WIND)


class Sizes:
    def __init__(self, rows, levels, lon):
        self.rows, self.levels, self.lon = rows, levels, lon
        self.half = levels // 2
        self.band = 2 * rows
        self.pad = lon + 2 * LANE
        self.code = lon + LANE
        self.edge = 2 * self.code + lon // 2
        self.middle = self.edge + lon // 2
        self.last = 2 * lon + lon // 2


def put_padded(ref, index, values, lon):
    ref[index + (Ellipsis, slice(LANE, LANE + lon))] = values
    ref[index + (Ellipsis, slice(0, LANE))] = values[..., lon - LANE :]
    ref[index + (Ellipsis, slice(LANE + lon, 2 * LANE + lon))] = values[..., :LANE]


def level_half(z, wind, upper):
    wind = wind.astype(jnp.float32)
    return jnp.where(upper == 1, wind[z.half :], wind[: z.half])


def edge_kernel(z, fields_ref, courant_ref, edge_ref, rows_ref, wind_ref, sems):
    p = lax.rem(lax.axis_index("lat"), 2)
    give = pl.multiple_of((1 - p) * z.half, z.half)
    copies = [
        pltpu.make_async_copy(
            fields_ref.at[f, 2 * p + r, pl.ds(give, z.half)],
            rows_ref.at[r, pl.ds(f * z.half, z.half)],
            sems.at[2 * r + f],
        )
        for r in range(2)
        for f in range(2)
    ]
    copies.append(pltpu.make_async_copy(courant_ref.at[1, 3 * p], wind_ref, sems.at[4]))
    for copy in copies:
        copy.start()
    for r in range(2):
        copies[2 * r].wait()
        copies[2 * r + 1].wait()
        encode_row(rows_ref[r], edge_ref, r * z.code)
    copies[4].wait()
    edge_ref[:, 2 * z.code :] = wind_codes(fold(level_half(z, wind_ref[...], 1 - p)))


def rest_kernel(z, par_ref, fields_ref, courant_ref, middle_ref, last_ref, own_ref):
    p = par_ref[0]
    keep = pl.multiple_of(p * z.half, z.half)
    give = pl.multiple_of((1 - p) * z.half, z.half)

    def field_row(row, start):
        return jnp.concatenate([fields_ref[f, row, pl.ds(start, z.half)] for f in range(2)], axis=0)

    def wind(k, row, upper):
        return level_half(z, courant_ref[k, row], upper)

    edge, inner = 2 * p, 2 * (1 - p)
    outer, near = 3 * p, 3 * (1 - p)
    for r in range(2):
        encode_row(field_row(edge + r, keep), own_ref, r * z.code)
        encode_row(field_row(inner + r, give), middle_ref, r * z.code)
    own_ref[:, 2 * z.code :] = wind_codes(fold(wind(1, outer, p)))
    lon = z.lon
    middle_ref[:, 2 * z.code : z.edge] = wind_codes(fold(wind(1, near, 1 - p)))
    middle_ref[:, z.edge :] = wind_codes(fold(wind(0, near, 1 - p)))
    last_ref[:, 2 * lon :] = wind_codes(fold(wind(0, outer, 1 - p)))
    for r in range(2):
        both = jnp.concatenate([wind(k, 1 + r, 1 - p) for k in range(2)], axis=0)
        last_ref[:, r * lon : (r + 1) * lon] = wind_codes(both)


def shifted(pieces, shift, lanes):
    turned = [pltpu.roll(v, (-shift) % LANE, 1) for v in pieces]
    if shift > 0:
        return [jnp.where(lanes < LANE - shift, a, b) for a, b in zip(turned[1:-1], turned[2:])]
    return [jnp.where(lanes < -shift, a, b) for a, b in zip(turned[:-2], turned[1:-1])]


def substep(z, count_rows, base, row_of, winds_ref, write):
    count = next(n for n in (4, 3, 2, 1) if z.lon % (n * LANE) == 0)
    width = count * LANE
    lanes = lax.broadcasted_iota(jnp.int32, (z.half, LANE), 1)

    def part(at):
        def piece(k):
            return pl.ds(at + k * LANE, LANE)

        def row(j, f):
            return [row_of(j, f, piece(k + 1)) for k in range(count)]

        def start(j, f):
            pieces = [row_of(j + 2, f, piece(k)) for k in range(count + 2)]
            return [shifted(pieces, s, lanes) for s in (-2, -1, 1, 2)]

        def lon_part(j, u, moved):
            out = []
            for k in range(count):
                m2, m1, p1, p2 = (m[k] for m in moved)
                east = 7.0 * (u[k] + p1) - (m1 + p2)
                west = 7.0 * (m1 + u[k]) - (m2 + p1)
                east = winds_ref[base + j, :, piece(k)] * east
                out.append(east - winds_ref[z.rows + base + j, :, piece(k)] * west)
            return out

        for f in range(2):
            rows = [row(j, f) for j in range(4)]
            sums = [[a + b for a, b in zip(rows[j], rows[j + 1])] for j in range(3)]
            flux = None
            moved = start(0, f)
            for j in range(count_rows + 1):
                later = start(j, f) if 0 < j < count_rows else None
                new = [
                    winds_ref[2 * z.rows + base + j, :, piece(k)] * (8.0 * sums[1][k] - (sums[0][k] + sums[2][k]))
                    for k in range(count)
                ]
                if j > 0:
                    u = rows[1]
                    change = lon_part(j - 1, u, moved)
                    for k in range(count):
                        write(j - 1, f, at, k, u[k] - change[k] - (new[k] - flux[k]))
                    moved = later
                flux = new
                if j < count_rows:
                    above = row(j + 4, f)
                    rows = rows[1:] + [above]
                    sums = sums[1:] + [[a + b for a, b in zip(rows[2], rows[3])]]

    for i in range(z.lon // width):
        part(i * width)


def filter_tables(lon):
    half = lon // 2
    points = np.arange(half)
    forward, back = [], []
    for parity in range(2):
        waves = np.arange(parity, KMAX, 2)
        angle = (points[:, None] * waves[None, :] % lon) * (2.0 * math.pi / lon)
        table = np.concatenate([np.cos(angle), np.sin(angle)], axis=1).astype(np.float32)
        high = table.astype(ml_dtypes.bfloat16)
        low = (table - high.astype(np.float32)).astype(ml_dtypes.bfloat16)
        forward.append(np.concatenate([high, low], axis=1))
        turned = np.concatenate([high.T, low.T], axis=0)
        back.append(np.concatenate(np.split(turned, half // (2 * KMAX), axis=1), axis=0))
    return np.stack(forward + back)


def split(values):
    high = values.astype(jnp.bfloat16)
    return high, (values - high.astype(jnp.float32)).astype(jnp.bfloat16)


def low_pass(z, rows, cuts, table_ref):
    half = z.lon // 2
    count = len(rows)
    tall = 2 * z.half
    total = count * tall
    flat = [row.reshape(tall, z.lon) for row in rows]
    folded = []
    for parity in range(2):
        parts = [
            row[:, :half] + row[:, half:] if parity == 0 else row[:, :half] - row[:, half:]
            for row in flat
        ]
        high, low = split(jnp.concatenate(parts, axis=0))
        both = jnp.concatenate([high, low], axis=0)
        got = jnp.dot(both, table_ref[parity], preferred_element_type=jnp.float32)
        wave = got[:total, :KMAX] + got[:total, KMAX:] + (got[total:, :KMAX] + got[total:, KMAX:])
        number = 2 * (lax.broadcasted_iota(jnp.int32, (tall, KMAX), 1) % (KMAX // 2)) + parity
        doubled = jnp.where(number == 0, 1.0, 2.0) * (1.0 / z.lon)
        weight = jnp.concatenate([jnp.where(number <= cut, doubled, 0.0) for cut in cuts], axis=0)
        high, low = split(wave * weight)
        both = jnp.concatenate(
            [jnp.concatenate([high, high], axis=1), jnp.concatenate([low, low], axis=1)], axis=0
        )
        got = []
        for at in range(0, half, 2 * KMAX):
            block = table_ref[2 + parity, at : at + 2 * KMAX]
            sums = jnp.dot(both, block, preferred_element_type=jnp.float32)
            got.append(sums[:total] + sums[total:])
        folded.append(jnp.concatenate(got, axis=1))
    left, right = folded[0] + folded[1], folded[0] - folded[1]
    smooth = jnp.concatenate([left, right], axis=1)
    return [smooth[i * tall : (i + 1) * tall].reshape(2, z.half, z.lon) for i in range(count)]


def filter_rows(z, cut_ref, first_row, start, table_ref, load, store):
    nyquist = z.lon // 2
    cuts = [cut_ref[first_row + start + r] for r in range(z.rows)]
    some = functools.reduce(jnp.logical_or, [cut < nyquist for cut in cuts])

    @pl.when(some)
    def _():
        smooth = low_pass(z, [load(start + r) for r in range(z.rows)], cuts, table_ref)
        for r in range(z.rows):

            @pl.when(cuts[r] < nyquist)
            def _():
                store(start + r, smooth[r])


def north_wind(z, in_ref):
    return unfold(wind_values(in_ref[:, 2 * z.code : z.edge]))


def faces(z, cx_ref, cy_ref, winds_ref):
    lanes = lax.broadcasted_iota(jnp.int32, (z.half, LANE), 1)
    for j in range(z.rows):
        pieces = [cx_ref[j, :, i : i + LANE] * (1.0 / 24.0) for i in range(0, z.pad, LANE)]
        for out, shift in ((j, 1), (z.rows + j, -1)):
            for k, moved in enumerate(shifted(pieces, shift, lanes)):
                winds_ref[out, :, k * LANE : (k + 1) * LANE] = pieces[k + 1] + moved
    for j in range(z.rows + 1):
        winds_ref[2 * z.rows + j] = (cy_ref[j] + cy_ref[j + 1]) * (1.0 / 24.0)


def writer(new_ref):
    def write(row, f, at, k, values):
        new_ref[row, f, :, pl.ds(at + (k + 1) * LANE, LANE)] = values

    return write


def wrap(z, new_ref, rows):
    for j in rows:
        new_ref[j, :, :, 0:LANE] = new_ref[j, :, :, z.lon : z.lon + LANE]
        new_ref[j, :, :, LANE + z.lon :] = new_ref[j, :, :, LANE : 2 * LANE]


def encode_new(z, new_ref, row, out_ref):
    for r in range(2):
        values = new_ref[row + r, :, :, LANE : LANE + z.lon]
        encode_row(values.reshape(2 * z.half, z.lon), out_ref, r * z.code)


def place_row(z, u_ref, row, in_ref, r):
    values = decode_row(in_ref, r * z.code, z.lon)
    put_padded(u_ref, (row + r,), values.reshape(2, z.half, z.lon), z.lon)


def own_kernel(
    z, par_ref, fields_ref, courant_ref, edge_ref, middle_ref, near_ref, far_ref,
    new_ref, winds_ref, code_ref, u_ref, cx_ref, cy_ref,
):
    p = par_ref[0]
    lon, half = z.lon, z.half
    keep = pl.multiple_of(p * half, half)
    for r in range(z.rows):
        own = jnp.stack([fields_ref[f, r, pl.ds(keep, half)] for f in range(2)])
        put_padded(u_ref, (z.rows * p + r + 2,), own, lon)
        put_padded(cx_ref, (r,), level_half(z, courant_ref[0, r], p), lon)
        cy_ref[r + 1] = level_half(z, courant_ref[1, r], p)
    for r in range(2):
        place_row(z, u_ref, 6 * (1 - p) + 2, edge_ref, r)
        place_row(z, u_ref, 4 - 2 * p + 2, middle_ref, r)
        place_row(z, u_ref, 10 * (1 - p), near_ref, r)
        place_row(z, u_ref, 10 * p, far_ref, r)
    cy_ref[5 * (1 - p)] = north_wind(z, middle_ref)
    cy_ref[5 * p] = north_wind(z, far_ref)
    faces(z, cx_ref, cy_ref, winds_ref)
    start = z.rows * p
    substep(z, z.rows, 0, lambda j, f, piece: u_ref[start + j, f, :, piece], winds_ref, writer(new_ref))
    encode_new(z, new_ref, 2 * p, code_ref)
    wrap(z, new_ref, range(z.rows))


def other_kernel(
    z, par_ref, courant_ref, edge_ref, middle_ref, last_ref, near_ref, u_ref,
    new_ref, winds_ref, code_ref, cx_ref, cy_ref,
):
    p = par_ref[0]
    lon, half = z.lon, z.half
    for r in range(2):
        both = wind_values(last_ref[:, r * lon : (r + 1) * lon])
        put_padded(cx_ref, (1 + r,), both[:half], lon)
        cy_ref[2 + r] = both[half:]
    easts = (last_ref[:, 2 * lon :], middle_ref[:, z.edge :])
    for east, row, in_ref in zip(easts, (3 * (1 - p), 3 * p), (edge_ref, middle_ref)):
        put_padded(cx_ref, (row,), unfold(wind_values(east)), lon)
        cy_ref[row + 1] = north_wind(z, in_ref)
    cy_ref[5 * p] = level_half(z, courant_ref[1, 3 * (1 - p)], p)
    cy_ref[5 * (1 - p)] = north_wind(z, near_ref)
    faces(z, cx_ref, cy_ref, winds_ref)
    outer = 2 * (1 - p)
    start = z.rows * (1 - p) + outer
    substep(z, 2, outer, lambda j, f, piece: u_ref[start + j, f, :, piece], winds_ref, writer(new_ref))
    encode_new(z, new_ref, 0, code_ref)
    wrap(z, new_ref, range(2))


def inner_kernel(
    z, par_ref, cut_ref, own_ref, other_ref, u_ref, own_winds_ref, other_winds_ref, table_ref, new_ref, inner_ref
):
    p = par_ref[0]
    own, other = z.rows * p, z.rows * (1 - p)
    for j in range(z.rows):
        new_ref[own + j] = own_ref[j]
    for j in range(2):
        new_ref[other + 2 * (1 - p) + j] = other_ref[j]
    start = other + 2 * p

    def write(row, f, at, k, values):
        writer(new_ref)(start + row, f, at, k, values)

    substep(z, 2, 2 * p, lambda j, f, piece: u_ref[start + j, f, :, piece], other_winds_ref, write)
    wrap(z, new_ref, (start, start + 1))

    def store(row, values):
        put_padded(new_ref, (row,), values, z.lon)

    for part in range(2):
        filter_rows(
            z, cut_ref, par_ref[1], part * z.rows, table_ref,
            lambda row: new_ref[row, :, :, LANE : LANE + z.lon], store,
        )
    for i, (low, base, winds_ref) in enumerate(
        ((2 * p, 2 * (1 - p), own_winds_ref), (2 * (1 - p), 2 * p, other_winds_ref))
    ):

        def keep(row, f, at, k, values):
            inner_ref[2 * i + row, f, :, pl.ds(at + k * LANE, LANE)] = values

        substep(z, 2, base, lambda j, f, piece: new_ref[low + j, f, :, piece], winds_ref, keep)


def outer_kernel(
    z, parts, par_ref, cut_ref, new_ref, inner_ref, own_winds_ref, other_winds_ref, near_ref, far_ref, table_ref, *refs
):
    out_refs, (u_ref, v_ref) = refs[: 2 * parts], refs[2 * parts :]
    p = par_ref[0]
    outer_half(
        z, parts, 1 - p, 2, par_ref, cut_ref, new_ref, inner_ref, other_winds_ref, near_ref, table_ref,
        out_refs[:parts], u_ref, v_ref,
    )
    outer_half(
        z, parts, p, 0, par_ref, cut_ref, new_ref, inner_ref, own_winds_ref, far_ref, table_ref,
        out_refs[parts:], u_ref, v_ref,
    )


def outer_half(
    z, parts, side, inner_at, par_ref, cut_ref, new_ref, inner_ref, winds_ref, halo_ref, table_ref,
    out_refs, u_ref, v_ref,
):
    lon = z.lon
    tall = 2 * z.half
    base = z.rows * side
    for r in range(2):
        place_row(z, u_ref, 4 * side, halo_ref, r)
    for r in range(4):
        u_ref[2 * (1 - side) + r] = new_ref[base + r]
    for r in range(2):
        v_ref[2 * (1 - side) + r] = inner_ref[inner_at + r]

    def write(row, f, at, k, values):
        v_ref[2 * side + row, f, :, pl.ds(at + k * LANE, LANE)] = values

    substep(z, 2, 2 * side, lambda j, f, piece: u_ref[j, f, :, piece], winds_ref, write)

    def store(row, values):
        v_ref[row] = values

    filter_rows(z, cut_ref, par_ref[1] + base, 0, table_ref, lambda row: v_ref[row], store)
    column = lon // parts
    for b in range(parts):
        at = pl.multiple_of(jnp.bitwise_xor(par_ref[2], b) * column, LANE)
        values = jnp.concatenate(
            [v_ref[r, :, :, pl.ds(at, column)].reshape(tall, column) for r in range(z.rows)], axis=1
        )
        encode_row(values, out_refs[b], 0)


def scale_kernel(at, *refs):
    for i, ref in enumerate(refs[:-1]):
        refs[-1][i] = decoder(ref[:, at : at + LANE])


def column_kernel(z, parts, far, par_ref, *refs):
    got, refs = refs[: 2 * parts], refs[2 * parts :]
    scales_ref, remap_ref, upward_ref, surface_ref, out_ref, geo_ref, x_ref, sums_ref, geo_sums_ref, sems = refs
    p, lev = par_ref[0], par_ref[2]
    count, column = sums_ref.shape[-2:]
    high, low = split(remap_ref[...])
    remap = jnp.concatenate([high, low, high], axis=1)
    both = jnp.concatenate([remap, upward_ref[...].astype(jnp.bfloat16)], axis=0)
    scales = [
        scales_ref[far.index(i)] if i in far else decoder(ref[:, z.rows * column :])
        for i, ref in enumerate(got)
    ]
    copies = []
    for row in range(z.rows):
        for i, ref in enumerate(got):
            side = 1 - p if i < parts else p
            s = jnp.bitwise_xor(lev, i % parts)
            codes = ref[:, row * column : (row + 1) * column].astype(jnp.int32).astype(jnp.float32)
            values = codes * tiled(scales[i], column)
            level = pl.multiple_of(s * z.levels + side * z.half, z.half)
            for f in range(2):
                x_ref[row, f, pl.ds(level, z.half)] = values[f * z.half : (f + 1) * z.half]
        for f in range(2):
            high, low = split(x_ref[row, f])
            stacked = jnp.concatenate([high, high, low], axis=0)
            result = jnp.dot(both if f else remap, stacked, preferred_element_type=jnp.float32)
            sums_ref[f, row] = result[:count]
            if f:
                geo_sums_ref[row] = surface_ref[row] + result[count:] * (count**-0.5)
        parts_out = [(sums_ref.at[f, row], out_ref.at[f, row]) for f in range(2)]
        parts_out.append((geo_sums_ref.at[row], geo_ref.at[row]))
        for k, (a, b) in enumerate(parts_out):
            copies.append(pltpu.make_async_copy(a, b, sems.at[3 * row + k]))
            copies[-1].start()
    for copy in copies:
        copy.wait()


def whole():
    return pl.BlockSpec(memory_space=pltpu.VMEM)


def scalars():
    return pl.BlockSpec(memory_space=pltpu.SMEM)


def far_memory():
    return pl.BlockSpec(memory_space=pltpu.HBM)


def params(limit=VMEM_LIMIT):
    return pltpu.CompilerParams(vmem_limit_bytes=limit)


def cost(flops=1000, data=1000):
    return pl.CostEstimate(flops=flops, bytes_accessed=data, transcendentals=0)


def shards(fields, courant, cutoffs, surface, remap_weights):
    _, rows, levels, lon = fields.shape
    z = Sizes(rows, levels, lon)
    lats, parts = lax.axis_size("lat"), lax.axis_size("lev")
    me = lax.axis_index("lat")
    parity = me % 2
    lev = lax.axis_index("lev")
    place = jnp.stack([parity, (me - parity) * rows, lev]).astype(jnp.int32)
    tall = 2 * z.half
    i16, f32 = jnp.int16, jnp.float32
    swap = [(i, i ^ 1) for i in range(lats)]
    rising = [(i, i + 2) for i in range(lats - 2)]
    near_pairs = [(i, j) if i % 2 else (j, i) for i, j in rising]
    far_pairs = [(j, i) if i % 2 else (i, j) for i, j in rising]

    def shape(*dims):
        return jax.ShapeDtypeStruct(dims, f32)

    def codes(*dims):
        return jax.ShapeDtypeStruct(dims, i16)

    edge = pl.pallas_call(
        functools.partial(edge_kernel, z),
        name="edge",
        in_specs=[far_memory(), far_memory()],
        out_specs=whole(),
        out_shape=codes(tall, z.edge),
        scratch_shapes=[
            pltpu.VMEM((2, tall, lon), f32),
            pltpu.VMEM((levels, lon), courant.dtype),
            pltpu.SemaphoreType.DMA((5,)),
        ],
        compiler_params=params(VMEM_MOST),
        cost_estimate=cost(),
    )(fields, courant)
    edge = lax.ppermute(edge, "lat", swap)
    middle, last, own = pl.pallas_call(
        functools.partial(rest_kernel, z),
        name="rest",
        in_specs=[scalars(), whole(), whole()],
        out_specs=[whole()] * 3,
        out_shape=[codes(tall, z.middle), codes(tall, z.last), codes(tall, z.edge)],
        compiler_params=params(),
        cost_estimate=cost(),
    )(place, fields, courant)
    near = lax.ppermute(own, "lat", near_pairs)
    middle = lax.ppermute(middle, "lat", swap)
    far = lax.ppermute(edge, "lat", far_pairs)
    last = lax.ppermute(last, "lat", swap)

    half_scratch = [
        pltpu.VMEM((z.rows, z.half, z.pad), f32),
        pltpu.VMEM((z.rows + 2, z.half, lon), f32),
    ]
    mine, own_winds, own_code, u = pl.pallas_call(
        functools.partial(own_kernel, z),
        name="own",
        in_specs=[scalars()] + [whole()] * 6,
        out_specs=[whole()] * 4,
        out_shape=[
            shape(z.rows, 2, z.half, z.pad),
            shape(3 * z.rows + 1, z.half, lon),
            codes(tall, 2 * z.code),
            shape(z.band + 4, 2, z.half, z.pad),
        ],
        scratch_shapes=half_scratch,
        compiler_params=params(),
        cost_estimate=cost(),
    )(place, fields, courant, edge, middle, near, far)
    near_code = lax.ppermute(own_code, "lat", near_pairs)
    other, other_winds, other_code = pl.pallas_call(
        functools.partial(other_kernel, z),
        name="other",
        in_specs=[scalars()] + [whole()] * 6,
        out_specs=[whole()] * 3,
        out_shape=[
            shape(2, 2, z.half, z.pad),
            shape(3 * z.rows + 1, z.half, lon),
            codes(tall, 2 * z.code),
        ],
        scratch_shapes=half_scratch,
        compiler_params=params(),
        cost_estimate=cost(),
    )(place, courant, edge, middle, last, near, u)
    far_code = lax.ppermute(other_code, "lat", far_pairs)

    tables = jnp.asarray(filter_tables(lon))
    new, inner = pl.pallas_call(
        functools.partial(inner_kernel, z),
        name="inner",
        in_specs=[scalars(), scalars()] + [whole()] * 6,
        out_specs=[whole()] * 2,
        out_shape=[shape(z.band, 2, z.half, z.pad), shape(z.rows, 2, z.half, lon)],
        compiler_params=params(),
        cost_estimate=cost(),
    )(place, cutoffs, mine, other, u, own_winds, other_winds, tables)

    column = lon // parts
    blocks = pl.pallas_call(
        functools.partial(outer_kernel, z, parts),
        name="outer",
        in_specs=[scalars(), scalars()] + [whole()] * 7,
        out_specs=[whole()] * (2 * parts),
        out_shape=[codes(tall, rows * column + LANE)] * (2 * parts),
        scratch_shapes=[
            pltpu.VMEM((6, 2, z.half, z.pad), f32),
            pltpu.VMEM((z.rows, 2, z.half, lon), f32),
        ],
        compiler_params=params(),
        cost_estimate=cost(),
    )(place, cutoffs, new, inner, own_winds, other_winds, near_code, far_code, tables)
    got = []
    for i, block in enumerate(blocks):
        b, across = i % parts, int(i < parts)
        pairs = [
            (k * parts + j, (k ^ across) * parts + (j ^ b)) for k in range(lats) for j in range(parts)
        ]
        got.append(lax.ppermute(block, ("lat", "lev"), pairs) if i != parts else block)
    far = [i for i in range(parts) if i % 2 == 0]
    scales = pl.pallas_call(
        functools.partial(scale_kernel, rows * column),
        name="scales",
        in_specs=[whole()] * len(far),
        out_specs=whole(),
        out_shape=shape(len(far), tall, LANE),
        compiler_params=params(),
        cost_estimate=cost(),
    )(*[got[i] for i in far])

    count = remap_weights.shape[0]
    upward = np.triu(np.ones((count, count), np.float32), 1) + 0.5 * np.eye(count, dtype=np.float32)
    upward = jnp.asarray(np.concatenate([upward, 0.0 * upward, upward], axis=1))
    surface = lax.dynamic_slice_in_dim(surface, lev * column, column, 1)
    remapped, geopotential = pl.pallas_call(
        functools.partial(column_kernel, z, parts, far),
        name="columns",
        in_specs=[scalars()] + [whole()] * (len(got) + 4),
        out_specs=[far_memory()] * 2,
        out_shape=[shape(2, rows, count, column), shape(rows, count, column)],
        scratch_shapes=[
            pltpu.VMEM((rows, 2, count, column), f32),
            pltpu.VMEM((2, rows, count, column), f32),
            pltpu.VMEM((rows, count, column), f32),
            pltpu.SemaphoreType.DMA((3 * rows,)),
        ],
        compiler_params=params(),
        cost_estimate=cost(),
    )(place, *got, scales, remap_weights, upward, surface[:, None, :])
    return remapped, geopotential


def with_halo(shard, width):
    size, length = lax.axis_size("lat"), shard.shape[1]
    up = [(i, (i + 1) % size) for i in range(size - 1)]
    down = [(j, i) for i, j in up]
    before = lax.ppermute(lax.slice_in_dim(shard, length - width, length, axis=1), "lat", up)
    after = lax.ppermute(lax.slice_in_dim(shard, 0, width, axis=1), "lat", down)
    return jnp.concatenate([before, shard, after], axis=1)


def plain_shards(fields, courant, cutoffs, surface, remap_weights):
    _, rows, _, lon = fields.shape
    exact = lax.Precision.HIGHEST
    cut = lax.dynamic_slice_in_dim(cutoffs, lax.axis_index("lat") * rows, rows)
    waves = np.arange(KMAX)
    angle = (np.arange(lon)[:, None] * waves[None, :] % lon) * (2.0 * math.pi / lon)
    table = jnp.asarray(np.concatenate([np.cos(angle), np.sin(angle)], axis=1).astype(np.float32))
    number = jnp.asarray(np.concatenate([waves, waves]).astype(np.int32))
    weight = jnp.where(number[None] <= cut[:, None], jnp.where(number == 0, 1.0, 2.0)[None] / lon, 0.0)
    flagged = cut < lon // 2

    def smooth(values):
        wave = jnp.einsum("frln,nk->frlk", values, table, precision=exact) * weight[None, :, None]
        low = jnp.einsum("frlk,nk->frln", wave, table, precision=exact)
        return jnp.where(flagged[None, :, None, None], low, values)

    winds = with_halo(courant, 1).astype(jnp.float32)
    east, north = winds[0, 1:-1], winds[1]
    face_x = (east + jnp.roll(east, -1, -1)) / 24.0
    face_y = (north[:-1] + north[1:]) / 24.0
    u = fields
    for _ in range(2):
        wide = with_halo(u, 2)
        pair = u + jnp.roll(u, -1, -1)
        fx = face_x * (8.0 * pair - (jnp.roll(pair, 1, -1) + jnp.roll(pair, -1, -1)))
        pair = wide[:, :-1] + wide[:, 1:]
        fy = face_y * (8.0 * pair[:, 1:-1] - (pair[:, :-2] + pair[:, 2:]))
        u = u - (fx - jnp.roll(fx, 1, -1)) - (fy[:, 1:] - fy[:, :-1])
        u = lax.cond(jnp.any(flagged), smooth, lambda values: values, u)
    columns = lax.all_to_all(u, "lev", split_axis=3, concat_axis=2, tiled=True)
    remapped = jnp.einsum("pk,fjkn->fjpn", remap_weights, columns, precision=exact)
    count = remap_weights.shape[0]
    upward = np.triu(np.ones((count, count), np.float32), 1) + 0.5 * np.eye(count, dtype=np.float32)
    upward = jnp.einsum("kl,jln->jkn", jnp.asarray(upward), columns[1], precision=exact)
    width = lon // lax.axis_size("lev")
    mine = lax.dynamic_slice_in_dim(surface, lax.axis_index("lev") * width, width, 1)
    return remapped, mine[:, None] + count**-0.5 * upward


def solution(mesh):
    def program(fields, courant, cutoffs, surface, remap_weights):
        lats, parts = mesh.shape["lat"], mesh.shape["lev"]
        rows, levels = fields.shape[1] // lats, fields.shape[2] // parts
        polar = fields.shape[1] // 8
        paired = (
            lats % 2 == 0
            and rows == 4
            and levels % 16 == 0
            and polar <= 2 * rows - 2
            and fields.shape[3] % (LANE * parts) == 0
            and parts & (parts - 1) == 0
            and fields.shape[3] % (4 * KMAX) == 0
        )
        return jax.shard_map(
            shards if paired else plain_shards,
            mesh=mesh,
            in_specs=(
                P(None, "lat", "lev", None),
                P(None, "lat", "lev", None),
                P(),
                P("lat", None),
                P(),
            ),
            out_specs=(P(None, "lat", None, "lev"), P("lat", None, "lev")),
            check_vma=False,
        )(fields, courant, cutoffs, surface, remap_weights)

    return program
```

```python
import functools
import math

import jax
import jax.numpy as jnp
import ml_dtypes
import numpy as np
from jax import lax
from jax.experimental import pallas as pl
from jax.experimental.pallas import tpu as pltpu
from jax.sharding import PartitionSpec as P

KMAX = 128
LANE = 128
TOP = 32767.0
STEPS = 256.0
TINY = 2.0**-100
WIND = 81920.0
ROUND = 1.5 * 2.0**23
VMEM_LIMIT = 12 * 2**20
VMEM_MOST = 63 * 2**20 + 2**19


def rounded(values):
    return ((values + ROUND) - ROUND).astype(jnp.int32).astype(jnp.int16)


def lane_max(values):
    chunks = [jnp.abs(values[:, i : i + LANE]) for i in range(0, values.shape[1], LANE)]
    while len(chunks) > 1:
        pairs = [jnp.maximum(a, b) for a, b in zip(chunks[0::2], chunks[1::2])]
        chunks = pairs + chunks[2 * len(pairs) :]
    return chunks[0]


def tiled(tile, width):
    return jnp.concatenate([tile] * (width // LANE), axis=1)


def scale_code(largest):
    return jnp.ceil(jnp.log2(jnp.maximum(largest, TINY)) * STEPS)


def encoder(code):
    return TOP / jnp.exp2(code * (1.0 / STEPS))


def decoder(code16):
    code = code16.astype(jnp.int32).astype(jnp.float32)
    return jnp.exp2(code * (1.0 / STEPS)) * (1.0 / TOP)


def encode_row(values, out_ref, at):
    width = values.shape[1]
    code = scale_code(lane_max(values))
    out_ref[:, at : at + width] = rounded(values * tiled(encoder(code), width))
    out_ref[:, at + width : at + width + LANE] = code.astype(jnp.int32).astype(jnp.int16)


def decode_row(in_ref, at, width):
    scale = decoder(in_ref[:, at + width : at + width + LANE])
    values = in_ref[:, at : at + width].astype(jnp.int32).astype(jnp.float32)
    return values * tiled(scale, width)


def fold(wind):
    middle = wind.shape[1] // 2
    return jnp.concatenate([wind[:, :middle], wind[:, middle:]], axis=0)


def unfold(values):
    half = values.shape[0] // 2
    return jnp.concatenate([values[:half], values[half:]], axis=1)


def wind_codes(values):
    return rounded(values * WIND)


def wind_values(codes):
    return codes.astype(jnp.int32).astype(jnp.float32) * (1.0 / WIND)


class Sizes:
    def __init__(self, rows, levels, lon):
        self.rows, self.levels, self.lon = rows, levels, lon
        self.half = levels // 2
        self.band = 2 * rows
        self.pad = lon + 2 * LANE
        self.code = lon + LANE
        self.edge = 2 * self.code + lon // 2
        self.middle = self.edge + lon // 2
        self.last = 2 * lon + lon // 2


def put_padded(ref, index, values, lon):
    ref[index + (Ellipsis, slice(LANE, LANE + lon))] = values
    ref[index + (Ellipsis, slice(0, LANE))] = values[..., lon - LANE :]
    ref[index + (Ellipsis, slice(LANE + lon, 2 * LANE + lon))] = values[..., :LANE]


def level_half(z, wind, upper):
    wind = wind.astype(jnp.float32)
    return jnp.where(upper == 1, wind[z.half :], wind[: z.half])


def edge_kernel(z, fields_ref, courant_ref, edge_ref, rows_ref, wind_ref, sems):
    p = lax.rem(lax.axis_index("lat"), 2)
    give = pl.multiple_of((1 - p) * z.half, z.half)
    copies = [
        pltpu.make_async_copy(
            fields_ref.at[f, 2 * p + r, pl.ds(give, z.half)],
            rows_ref.at[r, pl.ds(f * z.half, z.half)],
            sems.at[2 * r + f],
        )
        for r in range(2)
        for f in range(2)
    ]
    copies.append(pltpu.make_async_copy(courant_ref.at[1, 3 * p], wind_ref, sems.at[4]))
    for copy in copies:
        copy.start()
    for r in range(2):
        copies[2 * r].wait()
        copies[2 * r + 1].wait()
        encode_row(rows_ref[r], edge_ref, r * z.code)
    copies[4].wait()
    edge_ref[:, 2 * z.code :] = wind_codes(fold(level_half(z, wind_ref[...], 1 - p)))


def rest_kernel(z, par_ref, fields_ref, courant_ref, middle_ref, last_ref, own_ref):
    p = par_ref[0]
    keep = pl.multiple_of(p * z.half, z.half)
    give = pl.multiple_of((1 - p) * z.half, z.half)

    def field_row(row, start):
        return jnp.concatenate([fields_ref[f, row, pl.ds(start, z.half)] for f in range(2)], axis=0)

    def wind(k, row, upper):
        return level_half(z, courant_ref[k, row], upper)

    edge, inner = 2 * p, 2 * (1 - p)
    outer, near = 3 * p, 3 * (1 - p)
    for r in range(2):
        encode_row(field_row(edge + r, keep), own_ref, r * z.code)
        encode_row(field_row(inner + r, give), middle_ref, r * z.code)
    own_ref[:, 2 * z.code :] = wind_codes(fold(wind(1, outer, p)))
    lon = z.lon
    middle_ref[:, 2 * z.code : z.edge] = wind_codes(fold(wind(1, near, 1 - p)))
    middle_ref[:, z.edge :] = wind_codes(fold(wind(0, near, 1 - p)))
    last_ref[:, 2 * lon :] = wind_codes(fold(wind(0, outer, 1 - p)))
    for r in range(2):
        both = jnp.concatenate([wind(k, 1 + r, 1 - p) for k in range(2)], axis=0)
        last_ref[:, r * lon : (r + 1) * lon] = wind_codes(both)


def shifted(pieces, shift, lanes):
    turned = [pltpu.roll(v, (-shift) % LANE, 1) for v in pieces]
    if shift > 0:
        return [jnp.where(lanes < LANE - shift, a, b) for a, b in zip(turned[1:-1], turned[2:])]
    return [jnp.where(lanes < -shift, a, b) for a, b in zip(turned[:-2], turned[1:-1])]


def substep(z, count_rows, base, row_of, winds_ref, write):
    count = next(n for n in (4, 3, 2, 1) if z.lon % (n * LANE) == 0)
    width = count * LANE
    lanes = lax.broadcasted_iota(jnp.int32, (z.half, LANE), 1)

    def part(at):
        def piece(k):
            return pl.ds(at + k * LANE, LANE)

        def row(j, f):
            return [row_of(j, f, piece(k + 1)) for k in range(count)]

        def start(j, f):
            pieces = [row_of(j + 2, f, piece(k)) for k in range(count + 2)]
            return [shifted(pieces, s, lanes) for s in (-2, -1, 1, 2)]

        def lon_part(j, u, moved):
            out = []
            for k in range(count):
                m2, m1, p1, p2 = (m[k] for m in moved)
                east = 7.0 * (u[k] + p1) - (m1 + p2)
                west = 7.0 * (m1 + u[k]) - (m2 + p1)
                east = winds_ref[base + j, :, piece(k)] * east
                out.append(east - winds_ref[z.rows + base + j, :, piece(k)] * west)
            return out

        for f in range(2):
            rows = [row(j, f) for j in range(4)]
            sums = [[a + b for a, b in zip(rows[j], rows[j + 1])] for j in range(3)]
            flux = None
            moved = start(0, f)
            for j in range(count_rows + 1):
                later = start(j, f) if 0 < j < count_rows else None
                new = [
                    winds_ref[2 * z.rows + base + j, :, piece(k)] * (8.0 * sums[1][k] - (sums[0][k] + sums[2][k]))
                    for k in range(count)
                ]
                if j > 0:
                    u = rows[1]
                    change = lon_part(j - 1, u, moved)
                    for k in range(count):
                        write(j - 1, f, at, k, u[k] - change[k] - (new[k] - flux[k]))
                    moved = later
                flux = new
                if j < count_rows:
                    above = row(j + 4, f)
                    rows = rows[1:] + [above]
                    sums = sums[1:] + [[a + b for a, b in zip(rows[2], rows[3])]]

    for i in range(z.lon // width):
        part(i * width)


def filter_tables(lon):
    half = lon // 2
    points = np.arange(half)
    forward, back = [], []
    for parity in range(2):
        waves = np.arange(parity, KMAX, 2)
        angle = (points[:, None] * waves[None, :] % lon) * (2.0 * math.pi / lon)
        table = np.concatenate([np.cos(angle), np.sin(angle)], axis=1).astype(np.float32)
        high = table.astype(ml_dtypes.bfloat16)
        low = (table - high.astype(np.float32)).astype(ml_dtypes.bfloat16)
        forward.append(np.concatenate([high, low], axis=1))
        turned = np.concatenate([high.T, low.T], axis=0)
        back.append(np.concatenate(np.split(turned, half // (2 * KMAX), axis=1), axis=0))
    return np.stack(forward + back)


def split(values):
    high = values.astype(jnp.bfloat16)
    return high, (values - high.astype(jnp.float32)).astype(jnp.bfloat16)


def low_pass(z, rows, cuts, table_ref):
    half = z.lon // 2
    count = len(rows)
    tall = 2 * z.half
    total = count * tall
    flat = [row.reshape(tall, z.lon) for row in rows]
    folded = []
    for parity in range(2):
        parts = [
            row[:, :half] + row[:, half:] if parity == 0 else row[:, :half] - row[:, half:]
            for row in flat
        ]
        high, low = split(jnp.concatenate(parts, axis=0))
        both = jnp.concatenate([high, low], axis=0)
        got = jnp.dot(both, table_ref[parity], preferred_element_type=jnp.float32)
        wave = got[:total, :KMAX] + got[:total, KMAX:] + (got[total:, :KMAX] + got[total:, KMAX:])
        number = 2 * (lax.broadcasted_iota(jnp.int32, (tall, KMAX), 1) % (KMAX // 2)) + parity
        doubled = jnp.where(number == 0, 1.0, 2.0) * (1.0 / z.lon)
        weight = jnp.concatenate([jnp.where(number <= cut, doubled, 0.0) for cut in cuts], axis=0)
        high, low = split(wave * weight)
        both = jnp.concatenate(
            [jnp.concatenate([high, high], axis=1), jnp.concatenate([low, low], axis=1)], axis=0
        )
        got = []
        for at in range(0, half, 2 * KMAX):
            block = table_ref[2 + parity, at : at + 2 * KMAX]
            sums = jnp.dot(both, block, preferred_element_type=jnp.float32)
            got.append(sums[:total] + sums[total:])
        folded.append(jnp.concatenate(got, axis=1))
    left, right = folded[0] + folded[1], folded[0] - folded[1]
    smooth = jnp.concatenate([left, right], axis=1)
    return [smooth[i * tall : (i + 1) * tall].reshape(2, z.half, z.lon) for i in range(count)]


def filter_rows(z, cut_ref, first_row, start, table_ref, load, store):
    nyquist = z.lon // 2
    cuts = [cut_ref[first_row + start + r] for r in range(z.rows)]
    some = functools.reduce(jnp.logical_or, [cut < nyquist for cut in cuts])

    @pl.when(some)
    def _():
        smooth = low_pass(z, [load(start + r) for r in range(z.rows)], cuts, table_ref)
        for r in range(z.rows):

            @pl.when(cuts[r] < nyquist)
            def _():
                store(start + r, smooth[r])


def north_wind(z, in_ref):
    return unfold(wind_values(in_ref[:, 2 * z.code : z.edge]))


def faces(z, cx_ref, cy_ref, winds_ref):
    lanes = lax.broadcasted_iota(jnp.int32, (z.half, LANE), 1)
    for j in range(z.rows):
        pieces = [cx_ref[j, :, i : i + LANE] * (1.0 / 24.0) for i in range(0, z.pad, LANE)]
        for out, shift in ((j, 1), (z.rows + j, -1)):
            for k, moved in enumerate(shifted(pieces, shift, lanes)):
                winds_ref[out, :, k * LANE : (k + 1) * LANE] = pieces[k + 1] + moved
    for j in range(z.rows + 1):
        winds_ref[2 * z.rows + j] = (cy_ref[j] + cy_ref[j + 1]) * (1.0 / 24.0)


def writer(new_ref):
    def write(row, f, at, k, values):
        new_ref[row, f, :, pl.ds(at + (k + 1) * LANE, LANE)] = values

    return write


def wrap(z, new_ref, rows):
    for j in rows:
        new_ref[j, :, :, 0:LANE] = new_ref[j, :, :, z.lon : z.lon + LANE]
        new_ref[j, :, :, LANE + z.lon :] = new_ref[j, :, :, LANE : 2 * LANE]


def encode_new(z, new_ref, row, out_ref):
    for r in range(2):
        values = new_ref[row + r, :, :, LANE : LANE + z.lon]
        encode_row(values.reshape(2 * z.half, z.lon), out_ref, r * z.code)


def place_row(z, u_ref, row, in_ref, r):
    values = decode_row(in_ref, r * z.code, z.lon)
    put_padded(u_ref, (row + r,), values.reshape(2, z.half, z.lon), z.lon)


def own_kernel(
    z, par_ref, fields_ref, courant_ref, edge_ref, middle_ref, near_ref, far_ref,
    new_ref, winds_ref, code_ref, u_ref, cx_ref, cy_ref,
):
    p = par_ref[0]
    lon, half = z.lon, z.half
    keep = pl.multiple_of(p * half, half)
    for r in range(z.rows):
        own = jnp.stack([fields_ref[f, r, pl.ds(keep, half)] for f in range(2)])
        put_padded(u_ref, (z.rows * p + r + 2,), own, lon)
        put_padded(cx_ref, (r,), level_half(z, courant_ref[0, r], p), lon)
        cy_ref[r + 1] = level_half(z, courant_ref[1, r], p)
    for r in range(2):
        place_row(z, u_ref, 6 * (1 - p) + 2, edge_ref, r)
        place_row(z, u_ref, 4 - 2 * p + 2, middle_ref, r)
        place_row(z, u_ref, 10 * (1 - p), near_ref, r)
        place_row(z, u_ref, 10 * p, far_ref, r)
    cy_ref[5 * (1 - p)] = north_wind(z, middle_ref)
    cy_ref[5 * p] = north_wind(z, far_ref)
    faces(z, cx_ref, cy_ref, winds_ref)
    start = z.rows * p
    substep(z, z.rows, 0, lambda j, f, piece: u_ref[start + j, f, :, piece], winds_ref, writer(new_ref))
    encode_new(z, new_ref, 2 * p, code_ref)
    wrap(z, new_ref, range(z.rows))


def other_kernel(
    z, par_ref, courant_ref, edge_ref, middle_ref, last_ref, near_ref, u_ref, own_code_ref,
    new_ref, winds_ref, one_ref, two_ref, cx_ref, cy_ref,
):
    p = par_ref[0]
    lon, half = z.lon, z.half
    for r in range(2):
        both = wind_values(last_ref[:, r * lon : (r + 1) * lon])
        put_padded(cx_ref, (1 + r,), both[:half], lon)
        cy_ref[2 + r] = both[half:]
    easts = (last_ref[:, 2 * lon :], middle_ref[:, z.edge :])
    for east, row, in_ref in zip(easts, (3 * (1 - p), 3 * p), (edge_ref, middle_ref)):
        put_padded(cx_ref, (row,), unfold(wind_values(east)), lon)
        cy_ref[row + 1] = north_wind(z, in_ref)
    cy_ref[5 * p] = level_half(z, courant_ref[1, 3 * (1 - p)], p)
    cy_ref[5 * (1 - p)] = north_wind(z, near_ref)
    faces(z, cx_ref, cy_ref, winds_ref)
    outer = 2 * (1 - p)
    start = z.rows * (1 - p) + outer
    substep(z, 2, outer, lambda j, f, piece: u_ref[start + j, f, :, piece], winds_ref, writer(new_ref))

    def put_codes(own_ref, other_ref):
        own_ref[...] = own_code_ref[...]
        encode_new(z, new_ref, 0, other_ref)

    swapped = p + par_ref[3] == 1
    pl.when(swapped)(lambda: put_codes(one_ref, two_ref))
    pl.when(jnp.logical_not(swapped))(lambda: put_codes(two_ref, one_ref))
    wrap(z, new_ref, range(2))


def inner_kernel(
    z, par_ref, cut_ref, own_ref, other_ref, u_ref, own_winds_ref, other_winds_ref, table_ref, new_ref, inner_ref
):
    p = par_ref[0]
    own, other = z.rows * p, z.rows * (1 - p)
    for j in range(z.rows):
        new_ref[own + j] = own_ref[j]
    for j in range(2):
        new_ref[other + 2 * (1 - p) + j] = other_ref[j]
    start = other + 2 * p

    def write(row, f, at, k, values):
        writer(new_ref)(start + row, f, at, k, values)

    substep(z, 2, 2 * p, lambda j, f, piece: u_ref[start + j, f, :, piece], other_winds_ref, write)
    wrap(z, new_ref, (start, start + 1))

    def store(row, values):
        put_padded(new_ref, (row,), values, z.lon)

    for part in range(2):
        filter_rows(
            z, cut_ref, par_ref[1], part * z.rows, table_ref,
            lambda row: new_ref[row, :, :, LANE : LANE + z.lon], store,
        )
    for i, (low, base, winds_ref) in enumerate(
        ((2 * p, 2 * (1 - p), own_winds_ref), (2 * (1 - p), 2 * p, other_winds_ref))
    ):

        def keep(row, f, at, k, values):
            inner_ref[2 * i + row, f, :, pl.ds(at + k * LANE, LANE)] = values

        substep(z, 2, base, lambda j, f, piece: new_ref[low + j, f, :, piece], winds_ref, keep)


def outer_kernel(
    z, parts, par_ref, cut_ref, new_ref, inner_ref, own_winds_ref, other_winds_ref, one_ref, two_ref, table_ref, *refs
):
    out_refs, scratch = refs[: 2 * parts], refs[2 * parts :]
    p = par_ref[0]
    halos = (one_ref, two_ref)
    outer_half(
        z, parts, 1 - p, 2, par_ref, cut_ref, new_ref, inner_ref, other_winds_ref, halos, table_ref,
        out_refs[:parts], *scratch,
    )
    outer_half(
        z, parts, p, 0, par_ref, cut_ref, new_ref, inner_ref, own_winds_ref, halos, table_ref,
        out_refs[parts:], *scratch,
    )


def outer_half(
    z, parts, side, inner_at, par_ref, cut_ref, new_ref, inner_ref, winds_ref, halos, table_ref,
    out_refs, u_ref, v_ref,
):
    lon = z.lon
    tall = 2 * z.half
    base = z.rows * side

    def halo(in_ref):
        for r in range(2):
            place_row(z, u_ref, 4 * side, in_ref, r)

    first_swap = side + par_ref[3] == 1
    pl.when(first_swap)(lambda: halo(halos[0]))
    pl.when(jnp.logical_not(first_swap))(lambda: halo(halos[1]))
    for r in range(4):
        u_ref[2 * (1 - side) + r] = new_ref[base + r]
    for r in range(2):
        v_ref[2 * (1 - side) + r] = inner_ref[inner_at + r]

    def write(row, f, at, k, values):
        v_ref[2 * side + row, f, :, pl.ds(at + k * LANE, LANE)] = values

    substep(z, 2, 2 * side, lambda j, f, piece: u_ref[j, f, :, piece], winds_ref, write)

    def store(row, values):
        v_ref[row] = values

    filter_rows(z, cut_ref, par_ref[1] + base, 0, table_ref, lambda row: v_ref[row], store)
    column = lon // parts
    for b in range(parts):
        at = pl.multiple_of(jnp.bitwise_xor(par_ref[2], b) * column, LANE)
        values = jnp.concatenate(
            [v_ref[r, :, :, pl.ds(at, column)].reshape(tall, column) for r in range(z.rows)], axis=1
        )
        encode_row(values, out_refs[b], 0)


def scale_kernel(at, *refs):
    for i, ref in enumerate(refs[:-1]):
        refs[-1][i] = decoder(ref[:, at : at + LANE])


def column_kernel(z, parts, far, par_ref, *refs):
    got, refs = refs[: 2 * parts], refs[2 * parts :]
    scales_ref, remap_ref, upward_ref, surface_ref, out_ref, geo_ref, x_ref, sums_ref, geo_sums_ref, sems = refs
    p, lev = par_ref[0], par_ref[2]
    count, column = sums_ref.shape[-2:]
    high, low = split(remap_ref[...])
    remap = jnp.concatenate([high, low, high], axis=1)
    both = jnp.concatenate([remap, upward_ref[...].astype(jnp.bfloat16)], axis=0)
    scales = [
        scales_ref[far.index(i)] if i in far else decoder(ref[:, z.rows * column :])
        for i, ref in enumerate(got)
    ]
    copies = []
    for row in range(z.rows):
        for i, ref in enumerate(got):
            side = 1 - p if i < parts else p
            s = jnp.bitwise_xor(lev, i % parts)
            codes = ref[:, row * column : (row + 1) * column].astype(jnp.int32).astype(jnp.float32)
            values = codes * tiled(scales[i], column)
            level = pl.multiple_of(s * z.levels + side * z.half, z.half)
            for f in range(2):
                x_ref[row, f, pl.ds(level, z.half)] = values[f * z.half : (f + 1) * z.half]
        for f in range(2):
            high, low = split(x_ref[row, f])
            stacked = jnp.concatenate([high, high, low], axis=0)
            result = jnp.dot(both if f else remap, stacked, preferred_element_type=jnp.float32)
            sums_ref[f, row] = result[:count]
            if f:
                geo_sums_ref[row] = surface_ref[row] + result[count:] * (count**-0.5)
        parts_out = [(sums_ref.at[f, row], out_ref.at[f, row]) for f in range(2)]
        parts_out.append((geo_sums_ref.at[row], geo_ref.at[row]))
        for k, (a, b) in enumerate(parts_out):
            copies.append(pltpu.make_async_copy(a, b, sems.at[3 * row + k]))
            copies[-1].start()
    for copy in copies:
        copy.wait()


def whole():
    return pl.BlockSpec(memory_space=pltpu.VMEM)


def scalars():
    return pl.BlockSpec(memory_space=pltpu.SMEM)


def far_memory():
    return pl.BlockSpec(memory_space=pltpu.HBM)


def params(limit=VMEM_LIMIT):
    return pltpu.CompilerParams(vmem_limit_bytes=limit)


def cost(flops=1000, data=1000):
    return pl.CostEstimate(flops=flops, bytes_accessed=data, transcendentals=0)


def shards(fields, courant, cutoffs, surface, remap_weights):
    _, rows, levels, lon = fields.shape
    z = Sizes(rows, levels, lon)
    lats, parts = lax.axis_size("lat"), lax.axis_size("lev")
    me = lax.axis_index("lat")
    parity = me % 2
    lev = lax.axis_index("lev")
    place = jnp.stack([parity, (me - parity) * rows, lev, (me // 2) % 2]).astype(jnp.int32)
    tall = 2 * z.half
    i16, f32 = jnp.int16, jnp.float32
    swap = [(i, i ^ 1) for i in range(lats)]
    rising = [(i, i + 2) for i in range(lats - 2)]
    near_pairs = [(i, j) if i % 2 else (j, i) for i, j in rising]
    far_pairs = [(j, i) if i % 2 else (i, j) for i, j in rising]

    ones, twos = [
        [pair for i, j in rising if i // 2 % 2 == odd for pair in ((i, j), (j, i))] for odd in range(2)
    ]

    def shape(*dims):
        return jax.ShapeDtypeStruct(dims, f32)

    def codes(*dims):
        return jax.ShapeDtypeStruct(dims, i16)

    edge = pl.pallas_call(
        functools.partial(edge_kernel, z),
        name="edge",
        in_specs=[far_memory(), far_memory()],
        out_specs=whole(),
        out_shape=codes(tall, z.edge),
        scratch_shapes=[
            pltpu.VMEM((2, tall, lon), f32),
            pltpu.VMEM((levels, lon), courant.dtype),
            pltpu.SemaphoreType.DMA((5,)),
        ],
        compiler_params=params(VMEM_MOST),
        cost_estimate=cost(),
    )(fields, courant)
    edge = lax.ppermute(edge, "lat", swap)
    middle, last, own = pl.pallas_call(
        functools.partial(rest_kernel, z),
        name="rest",
        in_specs=[scalars(), whole(), whole()],
        out_specs=[whole()] * 3,
        out_shape=[codes(tall, z.middle), codes(tall, z.last), codes(tall, z.edge)],
        compiler_params=params(),
        cost_estimate=cost(),
    )(place, fields, courant)
    near = lax.ppermute(own, "lat", near_pairs)
    middle = lax.ppermute(middle, "lat", swap)
    far = lax.ppermute(edge, "lat", far_pairs)
    last = lax.ppermute(last, "lat", swap)

    half_scratch = [
        pltpu.VMEM((z.rows, z.half, z.pad), f32),
        pltpu.VMEM((z.rows + 2, z.half, lon), f32),
    ]
    mine, own_winds, own_code, u = pl.pallas_call(
        functools.partial(own_kernel, z),
        name="own",
        in_specs=[scalars()] + [whole()] * 6,
        out_specs=[whole()] * 4,
        out_shape=[
            shape(z.rows, 2, z.half, z.pad),
            shape(3 * z.rows + 1, z.half, lon),
            codes(tall, 2 * z.code),
            shape(z.band + 4, 2, z.half, z.pad),
        ],
        scratch_shapes=half_scratch,
        compiler_params=params(),
        cost_estimate=cost(),
    )(place, fields, courant, edge, middle, near, far)
    other, other_winds, one, two = pl.pallas_call(
        functools.partial(other_kernel, z),
        name="other",
        in_specs=[scalars()] + [whole()] * 7,
        out_specs=[whole()] * 4,
        out_shape=[
            shape(2, 2, z.half, z.pad),
            shape(3 * z.rows + 1, z.half, lon),
            codes(tall, 2 * z.code),
            codes(tall, 2 * z.code),
        ],
        scratch_shapes=half_scratch,
        compiler_params=params(),
        cost_estimate=cost(),
    )(place, courant, edge, middle, last, near, u, own_code)
    one = lax.ppermute(one, "lat", ones)
    two = lax.ppermute(two, "lat", twos)

    tables = jnp.asarray(filter_tables(lon))
    new, inner = pl.pallas_call(
        functools.partial(inner_kernel, z),
        name="inner",
        in_specs=[scalars(), scalars()] + [whole()] * 6,
        out_specs=[whole()] * 2,
        out_shape=[shape(z.band, 2, z.half, z.pad), shape(z.rows, 2, z.half, lon)],
        compiler_params=params(),
        cost_estimate=cost(),
    )(place, cutoffs, mine, other, u, own_winds, other_winds, tables)

    column = lon // parts
    blocks = pl.pallas_call(
        functools.partial(outer_kernel, z, parts),
        name="outer",
        in_specs=[scalars(), scalars()] + [whole()] * 7,
        out_specs=[whole()] * (2 * parts),
        out_shape=[codes(tall, rows * column + LANE)] * (2 * parts),
        scratch_shapes=[
            pltpu.VMEM((6, 2, z.half, z.pad), f32),
            pltpu.VMEM((z.rows, 2, z.half, lon), f32),
        ],
        compiler_params=params(),
        cost_estimate=cost(),
    )(place, cutoffs, new, inner, own_winds, other_winds, one, two, tables)
    got = []
    for i, block in enumerate(blocks):
        b, across = i % parts, int(i < parts)
        pairs = [
            (k * parts + j, (k ^ across) * parts + (j ^ b)) for k in range(lats) for j in range(parts)
        ]
        got.append(lax.ppermute(block, ("lat", "lev"), pairs) if i != parts else block)
    far = [i for i in range(2 * parts) if i % 2 == 0 and i != parts]
    scales = pl.pallas_call(
        functools.partial(scale_kernel, rows * column),
        name="scales",
        in_specs=[whole()] * len(far),
        out_specs=whole(),
        out_shape=shape(len(far), tall, LANE),
        compiler_params=params(),
        cost_estimate=cost(),
    )(*[got[i] for i in far])

    count = remap_weights.shape[0]
    upward = np.triu(np.ones((count, count), np.float32), 1) + 0.5 * np.eye(count, dtype=np.float32)
    upward = jnp.asarray(np.concatenate([upward, 0.0 * upward, upward], axis=1))
    surface = lax.dynamic_slice_in_dim(surface, lev * column, column, 1)
    remapped, geopotential = pl.pallas_call(
        functools.partial(column_kernel, z, parts, far),
        name="columns",
        in_specs=[scalars()] + [whole()] * (len(got) + 4),
        out_specs=[far_memory()] * 2,
        out_shape=[shape(2, rows, count, column), shape(rows, count, column)],
        scratch_shapes=[
            pltpu.VMEM((rows, 2, count, column), f32),
            pltpu.VMEM((2, rows, count, column), f32),
            pltpu.VMEM((rows, count, column), f32),
            pltpu.SemaphoreType.DMA((3 * rows,)),
        ],
        compiler_params=params(),
        cost_estimate=cost(),
    )(place, *got, scales, remap_weights, upward, surface[:, None, :])
    return remapped, geopotential


def with_halo(shard, width):
    size, length = lax.axis_size("lat"), shard.shape[1]
    up = [(i, (i + 1) % size) for i in range(size - 1)]
    down = [(j, i) for i, j in up]
    before = lax.ppermute(lax.slice_in_dim(shard, length - width, length, axis=1), "lat", up)
    after = lax.ppermute(lax.slice_in_dim(shard, 0, width, axis=1), "lat", down)
    return jnp.concatenate([before, shard, after], axis=1)


def plain_shards(fields, courant, cutoffs, surface, remap_weights):
    _, rows, _, lon = fields.shape
    exact = lax.Precision.HIGHEST
    cut = lax.dynamic_slice_in_dim(cutoffs, lax.axis_index("lat") * rows, rows)
    waves = np.arange(KMAX)
    angle = (np.arange(lon)[:, None] * waves[None, :] % lon) * (2.0 * math.pi / lon)
    table = jnp.asarray(np.concatenate([np.cos(angle), np.sin(angle)], axis=1).astype(np.float32))
    number = jnp.asarray(np.concatenate([waves, waves]).astype(np.int32))
    weight = jnp.where(number[None] <= cut[:, None], jnp.where(number == 0, 1.0, 2.0)[None] / lon, 0.0)
    flagged = cut < lon // 2

    def smooth(values):
        wave = jnp.einsum("frln,nk->frlk", values, table, precision=exact) * weight[None, :, None]
        low = jnp.einsum("frlk,nk->frln", wave, table, precision=exact)
        return jnp.where(flagged[None, :, None, None], low, values)

    winds = with_halo(courant, 1).astype(jnp.float32)
    east, north = winds[0, 1:-1], winds[1]
    face_x = (east + jnp.roll(east, -1, -1)) / 24.0
    face_y = (north[:-1] + north[1:]) / 24.0
    u = fields
    for _ in range(2):
        wide = with_halo(u, 2)
        pair = u + jnp.roll(u, -1, -1)
        fx = face_x * (8.0 * pair - (jnp.roll(pair, 1, -1) + jnp.roll(pair, -1, -1)))
        pair = wide[:, :-1] + wide[:, 1:]
        fy = face_y * (8.0 * pair[:, 1:-1] - (pair[:, :-2] + pair[:, 2:]))
        u = u - (fx - jnp.roll(fx, 1, -1)) - (fy[:, 1:] - fy[:, :-1])
        u = lax.cond(jnp.any(flagged), smooth, lambda values: values, u)
    columns = lax.all_to_all(u, "lev", split_axis=3, concat_axis=2, tiled=True)
    remapped = jnp.einsum("pk,fjkn->fjpn", remap_weights, columns, precision=exact)
    count = remap_weights.shape[0]
    upward = np.triu(np.ones((count, count), np.float32), 1) + 0.5 * np.eye(count, dtype=np.float32)
    upward = jnp.einsum("kl,jln->jkn", jnp.asarray(upward), columns[1], precision=exact)
    width = lon // lax.axis_size("lev")
    mine = lax.dynamic_slice_in_dim(surface, lax.axis_index("lev") * width, width, 1)
    return remapped, mine[:, None] + count**-0.5 * upward


def solution(mesh):
    def program(fields, courant, cutoffs, surface, remap_weights):
        lats, parts = mesh.shape["lat"], mesh.shape["lev"]
        rows, levels = fields.shape[1] // lats, fields.shape[2] // parts
        polar = fields.shape[1] // 8
        paired = (
            lats % 2 == 0
            and rows == 4
            and levels % 16 == 0
            and polar <= 2 * rows - 2
            and fields.shape[3] % (LANE * parts) == 0
            and parts & (parts - 1) == 0
            and fields.shape[3] % (4 * KMAX) == 0
        )
        return jax.shard_map(
            shards if paired else plain_shards,
            mesh=mesh,
            in_specs=(
                P(None, "lat", "lev", None),
                P(None, "lat", "lev", None),
                P(),
                P("lat", None),
                P(),
            ),
            out_specs=(P(None, "lat", None, "lev"), P("lat", None, "lev")),
            check_vma=False,
        )(fields, courant, cutoffs, surface, remap_weights)

    return program
```

```python
import functools
import math

import jax
import jax.numpy as jnp
import ml_dtypes
import numpy as np
from jax import lax
from jax.experimental import pallas as pl
from jax.experimental.pallas import tpu as pltpu
from jax.sharding import PartitionSpec as P

KMAX = 128
LANE = 128
TOP = 32767.0
STEPS = 256.0
TINY = 2.0**-100
WIND = 81920.0
ROUND = 1.5 * 2.0**23
VMEM_LIMIT = 12 * 2**20
VMEM_MOST = 63 * 2**20 + 2**19


def rounded(values):
    return ((values + ROUND) - ROUND).astype(jnp.int32).astype(jnp.int16)


def lane_max(values):
    chunks = [jnp.abs(values[:, i : i + LANE]) for i in range(0, values.shape[1], LANE)]
    while len(chunks) > 1:
        pairs = [jnp.maximum(a, b) for a, b in zip(chunks[0::2], chunks[1::2])]
        chunks = pairs + chunks[2 * len(pairs) :]
    return chunks[0]


def tiled(tile, width):
    return jnp.concatenate([tile] * (width // LANE), axis=1)


def scale_code(largest):
    return jnp.ceil(jnp.log2(jnp.maximum(largest, TINY)) * STEPS)


def encoder(code):
    return TOP / jnp.exp2(code * (1.0 / STEPS))


def decoder(code16):
    code = code16.astype(jnp.int32).astype(jnp.float32)
    return jnp.exp2(code * (1.0 / STEPS)) * (1.0 / TOP)


def encode_row(values, out_ref, at):
    width = values.shape[1]
    code = scale_code(lane_max(values))
    out_ref[:, at : at + width] = rounded(values * tiled(encoder(code), width))
    out_ref[:, at + width : at + width + LANE] = code.astype(jnp.int32).astype(jnp.int16)


def decode_row(in_ref, at, width):
    scale = decoder(in_ref[:, at + width : at + width + LANE])
    values = in_ref[:, at : at + width].astype(jnp.int32).astype(jnp.float32)
    return values * tiled(scale, width)


def fold(wind):
    middle = wind.shape[1] // 2
    return jnp.concatenate([wind[:, :middle], wind[:, middle:]], axis=0)


def unfold(values):
    half = values.shape[0] // 2
    return jnp.concatenate([values[:half], values[half:]], axis=1)


def wind_codes(values):
    return rounded(values * WIND)


def wind_values(codes):
    return codes.astype(jnp.int32).astype(jnp.float32) * (1.0 / WIND)


class Sizes:
    def __init__(self, rows, levels, lon):
        self.rows, self.levels, self.lon = rows, levels, lon
        self.half = levels // 2
        self.band = 2 * rows
        self.pad = lon + 2 * LANE
        self.code = lon + LANE
        self.edge = 2 * self.code + lon // 2
        self.middle = self.edge + lon // 2
        self.last = 2 * lon + lon // 2


def put_padded(ref, index, values, lon):
    ref[index + (Ellipsis, slice(LANE, LANE + lon))] = values
    ref[index + (Ellipsis, slice(0, LANE))] = values[..., lon - LANE :]
    ref[index + (Ellipsis, slice(LANE + lon, 2 * LANE + lon))] = values[..., :LANE]


def level_half(z, wind, upper):
    wind = wind.astype(jnp.float32)
    return jnp.where(upper == 1, wind[z.half :], wind[: z.half])


def edge_kernel(z, fields_ref, courant_ref, edge_ref, rows_ref, wind_ref, sems):
    p = lax.rem(lax.axis_index("lat"), 2)
    give = pl.multiple_of((1 - p) * z.half, z.half)
    copies = [
        pltpu.make_async_copy(
            fields_ref.at[f, 2 * p + r, pl.ds(give, z.half)],
            rows_ref.at[r, pl.ds(f * z.half, z.half)],
            sems.at[2 * r + f],
        )
        for r in range(2)
        for f in range(2)
    ]
    copies.append(pltpu.make_async_copy(courant_ref.at[1, 3 * p], wind_ref, sems.at[4]))
    for copy in copies:
        copy.start()
    for r in range(2):
        copies[2 * r].wait()
        copies[2 * r + 1].wait()
        encode_row(rows_ref[r], edge_ref, r * z.code)
    copies[4].wait()
    edge_ref[:, 2 * z.code :] = wind_codes(fold(level_half(z, wind_ref[...], 1 - p)))


def rest_kernel(z, par_ref, fields_ref, courant_ref, middle_ref, last_ref, own_ref):
    p = par_ref[0]
    keep = pl.multiple_of(p * z.half, z.half)
    give = pl.multiple_of((1 - p) * z.half, z.half)

    def field_row(row, start):
        return jnp.concatenate([fields_ref[f, row, pl.ds(start, z.half)] for f in range(2)], axis=0)

    def wind(k, row, upper):
        return level_half(z, courant_ref[k, row], upper)

    edge, inner = 2 * p, 2 * (1 - p)
    outer, near = 3 * p, 3 * (1 - p)
    for r in range(2):
        encode_row(field_row(edge + r, keep), own_ref, r * z.code)
        encode_row(field_row(inner + r, give), middle_ref, r * z.code)
    own_ref[:, 2 * z.code :] = wind_codes(fold(wind(1, outer, p)))
    lon = z.lon
    middle_ref[:, 2 * z.code : z.edge] = wind_codes(fold(wind(1, near, 1 - p)))
    middle_ref[:, z.edge :] = wind_codes(fold(wind(0, near, 1 - p)))
    last_ref[:, 2 * lon :] = wind_codes(fold(wind(0, outer, 1 - p)))
    for r in range(2):
        both = jnp.concatenate([wind(k, 1 + r, 1 - p) for k in range(2)], axis=0)
        last_ref[:, r * lon : (r + 1) * lon] = wind_codes(both)


def shifted(pieces, shift, lanes):
    turned = [pltpu.roll(v, (-shift) % LANE, 1) for v in pieces]
    if shift > 0:
        return [jnp.where(lanes < LANE - shift, a, b) for a, b in zip(turned[1:-1], turned[2:])]
    return [jnp.where(lanes < -shift, a, b) for a, b in zip(turned[:-2], turned[1:-1])]


def substep(z, count_rows, base, row_of, winds_ref, write):
    count = next(n for n in (4, 3, 2, 1) if z.lon % (n * LANE) == 0)
    width = count * LANE
    lanes = lax.broadcasted_iota(jnp.int32, (z.half, LANE), 1)

    def part(at):
        def piece(k):
            return pl.ds(at + k * LANE, LANE)

        def row(j, f):
            return [row_of(j, f, piece(k + 1)) for k in range(count)]

        def start(j, f):
            pieces = [row_of(j + 2, f, piece(k)) for k in range(count + 2)]
            return [shifted(pieces, s, lanes) for s in (-2, -1, 1, 2)]

        def lon_part(j, u, moved):
            out = []
            for k in range(count):
                m2, m1, p1, p2 = (m[k] for m in moved)
                east = 7.0 * (u[k] + p1) - (m1 + p2)
                west = 7.0 * (m1 + u[k]) - (m2 + p1)
                east = winds_ref[base + j, :, piece(k)] * east
                out.append(east - winds_ref[z.rows + base + j, :, piece(k)] * west)
            return out

        for f in range(2):
            rows = [row(j, f) for j in range(4)]
            sums = [[a + b for a, b in zip(rows[j], rows[j + 1])] for j in range(3)]
            flux = None
            moved = start(0, f)
            for j in range(count_rows + 1):
                later = start(j, f) if 0 < j < count_rows else None
                new = [
                    winds_ref[2 * z.rows + base + j, :, piece(k)] * (8.0 * sums[1][k] - (sums[0][k] + sums[2][k]))
                    for k in range(count)
                ]
                if j > 0:
                    u = rows[1]
                    change = lon_part(j - 1, u, moved)
                    for k in range(count):
                        write(j - 1, f, at, k, u[k] - change[k] - (new[k] - flux[k]))
                    moved = later
                flux = new
                if j < count_rows:
                    above = row(j + 4, f)
                    rows = rows[1:] + [above]
                    sums = sums[1:] + [[a + b for a, b in zip(rows[2], rows[3])]]

    for i in range(z.lon // width):
        part(i * width)


def filter_tables(lon):
    half = lon // 2
    points = np.arange(half)
    forward, back = [], []
    for parity in range(2):
        waves = np.arange(parity, KMAX, 2)
        angle = (points[:, None] * waves[None, :] % lon) * (2.0 * math.pi / lon)
        table = np.concatenate([np.cos(angle), np.sin(angle)], axis=1).astype(np.float32)
        high = table.astype(ml_dtypes.bfloat16)
        low = (table - high.astype(np.float32)).astype(ml_dtypes.bfloat16)
        forward.append(np.concatenate([high, low], axis=1))
        turned = np.concatenate([high.T, low.T], axis=0)
        back.append(np.concatenate(np.split(turned, half // (2 * KMAX), axis=1), axis=0))
    return np.stack(forward + back)


def split(values):
    high = values.astype(jnp.bfloat16)
    return high, (values - high.astype(jnp.float32)).astype(jnp.bfloat16)


def low_pass(z, rows, cuts, table_ref):
    half = z.lon // 2
    count = len(rows)
    tall = 2 * z.half
    total = count * tall
    flat = [row.reshape(tall, z.lon) for row in rows]
    folded = []
    for parity in range(2):
        parts = [
            row[:, :half] + row[:, half:] if parity == 0 else row[:, :half] - row[:, half:]
            for row in flat
        ]
        high, low = split(jnp.concatenate(parts, axis=0))
        both = jnp.concatenate([high, low], axis=0)
        got = jnp.dot(both, table_ref[parity], preferred_element_type=jnp.float32)
        wave = got[:total, :KMAX] + got[:total, KMAX:] + (got[total:, :KMAX] + got[total:, KMAX:])
        number = 2 * (lax.broadcasted_iota(jnp.int32, (tall, KMAX), 1) % (KMAX // 2)) + parity
        doubled = jnp.where(number == 0, 1.0, 2.0) * (1.0 / z.lon)
        weight = jnp.concatenate([jnp.where(number <= cut, doubled, 0.0) for cut in cuts], axis=0)
        high, low = split(wave * weight)
        both = jnp.concatenate(
            [jnp.concatenate([high, high], axis=1), jnp.concatenate([low, low], axis=1)], axis=0
        )
        got = []
        for at in range(0, half, 2 * KMAX):
            block = table_ref[2 + parity, at : at + 2 * KMAX]
            sums = jnp.dot(both, block, preferred_element_type=jnp.float32)
            got.append(sums[:total] + sums[total:])
        folded.append(jnp.concatenate(got, axis=1))
    left, right = folded[0] + folded[1], folded[0] - folded[1]
    smooth = jnp.concatenate([left, right], axis=1)
    return [smooth[i * tall : (i + 1) * tall].reshape(2, z.half, z.lon) for i in range(count)]


def filter_rows(z, cut_ref, first_row, start, table_ref, load, store):
    nyquist = z.lon // 2
    cuts = [cut_ref[first_row + start + r] for r in range(z.rows)]
    some = functools.reduce(jnp.logical_or, [cut < nyquist for cut in cuts])

    @pl.when(some)
    def _():
        smooth = low_pass(z, [load(start + r) for r in range(z.rows)], cuts, table_ref)
        for r in range(z.rows):

            @pl.when(cuts[r] < nyquist)
            def _():
                store(start + r, smooth[r])


def north_wind(z, in_ref):
    return unfold(wind_values(in_ref[:, 2 * z.code : z.edge]))


def faces(z, cx_ref, cy_ref, winds_ref):
    lanes = lax.broadcasted_iota(jnp.int32, (z.half, LANE), 1)
    for j in range(z.rows):
        pieces = [cx_ref[j, :, i : i + LANE] * (1.0 / 24.0) for i in range(0, z.pad, LANE)]
        for out, shift in ((j, 1), (z.rows + j, -1)):
            for k, moved in enumerate(shifted(pieces, shift, lanes)):
                winds_ref[out, :, k * LANE : (k + 1) * LANE] = pieces[k + 1] + moved
    for j in range(z.rows + 1):
        winds_ref[2 * z.rows + j] = (cy_ref[j] + cy_ref[j + 1]) * (1.0 / 24.0)


def writer(new_ref):
    def write(row, f, at, k, values):
        new_ref[row, f, :, pl.ds(at + (k + 1) * LANE, LANE)] = values

    return write


def wrap(z, new_ref, rows):
    for j in rows:
        new_ref[j, :, :, 0:LANE] = new_ref[j, :, :, z.lon : z.lon + LANE]
        new_ref[j, :, :, LANE + z.lon :] = new_ref[j, :, :, LANE : 2 * LANE]


def encode_new(z, new_ref, row, out_ref):
    for r in range(2):
        values = new_ref[row + r, :, :, LANE : LANE + z.lon]
        encode_row(values.reshape(2 * z.half, z.lon), out_ref, r * z.code)


def place_row(z, u_ref, row, in_ref, r):
    values = decode_row(in_ref, r * z.code, z.lon)
    put_padded(u_ref, (row + r,), values.reshape(2, z.half, z.lon), z.lon)


def own_kernel(
    z, par_ref, fields_ref, courant_ref, edge_ref, middle_ref, near_ref, far_ref,
    new_ref, winds_ref, code_ref, u_ref, cx_ref, cy_ref,
):
    p = par_ref[0]
    lon, half = z.lon, z.half
    keep = pl.multiple_of(p * half, half)
    for r in range(z.rows):
        own = jnp.stack([fields_ref[f, r, pl.ds(keep, half)] for f in range(2)])
        put_padded(u_ref, (z.rows * p + r + 2,), own, lon)
        put_padded(cx_ref, (r,), level_half(z, courant_ref[0, r], p), lon)
        cy_ref[r + 1] = level_half(z, courant_ref[1, r], p)
    for r in range(2):
        place_row(z, u_ref, 6 * (1 - p) + 2, edge_ref, r)
        place_row(z, u_ref, 4 - 2 * p + 2, middle_ref, r)
        place_row(z, u_ref, 10 * (1 - p), near_ref, r)
        place_row(z, u_ref, 10 * p, far_ref, r)
    cy_ref[5 * (1 - p)] = north_wind(z, middle_ref)
    cy_ref[5 * p] = north_wind(z, far_ref)
    faces(z, cx_ref, cy_ref, winds_ref)
    start = z.rows * p
    substep(z, z.rows, 0, lambda j, f, piece: u_ref[start + j, f, :, piece], winds_ref, writer(new_ref))
    encode_new(z, new_ref, 2 * p, code_ref)
    wrap(z, new_ref, range(z.rows))


def other_kernel(
    z, par_ref, courant_ref, edge_ref, middle_ref, last_ref, near_ref, u_ref, own_code_ref,
    new_ref, winds_ref, one_ref, two_ref, cx_ref, cy_ref,
):
    p = par_ref[0]
    lon, half = z.lon, z.half
    for r in range(2):
        both = wind_values(last_ref[:, r * lon : (r + 1) * lon])
        put_padded(cx_ref, (1 + r,), both[:half], lon)
        cy_ref[2 + r] = both[half:]
    easts = (last_ref[:, 2 * lon :], middle_ref[:, z.edge :])
    for east, row, in_ref in zip(easts, (3 * (1 - p), 3 * p), (edge_ref, middle_ref)):
        put_padded(cx_ref, (row,), unfold(wind_values(east)), lon)
        cy_ref[row + 1] = north_wind(z, in_ref)
    cy_ref[5 * p] = level_half(z, courant_ref[1, 3 * (1 - p)], p)
    cy_ref[5 * (1 - p)] = north_wind(z, near_ref)
    faces(z, cx_ref, cy_ref, winds_ref)
    outer = 2 * (1 - p)
    start = z.rows * (1 - p) + outer
    substep(z, 2, outer, lambda j, f, piece: u_ref[start + j, f, :, piece], winds_ref, writer(new_ref))

    def put_codes(own_ref, other_ref):
        own_ref[...] = own_code_ref[...]
        encode_new(z, new_ref, 0, other_ref)

    swapped = p + par_ref[3] == 1
    pl.when(swapped)(lambda: put_codes(one_ref, two_ref))
    pl.when(jnp.logical_not(swapped))(lambda: put_codes(two_ref, one_ref))
    wrap(z, new_ref, range(2))


def inner_kernel(
    z, par_ref, cut_ref, own_ref, other_ref, u_ref, own_winds_ref, other_winds_ref, table_ref, new_ref, inner_ref
):
    p = par_ref[0]
    own, other = z.rows * p, z.rows * (1 - p)
    for j in range(z.rows):
        new_ref[own + j] = own_ref[j]
    for j in range(2):
        new_ref[other + 2 * (1 - p) + j] = other_ref[j]
    start = other + 2 * p

    def write(row, f, at, k, values):
        writer(new_ref)(start + row, f, at, k, values)

    substep(z, 2, 2 * p, lambda j, f, piece: u_ref[start + j, f, :, piece], other_winds_ref, write)
    wrap(z, new_ref, (start, start + 1))

    def store(row, values):
        put_padded(new_ref, (row,), values, z.lon)

    for part in range(2):
        filter_rows(
            z, cut_ref, par_ref[1], part * z.rows, table_ref,
            lambda row: new_ref[row, :, :, LANE : LANE + z.lon], store,
        )
    for i, (low, base, winds_ref) in enumerate(
        ((2 * p, 2 * (1 - p), own_winds_ref), (2 * (1 - p), 2 * p, other_winds_ref))
    ):

        def keep(row, f, at, k, values):
            inner_ref[2 * i + row, f, :, pl.ds(at + k * LANE, LANE)] = values

        substep(z, 2, base, lambda j, f, piece: new_ref[low + j, f, :, piece], winds_ref, keep)


def early_kernel(z, parts, par_ref, cut_ref, new_ref, inner_ref, own_winds_ref, other_winds_ref, one_ref, table_ref, *refs):
    side = 1 - par_ref[3]
    out_refs, scratch = refs[:parts], refs[parts:]
    halves(z, parts, side, par_ref, cut_ref, new_ref, inner_ref, own_winds_ref, other_winds_ref, one_ref, table_ref, out_refs, scratch)


def late_kernel(z, parts, par_ref, cut_ref, new_ref, inner_ref, own_winds_ref, other_winds_ref, two_ref, table_ref, *refs):
    side = par_ref[3]
    early_refs, out_refs, scratch = refs[:parts], refs[parts : 3 * parts], refs[3 * parts :]
    out_refs, other_refs = out_refs[:parts], out_refs[parts:]
    own = side == par_ref[0]

    def hand_on(mine_refs, rest_refs):
        halves(z, parts, side, par_ref, cut_ref, new_ref, inner_ref, own_winds_ref, other_winds_ref, two_ref, table_ref, mine_refs, scratch)
        for a, b in zip(early_refs, rest_refs):
            b[...] = a[...]

    pl.when(own)(lambda: hand_on(other_refs, out_refs))
    pl.when(jnp.logical_not(own))(lambda: hand_on(out_refs, other_refs))


def halves(z, parts, side, par_ref, cut_ref, new_ref, inner_ref, own_winds_ref, other_winds_ref, halo_ref, table_ref, out_refs, scratch):
    winds_ref, u_ref, v_ref = scratch
    own = side == par_ref[0]
    inner_at = jnp.where(own, 0, 2)
    rows = [offset + 2 * side + r for offset, n in ((0, 2), (z.rows, 2), (2 * z.rows, 3)) for r in range(n)]

    def take(from_ref):
        for row in rows:
            winds_ref[row] = from_ref[row]

    pl.when(own)(lambda: take(own_winds_ref))
    pl.when(jnp.logical_not(own))(lambda: take(other_winds_ref))
    outer_half(z, parts, side, inner_at, par_ref, cut_ref, new_ref, inner_ref, winds_ref, halo_ref, table_ref, out_refs, u_ref, v_ref)


def outer_half(
    z, parts, side, inner_at, par_ref, cut_ref, new_ref, inner_ref, winds_ref, halo_ref, table_ref,
    out_refs, u_ref, v_ref,
):
    lon = z.lon
    tall = 2 * z.half
    base = z.rows * side

    for r in range(2):
        place_row(z, u_ref, 4 * side, halo_ref, r)
    for r in range(4):
        u_ref[2 * (1 - side) + r] = new_ref[base + r]
    for r in range(2):
        v_ref[2 * (1 - side) + r] = inner_ref[inner_at + r]

    def write(row, f, at, k, values):
        v_ref[2 * side + row, f, :, pl.ds(at + k * LANE, LANE)] = values

    substep(z, 2, 2 * side, lambda j, f, piece: u_ref[j, f, :, piece], winds_ref, write)

    def store(row, values):
        v_ref[row] = values

    filter_rows(z, cut_ref, par_ref[1] + base, 0, table_ref, lambda row: v_ref[row], store)
    column = lon // parts
    for b in range(parts):
        at = pl.multiple_of(jnp.bitwise_xor(par_ref[2], b) * column, LANE)
        values = jnp.concatenate(
            [v_ref[r, :, :, pl.ds(at, column)].reshape(tall, column) for r in range(z.rows)], axis=1
        )
        encode_row(values, out_refs[b], 0)


def scale_kernel(at, *refs):
    for i, ref in enumerate(refs[:-1]):
        refs[-1][i] = decoder(ref[:, at : at + LANE])


def column_kernel(z, parts, far, par_ref, *refs):
    got, refs = refs[: 2 * parts], refs[2 * parts :]
    scales_ref, remap_ref, upward_ref, surface_ref, out_ref, geo_ref, x_ref, sums_ref, geo_sums_ref, sems = refs
    p, lev = par_ref[0], par_ref[2]
    count, column = sums_ref.shape[-2:]
    high, low = split(remap_ref[...])
    remap = jnp.concatenate([high, low, high], axis=1)
    both = jnp.concatenate([remap, upward_ref[...].astype(jnp.bfloat16)], axis=0)
    scales = [
        scales_ref[far.index(i)] if i in far else decoder(ref[:, z.rows * column :])
        for i, ref in enumerate(got)
    ]
    copies = []
    for row in range(z.rows):
        for i, ref in enumerate(got):
            side = 1 - p if i < parts else p
            s = jnp.bitwise_xor(lev, i % parts)
            codes = ref[:, row * column : (row + 1) * column].astype(jnp.int32).astype(jnp.float32)
            values = codes * tiled(scales[i], column)
            level = pl.multiple_of(s * z.levels + side * z.half, z.half)
            for f in range(2):
                x_ref[row, f, pl.ds(level, z.half)] = values[f * z.half : (f + 1) * z.half]
        for f in range(2):
            high, low = split(x_ref[row, f])
            stacked = jnp.concatenate([high, high, low], axis=0)
            result = jnp.dot(both if f else remap, stacked, preferred_element_type=jnp.float32)
            sums_ref[f, row] = result[:count]
            if f:
                geo_sums_ref[row] = surface_ref[row] + result[count:] * (count**-0.5)
        parts_out = [(sums_ref.at[f, row], out_ref.at[f, row]) for f in range(2)]
        parts_out.append((geo_sums_ref.at[row], geo_ref.at[row]))
        for k, (a, b) in enumerate(parts_out):
            copies.append(pltpu.make_async_copy(a, b, sems.at[3 * row + k]))
            copies[-1].start()
    for copy in copies:
        copy.wait()


def whole():
    return pl.BlockSpec(memory_space=pltpu.VMEM)


def scalars():
    return pl.BlockSpec(memory_space=pltpu.SMEM)


def far_memory():
    return pl.BlockSpec(memory_space=pltpu.HBM)


def params(limit=VMEM_LIMIT):
    return pltpu.CompilerParams(vmem_limit_bytes=limit)


def cost(flops=1000, data=1000):
    return pl.CostEstimate(flops=flops, bytes_accessed=data, transcendentals=0)


def shards(fields, courant, cutoffs, surface, remap_weights):
    _, rows, levels, lon = fields.shape
    z = Sizes(rows, levels, lon)
    lats, parts = lax.axis_size("lat"), lax.axis_size("lev")
    me = lax.axis_index("lat")
    parity = me % 2
    lev = lax.axis_index("lev")
    place = jnp.stack([parity, (me - parity) * rows, lev, (me // 2) % 2]).astype(jnp.int32)
    tall = 2 * z.half
    i16, f32 = jnp.int16, jnp.float32
    swap = [(i, i ^ 1) for i in range(lats)]
    rising = [(i, i + 2) for i in range(lats - 2)]
    near_pairs = [(i, j) if i % 2 else (j, i) for i, j in rising]
    far_pairs = [(j, i) if i % 2 else (i, j) for i, j in rising]

    ones, twos = [
        [pair for i, j in rising if i // 2 % 2 == odd for pair in ((i, j), (j, i))] for odd in range(2)
    ]

    def shape(*dims):
        return jax.ShapeDtypeStruct(dims, f32)

    def codes(*dims):
        return jax.ShapeDtypeStruct(dims, i16)

    edge = pl.pallas_call(
        functools.partial(edge_kernel, z),
        name="edge",
        in_specs=[far_memory(), far_memory()],
        out_specs=whole(),
        out_shape=codes(tall, z.edge),
        scratch_shapes=[
            pltpu.VMEM((2, tall, lon), f32),
            pltpu.VMEM((levels, lon), courant.dtype),
            pltpu.SemaphoreType.DMA((5,)),
        ],
        compiler_params=params(VMEM_MOST),
        cost_estimate=cost(),
    )(fields, courant)
    edge = lax.ppermute(edge, "lat", swap)
    middle, last, own = pl.pallas_call(
        functools.partial(rest_kernel, z),
        name="rest",
        in_specs=[scalars(), whole(), whole()],
        out_specs=[whole()] * 3,
        out_shape=[codes(tall, z.middle), codes(tall, z.last), codes(tall, z.edge)],
        compiler_params=params(),
        cost_estimate=cost(),
    )(place, fields, courant)
    near = lax.ppermute(own, "lat", near_pairs)
    middle = lax.ppermute(middle, "lat", swap)
    far = lax.ppermute(edge, "lat", far_pairs)
    last = lax.ppermute(last, "lat", swap)

    half_scratch = [
        pltpu.VMEM((z.rows, z.half, z.pad), f32),
        pltpu.VMEM((z.rows + 2, z.half, lon), f32),
    ]
    mine, own_winds, own_code, u = pl.pallas_call(
        functools.partial(own_kernel, z),
        name="own",
        in_specs=[scalars()] + [whole()] * 6,
        out_specs=[whole()] * 4,
        out_shape=[
            shape(z.rows, 2, z.half, z.pad),
            shape(3 * z.rows + 1, z.half, lon),
            codes(tall, 2 * z.code),
            shape(z.band + 4, 2, z.half, z.pad),
        ],
        scratch_shapes=half_scratch,
        compiler_params=params(),
        cost_estimate=cost(),
    )(place, fields, courant, edge, middle, near, far)
    other, other_winds, one, two = pl.pallas_call(
        functools.partial(other_kernel, z),
        name="other",
        in_specs=[scalars()] + [whole()] * 7,
        out_specs=[whole()] * 4,
        out_shape=[
            shape(2, 2, z.half, z.pad),
            shape(3 * z.rows + 1, z.half, lon),
            codes(tall, 2 * z.code),
            codes(tall, 2 * z.code),
        ],
        scratch_shapes=half_scratch,
        compiler_params=params(),
        cost_estimate=cost(),
    )(place, courant, edge, middle, last, near, u, own_code)
    one = lax.ppermute(one, "lat", ones)
    two = lax.ppermute(two, "lat", twos)

    tables = jnp.asarray(filter_tables(lon))
    new, inner = pl.pallas_call(
        functools.partial(inner_kernel, z),
        name="inner",
        in_specs=[scalars(), scalars()] + [whole()] * 6,
        out_specs=[whole()] * 2,
        out_shape=[shape(z.band, 2, z.half, z.pad), shape(z.rows, 2, z.half, lon)],
        compiler_params=params(),
        cost_estimate=cost(),
    )(place, cutoffs, mine, other, u, own_winds, other_winds, tables)

    column = lon // parts
    def outer(kernel, name, halo, early):
        count = parts + len(early)
        return pl.pallas_call(
            functools.partial(kernel, z, parts),
            name=name,
            in_specs=[scalars(), scalars()] + [whole()] * (6 + len(early)),
            out_specs=[whole()] * count,
            out_shape=[codes(tall, rows * column + LANE)] * count,
            scratch_shapes=[
                pltpu.VMEM((3 * z.rows + 1, z.half, lon), f32),
                pltpu.VMEM((6, 2, z.half, z.pad), f32),
                pltpu.VMEM((z.rows, 2, z.half, lon), f32),
            ],
            compiler_params=params(),
            cost_estimate=cost(),
        )(place, cutoffs, new, inner, own_winds, other_winds, halo, tables, *early)

    blocks = outer(late_kernel, "late", two, outer(early_kernel, "early", one, []))

    got = []
    for i, block in enumerate(blocks):
        b, across = i % parts, int(i < parts)
        pairs = [
            (k * parts + j, (k ^ across) * parts + (j ^ b)) for k in range(lats) for j in range(parts)
        ]
        got.append(lax.ppermute(block, ("lat", "lev"), pairs) if i != parts else block)
    far = [i for i in range(2 * parts) if i % 2 == 0 and i != parts]
    scales = pl.pallas_call(
        functools.partial(scale_kernel, rows * column),
        name="scales",
        in_specs=[whole()] * len(far),
        out_specs=whole(),
        out_shape=shape(len(far), tall, LANE),
        compiler_params=params(),
        cost_estimate=cost(),
    )(*[got[i] for i in far])

    count = remap_weights.shape[0]
    upward = np.triu(np.ones((count, count), np.float32), 1) + 0.5 * np.eye(count, dtype=np.float32)
    upward = jnp.asarray(np.concatenate([upward, 0.0 * upward, upward], axis=1))
    surface = lax.dynamic_slice_in_dim(surface, lev * column, column, 1)
    remapped, geopotential = pl.pallas_call(
        functools.partial(column_kernel, z, parts, far),
        name="columns",
        in_specs=[scalars()] + [whole()] * (len(got) + 4),
        out_specs=[far_memory()] * 2,
        out_shape=[shape(2, rows, count, column), shape(rows, count, column)],
        scratch_shapes=[
            pltpu.VMEM((rows, 2, count, column), f32),
            pltpu.VMEM((2, rows, count, column), f32),
            pltpu.VMEM((rows, count, column), f32),
            pltpu.SemaphoreType.DMA((3 * rows,)),
        ],
        compiler_params=params(),
        cost_estimate=cost(),
    )(place, *got, scales, remap_weights, upward, surface[:, None, :])
    return remapped, geopotential


def with_halo(shard, width):
    size, length = lax.axis_size("lat"), shard.shape[1]
    up = [(i, (i + 1) % size) for i in range(size - 1)]
    down = [(j, i) for i, j in up]
    before = lax.ppermute(lax.slice_in_dim(shard, length - width, length, axis=1), "lat", up)
    after = lax.ppermute(lax.slice_in_dim(shard, 0, width, axis=1), "lat", down)
    return jnp.concatenate([before, shard, after], axis=1)


def plain_shards(fields, courant, cutoffs, surface, remap_weights):
    _, rows, _, lon = fields.shape
    exact = lax.Precision.HIGHEST
    cut = lax.dynamic_slice_in_dim(cutoffs, lax.axis_index("lat") * rows, rows)
    waves = np.arange(KMAX)
    angle = (np.arange(lon)[:, None] * waves[None, :] % lon) * (2.0 * math.pi / lon)
    table = jnp.asarray(np.concatenate([np.cos(angle), np.sin(angle)], axis=1).astype(np.float32))
    number = jnp.asarray(np.concatenate([waves, waves]).astype(np.int32))
    weight = jnp.where(number[None] <= cut[:, None], jnp.where(number == 0, 1.0, 2.0)[None] / lon, 0.0)
    flagged = cut < lon // 2

    def smooth(values):
        wave = jnp.einsum("frln,nk->frlk", values, table, precision=exact) * weight[None, :, None]
        low = jnp.einsum("frlk,nk->frln", wave, table, precision=exact)
        return jnp.where(flagged[None, :, None, None], low, values)

    winds = with_halo(courant, 1).astype(jnp.float32)
    east, north = winds[0, 1:-1], winds[1]
    face_x = (east + jnp.roll(east, -1, -1)) / 24.0
    face_y = (north[:-1] + north[1:]) / 24.0
    u = fields
    for _ in range(2):
        wide = with_halo(u, 2)
        pair = u + jnp.roll(u, -1, -1)
        fx = face_x * (8.0 * pair - (jnp.roll(pair, 1, -1) + jnp.roll(pair, -1, -1)))
        pair = wide[:, :-1] + wide[:, 1:]
        fy = face_y * (8.0 * pair[:, 1:-1] - (pair[:, :-2] + pair[:, 2:]))
        u = u - (fx - jnp.roll(fx, 1, -1)) - (fy[:, 1:] - fy[:, :-1])
        u = lax.cond(jnp.any(flagged), smooth, lambda values: values, u)
    columns = lax.all_to_all(u, "lev", split_axis=3, concat_axis=2, tiled=True)
    remapped = jnp.einsum("pk,fjkn->fjpn", remap_weights, columns, precision=exact)
    count = remap_weights.shape[0]
    upward = np.triu(np.ones((count, count), np.float32), 1) + 0.5 * np.eye(count, dtype=np.float32)
    upward = jnp.einsum("kl,jln->jkn", jnp.asarray(upward), columns[1], precision=exact)
    width = lon // lax.axis_size("lev")
    mine = lax.dynamic_slice_in_dim(surface, lax.axis_index("lev") * width, width, 1)
    return remapped, mine[:, None] + count**-0.5 * upward


def solution(mesh):
    def program(fields, courant, cutoffs, surface, remap_weights):
        lats, parts = mesh.shape["lat"], mesh.shape["lev"]
        rows, levels = fields.shape[1] // lats, fields.shape[2] // parts
        polar = fields.shape[1] // 8
        paired = (
            lats % 2 == 0
            and rows == 4
            and levels % 16 == 0
            and polar <= 2 * rows - 2
            and fields.shape[3] % (LANE * parts) == 0
            and parts & (parts - 1) == 0
            and fields.shape[3] % (4 * KMAX) == 0
        )
        return jax.shard_map(
            shards if paired else plain_shards,
            mesh=mesh,
            in_specs=(
                P(None, "lat", "lev", None),
                P(None, "lat", "lev", None),
                P(),
                P("lat", None),
                P(),
            ),
            out_specs=(P(None, "lat", None, "lev"), P("lat", None, "lev")),
            check_vma=False,
        )(fields, courant, cutoffs, surface, remap_weights)

    return program
```

```python
import functools
import math

import jax
import jax.numpy as jnp
import ml_dtypes
import numpy as np
from jax import lax
from jax.experimental import pallas as pl
from jax.experimental.pallas import tpu as pltpu
from jax.sharding import PartitionSpec as P

KMAX = 128
LANE = 128
TOP = 32767.0
STEPS = 256.0
TINY = 2.0**-100
WIND = 81920.0
ROUND = 1.5 * 2.0**23
VMEM_LIMIT = 12 * 2**20
VMEM_MOST = 63 * 2**20 + 2**19


def rounded(values):
    return ((values + ROUND) - ROUND).astype(jnp.int32).astype(jnp.int16)


def lane_max(values):
    chunks = [jnp.abs(values[:, i : i + LANE]) for i in range(0, values.shape[1], LANE)]
    while len(chunks) > 1:
        pairs = [jnp.maximum(a, b) for a, b in zip(chunks[0::2], chunks[1::2])]
        chunks = pairs + chunks[2 * len(pairs) :]
    return chunks[0]


def tiled(tile, width):
    return jnp.concatenate([tile] * (width // LANE), axis=1)


def scale_code(largest):
    return jnp.ceil(jnp.log2(jnp.maximum(largest, TINY)) * STEPS)


def encoder(code):
    return TOP / jnp.exp2(code * (1.0 / STEPS))


def decoder(code16):
    code = code16.astype(jnp.int32).astype(jnp.float32)
    return jnp.exp2(code * (1.0 / STEPS)) * (1.0 / TOP)


def encode_row(values, out_ref, at):
    width = values.shape[1]
    code = scale_code(lane_max(values))
    out_ref[:, at : at + width] = rounded(values * tiled(encoder(code), width))
    out_ref[:, at + width : at + width + LANE] = code.astype(jnp.int32).astype(jnp.int16)


def decode_row(in_ref, at, width):
    scale = decoder(in_ref[:, at + width : at + width + LANE])
    values = in_ref[:, at : at + width].astype(jnp.int32).astype(jnp.float32)
    return values * tiled(scale, width)


def fold(wind):
    middle = wind.shape[1] // 2
    return jnp.concatenate([wind[:, :middle], wind[:, middle:]], axis=0)


def unfold(values):
    half = values.shape[0] // 2
    return jnp.concatenate([values[:half], values[half:]], axis=1)


def wind_codes(values):
    return rounded(values * WIND)


def wind_values(codes):
    return codes.astype(jnp.int32).astype(jnp.float32) * (1.0 / WIND)


class Sizes:
    def __init__(self, rows, levels, lon):
        self.rows, self.levels, self.lon = rows, levels, lon
        self.half = levels // 2
        self.band = 2 * rows
        self.pad = lon + 2 * LANE
        self.code = lon + LANE
        self.edge = 2 * self.code + lon // 2
        self.middle = self.edge + lon // 2
        self.last = 2 * lon + lon // 2


def put_padded(ref, index, values, lon):
    ref[index + (Ellipsis, slice(LANE, LANE + lon))] = values
    ref[index + (Ellipsis, slice(0, LANE))] = values[..., lon - LANE :]
    ref[index + (Ellipsis, slice(LANE + lon, 2 * LANE + lon))] = values[..., :LANE]


def level_half(z, wind, upper):
    wind = wind.astype(jnp.float32)
    return jnp.where(upper == 1, wind[z.half :], wind[: z.half])


def edge_kernel(z, fields_ref, courant_ref, edge_ref, rows_ref, wind_ref, sems):
    p = lax.rem(lax.axis_index("lat"), 2)
    give = pl.multiple_of((1 - p) * z.half, z.half)
    copies = [
        pltpu.make_async_copy(
            fields_ref.at[f, 2 * p + r, pl.ds(give, z.half)],
            rows_ref.at[r, pl.ds(f * z.half, z.half)],
            sems.at[2 * r + f],
        )
        for r in range(2)
        for f in range(2)
    ]
    copies.append(pltpu.make_async_copy(courant_ref.at[1, 3 * p], wind_ref, sems.at[4]))
    for copy in copies:
        copy.start()
    for r in range(2):
        copies[2 * r].wait()
        copies[2 * r + 1].wait()
        encode_row(rows_ref[r], edge_ref, r * z.code)
    copies[4].wait()
    edge_ref[:, 2 * z.code :] = wind_codes(fold(level_half(z, wind_ref[...], 1 - p)))


def rest_kernel(z, par_ref, fields_ref, courant_ref, middle_ref, last_ref, own_ref):
    p = par_ref[0]
    keep = pl.multiple_of(p * z.half, z.half)
    give = pl.multiple_of((1 - p) * z.half, z.half)

    def field_row(row, start):
        return jnp.concatenate([fields_ref[f, row, pl.ds(start, z.half)] for f in range(2)], axis=0)

    def wind(k, row, upper):
        return level_half(z, courant_ref[k, row], upper)

    edge, inner = 2 * p, 2 * (1 - p)
    outer, near = 3 * p, 3 * (1 - p)
    for r in range(2):
        encode_row(field_row(edge + r, keep), own_ref, r * z.code)
        encode_row(field_row(inner + r, give), middle_ref, r * z.code)
    own_ref[:, 2 * z.code :] = wind_codes(fold(wind(1, outer, p)))
    lon = z.lon
    middle_ref[:, 2 * z.code : z.edge] = wind_codes(fold(wind(1, near, 1 - p)))
    middle_ref[:, z.edge :] = wind_codes(fold(wind(0, near, 1 - p)))
    last_ref[:, 2 * lon :] = wind_codes(fold(wind(0, outer, 1 - p)))
    for r in range(2):
        both = jnp.concatenate([wind(k, 1 + r, 1 - p) for k in range(2)], axis=0)
        last_ref[:, r * lon : (r + 1) * lon] = wind_codes(both)


def shifted(pieces, shift, lanes):
    turned = [pltpu.roll(v, (-shift) % LANE, 1) for v in pieces]
    if shift > 0:
        return [jnp.where(lanes < LANE - shift, a, b) for a, b in zip(turned[1:-1], turned[2:])]
    return [jnp.where(lanes < -shift, a, b) for a, b in zip(turned[:-2], turned[1:-1])]


def substep(z, count_rows, base, row_of, winds_ref, write):
    count = next(n for n in (4, 3, 2, 1) if z.lon % (n * LANE) == 0)
    width = count * LANE
    lanes = lax.broadcasted_iota(jnp.int32, (z.half, LANE), 1)

    def part(at):
        def piece(k):
            return pl.ds(at + k * LANE, LANE)

        def row(j, f):
            return [row_of(j, f, piece(k + 1)) for k in range(count)]

        def start(j, f):
            pieces = [row_of(j + 2, f, piece(k)) for k in range(count + 2)]
            return [shifted(pieces, s, lanes) for s in (-2, -1, 1, 2)]

        def lon_part(j, u, moved):
            out = []
            for k in range(count):
                m2, m1, p1, p2 = (m[k] for m in moved)
                east = 7.0 * (u[k] + p1) - (m1 + p2)
                west = 7.0 * (m1 + u[k]) - (m2 + p1)
                east = winds_ref[base + j, :, piece(k)] * east
                out.append(east - winds_ref[z.rows + base + j, :, piece(k)] * west)
            return out

        for f in range(2):
            rows = [row(j, f) for j in range(4)]
            sums = [[a + b for a, b in zip(rows[j], rows[j + 1])] for j in range(3)]
            flux = None
            moved = start(0, f)
            for j in range(count_rows + 1):
                later = start(j, f) if 0 < j < count_rows else None
                new = [
                    winds_ref[2 * z.rows + base + j, :, piece(k)] * (8.0 * sums[1][k] - (sums[0][k] + sums[2][k]))
                    for k in range(count)
                ]
                if j > 0:
                    u = rows[1]
                    change = lon_part(j - 1, u, moved)
                    for k in range(count):
                        write(j - 1, f, at, k, u[k] - change[k] - (new[k] - flux[k]))
                    moved = later
                flux = new
                if j < count_rows:
                    above = row(j + 4, f)
                    rows = rows[1:] + [above]
                    sums = sums[1:] + [[a + b for a, b in zip(rows[2], rows[3])]]

    for i in range(z.lon // width):
        part(i * width)


def filter_tables(lon):
    half = lon // 2
    points = np.arange(half)
    forward, back = [], []
    for parity in range(2):
        waves = np.arange(parity, KMAX, 2)
        angle = (points[:, None] * waves[None, :] % lon) * (2.0 * math.pi / lon)
        table = np.concatenate([np.cos(angle), np.sin(angle)], axis=1).astype(np.float32)
        high = table.astype(ml_dtypes.bfloat16)
        low = (table - high.astype(np.float32)).astype(ml_dtypes.bfloat16)
        forward.append(np.concatenate([high, low], axis=1))
        turned = np.concatenate([high.T, low.T], axis=0)
        back.append(np.concatenate(np.split(turned, half // (2 * KMAX), axis=1), axis=0))
    return np.stack(forward + back)


def split(values):
    high = values.astype(jnp.bfloat16)
    return high, (values - high.astype(jnp.float32)).astype(jnp.bfloat16)


def low_pass(z, rows, cuts, table_ref):
    half = z.lon // 2
    count = len(rows)
    tall = 2 * z.half
    total = count * tall
    flat = [row.reshape(tall, z.lon) for row in rows]
    folded = []
    for parity in range(2):
        parts = [
            row[:, :half] + row[:, half:] if parity == 0 else row[:, :half] - row[:, half:]
            for row in flat
        ]
        high, low = split(jnp.concatenate(parts, axis=0))
        both = jnp.concatenate([high, low], axis=0)
        got = jnp.dot(both, table_ref[parity], preferred_element_type=jnp.float32)
        wave = got[:total, :KMAX] + got[:total, KMAX:] + (got[total:, :KMAX] + got[total:, KMAX:])
        number = 2 * (lax.broadcasted_iota(jnp.int32, (tall, KMAX), 1) % (KMAX // 2)) + parity
        doubled = jnp.where(number == 0, 1.0, 2.0) * (1.0 / z.lon)
        weight = jnp.concatenate([jnp.where(number <= cut, doubled, 0.0) for cut in cuts], axis=0)
        high, low = split(wave * weight)
        both = jnp.concatenate(
            [jnp.concatenate([high, high], axis=1), jnp.concatenate([low, low], axis=1)], axis=0
        )
        got = []
        for at in range(0, half, 2 * KMAX):
            block = table_ref[2 + parity, at : at + 2 * KMAX]
            sums = jnp.dot(both, block, preferred_element_type=jnp.float32)
            got.append(sums[:total] + sums[total:])
        folded.append(jnp.concatenate(got, axis=1))
    left, right = folded[0] + folded[1], folded[0] - folded[1]
    smooth = jnp.concatenate([left, right], axis=1)
    return [smooth[i * tall : (i + 1) * tall].reshape(2, z.half, z.lon) for i in range(count)]


def filter_rows(z, cut_ref, first_row, start, table_ref, load, store):
    nyquist = z.lon // 2
    cuts = [cut_ref[first_row + start + r] for r in range(z.rows)]
    some = functools.reduce(jnp.logical_or, [cut < nyquist for cut in cuts])

    @pl.when(some)
    def _():
        smooth = low_pass(z, [load(start + r) for r in range(z.rows)], cuts, table_ref)
        for r in range(z.rows):

            @pl.when(cuts[r] < nyquist)
            def _():
                store(start + r, smooth[r])


def north_wind(z, in_ref):
    return unfold(wind_values(in_ref[:, 2 * z.code : z.edge]))


def faces(z, cx_ref, cy_ref, winds_ref):
    lanes = lax.broadcasted_iota(jnp.int32, (z.half, LANE), 1)
    for j in range(z.rows):
        pieces = [cx_ref[j, :, i : i + LANE] * (1.0 / 24.0) for i in range(0, z.pad, LANE)]
        for out, shift in ((j, 1), (z.rows + j, -1)):
            for k, moved in enumerate(shifted(pieces, shift, lanes)):
                winds_ref[out, :, k * LANE : (k + 1) * LANE] = pieces[k + 1] + moved
    for j in range(z.rows + 1):
        winds_ref[2 * z.rows + j] = (cy_ref[j] + cy_ref[j + 1]) * (1.0 / 24.0)


def writer(new_ref):
    def write(row, f, at, k, values):
        new_ref[row, f, :, pl.ds(at + (k + 1) * LANE, LANE)] = values

    return write


def wrap(z, new_ref, rows):
    for j in rows:
        new_ref[j, :, :, 0:LANE] = new_ref[j, :, :, z.lon : z.lon + LANE]
        new_ref[j, :, :, LANE + z.lon :] = new_ref[j, :, :, LANE : 2 * LANE]


def encode_new(z, new_ref, row, out_ref):
    for r in range(2):
        values = new_ref[row + r, :, :, LANE : LANE + z.lon]
        encode_row(values.reshape(2 * z.half, z.lon), out_ref, r * z.code)


def place_row(z, u_ref, row, in_ref, r):
    values = decode_row(in_ref, r * z.code, z.lon)
    put_padded(u_ref, (row + r,), values.reshape(2, z.half, z.lon), z.lon)


def own_kernel(
    z, par_ref, fields_ref, courant_ref, edge_ref, middle_ref, near_ref, far_ref,
    new_ref, winds_ref, code_ref, u_ref, cx_ref, cy_ref,
):
    p = par_ref[0]
    lon, half = z.lon, z.half
    keep = pl.multiple_of(p * half, half)
    for r in range(z.rows):
        own = jnp.stack([fields_ref[f, r, pl.ds(keep, half)] for f in range(2)])
        put_padded(u_ref, (z.rows * p + r + 2,), own, lon)
        put_padded(cx_ref, (r,), level_half(z, courant_ref[0, r], p), lon)
        cy_ref[r + 1] = level_half(z, courant_ref[1, r], p)
    for r in range(2):
        place_row(z, u_ref, 6 * (1 - p) + 2, edge_ref, r)
        place_row(z, u_ref, 4 - 2 * p + 2, middle_ref, r)
        place_row(z, u_ref, 10 * (1 - p), near_ref, r)
        place_row(z, u_ref, 10 * p, far_ref, r)
    cy_ref[5 * (1 - p)] = north_wind(z, middle_ref)
    cy_ref[5 * p] = north_wind(z, far_ref)
    faces(z, cx_ref, cy_ref, winds_ref)
    start = z.rows * p
    substep(z, z.rows, 0, lambda j, f, piece: u_ref[start + j, f, :, piece], winds_ref, writer(new_ref))
    encode_new(z, new_ref, 2 * p, code_ref)
    wrap(z, new_ref, range(z.rows))


def other_kernel(
    z, par_ref, courant_ref, edge_ref, middle_ref, last_ref, near_ref, u_ref, own_code_ref,
    new_ref, winds_ref, one_ref, two_ref, cx_ref, cy_ref,
):
    p = par_ref[0]
    lon, half = z.lon, z.half
    for r in range(2):
        both = wind_values(last_ref[:, r * lon : (r + 1) * lon])
        put_padded(cx_ref, (1 + r,), both[:half], lon)
        cy_ref[2 + r] = both[half:]
    easts = (last_ref[:, 2 * lon :], middle_ref[:, z.edge :])
    for east, row, in_ref in zip(easts, (3 * (1 - p), 3 * p), (edge_ref, middle_ref)):
        put_padded(cx_ref, (row,), unfold(wind_values(east)), lon)
        cy_ref[row + 1] = north_wind(z, in_ref)
    cy_ref[5 * p] = level_half(z, courant_ref[1, 3 * (1 - p)], p)
    cy_ref[5 * (1 - p)] = north_wind(z, near_ref)
    faces(z, cx_ref, cy_ref, winds_ref)
    outer = 2 * (1 - p)
    start = z.rows * (1 - p) + outer
    substep(z, 2, outer, lambda j, f, piece: u_ref[start + j, f, :, piece], winds_ref, writer(new_ref))

    def put_codes(own_ref, other_ref):
        own_ref[...] = own_code_ref[...]
        encode_new(z, new_ref, 0, other_ref)

    swapped = p + par_ref[3] == 1
    pl.when(swapped)(lambda: put_codes(one_ref, two_ref))
    pl.when(jnp.logical_not(swapped))(lambda: put_codes(two_ref, one_ref))
    wrap(z, new_ref, range(2))


def inner_kernel(
    z, par_ref, cut_ref, own_ref, other_ref, u_ref, own_winds_ref, other_winds_ref, table_ref, new_ref, inner_ref
):
    p = par_ref[0]
    own, other = z.rows * p, z.rows * (1 - p)
    for j in range(z.rows):
        new_ref[own + j] = own_ref[j]
    for j in range(2):
        new_ref[other + 2 * (1 - p) + j] = other_ref[j]
    start = other + 2 * p

    def write(row, f, at, k, values):
        writer(new_ref)(start + row, f, at, k, values)

    substep(z, 2, 2 * p, lambda j, f, piece: u_ref[start + j, f, :, piece], other_winds_ref, write)
    wrap(z, new_ref, (start, start + 1))

    def store(row, values):
        put_padded(new_ref, (row,), values, z.lon)

    for part in range(2):
        filter_rows(
            z, cut_ref, par_ref[1], part * z.rows, table_ref,
            lambda row: new_ref[row, :, :, LANE : LANE + z.lon], store,
        )
    for i, (low, base, winds_ref) in enumerate(
        ((2 * p, 2 * (1 - p), own_winds_ref), (2 * (1 - p), 2 * p, other_winds_ref))
    ):

        def keep(row, f, at, k, values):
            inner_ref[2 * i + row, f, :, pl.ds(at + k * LANE, LANE)] = values

        substep(z, 2, base, lambda j, f, piece: new_ref[low + j, f, :, piece], winds_ref, keep)


def early_kernel(z, parts, par_ref, cut_ref, new_ref, inner_ref, own_winds_ref, other_winds_ref, one_ref, table_ref, *refs):
    side = 1 - par_ref[3]
    out_refs, scratch = refs[:parts], refs[parts:]
    halves(z, parts, side, par_ref, cut_ref, new_ref, inner_ref, own_winds_ref, other_winds_ref, one_ref, table_ref, out_refs, scratch)


def late_kernel(z, parts, par_ref, cut_ref, new_ref, inner_ref, own_winds_ref, other_winds_ref, two_ref, table_ref, *refs):
    side = par_ref[3]
    early_refs, out_refs, scratch = refs[:parts], refs[parts : 3 * parts], refs[3 * parts :]
    out_refs, other_refs = out_refs[:parts], out_refs[parts:]
    own = side == par_ref[0]

    def hand_on(mine_refs, rest_refs):
        halves(z, parts, side, par_ref, cut_ref, new_ref, inner_ref, own_winds_ref, other_winds_ref, two_ref, table_ref, mine_refs, scratch)
        for a, b in zip(early_refs, rest_refs):
            b[...] = a[...]

    pl.when(own)(lambda: hand_on(other_refs, out_refs))
    pl.when(jnp.logical_not(own))(lambda: hand_on(out_refs, other_refs))


def halves(z, parts, side, par_ref, cut_ref, new_ref, inner_ref, own_winds_ref, other_winds_ref, halo_ref, table_ref, out_refs, scratch):
    winds_ref, u_ref, v_ref = scratch
    own = side == par_ref[0]
    inner_at = jnp.where(own, 0, 2)
    rows = [offset + 2 * side + r for offset, n in ((0, 2), (z.rows, 2), (2 * z.rows, 3)) for r in range(n)]

    def take(from_ref):
        for row in rows:
            winds_ref[row] = from_ref[row]

    pl.when(own)(lambda: take(own_winds_ref))
    pl.when(jnp.logical_not(own))(lambda: take(other_winds_ref))
    outer_half(z, parts, side, inner_at, par_ref, cut_ref, new_ref, inner_ref, winds_ref, halo_ref, table_ref, out_refs, u_ref, v_ref)


def outer_half(
    z, parts, side, inner_at, par_ref, cut_ref, new_ref, inner_ref, winds_ref, halo_ref, table_ref,
    out_refs, u_ref, v_ref,
):
    lon = z.lon
    tall = 2 * z.half
    base = z.rows * side

    for r in range(2):
        place_row(z, u_ref, 4 * side, halo_ref, r)
    for r in range(4):
        u_ref[2 * (1 - side) + r] = new_ref[base + r]
    for r in range(2):
        v_ref[2 * (1 - side) + r] = inner_ref[inner_at + r]

    def write(row, f, at, k, values):
        v_ref[2 * side + row, f, :, pl.ds(at + k * LANE, LANE)] = values

    substep(z, 2, 2 * side, lambda j, f, piece: u_ref[j, f, :, piece], winds_ref, write)

    def store(row, values):
        v_ref[row] = values

    filter_rows(z, cut_ref, par_ref[1] + base, 0, table_ref, lambda row: v_ref[row], store)
    column = lon // parts
    for b in range(parts):
        at = pl.multiple_of(jnp.bitwise_xor(par_ref[2], b) * column, LANE)
        values = jnp.concatenate(
            [v_ref[r, :, :, pl.ds(at, column)].reshape(tall, column) for r in range(z.rows)], axis=1
        )
        encode_row(values, out_refs[b], 0)


def scale_kernel(at, *refs):
    for i, ref in enumerate(refs[:-1]):
        refs[-1][i] = decoder(ref[:, at : at + LANE])


def column_kernel(z, parts, far, par_ref, *refs):
    got, refs = refs[: 2 * parts], refs[2 * parts :]
    scales_ref, remap_ref, upward_ref, surface_ref, out_ref, geo_ref, sums_ref, geo_sums_ref, sems = refs
    p, lev = par_ref[0], par_ref[2]
    count, column = sums_ref.shape[-2:]
    level = lax.broadcasted_iota(jnp.int32, (count, count), 1)
    within, group = level % z.half, level // z.half
    for i in range(len(got)):
        start = jnp.bitwise_xor(lev, i % parts) * z.levels + (1 - p if i < parts else p) * z.half
        level = jnp.where(group == i, start + within, level)
    order = jnp.where(lax.broadcasted_iota(jnp.int32, (count, count), 0) == level, 1.0, 0.0).astype(jnp.bfloat16)
    high, low = split(remap_ref[...])
    rows = jnp.concatenate([high, low, upward_ref[...].astype(jnp.bfloat16)], axis=0)
    rows = jnp.dot(rows, order, preferred_element_type=jnp.float32).astype(jnp.bfloat16)
    high, low, upward = (rows[i * count : (i + 1) * count] for i in range(3))
    remap = jnp.concatenate([high, low, high], axis=1)
    both = jnp.concatenate([remap, jnp.concatenate([upward, jnp.zeros_like(upward), upward], axis=1)], axis=0)
    scales = [
        scales_ref[far.index(i)] if i in far else decoder(ref[:, z.rows * column :])
        for i, ref in enumerate(got)
    ]
    copies = []
    for row in range(z.rows):
        tiles = []
        for i, ref in enumerate(got):
            codes = ref[:, row * column : (row + 1) * column].astype(jnp.int32).astype(jnp.float32)
            tiles.append(codes * tiled(scales[i], column))
        for f in range(2):
            high, low = split(jnp.concatenate([t[f * z.half : (f + 1) * z.half] for t in tiles], axis=0))
            stacked = jnp.concatenate([high, high, low], axis=0)
            result = jnp.dot(both if f else remap, stacked, preferred_element_type=jnp.float32)
            sums_ref[f, row] = result[:count]
            if f:
                geo_sums_ref[row] = surface_ref[row] + result[count:] * (count**-0.5)
        parts_out = [(sums_ref.at[f, row], out_ref.at[f, row]) for f in range(2)]
        parts_out.append((geo_sums_ref.at[row], geo_ref.at[row]))
        for k, (a, b) in enumerate(parts_out):
            copies.append(pltpu.make_async_copy(a, b, sems.at[3 * row + k]))
            copies[-1].start()
    for copy in copies:
        copy.wait()


def whole():
    return pl.BlockSpec(memory_space=pltpu.VMEM)


def scalars():
    return pl.BlockSpec(memory_space=pltpu.SMEM)


def far_memory():
    return pl.BlockSpec(memory_space=pltpu.HBM)


def params(limit=VMEM_LIMIT):
    return pltpu.CompilerParams(vmem_limit_bytes=limit)


def cost(flops=1000, data=1000):
    return pl.CostEstimate(flops=flops, bytes_accessed=data, transcendentals=0)


def shards(fields, courant, cutoffs, surface, remap_weights):
    _, rows, levels, lon = fields.shape
    z = Sizes(rows, levels, lon)
    lats, parts = lax.axis_size("lat"), lax.axis_size("lev")
    me = lax.axis_index("lat")
    parity = me % 2
    lev = lax.axis_index("lev")
    place = jnp.stack([parity, (me - parity) * rows, lev, (me // 2) % 2]).astype(jnp.int32)
    tall = 2 * z.half
    i16, f32 = jnp.int16, jnp.float32
    swap = [(i, i ^ 1) for i in range(lats)]
    rising = [(i, i + 2) for i in range(lats - 2)]
    near_pairs = [(i, j) if i % 2 else (j, i) for i, j in rising]
    far_pairs = [(j, i) if i % 2 else (i, j) for i, j in rising]

    ones, twos = [
        [pair for i, j in rising if i // 2 % 2 == odd for pair in ((i, j), (j, i))] for odd in range(2)
    ]

    def shape(*dims):
        return jax.ShapeDtypeStruct(dims, f32)

    def codes(*dims):
        return jax.ShapeDtypeStruct(dims, i16)

    edge = pl.pallas_call(
        functools.partial(edge_kernel, z),
        name="edge",
        in_specs=[far_memory(), far_memory()],
        out_specs=whole(),
        out_shape=codes(tall, z.edge),
        scratch_shapes=[
            pltpu.VMEM((2, tall, lon), f32),
            pltpu.VMEM((levels, lon), courant.dtype),
            pltpu.SemaphoreType.DMA((5,)),
        ],
        compiler_params=params(VMEM_MOST),
        cost_estimate=cost(),
    )(fields, courant)
    edge = lax.ppermute(edge, "lat", swap)
    middle, last, own = pl.pallas_call(
        functools.partial(rest_kernel, z),
        name="rest",
        in_specs=[scalars(), whole(), whole()],
        out_specs=[whole()] * 3,
        out_shape=[codes(tall, z.middle), codes(tall, z.last), codes(tall, z.edge)],
        compiler_params=params(),
        cost_estimate=cost(),
    )(place, fields, courant)
    near = lax.ppermute(own, "lat", near_pairs)
    middle = lax.ppermute(middle, "lat", swap)
    far = lax.ppermute(edge, "lat", far_pairs)
    last = lax.ppermute(last, "lat", swap)

    half_scratch = [
        pltpu.VMEM((z.rows, z.half, z.pad), f32),
        pltpu.VMEM((z.rows + 2, z.half, lon), f32),
    ]
    mine, own_winds, own_code, u = pl.pallas_call(
        functools.partial(own_kernel, z),
        name="own",
        in_specs=[scalars()] + [whole()] * 6,
        out_specs=[whole()] * 4,
        out_shape=[
            shape(z.rows, 2, z.half, z.pad),
            shape(3 * z.rows + 1, z.half, lon),
            codes(tall, 2 * z.code),
            shape(z.band + 4, 2, z.half, z.pad),
        ],
        scratch_shapes=half_scratch,
        compiler_params=params(),
        cost_estimate=cost(),
    )(place, fields, courant, edge, middle, near, far)
    other, other_winds, one, two = pl.pallas_call(
        functools.partial(other_kernel, z),
        name="other",
        in_specs=[scalars()] + [whole()] * 7,
        out_specs=[whole()] * 4,
        out_shape=[
            shape(2, 2, z.half, z.pad),
            shape(3 * z.rows + 1, z.half, lon),
            codes(tall, 2 * z.code),
            codes(tall, 2 * z.code),
        ],
        scratch_shapes=half_scratch,
        compiler_params=params(),
        cost_estimate=cost(),
    )(place, courant, edge, middle, last, near, u, own_code)
    one = lax.ppermute(one, "lat", ones)
    two = lax.ppermute(two, "lat", twos)

    tables = jnp.asarray(filter_tables(lon))
    new, inner = pl.pallas_call(
        functools.partial(inner_kernel, z),
        name="inner",
        in_specs=[scalars(), scalars()] + [whole()] * 6,
        out_specs=[whole()] * 2,
        out_shape=[shape(z.band, 2, z.half, z.pad), shape(z.rows, 2, z.half, lon)],
        compiler_params=params(),
        cost_estimate=cost(),
    )(place, cutoffs, mine, other, u, own_winds, other_winds, tables)

    column = lon // parts
    def outer(kernel, name, halo, early):
        count = parts + len(early)
        return pl.pallas_call(
            functools.partial(kernel, z, parts),
            name=name,
            in_specs=[scalars(), scalars()] + [whole()] * (6 + len(early)),
            out_specs=[whole()] * count,
            out_shape=[codes(tall, rows * column + LANE)] * count,
            scratch_shapes=[
                pltpu.VMEM((3 * z.rows + 1, z.half, lon), f32),
                pltpu.VMEM((6, 2, z.half, z.pad), f32),
                pltpu.VMEM((z.rows, 2, z.half, lon), f32),
            ],
            compiler_params=params(),
            cost_estimate=cost(),
        )(place, cutoffs, new, inner, own_winds, other_winds, halo, tables, *early)

    blocks = outer(late_kernel, "late", two, outer(early_kernel, "early", one, []))

    got = []
    for i, block in enumerate(blocks):
        b, across = i % parts, int(i < parts)
        pairs = [
            (k * parts + j, (k ^ across) * parts + (j ^ b)) for k in range(lats) for j in range(parts)
        ]
        got.append(lax.ppermute(block, ("lat", "lev"), pairs) if i != parts else block)
    far = [i for i in range(2 * parts) if i % 2 == 0 and i != parts]
    scales = pl.pallas_call(
        functools.partial(scale_kernel, rows * column),
        name="scales",
        in_specs=[whole()] * len(far),
        out_specs=whole(),
        out_shape=shape(len(far), tall, LANE),
        compiler_params=params(),
        cost_estimate=cost(),
    )(*[got[i] for i in far])

    count = remap_weights.shape[0]
    upward = np.triu(np.ones((count, count), np.float32), 1) + 0.5 * np.eye(count, dtype=np.float32)
    upward = jnp.asarray(upward)
    surface = lax.dynamic_slice_in_dim(surface, lev * column, column, 1)
    remapped, geopotential = pl.pallas_call(
        functools.partial(column_kernel, z, parts, far),
        name="columns",
        in_specs=[scalars()] + [whole()] * (len(got) + 4),
        out_specs=[far_memory()] * 2,
        out_shape=[shape(2, rows, count, column), shape(rows, count, column)],
        scratch_shapes=[
            pltpu.VMEM((2, rows, count, column), f32),
            pltpu.VMEM((rows, count, column), f32),
            pltpu.SemaphoreType.DMA((3 * rows,)),
        ],
        compiler_params=params(),
        cost_estimate=cost(),
    )(place, *got, scales, remap_weights, upward, surface[:, None, :])
    return remapped, geopotential


def with_halo(shard, width):
    size, length = lax.axis_size("lat"), shard.shape[1]
    up = [(i, (i + 1) % size) for i in range(size - 1)]
    down = [(j, i) for i, j in up]
    before = lax.ppermute(lax.slice_in_dim(shard, length - width, length, axis=1), "lat", up)
    after = lax.ppermute(lax.slice_in_dim(shard, 0, width, axis=1), "lat", down)
    return jnp.concatenate([before, shard, after], axis=1)


def plain_shards(fields, courant, cutoffs, surface, remap_weights):
    _, rows, _, lon = fields.shape
    exact = lax.Precision.HIGHEST
    cut = lax.dynamic_slice_in_dim(cutoffs, lax.axis_index("lat") * rows, rows)
    waves = np.arange(KMAX)
    angle = (np.arange(lon)[:, None] * waves[None, :] % lon) * (2.0 * math.pi / lon)
    table = jnp.asarray(np.concatenate([np.cos(angle), np.sin(angle)], axis=1).astype(np.float32))
    number = jnp.asarray(np.concatenate([waves, waves]).astype(np.int32))
    weight = jnp.where(number[None] <= cut[:, None], jnp.where(number == 0, 1.0, 2.0)[None] / lon, 0.0)
    flagged = cut < lon // 2

    def smooth(values):
        wave = jnp.einsum("frln,nk->frlk", values, table, precision=exact) * weight[None, :, None]
        low = jnp.einsum("frlk,nk->frln", wave, table, precision=exact)
        return jnp.where(flagged[None, :, None, None], low, values)

    winds = with_halo(courant, 1).astype(jnp.float32)
    east, north = winds[0, 1:-1], winds[1]
    face_x = (east + jnp.roll(east, -1, -1)) / 24.0
    face_y = (north[:-1] + north[1:]) / 24.0
    u = fields
    for _ in range(2):
        wide = with_halo(u, 2)
        pair = u + jnp.roll(u, -1, -1)
        fx = face_x * (8.0 * pair - (jnp.roll(pair, 1, -1) + jnp.roll(pair, -1, -1)))
        pair = wide[:, :-1] + wide[:, 1:]
        fy = face_y * (8.0 * pair[:, 1:-1] - (pair[:, :-2] + pair[:, 2:]))
        u = u - (fx - jnp.roll(fx, 1, -1)) - (fy[:, 1:] - fy[:, :-1])
        u = lax.cond(jnp.any(flagged), smooth, lambda values: values, u)
    columns = lax.all_to_all(u, "lev", split_axis=3, concat_axis=2, tiled=True)
    remapped = jnp.einsum("pk,fjkn->fjpn", remap_weights, columns, precision=exact)
    count = remap_weights.shape[0]
    upward = np.triu(np.ones((count, count), np.float32), 1) + 0.5 * np.eye(count, dtype=np.float32)
    upward = jnp.einsum("kl,jln->jkn", jnp.asarray(upward), columns[1], precision=exact)
    width = lon // lax.axis_size("lev")
    mine = lax.dynamic_slice_in_dim(surface, lax.axis_index("lev") * width, width, 1)
    return remapped, mine[:, None] + count**-0.5 * upward


def solution(mesh):
    def program(fields, courant, cutoffs, surface, remap_weights):
        lats, parts = mesh.shape["lat"], mesh.shape["lev"]
        rows, levels = fields.shape[1] // lats, fields.shape[2] // parts
        polar = fields.shape[1] // 8
        paired = (
            lats % 2 == 0
            and rows == 4
            and levels % 16 == 0
            and polar <= 2 * rows - 2
            and fields.shape[3] % (LANE * parts) == 0
            and parts & (parts - 1) == 0
            and fields.shape[3] % (4 * KMAX) == 0
        )
        return jax.shard_map(
            shards if paired else plain_shards,
            mesh=mesh,
            in_specs=(
                P(None, "lat", "lev", None),
                P(None, "lat", "lev", None),
                P(),
                P("lat", None),
                P(),
            ),
            out_specs=(P(None, "lat", None, "lev"), P("lat", None, "lev")),
            check_vma=False,
        )(fields, courant, cutoffs, surface, remap_weights)

    return program
```

```python
import functools
import math

import jax
import jax.numpy as jnp
import ml_dtypes
import numpy as np
from jax import lax
from jax.experimental import pallas as pl
from jax.experimental.pallas import tpu as pltpu
from jax.sharding import PartitionSpec as P

KMAX = 128
LANE = 128
TOP = 32767.0
STEPS = 256.0
TINY = 2.0**-100
WIND = 81920.0
ROUND = 1.5 * 2.0**23
VMEM_LIMIT = 12 * 2**20
VMEM_MOST = 63 * 2**20


def rounded(values):
    return ((values + ROUND) - ROUND).astype(jnp.int32).astype(jnp.int16)


def lane_max(values):
    chunks = [jnp.abs(values[:, i : i + LANE]) for i in range(0, values.shape[1], LANE)]
    while len(chunks) > 1:
        pairs = [jnp.maximum(a, b) for a, b in zip(chunks[0::2], chunks[1::2])]
        chunks = pairs + chunks[2 * len(pairs) :]
    return chunks[0]


def tiled(tile, width):
    return jnp.concatenate([tile] * (width // LANE), axis=1)


def scale_code(largest):
    return jnp.ceil(jnp.log2(jnp.maximum(largest, TINY)) * STEPS)


def encoder(code):
    return TOP / jnp.exp2(code * (1.0 / STEPS))


def decoder(code16):
    code = code16.astype(jnp.int32).astype(jnp.float32)
    return jnp.exp2(code * (1.0 / STEPS)) * (1.0 / TOP)


def encode_row(values, out_ref, at):
    width = values.shape[1]
    code = scale_code(lane_max(values))
    out_ref[:, at : at + width] = rounded(values * tiled(encoder(code), width))
    out_ref[:, at + width : at + width + LANE] = code.astype(jnp.int32).astype(jnp.int16)


def decode_row(in_ref, at, width):
    scale = decoder(in_ref[:, at + width : at + width + LANE])
    values = in_ref[:, at : at + width].astype(jnp.int32).astype(jnp.float32)
    return values * tiled(scale, width)


def fold(wind):
    middle = wind.shape[1] // 2
    return jnp.concatenate([wind[:, :middle], wind[:, middle:]], axis=0)


def unfold(values):
    half = values.shape[0] // 2
    return jnp.concatenate([values[:half], values[half:]], axis=1)


def wind_codes(values):
    return rounded(values * WIND)


def wind_values(codes):
    return codes.astype(jnp.int32).astype(jnp.float32) * (1.0 / WIND)


class Sizes:
    def __init__(self, rows, levels, lon):
        self.rows, self.levels, self.lon = rows, levels, lon
        self.half = levels // 2
        self.band = 2 * rows
        self.pad = lon + 2 * LANE
        self.code = lon + LANE
        self.edge = 2 * self.code + lon // 2
        self.middle = self.edge + lon // 2
        self.last = 2 * lon + lon // 2


def put_padded(ref, index, values, lon):
    ref[index + (Ellipsis, slice(LANE, LANE + lon))] = values
    ref[index + (Ellipsis, slice(0, LANE))] = values[..., lon - LANE :]
    ref[index + (Ellipsis, slice(LANE + lon, 2 * LANE + lon))] = values[..., :LANE]


def level_half(z, wind, upper):
    wind = wind.astype(jnp.float32)
    return jnp.where(upper == 1, wind[z.half :], wind[: z.half])


def edge_kernel(z, fields_ref, courant_ref, edge_ref, rows_ref, wind_ref, sems):
    p = lax.rem(lax.axis_index("lat"), 2)
    give = pl.multiple_of((1 - p) * z.half, z.half)
    copies = [
        pltpu.make_async_copy(
            fields_ref.at[f, 2 * p + r, pl.ds(give, z.half)],
            rows_ref.at[r, pl.ds(f * z.half, z.half)],
            sems.at[2 * r + f],
        )
        for r in range(2)
        for f in range(2)
    ]
    copies.append(pltpu.make_async_copy(courant_ref.at[1, 3 * p], wind_ref, sems.at[4]))
    for copy in copies:
        copy.start()
    for r in range(2):
        copies[2 * r].wait()
        copies[2 * r + 1].wait()
        encode_row(rows_ref[r], edge_ref, r * z.code)
    copies[4].wait()
    edge_ref[:, 2 * z.code :] = wind_codes(fold(level_half(z, wind_ref[...], 1 - p)))


def rest_kernel(z, par_ref, fields_ref, courant_ref, middle_ref, last_ref, own_ref):
    p = par_ref[0]
    keep = pl.multiple_of(p * z.half, z.half)
    give = pl.multiple_of((1 - p) * z.half, z.half)

    def field_row(row, start):
        return jnp.concatenate([fields_ref[f, row, pl.ds(start, z.half)] for f in range(2)], axis=0)

    def wind(k, row, upper):
        return level_half(z, courant_ref[k, row], upper)

    edge, inner = 2 * p, 2 * (1 - p)
    outer, near = 3 * p, 3 * (1 - p)
    for r in range(2):
        encode_row(field_row(edge + r, keep), own_ref, r * z.code)
        encode_row(field_row(inner + r, give), middle_ref, r * z.code)
    own_ref[:, 2 * z.code :] = wind_codes(fold(wind(1, outer, p)))
    lon = z.lon
    middle_ref[:, 2 * z.code : z.edge] = wind_codes(fold(wind(1, near, 1 - p)))
    middle_ref[:, z.edge :] = wind_codes(fold(wind(0, near, 1 - p)))
    last_ref[:, 2 * lon :] = wind_codes(fold(wind(0, outer, 1 - p)))
    for r in range(2):
        both = jnp.concatenate([wind(k, 1 + r, 1 - p) for k in range(2)], axis=0)
        last_ref[:, r * lon : (r + 1) * lon] = wind_codes(both)


def shifted(pieces, shift, lanes):
    turned = [pltpu.roll(v, (-shift) % LANE, 1) for v in pieces]
    if shift > 0:
        return [jnp.where(lanes < LANE - shift, a, b) for a, b in zip(turned[1:-1], turned[2:])]
    return [jnp.where(lanes < -shift, a, b) for a, b in zip(turned[:-2], turned[1:-1])]


def substep(z, count_rows, base, row_of, winds_ref, write):
    count = next(n for n in (4, 3, 2, 1) if z.lon % (n * LANE) == 0)
    width = count * LANE
    lanes = lax.broadcasted_iota(jnp.int32, (z.half, LANE), 1)

    def part(at):
        def piece(k):
            return pl.ds(at + k * LANE, LANE)

        def row(j, f):
            return [row_of(j, f, piece(k + 1)) for k in range(count)]

        def start(j, f):
            pieces = [row_of(j + 2, f, piece(k)) for k in range(count + 2)]
            return [shifted(pieces, s, lanes) for s in (-2, -1, 1, 2)]

        def lon_part(j, u, moved):
            out = []
            for k in range(count):
                m2, m1, p1, p2 = (m[k] for m in moved)
                east = 7.0 * (u[k] + p1) - (m1 + p2)
                west = 7.0 * (m1 + u[k]) - (m2 + p1)
                east = winds_ref[base + j, :, piece(k)] * east
                out.append(east - winds_ref[z.rows + base + j, :, piece(k)] * west)
            return out

        for f in range(2):
            rows = [row(j, f) for j in range(4)]
            sums = [[a + b for a, b in zip(rows[j], rows[j + 1])] for j in range(3)]
            flux = None
            moved = start(0, f)
            for j in range(count_rows + 1):
                later = start(j, f) if 0 < j < count_rows else None
                new = [
                    winds_ref[2 * z.rows + base + j, :, piece(k)] * (8.0 * sums[1][k] - (sums[0][k] + sums[2][k]))
                    for k in range(count)
                ]
                if j > 0:
                    u = rows[1]
                    change = lon_part(j - 1, u, moved)
                    for k in range(count):
                        write(j - 1, f, at, k, u[k] - change[k] - (new[k] - flux[k]))
                    moved = later
                flux = new
                if j < count_rows:
                    above = row(j + 4, f)
                    rows = rows[1:] + [above]
                    sums = sums[1:] + [[a + b for a, b in zip(rows[2], rows[3])]]

    for i in range(z.lon // width):
        part(i * width)


def filter_tables(lon):
    half = lon // 2
    points = np.arange(half)
    forward, back = [], []
    for parity in range(2):
        waves = np.arange(parity, KMAX, 2)
        angle = (points[:, None] * waves[None, :] % lon) * (2.0 * math.pi / lon)
        table = np.concatenate([np.cos(angle), np.sin(angle)], axis=1).astype(np.float32)
        high = table.astype(ml_dtypes.bfloat16)
        low = (table - high.astype(np.float32)).astype(ml_dtypes.bfloat16)
        forward.append(np.concatenate([high, low], axis=1))
        turned = np.concatenate([high.T, low.T], axis=0)
        back.append(np.concatenate(np.split(turned, half // (2 * KMAX), axis=1), axis=0))
    return np.stack(forward + back)


def split(values):
    high = values.astype(jnp.bfloat16)
    return high, (values - high.astype(jnp.float32)).astype(jnp.bfloat16)


def low_pass(z, rows, cuts, table_ref):
    half = z.lon // 2
    count = len(rows)
    tall = 2 * z.half
    total = count * tall
    flat = [row.reshape(tall, z.lon) for row in rows]
    folded = []
    for parity in range(2):
        parts = [
            row[:, :half] + row[:, half:] if parity == 0 else row[:, :half] - row[:, half:]
            for row in flat
        ]
        high, low = split(jnp.concatenate(parts, axis=0))
        both = jnp.concatenate([high, low], axis=0)
        got = jnp.dot(both, table_ref[parity], preferred_element_type=jnp.float32)
        wave = got[:total, :KMAX] + got[:total, KMAX:] + (got[total:, :KMAX] + got[total:, KMAX:])
        number = 2 * (lax.broadcasted_iota(jnp.int32, (tall, KMAX), 1) % (KMAX // 2)) + parity
        doubled = jnp.where(number == 0, 1.0, 2.0) * (1.0 / z.lon)
        weight = jnp.concatenate([jnp.where(number <= cut, doubled, 0.0) for cut in cuts], axis=0)
        high, low = split(wave * weight)
        both = jnp.concatenate(
            [jnp.concatenate([high, high], axis=1), jnp.concatenate([low, low], axis=1)], axis=0
        )
        got = []
        for at in range(0, half, 2 * KMAX):
            block = table_ref[2 + parity, at : at + 2 * KMAX]
            sums = jnp.dot(both, block, preferred_element_type=jnp.float32)
            got.append(sums[:total] + sums[total:])
        folded.append(jnp.concatenate(got, axis=1))
    left, right = folded[0] + folded[1], folded[0] - folded[1]
    smooth = jnp.concatenate([left, right], axis=1)
    return [smooth[i * tall : (i + 1) * tall].reshape(2, z.half, z.lon) for i in range(count)]


def filter_rows(z, cut_ref, first_row, start, table_ref, load, store):
    nyquist = z.lon // 2
    cuts = [cut_ref[first_row + start + r] for r in range(z.rows)]
    some = functools.reduce(jnp.logical_or, [cut < nyquist for cut in cuts])

    @pl.when(some)
    def _():
        smooth = low_pass(z, [load(start + r) for r in range(z.rows)], cuts, table_ref)
        for r in range(z.rows):

            @pl.when(cuts[r] < nyquist)
            def _():
                store(start + r, smooth[r])


def north_wind(z, in_ref):
    return unfold(wind_values(in_ref[:, 2 * z.code : z.edge]))


def faces(z, cx_ref, cy_ref, winds_ref):
    lanes = lax.broadcasted_iota(jnp.int32, (z.half, LANE), 1)
    for j in range(z.rows):
        pieces = [cx_ref[j, :, i : i + LANE] * (1.0 / 24.0) for i in range(0, z.pad, LANE)]
        for out, shift in ((j, 1), (z.rows + j, -1)):
            for k, moved in enumerate(shifted(pieces, shift, lanes)):
                winds_ref[out, :, k * LANE : (k + 1) * LANE] = pieces[k + 1] + moved
    for j in range(z.rows + 1):
        winds_ref[2 * z.rows + j] = (cy_ref[j] + cy_ref[j + 1]) * (1.0 / 24.0)


def writer(new_ref):
    def write(row, f, at, k, values):
        new_ref[row, f, :, pl.ds(at + (k + 1) * LANE, LANE)] = values

    return write


def wrap(z, new_ref, rows):
    for j in rows:
        new_ref[j, :, :, 0:LANE] = new_ref[j, :, :, z.lon : z.lon + LANE]
        new_ref[j, :, :, LANE + z.lon :] = new_ref[j, :, :, LANE : 2 * LANE]


def encode_new(z, new_ref, row, out_ref):
    for r in range(2):
        values = new_ref[row + r, :, :, LANE : LANE + z.lon]
        encode_row(values.reshape(2 * z.half, z.lon), out_ref, r * z.code)


def place_row(z, u_ref, row, in_ref, r):
    values = decode_row(in_ref, r * z.code, z.lon)
    put_padded(u_ref, (row + r,), values.reshape(2, z.half, z.lon), z.lon)


def own_kernel(
    z, par_ref, fields_ref, courant_ref, edge_ref, middle_ref, near_ref, far_ref,
    new_ref, winds_ref, code_ref, u_ref, cx_ref, cy_ref,
):
    p = par_ref[0]
    lon, half = z.lon, z.half
    keep = pl.multiple_of(p * half, half)
    for r in range(z.rows):
        own = jnp.stack([fields_ref[f, r, pl.ds(keep, half)] for f in range(2)])
        put_padded(u_ref, (z.rows * p + r + 2,), own, lon)
        put_padded(cx_ref, (r,), level_half(z, courant_ref[0, r], p), lon)
        cy_ref[r + 1] = level_half(z, courant_ref[1, r], p)
    for r in range(2):
        place_row(z, u_ref, 6 * (1 - p) + 2, edge_ref, r)
        place_row(z, u_ref, 4 - 2 * p + 2, middle_ref, r)
        place_row(z, u_ref, 10 * (1 - p), near_ref, r)
        place_row(z, u_ref, 10 * p, far_ref, r)
    cy_ref[5 * (1 - p)] = north_wind(z, middle_ref)
    cy_ref[5 * p] = north_wind(z, far_ref)
    faces(z, cx_ref, cy_ref, winds_ref)
    start = z.rows * p
    substep(z, z.rows, 0, lambda j, f, piece: u_ref[start + j, f, :, piece], winds_ref, writer(new_ref))
    encode_new(z, new_ref, 2 * p, code_ref)
    wrap(z, new_ref, range(z.rows))


def other_kernel(
    z, par_ref, courant_ref, edge_ref, middle_ref, last_ref, near_ref, u_ref, own_code_ref,
    new_ref, winds_ref, one_ref, two_ref, cx_ref, cy_ref,
):
    p = par_ref[0]
    lon, half = z.lon, z.half
    for r in range(2):
        both = wind_values(last_ref[:, r * lon : (r + 1) * lon])
        put_padded(cx_ref, (1 + r,), both[:half], lon)
        cy_ref[2 + r] = both[half:]
    easts = (last_ref[:, 2 * lon :], middle_ref[:, z.edge :])
    for east, row, in_ref in zip(easts, (3 * (1 - p), 3 * p), (edge_ref, middle_ref)):
        put_padded(cx_ref, (row,), unfold(wind_values(east)), lon)
        cy_ref[row + 1] = north_wind(z, in_ref)
    cy_ref[5 * p] = level_half(z, courant_ref[1, 3 * (1 - p)], p)
    cy_ref[5 * (1 - p)] = north_wind(z, near_ref)
    faces(z, cx_ref, cy_ref, winds_ref)
    outer = 2 * (1 - p)
    start = z.rows * (1 - p) + outer
    substep(z, 2, outer, lambda j, f, piece: u_ref[start + j, f, :, piece], winds_ref, writer(new_ref))

    def put_codes(own_ref, other_ref):
        own_ref[...] = own_code_ref[...]
        encode_new(z, new_ref, 0, other_ref)

    swapped = p + par_ref[3] == 1
    pl.when(swapped)(lambda: put_codes(one_ref, two_ref))
    pl.when(jnp.logical_not(swapped))(lambda: put_codes(two_ref, one_ref))
    wrap(z, new_ref, range(2))


def inner_kernel(
    z, par_ref, cut_ref, own_ref, other_ref, u_ref, own_winds_ref, other_winds_ref, table_ref, new_ref, inner_ref
):
    p = par_ref[0]
    own, other = z.rows * p, z.rows * (1 - p)
    for j in range(z.rows):
        new_ref[own + j] = own_ref[j]
    for j in range(2):
        new_ref[other + 2 * (1 - p) + j] = other_ref[j]
    start = other + 2 * p

    def write(row, f, at, k, values):
        writer(new_ref)(start + row, f, at, k, values)

    substep(z, 2, 2 * p, lambda j, f, piece: u_ref[start + j, f, :, piece], other_winds_ref, write)
    wrap(z, new_ref, (start, start + 1))

    def store(row, values):
        put_padded(new_ref, (row,), values, z.lon)

    for part in range(2):
        filter_rows(
            z, cut_ref, par_ref[1], part * z.rows, table_ref,
            lambda row: new_ref[row, :, :, LANE : LANE + z.lon], store,
        )
    for i, (low, base, winds_ref) in enumerate(
        ((2 * p, 2 * (1 - p), own_winds_ref), (2 * (1 - p), 2 * p, other_winds_ref))
    ):

        def keep(row, f, at, k, values):
            inner_ref[2 * i + row, f, :, pl.ds(at + k * LANE, LANE)] = values

        substep(z, 2, base, lambda j, f, piece: new_ref[low + j, f, :, piece], winds_ref, keep)


def early_kernel(z, parts, par_ref, cut_ref, new_ref, inner_ref, own_winds_ref, other_winds_ref, one_ref, table_ref, *refs):
    side = 1 - par_ref[3]
    out_refs, scratch = refs[:parts], refs[parts:]
    halves(z, parts, side, par_ref, cut_ref, new_ref, inner_ref, own_winds_ref, other_winds_ref, one_ref, table_ref, out_refs, scratch)


def late_kernel(z, parts, par_ref, cut_ref, new_ref, inner_ref, own_winds_ref, other_winds_ref, two_ref, table_ref, *refs):
    side = par_ref[3]
    early_refs, out_refs, scratch = refs[:parts], refs[parts : 3 * parts], refs[3 * parts :]
    out_refs, other_refs = out_refs[:parts], out_refs[parts:]
    own = side == par_ref[0]

    def hand_on(mine_refs, rest_refs):
        halves(z, parts, side, par_ref, cut_ref, new_ref, inner_ref, own_winds_ref, other_winds_ref, two_ref, table_ref, mine_refs, scratch)
        for a, b in zip(early_refs, rest_refs):
            b[...] = a[...]

    pl.when(own)(lambda: hand_on(other_refs, out_refs))
    pl.when(jnp.logical_not(own))(lambda: hand_on(out_refs, other_refs))


def halves(z, parts, side, par_ref, cut_ref, new_ref, inner_ref, own_winds_ref, other_winds_ref, halo_ref, table_ref, out_refs, scratch):
    winds_ref, u_ref, v_ref = scratch
    own = side == par_ref[0]
    inner_at = jnp.where(own, 0, 2)
    rows = [offset + 2 * side + r for offset, n in ((0, 2), (z.rows, 2), (2 * z.rows, 3)) for r in range(n)]

    def take(from_ref):
        for row in rows:
            winds_ref[row] = from_ref[row]

    pl.when(own)(lambda: take(own_winds_ref))
    pl.when(jnp.logical_not(own))(lambda: take(other_winds_ref))
    outer_half(z, parts, side, inner_at, par_ref, cut_ref, new_ref, inner_ref, winds_ref, halo_ref, table_ref, out_refs, u_ref, v_ref)


def outer_half(
    z, parts, side, inner_at, par_ref, cut_ref, new_ref, inner_ref, winds_ref, halo_ref, table_ref,
    out_refs, u_ref, v_ref,
):
    lon = z.lon
    tall = 2 * z.half
    base = z.rows * side

    for r in range(2):
        place_row(z, u_ref, 4 * side, halo_ref, r)
    for r in range(4):
        u_ref[2 * (1 - side) + r] = new_ref[base + r]
    for r in range(2):
        v_ref[2 * (1 - side) + r] = inner_ref[inner_at + r]

    def write(row, f, at, k, values):
        v_ref[2 * side + row, f, :, pl.ds(at + k * LANE, LANE)] = values

    substep(z, 2, 2 * side, lambda j, f, piece: u_ref[j, f, :, piece], winds_ref, write)

    def store(row, values):
        v_ref[row] = values

    filter_rows(z, cut_ref, par_ref[1] + base, 0, table_ref, lambda row: v_ref[row], store)
    column = lon // parts
    for b in range(parts):
        at = pl.multiple_of(jnp.bitwise_xor(par_ref[2], b) * column, LANE)
        values = jnp.concatenate(
            [v_ref[r, :, :, pl.ds(at, column)].reshape(tall, column) for r in range(z.rows)], axis=1
        )
        encode_row(values, out_refs[b], 0)


def scale_kernel(at, *refs):
    for i, ref in enumerate(refs[:-1]):
        refs[-1][i] = decoder(ref[:, at : at + LANE])


def column_kernel(z, parts, far, par_ref, *refs):
    got, refs = refs[: 2 * parts], refs[2 * parts :]
    scales_ref, remap_ref, upward_ref, surface_ref, out_ref, geo_ref, sums_ref, geo_sums_ref, sems = refs
    p, lev = par_ref[0], par_ref[2]
    count, column = sums_ref.shape[-2:]
    level = lax.broadcasted_iota(jnp.int32, (count, count), 1)
    within, group = level % z.half, level // z.half
    for i in range(len(got)):
        start = jnp.bitwise_xor(lev, i % parts) * z.levels + (1 - p if i < parts else p) * z.half
        level = jnp.where(group == i, start + within, level)
    order = jnp.where(lax.broadcasted_iota(jnp.int32, (count, count), 0) == level, 1.0, 0.0).astype(jnp.bfloat16)
    high, low = split(remap_ref[...])
    rows = jnp.concatenate([high, low, upward_ref[...].astype(jnp.bfloat16)], axis=0)
    rows = jnp.dot(rows, order, preferred_element_type=jnp.float32).astype(jnp.bfloat16)
    high, low, upward = (rows[i * count : (i + 1) * count] for i in range(3))
    remap = jnp.concatenate([high, low, high], axis=1)
    both = jnp.concatenate([remap, jnp.concatenate([upward, jnp.zeros_like(upward), upward], axis=1)], axis=0)
    scales = [
        scales_ref[far.index(i)] if i in far else decoder(ref[:, z.rows * column :])
        for i, ref in enumerate(got)
    ]
    copies = []
    for row in range(z.rows):
        tiles = []
        for i, ref in enumerate(got):
            codes = ref[:, row * column : (row + 1) * column].astype(jnp.int32).astype(jnp.float32)
            tiles.append(codes * tiled(scales[i], column))
        for f in range(2):
            high, low = split(jnp.concatenate([t[f * z.half : (f + 1) * z.half] for t in tiles], axis=0))
            stacked = jnp.concatenate([high, high, low], axis=0)
            result = jnp.dot(both if f else remap, stacked, preferred_element_type=jnp.float32)
            sums_ref[f, row] = result[:count]
            if f:
                geo_sums_ref[row] = surface_ref[row] + result[count:] * (count**-0.5)
        parts_out = [(sums_ref.at[f, row], out_ref.at[f, row]) for f in range(2)]
        parts_out.append((geo_sums_ref.at[row], geo_ref.at[row]))
        for k, (a, b) in enumerate(parts_out):
            copies.append(pltpu.make_async_copy(a, b, sems.at[3 * row + k]))
            copies[-1].start()
    for copy in copies:
        copy.wait()


def whole():
    return pl.BlockSpec(memory_space=pltpu.VMEM)


def scalars():
    return pl.BlockSpec(memory_space=pltpu.SMEM)


def far_memory():
    return pl.BlockSpec(memory_space=pltpu.HBM)


def params(limit=VMEM_LIMIT):
    return pltpu.CompilerParams(vmem_limit_bytes=limit)


def cost(flops=1000, data=1000):
    return pl.CostEstimate(flops=flops, bytes_accessed=data, transcendentals=0)


def shards(fields, courant, cutoffs, surface, remap_weights):
    _, rows, levels, lon = fields.shape
    z = Sizes(rows, levels, lon)
    lats, parts = lax.axis_size("lat"), lax.axis_size("lev")
    me = lax.axis_index("lat")
    parity = me % 2
    lev = lax.axis_index("lev")
    place = jnp.stack([parity, (me - parity) * rows, lev, (me // 2) % 2]).astype(jnp.int32)
    tall = 2 * z.half
    i16, f32 = jnp.int16, jnp.float32
    swap = [(i, i ^ 1) for i in range(lats)]
    rising = [(i, i + 2) for i in range(lats - 2)]
    near_pairs = [(i, j) if i % 2 else (j, i) for i, j in rising]
    far_pairs = [(j, i) if i % 2 else (i, j) for i, j in rising]

    ones, twos = [
        [pair for i, j in rising if i // 2 % 2 == odd for pair in ((i, j), (j, i))] for odd in range(2)
    ]

    def shape(*dims):
        return jax.ShapeDtypeStruct(dims, f32)

    def codes(*dims):
        return jax.ShapeDtypeStruct(dims, i16)

    edge = pl.pallas_call(
        functools.partial(edge_kernel, z),
        name="edge",
        in_specs=[far_memory(), far_memory()],
        out_specs=whole(),
        out_shape=codes(tall, z.edge),
        scratch_shapes=[
            pltpu.VMEM((2, tall, lon), f32),
            pltpu.VMEM((levels, lon), courant.dtype),
            pltpu.SemaphoreType.DMA((5,)),
        ],
        compiler_params=params(VMEM_MOST),
        cost_estimate=cost(),
    )(fields, courant)
    edge = lax.ppermute(edge, "lat", swap)
    middle, last, own = pl.pallas_call(
        functools.partial(rest_kernel, z),
        name="rest",
        in_specs=[scalars(), whole(), whole()],
        out_specs=[whole()] * 3,
        out_shape=[codes(tall, z.middle), codes(tall, z.last), codes(tall, z.edge)],
        compiler_params=params(),
        cost_estimate=cost(),
    )(place, fields, courant)
    near = lax.ppermute(own, "lat", near_pairs)
    middle = lax.ppermute(middle, "lat", swap)
    far = lax.ppermute(edge, "lat", far_pairs)
    last = lax.ppermute(last, "lat", swap)

    half_scratch = [
        pltpu.VMEM((z.rows, z.half, z.pad), f32),
        pltpu.VMEM((z.rows + 2, z.half, lon), f32),
    ]
    mine, own_winds, own_code, u = pl.pallas_call(
        functools.partial(own_kernel, z),
        name="own",
        in_specs=[scalars()] + [whole()] * 6,
        out_specs=[whole()] * 4,
        out_shape=[
            shape(z.rows, 2, z.half, z.pad),
            shape(3 * z.rows + 1, z.half, lon),
            codes(tall, 2 * z.code),
            shape(z.band + 4, 2, z.half, z.pad),
        ],
        scratch_shapes=half_scratch,
        compiler_params=params(),
        cost_estimate=cost(),
    )(place, fields, courant, edge, middle, near, far)
    other, other_winds, one, two = pl.pallas_call(
        functools.partial(other_kernel, z),
        name="other",
        in_specs=[scalars()] + [whole()] * 7,
        out_specs=[whole()] * 4,
        out_shape=[
            shape(2, 2, z.half, z.pad),
            shape(3 * z.rows + 1, z.half, lon),
            codes(tall, 2 * z.code),
            codes(tall, 2 * z.code),
        ],
        scratch_shapes=half_scratch,
        compiler_params=params(),
        cost_estimate=cost(),
    )(place, courant, edge, middle, last, near, u, own_code)
    one = lax.ppermute(one, "lat", ones)
    two = lax.ppermute(two, "lat", twos)

    tables = jnp.asarray(filter_tables(lon))
    new, inner = pl.pallas_call(
        functools.partial(inner_kernel, z),
        name="inner",
        in_specs=[scalars(), scalars()] + [whole()] * 6,
        out_specs=[whole()] * 2,
        out_shape=[shape(z.band, 2, z.half, z.pad), shape(z.rows, 2, z.half, lon)],
        compiler_params=params(),
        cost_estimate=cost(),
    )(place, cutoffs, mine, other, u, own_winds, other_winds, tables)

    column = lon // parts
    def outer(kernel, name, halo, early):
        count = parts + len(early)
        return pl.pallas_call(
            functools.partial(kernel, z, parts),
            name=name,
            in_specs=[scalars(), scalars()] + [whole()] * (6 + len(early)),
            out_specs=[whole()] * count,
            out_shape=[codes(tall, rows * column + LANE)] * count,
            scratch_shapes=[
                pltpu.VMEM((3 * z.rows + 1, z.half, lon), f32),
                pltpu.VMEM((6, 2, z.half, z.pad), f32),
                pltpu.VMEM((z.rows, 2, z.half, lon), f32),
            ],
            compiler_params=params(),
            cost_estimate=cost(),
        )(place, cutoffs, new, inner, own_winds, other_winds, halo, tables, *early)

    blocks = outer(late_kernel, "late", two, outer(early_kernel, "early", one, []))

    got = []
    for i, block in enumerate(blocks):
        b, across = i % parts, int(i < parts)
        pairs = [
            (k * parts + j, (k ^ across) * parts + (j ^ b)) for k in range(lats) for j in range(parts)
        ]
        got.append(lax.ppermute(block, ("lat", "lev"), pairs) if i != parts else block)
    far = [i for i in range(2 * parts) if i % 2 == 0 and i != parts]
    scales = pl.pallas_call(
        functools.partial(scale_kernel, rows * column),
        name="scales",
        in_specs=[whole()] * len(far),
        out_specs=whole(),
        out_shape=shape(len(far), tall, LANE),
        compiler_params=params(),
        cost_estimate=cost(),
    )(*[got[i] for i in far])

    count = remap_weights.shape[0]
    upward = np.triu(np.ones((count, count), np.float32), 1) + 0.5 * np.eye(count, dtype=np.float32)
    upward = jnp.asarray(upward)
    surface = lax.dynamic_slice_in_dim(surface, lev * column, column, 1)
    remapped, geopotential = pl.pallas_call(
        functools.partial(column_kernel, z, parts, far),
        name="columns",
        in_specs=[scalars()] + [whole()] * (len(got) + 4),
        out_specs=[far_memory()] * 2,
        out_shape=[shape(2, rows, count, column), shape(rows, count, column)],
        scratch_shapes=[
            pltpu.VMEM((2, rows, count, column), f32),
            pltpu.VMEM((rows, count, column), f32),
            pltpu.SemaphoreType.DMA((3 * rows,)),
        ],
        compiler_params=params(),
        cost_estimate=cost(),
    )(place, *got, scales, remap_weights, upward, surface[:, None, :])
    return remapped, geopotential


def with_halo(shard, width):
    size, length = lax.axis_size("lat"), shard.shape[1]
    up = [(i, (i + 1) % size) for i in range(size - 1)]
    down = [(j, i) for i, j in up]
    before = lax.ppermute(lax.slice_in_dim(shard, length - width, length, axis=1), "lat", up)
    after = lax.ppermute(lax.slice_in_dim(shard, 0, width, axis=1), "lat", down)
    return jnp.concatenate([before, shard, after], axis=1)


def plain_shards(fields, courant, cutoffs, surface, remap_weights):
    _, rows, _, lon = fields.shape
    exact = lax.Precision.HIGHEST
    cut = lax.dynamic_slice_in_dim(cutoffs, lax.axis_index("lat") * rows, rows)
    waves = np.arange(KMAX)
    angle = (np.arange(lon)[:, None] * waves[None, :] % lon) * (2.0 * math.pi / lon)
    table = jnp.asarray(np.concatenate([np.cos(angle), np.sin(angle)], axis=1).astype(np.float32))
    number = jnp.asarray(np.concatenate([waves, waves]).astype(np.int32))
    weight = jnp.where(number[None] <= cut[:, None], jnp.where(number == 0, 1.0, 2.0)[None] / lon, 0.0)
    flagged = cut < lon // 2

    def smooth(values):
        wave = jnp.einsum("frln,nk->frlk", values, table, precision=exact) * weight[None, :, None]
        low = jnp.einsum("frlk,nk->frln", wave, table, precision=exact)
        return jnp.where(flagged[None, :, None, None], low, values)

    winds = with_halo(courant, 1).astype(jnp.float32)
    east, north = winds[0, 1:-1], winds[1]
    face_x = (east + jnp.roll(east, -1, -1)) / 24.0
    face_y = (north[:-1] + north[1:]) / 24.0
    u = fields
    for _ in range(2):
        wide = with_halo(u, 2)
        pair = u + jnp.roll(u, -1, -1)
        fx = face_x * (8.0 * pair - (jnp.roll(pair, 1, -1) + jnp.roll(pair, -1, -1)))
        pair = wide[:, :-1] + wide[:, 1:]
        fy = face_y * (8.0 * pair[:, 1:-1] - (pair[:, :-2] + pair[:, 2:]))
        u = u - (fx - jnp.roll(fx, 1, -1)) - (fy[:, 1:] - fy[:, :-1])
        u = lax.cond(jnp.any(flagged), smooth, lambda values: values, u)
    columns = lax.all_to_all(u, "lev", split_axis=3, concat_axis=2, tiled=True)
    remapped = jnp.einsum("pk,fjkn->fjpn", remap_weights, columns, precision=exact)
    count = remap_weights.shape[0]
    upward = np.triu(np.ones((count, count), np.float32), 1) + 0.5 * np.eye(count, dtype=np.float32)
    upward = jnp.einsum("kl,jln->jkn", jnp.asarray(upward), columns[1], precision=exact)
    width = lon // lax.axis_size("lev")
    mine = lax.dynamic_slice_in_dim(surface, lax.axis_index("lev") * width, width, 1)
    return remapped, mine[:, None] + count**-0.5 * upward


def solution(mesh):
    def program(fields, courant, cutoffs, surface, remap_weights):
        lats, parts = mesh.shape["lat"], mesh.shape["lev"]
        rows, levels = fields.shape[1] // lats, fields.shape[2] // parts
        polar = fields.shape[1] // 8
        paired = (
            lats % 2 == 0
            and rows == 4
            and levels % 16 == 0
            and polar <= 2 * rows - 2
            and fields.shape[3] % (LANE * parts) == 0
            and parts & (parts - 1) == 0
            and fields.shape[3] % (4 * KMAX) == 0
        )
        return jax.shard_map(
            shards if paired else plain_shards,
            mesh=mesh,
            in_specs=(
                P(None, "lat", "lev", None),
                P(None, "lat", "lev", None),
                P(),
                P("lat", None),
                P(),
            ),
            out_specs=(P(None, "lat", None, "lev"), P("lat", None, "lev")),
            check_vma=False,
        )(fields, courant, cutoffs, surface, remap_weights)

    return program
```
